32 devices in a mesh: section: 4 (over x, core), dp: 8 (over z, y).
Axes of the slice: x: 2, y: 2, z: 4, core: 2. Of those that a mesh axis runs over, the one named last changes fastest.
Arguments:
- x_in: bfloat16 [16384, 384], P('dp'), may hold values from -6 to 6
- targets: float32 [16384, 192], P('dp'), may hold values from 0.02 to 20
- valid_len: int32 [32], replicated, may hold values from 64 to 512, as said below
- present_stems: int32 [32, 4], replicated, may hold values 0 or 1
- w_master: float32 [4, 192, 9216], P('section', 'dp'), may hold values from -3 to 3
- norm_gains: float32 [4, 2, 384], P('section', None, 'dp'), may hold values from 0.5 to 1.5
- gain_m: float32 [4, 2, 384], P('section', None, 'dp'), may hold values from -0.00030517578 to 0.00030517578
- gain_v: float32 [4, 2, 384], P('section', None, 'dp'), may hold values from 8e-11 to 1.3e-09
- l_stats: float32 [4, 192, 9216], P('section', 'dp'), may hold values from -1 to 1, as said below
- r_stats: float32 [4, 192, 9216], P('section', 'dp'), may hold values from -1 to 1, as said below
- l_roots: float32 [4, 192, 9216], P('section', 'dp'), may hold values from -20 to 120, as said below
- r_roots: float32 [4, 192, 9216], P('section', 'dp'), may hold values from -20 to 120, as said below
- step_count: int32 [1], replicated, may hold values from 2 to 20
Outputs:
- w_new: float32 [4, 192, 9216], P('section', 'dp')
- grad_blocks: float32 [4, 192, 9216], P('section', 'dp')
- l_new: float32 [4, 192, 9216], P('section', 'dp')
- r_new: float32 [4, 192, 9216], P('section', 'dp')
- gains_new: float32 [4, 2, 384], P('section', None, 'dp')
- m_new: float32 [4, 2, 384], P('section', None, 'dp')
- v_new: float32 [4, 2, 384], P('section', None, 'dp')
- loss_value: float32 [], replicated
- grad_norm: float32 [], replicated
- rms: float32 [4, 3], P('section')
The draws below stay inside these ranges and needn't reach their ends.
Inputs may be any that keep to these rules, and one draw needn't show every extreme that they name: `valid_len`: some segment has all 512 frames valid. `l_stats`: each block is symmetric. `r_stats`: each block is symmetric. `l_roots`: each block is symmetric. `r_roots`: each block is symmetric.
All inputs are finite; a program needn't handle non-finite values.
Results may differ from the reference program's by a relative error of at most 0.012.
The reference program's roundings to bfloat16 on the way count: a program that leaves them out, or rounds other values in their place, can miss the bound.
Values may be sent and summed in bfloat16 or wider, within the bound.
A program may use at most 128 MiB of HBM per device.

```python
import math
import jax
import jax.numpy as jnp
from jax import lax

D = 384
FF = 1536
HEADS = 8
SEG = 512
MICRO = 4
BLK = 96
NBLK = 192
SEGS = 32
TOKENS = 16384
N_SECTION = 4


def draw_targets(key, part):
    shape = (TOKENS, D // 2)
    low_log = math.log(0.02)
    high_log = math.log(20.0)
    first = jax.random.uniform(jax.random.fold_in(key, 21), shape, jnp.float32, low_log, high_log)
    return jnp.exp(first)


def draw_valid_len(key, part):
    groups = SEGS // MICRO
    group_of = jnp.arange(SEGS) // MICRO
    lowest = SEG // 8
    upper_len = lowest + (SEG - lowest) * (group_of + 1) // groups
    lengths = jax.random.randint(jax.random.fold_in(key, 1), (SEGS,), lowest, upper_len + 1)
    chosen = jax.random.randint(jax.random.fold_in(key, 2), (), SEGS - MICRO, SEGS)
    return jnp.where(jnp.arange(SEGS) == chosen, SEG, lengths).astype(jnp.int32)


def draw_w_master(key, part):
    block_size = D // 4
    area = block_size * block_size
    qkv_end = 3 * D * D // area
    out_end = qkv_end + D * D // area
    up_end = out_end + D * FF // area
    block_idx = jnp.arange(NBLK)
    spread = jnp.where(block_idx < qkv_end, D ** (-0.5), jnp.where(block_idx < out_end, 4.0 * D ** (-0.5), jnp.where(block_idx < up_end, D ** (-0.5), FF ** (-0.5)))).astype(jnp.float32)
    raw_vals = jnp.clip(jax.random.normal(key, (N_SECTION, NBLK, area), jnp.float32), -3.0, 3.0)
    return raw_vals * spread[None, :, None]


def square_blocks(key, level_lo, level_hi):
    block_size = D // 4
    level_scale = jnp.exp(jax.random.uniform(jax.random.fold_in(key, 11), (N_SECTION, NBLK, 1, 1), jnp.float32, math.log(level_lo), math.log(level_hi)))
    diag_part = jax.random.uniform(jax.random.fold_in(key, 12), (N_SECTION, NBLK, block_size), jnp.float32, 1.0, 2.0)
    off_noise = jnp.clip(jax.random.normal(jax.random.fold_in(key, 13), (N_SECTION, NBLK, block_size, block_size), jnp.float32), -4.0, 4.0)
    off_noise = (off_noise + jnp.swapaxes(off_noise, 2, 3)) * (0.3 / math.sqrt(2.0 * block_size))
    identity = jnp.eye(block_size, dtype=jnp.float32)
    matrix = level_scale * (identity * diag_part[:, :, :, None] + off_noise)
    return matrix.reshape(N_SECTION, NBLK, block_size * block_size)


def draw_l_stats(key, part):
    return square_blocks(jax.random.fold_in(key, 101), D // 4 * 1.2e-09, D // 4 * 4.8e-09)


def draw_r_stats(key, part):
    return square_blocks(jax.random.fold_in(key, 202), D // 4 * 1.2e-09, D // 4 * 4.8e-09)


def draw_l_roots(key, part):
    return square_blocks(jax.random.fold_in(key, 303), 15.0, 25.0)


def draw_r_roots(key, part):
    return square_blocks(jax.random.fold_in(key, 404), 15.0, 25.0)


def set_ends(drawn, key, smallest, largest):
    extent = drawn.shape
    spot = [jax.random.randint(jax.random.fold_in(key, axis), (), 0, extent[axis]) for axis in range(len(extent))]
    drawn = drawn.at[tuple(spot)].set(smallest)
    longest = extent.index(max(extent))
    spot[longest] = (spot[longest] + 1) % extent[longest]
    return drawn.at[tuple(spot)].set(largest)


def shard_levels(stream_key, extent, cuts, least, largest):
    loudness = 1.0
    for dim, shards_of in cuts:
        heights = jax.random.uniform(jax.random.fold_in(jax.random.fold_in(stream_key, 6), dim), (shards_of,), jnp.float32, least / len(cuts), largest / len(cuts))
        loudness = loudness * jnp.repeat(jnp.exp(heights), extent[dim] // shards_of).reshape((-1,) + (1,) * (len(extent) - 1 - dim))
    return loudness


def gaussian(own_key, shape, width, bound, split=(), kind=jnp.bfloat16):
    entries = width * jax.random.normal(own_key, shape, jnp.float32)
    if split:
        entries = entries * shard_levels(own_key, shape, split, -0.22, 0.18)
    return jnp.clip(entries, -bound, bound).astype(kind)


def setup_inputs(seed: int = 0) -> dict:
    keys = jax.random.split(jax.random.key(seed), 14)
    x_in = gaussian(keys[0], (TOKENS, D), 1.0, 6.0, ((0, 8),))
    targets = draw_targets(jax.random.fold_in(keys[13], 71), 0)
    valid_len = draw_valid_len(jax.random.fold_in(keys[13], 71), 0)
    present_stems = set_ends((jax.random.randint(keys[3], (SEGS, 4), 0, 4) < 3).astype(jnp.int32), jax.random.fold_in(keys[3], 1), 0, 1)
    w_master = draw_w_master(jax.random.fold_in(keys[13], 71), 0)
    norm_gains = jnp.clip(1.0 + 0.1 * jax.random.normal(keys[5], (N_SECTION, 2, D), jnp.float32), 0.5, 1.5)
    gain_m = gaussian(keys[6], (N_SECTION, 2, D), 0.00005, 0.00030517578, ((0, 4), (2, 8)), jnp.float32)
    gain_v = jnp.clip(jnp.exp(math.log(1.2999999965401798e-09) - 2.7880929 * jax.random.uniform(keys[7], (N_SECTION, 2, D), jnp.float32) ** shard_levels(keys[7], (N_SECTION, 2, D), ((0, 4), (2, 8)), -0.2, 0.2)), 7.999999968033578e-11, 1.2999999965401798e-09)
    l_stats = draw_l_stats(jax.random.fold_in(keys[13], 71), 0)
    r_stats = draw_r_stats(jax.random.fold_in(keys[13], 71), 0)
    l_roots = draw_l_roots(jax.random.fold_in(keys[13], 71), 0)
    r_roots = draw_r_roots(jax.random.fold_in(keys[13], 71), 0)
    step_count = jax.random.randint(keys[12], (1,), 2, 21).astype(jnp.int32)
    return {"x_in": x_in, "targets": targets, "valid_len": valid_len, "present_stems": present_stems, "w_master": w_master, "norm_gains": norm_gains, "gain_m": gain_m, "gain_v": gain_v, "l_stats": l_stats, "r_stats": r_stats, "l_roots": l_roots, "r_roots": r_roots, "step_count": step_count}


@jax.custom_vjp
def low(v):
    return lax.optimization_barrier(v.astype(jnp.bfloat16)).astype(jnp.float32)

@jax.custom_vjp
def low_back(v):
    return v

def low_keep(v):
    return (low(v), None)

def low_pass(kept, grad):
    return (grad,)

def back_keep(v):
    return (v, None)

def back_low(kept, grad):
    return (low(grad),)
low.defvjp(low_keep, low_pass)
low_back.defvjp(back_keep, back_low)
HIGHEST = lax.Precision.HIGHEST

def matmul(left, right):
    return jnp.dot(left, right, precision=HIGHEST, preferred_element_type=jnp.float32)

def unblock(blocks, row_count, col_count):
    return blocks.reshape(row_count // BLK, col_count // BLK, BLK, BLK).transpose(0, 2, 1, 3).reshape(row_count, col_count)

def split_matrices(section_blocks):
    shapes = ((D, 3 * D), (D, D), (D, FF), (FF, D))
    result = []
    offset = 0
    for row_count, col_count in shapes:
        number = row_count * col_count // (BLK * BLK)
        result.append(unblock(section_blocks[offset:offset + number], row_count, col_count))
        offset = offset + number
    return result

def rms_norm(stream, gain):
    return stream * lax.rsqrt(lax.optimization_barrier(jnp.mean(stream * stream, axis=-1, keepdims=True)) + 1e-06) * gain

def layer_forward(stream, matrices, gain_pair, length):
    w_qkv, w_out, w_up, w_down = matrices
    head_dim = D // HEADS
    frames = jnp.arange(SEG)
    normed = low(rms_norm(stream, gain_pair[0]))
    qkv_all = low_back(low(matmul(normed, w_qkv)))
    queries = qkv_all[:, :D].reshape(SEG, HEADS, head_dim)
    key_rows = qkv_all[:, D:2 * D].reshape(SEG, HEADS, head_dim)
    value_rows = qkv_all[:, 2 * D:].reshape(SEG, HEADS, head_dim)
    masking = jnp.where(frames < length, 0.0, -1e+30).astype(jnp.float32)
    scores = jnp.einsum('qhe,khe->hqk', queries, key_rows, precision=HIGHEST) * head_dim ** (-0.5)
    scores = low_back(scores + masking[None, None, :])
    attn_probs = jax.nn.softmax(scores, axis=-1)
    attended = jnp.einsum('hqk,khe->qhe', low(attn_probs), value_rows, precision=HIGHEST).reshape(SEG, D)
    attended = low_back(low(attended))
    branch_attn = low_back(matmul(attended, w_out))
    middle = stream + branch_attn
    normed_two = low(rms_norm(middle, gain_pair[1]))
    pre_act = low_back(matmul(normed_two, w_up))
    hidden = low(jax.nn.gelu(pre_act, approximate=False))
    branch_ffn = low_back(matmul(hidden, w_down))
    valid = (frames < length).astype(jnp.float32)[:, None]
    sq_sums = jnp.stack([jnp.sum(valid * stream * stream), jnp.sum(valid * branch_attn * branch_attn), jnp.sum(valid * branch_ffn * branch_ffn)])
    return (middle + branch_ffn, sq_sums)

def spectral_loss(output, target, length, present_row):
    bin_count = D // 8
    spectra = output.reshape(SEG, 4, 2, bin_count)
    magnitude = jnp.sqrt(spectra[:, :, 0] ** 2 + spectra[:, :, 1] ** 2 + 0.01)
    differ = magnitude - target.reshape(SEG, 4, bin_count)
    smooth_err = jnp.sqrt(differ * differ + 0.01)
    weight = (jnp.arange(SEG) < length).astype(jnp.float32)[:, None, None] * present_row.astype(jnp.float32)[None, :, None]
    return jnp.sum(smooth_err * weight)

def run_segment(blocks_all, gains_all, segment):
    x_seg, target, length, present_row = segment
    half_way = N_SECTION // 2
    sent_list = []
    sq_rows = []
    stream = x_seg.astype(jnp.float32)
    output = stream
    for section_num in range(N_SECTION):
        if section_num > 0:
            stream = low_back(sent_list[section_num - 1])
            if section_num >= half_way:
                stream = stream + low_back(sent_list[section_num - half_way])
        output, sq_sums = layer_forward(stream, split_matrices(blocks_all[section_num]), gains_all[section_num], length)
        sq_rows.append(sq_sums)
        sent_list.append(low(output))
    return (spectral_loss(output, target, length, present_row), jnp.stack(sq_rows))

def reference(x_in, targets, valid_len, present_stems, w_master, norm_gains, gain_m, gain_v, l_stats, r_stats, l_roots, r_roots, step_count):
    frame_count = jnp.sum(valid_len).astype(jnp.float32)
    segments = (x_in.reshape(SEGS, SEG, D), targets.reshape(SEGS, SEG, D // 2), valid_len, present_stems)

    def objective(master, gain_all):
        blocks_all = low(master)
        gains_low = low(gain_all)

        def segment_fn(segment):
            return run_segment(blocks_all, gains_low, segment)
        checked = jax.checkpoint(segment_fn)

        def step_fn(loop_state, segment):
            seg_loss, sq_rows = checked(segment)
            return ((loop_state[0] + seg_loss, loop_state[1] + sq_rows), None)
        start = (jnp.zeros((), jnp.float32), jnp.zeros((N_SECTION, 3), jnp.float32))
        (total, sq_rows), unused = lax.scan(step_fn, start, segments)
        return (total / frame_count, sq_rows)
    loss_value, pullback, sq_rows = jax.vjp(objective, w_master, norm_gains, has_aux=True)
    grad_w, grad_g = pullback(jnp.ones_like(loss_value))
    rms = jnp.sqrt(sq_rows / (frame_count * D))
    grad_norm = jnp.sqrt(jnp.sum(grad_w * grad_w) + jnp.sum(grad_g * grad_g))
    clip_limit = 0.00015 * math.sqrt(N_SECTION * (NBLK * BLK * BLK + 2 * D))
    factor = clip_limit / jnp.maximum(grad_norm, clip_limit)
    grad_blocks = grad_w * factor
    square = (N_SECTION, NBLK, BLK, BLK)
    shaped = grad_blocks.reshape(square)
    l_new = 0.95 * l_stats.reshape(square) + 0.05 * jnp.einsum('sbij,sbkj->sbik', shaped, shaped, precision=HIGHEST)
    r_new = 0.95 * r_stats.reshape(square) + 0.05 * jnp.einsum('sbji,sbjk->sbik', shaped, shaped, precision=HIGHEST)
    left_side = jnp.einsum('sbij,sbjk->sbik', l_roots.reshape(square), shaped, precision=HIGHEST)
    precond = jnp.einsum('sbij,sbjk->sbik', left_side, r_roots.reshape(square), precision=HIGHEST)
    w_new = w_master - 0.5 * (precond.reshape(w_master.shape) + 0.01 * w_master)
    grad_gains = grad_g * factor
    m_new = 0.9 * gain_m + 0.1 * grad_gains
    v_new = 0.999 * gain_v + 0.001 * grad_gains * grad_gains
    step_num = step_count[0].astype(jnp.float32)
    m_hat = m_new / (1.0 - jnp.power(0.9, step_num))
    v_hat = v_new / (1.0 - jnp.power(0.999, step_num))
    gains_new = norm_gains - 0.5 * m_hat / (jnp.sqrt(v_hat) + 1e-08)
    return (w_new, grad_blocks, l_new.reshape(w_master.shape), r_new.reshape(w_master.shape), gains_new, m_new, v_new, loss_value, grad_norm, rms)
```

```python
import functools
import math

import jax
import jax.numpy as jnp
from jax import lax
from jax.experimental import pallas as pl
from jax.experimental.pallas import tpu as pltpu
from jax.sharding import PartitionSpec as P

HEADS = 8
F32 = jnp.float32
BF16 = jnp.bfloat16
VMEM_LIMIT = 60 * 1024 * 1024


def dot_nn(a, b):
    return lax.dot_general(a, b, (((1,), (0,)), ((), ())), preferred_element_type=F32)


def dot_nt(a, b):
    return lax.dot_general(a, b, (((1,), (1,)), ((), ())), preferred_element_type=F32)


def dot_tn(a, b):
    return lax.dot_general(a, b, (((0,), (0,)), ((), ())), preferred_element_type=F32)


def gelu_parts(x):
    ax = jnp.abs(x)
    bell = jnp.exp(-0.5 * x * x)
    t = 1.0 / (1.0 + (0.3275911 * 0.7071067811865476) * ax)
    poly = t * (
        0.5 * 0.254829592
        + t
        * (
            0.5 * -0.284496736
            + t * (0.5 * 1.421413741 + t * (0.5 * -1.453152027 + t * (0.5 * 1.061405429)))
        )
    )
    tail = poly * bell
    cdf = jnp.where(x >= 0.0, 1.0 - tail, tail)
    return x * cdf, cdf + x * bell * 0.3989422804014327


def stack_quads(w_ref, first, step, number):
    return jnp.concatenate([w_ref[0, first + step * i] for i in range(number)], axis=0)


def forward_kernel(
    layers, half, info_ref, scale_ref, x_ref, target_ref, w_ref, gain_ref,
    probs_ref, heads_ref, att_ref, middle_ref, hidden_ref, slope_ref, sent_ref, loss_grad_ref, stats_ref,
    hold_ref, out_ref,
):
    seg, width = x_ref.shape
    dim = width // HEADS
    part = width // 4
    layer = pl.program_id(0)
    rows = 256
    chunks = seg // rows
    length = info_ref[0]

    @pl.when(layer == 0)
    def _():
        sent_ref[0] = x_ref[...]
        stats_ref[...] = jnp.zeros_like(stats_ref)

    def stream_of(at):
        prev = sent_ref[layer, at].astype(F32)
        skip = sent_ref[jnp.maximum(layer + 1 - half, 0), at].astype(F32)
        return prev + jnp.where(layer >= half, skip, 0.0)

    gain_one = gain_ref[0, 0:1]
    gain_two = gain_ref[0, 1:2]

    def qkv_step(i, _):
        at = pl.ds(pl.multiple_of(i * rows, rows), rows)
        stream = stream_of(at)
        factor = lax.rsqrt(jnp.mean(stream * stream, axis=-1, keepdims=True) + 1e-06)
        normed = (stream * factor * gain_one).astype(BF16)
        for t in range(3):
            qkv = dot_nn(normed, stack_quads(w_ref, t, 3, 4)).astype(BF16)
            for h in range(HEADS):
                heads_ref[0, t * HEADS + h, at] = qkv[:, h * dim : (h + 1) * dim]
        return 0

    lax.fori_loop(0, chunks, qkv_step, 0)
    frames = lax.broadcasted_iota(jnp.int32, (1, seg), 1)
    masking = jnp.where(frames < length, 0.0, -1e30).astype(F32)

    def head_step(h, _):
        keys = heads_ref[0, HEADS + h]
        values = heads_ref[0, 2 * HEADS + h]
        for i in range(chunks):
            at = pl.ds(i * rows, rows)
            scores = dot_nt(heads_ref[0, h, at], keys) * dim ** (-0.5) + masking
            top = jnp.max(scores, axis=-1, keepdims=True)
            expd = jnp.exp(scores - top)
            probs = (expd * (1.0 / jnp.sum(expd, axis=-1, keepdims=True))).astype(BF16)
            probs_ref[0, h, at] = probs
            hold_ref[h, at] = dot_nn(probs, values).astype(BF16)
        return 0

    lax.fori_loop(0, HEADS, head_step, 0)

    def ffn_step(i, _):
        at = pl.ds(pl.multiple_of(i * rows, rows), rows)
        attended = jnp.concatenate([hold_ref[h, at] for h in range(HEADS)], axis=1)
        att_ref[0, at] = attended
        branch_attn = dot_nn(attended, stack_quads(w_ref, 12, 1, 4))
        stream = stream_of(at)
        middle = stream + branch_attn
        middle_ref[0, at] = middle
        factor = lax.rsqrt(jnp.mean(middle * middle, axis=-1, keepdims=True) + 1e-06)
        normed = (middle * factor * gain_two).astype(BF16)
        branch_ffn = jnp.zeros((rows, width), F32)
        for c in range(4):
            pre_act = dot_nn(normed, stack_quads(w_ref, 16 + c, 4, 4))
            hidden, slope = gelu_parts(pre_act)
            hidden = hidden.astype(BF16)
            hidden_ref[0, c, at] = hidden
            slope_ref[0, c, at] = slope.astype(BF16)
            branch_ffn = branch_ffn + dot_nn(hidden, stack_quads(w_ref, 32 + 4 * c, 1, 4))
        output = middle + branch_ffn
        out_ref[at] = output
        sent_ref[jnp.minimum(layer + 1, layers - 1), at] = jnp.where(
            layer + 1 < layers, output.astype(BF16), sent_ref[layers - 1, at]
        )
        valid = (lax.broadcasted_iota(jnp.int32, (rows, 1), 0) + i * rows < length).astype(F32)
        for k, value in enumerate((stream, branch_attn, branch_ffn)):
            stats_ref[layer, k : k + 1] += jnp.sum(valid * value * value, axis=0, keepdims=True)
        return 0

    lax.fori_loop(0, chunks, ffn_step, 0)

    @pl.when(layer == layers - 1)
    def _():
        bins = width // 8
        lane = lax.broadcasted_iota(jnp.int32, (1, width), 1)
        is_real = lax.rem(lane, 2 * bins) < bins
        stem = lane // (2 * bins)
        present = jnp.zeros((1, width), F32)
        for k in range(4):
            present = jnp.where(stem == k, info_ref[1 + k].astype(F32), present)
        inverse = scale_ref[0]

        def loss_step(i, _):
            at = pl.ds(pl.multiple_of(i * rows, rows), rows)
            output = out_ref[at]
            square = output * output
            other = jnp.where(
                is_real, pltpu.roll(square, width - bins, 1), pltpu.roll(square, bins, 1)
            )
            magnitude = jnp.sqrt(square + other + 0.01)
            goal = target_ref[at]
            goal = jnp.concatenate(
                [goal[:, (k // 2) * bins : (k // 2 + 1) * bins] for k in range(8)], axis=1
            )
            differ = magnitude - goal
            smooth = jnp.sqrt(differ * differ + 0.01)
            valid = (lax.broadcasted_iota(jnp.int32, (rows, 1), 0) + i * rows < length).astype(F32)
            weight = valid * present
            loss_grad_ref[at] = weight * differ * output * inverse / (smooth * magnitude)
            stats_ref[0, 3:4] += jnp.sum(
                jnp.where(is_real, weight * smooth, 0.0), axis=0, keepdims=True
            )
            return 0

        lax.fori_loop(0, chunks, loss_step, 0)


def norm_reverse(value, gain, grad):
    factor = lax.rsqrt(jnp.mean(value * value, axis=-1, keepdims=True) + 1e-06)
    scaled = grad * gain
    mean = jnp.mean(value * scaled, axis=-1, keepdims=True)
    unit = value * factor
    back = factor * scaled - unit * (factor * factor * mean)
    return back, jnp.sum(grad * unit, axis=0, keepdims=True), (unit * gain).astype(BF16)


def backward_kernel(
    layers, half, loss_grad_ref, w_ref, gain_ref, sent_ref,
    probs_ref, heads_ref, att_ref, middle_ref, hidden_ref, slope_ref,
    grads_ref, gain_grad_ref,
    sends_ref, dffn_ref, dpre_ref, normed_ref, dmid_ref, datt_ref, dhold_ref, dheads_ref, dqkv_ref,
):
    seg, width = loss_grad_ref.shape
    dim = width // HEADS
    part = width // 4
    layer = layers - 1 - pl.program_id(0)
    rows = 256
    chunks = seg // rows
    gain_one = gain_ref[0, 0:1]
    gain_two = gain_ref[0, 1:2]
    gain_grad_ref[...] = jnp.zeros_like(gain_grad_ref)

    @pl.when(layer == layers - 1)
    def _():
        sends_ref[...] = jnp.zeros_like(sends_ref)

    def put_grad(first, step, value):
        for r in range(4):
            grads_ref[0, first + step * r] = value[r * part : (r + 1) * part].astype(grads_ref.dtype)

    def ffn_step(i, _):
        at = pl.ds(pl.multiple_of(i * rows, rows), rows)
        later = sends_ref[jnp.minimum(layer + 1, layers - 1), at].astype(F32)
        skip = sends_ref[jnp.minimum(layer + half, layers - 1), at].astype(F32)
        upstream = jnp.where(
            layer == layers - 1, loss_grad_ref[at], later + jnp.where(layer + half < layers, skip, 0.0)
        )
        dffn = upstream.astype(BF16)
        dffn_ref[at] = dffn
        dnormed = jnp.zeros((rows, width), F32)
        for c in range(4):
            dhidden = dot_nt(dffn, stack_quads(w_ref, 32 + 4 * c, 1, 4))
            dpre = (dhidden * slope_ref[0, c, at].astype(F32)).astype(BF16)
            dpre_ref[c, at] = dpre
            dnormed = dnormed + dot_nt(dpre, stack_quads(w_ref, 16 + c, 4, 4))
        back, gain_grad, normed = norm_reverse(middle_ref[0, at], gain_two, dnormed)
        gain_grad_ref[0, 1:2] += gain_grad
        normed_ref[at] = normed
        dmid = upstream + back
        dmid_ref[at] = dmid
        datt = dmid.astype(BF16)
        datt_ref[at] = datt
        dattended = dot_nt(datt, stack_quads(w_ref, 12, 1, 4)).astype(BF16)
        for h in range(HEADS):
            dhold_ref[h, at] = dattended[:, h * dim : (h + 1) * dim]
        return 0

    lax.fori_loop(0, chunks, ffn_step, 0)

    def ffn_grad_step(c, _):
        put_grad(32 + 4 * c, 1, dot_tn(hidden_ref[0, c], dffn_ref[...]))
        put_grad(16 + c, 4, dot_tn(normed_ref[...], dpre_ref[c]))
        return 0

    lax.fori_loop(0, 4, ffn_grad_step, 0)
    put_grad(12, 1, dot_tn(att_ref[0], datt_ref[...]))

    def head_step(h, _):
        queries = heads_ref[0, h]
        keys = heads_ref[0, HEADS + h]
        values = heads_ref[0, 2 * HEADS + h]
        dkeys = jnp.zeros((seg, dim), F32)
        dvalues = jnp.zeros((seg, dim), F32)
        for i in range(chunks):
            at = pl.ds(i * rows, rows)
            probs = probs_ref[0, h, at]
            dhold = dhold_ref[h, at]
            dprobs = dot_nt(dhold, values)
            wide = probs.astype(F32)
            dot_sum = jnp.sum(wide * dprobs, axis=-1, keepdims=True)
            dscores = (wide * (dprobs - dot_sum)).astype(BF16)
            dheads_ref[h, at] = (dot_nn(dscores, keys) * dim ** (-0.5)).astype(BF16)
            dvalues = dvalues + dot_tn(probs, dhold)
            dkeys = dkeys + dot_tn(dscores, heads_ref[0, h, at])
        dheads_ref[HEADS + h] = (dkeys * dim ** (-0.5)).astype(BF16)
        dheads_ref[2 * HEADS + h] = dvalues.astype(BF16)
        return 0

    lax.fori_loop(0, HEADS, head_step, 0)

    def qkv_step(i, _):
        at = pl.ds(pl.multiple_of(i * rows, rows), rows)
        dnormed = jnp.zeros((rows, width), F32)
        for t in range(3):
            dqkv = jnp.concatenate([dheads_ref[t * HEADS + h, at] for h in range(HEADS)], axis=1)
            dqkv_ref[t, at] = dqkv
            dnormed = dnormed + dot_nt(dqkv, stack_quads(w_ref, t, 3, 4))
        prev = sent_ref[layer, at].astype(F32)
        skip = sent_ref[jnp.maximum(layer + 1 - half, 0), at].astype(F32)
        stream = prev + jnp.where(layer >= half, skip, 0.0)
        back, gain_grad, normed = norm_reverse(stream, gain_one, dnormed)
        gain_grad_ref[0, 0:1] += gain_grad
        normed_ref[at] = normed
        sends_ref[layer, at] = (dmid_ref[at] + back).astype(BF16)
        return 0

    lax.fori_loop(0, chunks, qkv_step, 0)

    def qkv_grad_step(t, _):
        put_grad(t, 3, dot_tn(normed_ref[...], dqkv_ref[t]))
        return 0

    lax.fori_loop(0, 3, qkv_grad_step, 0)


FF = 1536


def from_behind(value, axis, by):
    peers = lax.axis_size(axis)
    pairs = [(i, i + by) for i in range(peers) if 0 <= i + by < peers]
    return lax.ppermute(value, axis, pairs)


def unblock(blocks, row_count, col_count, block_size):
    return (
        blocks.reshape(row_count // block_size, col_count // block_size, block_size, block_size)
        .transpose(0, 2, 1, 3)
        .reshape(row_count, col_count)
    )


def to_blocks(matrix, block_size):
    row_count, col_count = matrix.shape
    return (
        matrix.reshape(row_count // block_size, block_size, col_count // block_size, block_size)
        .transpose(0, 2, 1, 3)
        .reshape(-1, block_size * block_size)
    )


def split_matrices(blocks, model_width):
    block_size = model_width // 4
    shapes = (
        (model_width, 3 * model_width),
        (model_width, model_width),
        (model_width, FF),
        (FF, model_width),
    )
    result = []
    offset = 0
    for row_count, col_count in shapes:
        number = row_count * col_count // (block_size * block_size)
        result.append(unblock(blocks[offset : offset + number], row_count, col_count, block_size))
        offset = offset + number
    return result


def rms_norm(stream, gain):
    factor = lax.rsqrt(jnp.mean(stream * stream, axis=-1, keepdims=True) + 1e-06)
    return (stream * factor * gain, factor)


def norm_back(stream, factor, gain, grad):
    scaled = grad * gain
    grad_in = factor * scaled - stream * factor**3 * jnp.mean(
        stream * scaled, axis=-1, keepdims=True
    )
    return (grad_in, jnp.sum(grad * stream * factor, axis=0))


def gelu_slope(pre_act):
    return (
        0.5 * (1.0 + lax.erf(pre_act * 0.7071067811865476))
        + pre_act * jnp.exp(-0.5 * pre_act * pre_act) * 0.3989422804014327
    )


def layer_forward(stream, matrices, gain_pair, length):
    w_qkv, w_out, w_up, w_down = matrices
    row_count, model_width = stream.shape
    head_dim = model_width // HEADS
    frames = jnp.arange(row_count)
    norm_one, scale_one = rms_norm(stream, gain_pair[0])
    normed = norm_one.astype(BF16)
    qkv_all = jnp.dot(normed, w_qkv, preferred_element_type=jnp.float32).astype(BF16)
    queries = qkv_all[:, :model_width].reshape(row_count, HEADS, head_dim)
    key_rows = qkv_all[:, model_width : 2 * model_width].reshape(row_count, HEADS, head_dim)
    value_rows = qkv_all[:, 2 * model_width :].reshape(row_count, HEADS, head_dim)
    masking = jnp.where(frames < length, 0.0, -1e30).astype(jnp.float32)
    scores = jnp.einsum(
        "qhe,khe->hqk", queries, key_rows, preferred_element_type=jnp.float32
    ) * head_dim ** (-0.5)
    attn_probs = jax.nn.softmax(scores + masking[None, None, :], axis=-1)
    probs_low = attn_probs.astype(BF16)
    attended = (
        jnp.einsum("hqk,khe->qhe", probs_low, value_rows, preferred_element_type=jnp.float32)
        .reshape(row_count, model_width)
        .astype(BF16)
    )
    branch_attn = jnp.dot(attended, w_out, preferred_element_type=jnp.float32)
    middle = stream + branch_attn
    norm_two, scale_two = rms_norm(middle, gain_pair[1])
    normed_two = norm_two.astype(BF16)
    pre_act = jnp.dot(normed_two, w_up, preferred_element_type=jnp.float32)
    hidden = jax.nn.gelu(pre_act, approximate=False).astype(BF16)
    branch_ffn = jnp.dot(hidden, w_down, preferred_element_type=jnp.float32)
    kept_vals = (
        scale_one,
        normed,
        queries,
        key_rows,
        value_rows,
        attn_probs,
        probs_low,
        attended,
        middle,
        scale_two,
        normed_two,
        pre_act,
        hidden,
    )
    return (middle + branch_ffn, branch_attn, branch_ffn, kept_vals)


def layer_backward(stream, matrices, gain_pair, length, upstream):
    w_qkv, w_out, w_up, w_down = matrices
    row_count, model_width = stream.shape
    head_dim = model_width // HEADS
    output, branch_attn, branch_ffn, kept_vals = layer_forward(stream, matrices, gain_pair, length)
    (
        scale_one,
        normed,
        queries,
        key_rows,
        value_rows,
        attn_probs,
        probs_low,
        attended,
        middle,
        scale_two,
        normed_two,
        pre_act,
        hidden,
    ) = kept_vals
    grad_ffn = upstream.astype(BF16)
    grad_down = jnp.dot(hidden.T, grad_ffn, preferred_element_type=jnp.float32)
    grad_hidden = jnp.dot(grad_ffn, w_down.T, preferred_element_type=jnp.float32)
    grad_pre = (grad_hidden * gelu_slope(pre_act)).astype(BF16)
    grad_up = jnp.dot(normed_two.T, grad_pre, preferred_element_type=jnp.float32)
    back_mid, gain_two = norm_back(
        middle,
        scale_two,
        gain_pair[1],
        jnp.dot(grad_pre, w_up.T, preferred_element_type=jnp.float32),
    )
    grad_mid = upstream + back_mid
    grad_branch = grad_mid.astype(BF16)
    grad_out = jnp.dot(attended.T, grad_branch, preferred_element_type=jnp.float32)
    grad_att = (
        jnp.dot(grad_branch, w_out.T, preferred_element_type=jnp.float32)
        .astype(BF16)
        .reshape(row_count, HEADS, head_dim)
    )
    grad_value = jnp.einsum("hqk,qhe->khe", probs_low, grad_att, preferred_element_type=jnp.float32)
    grad_probs = jnp.einsum(
        "qhe,khe->hqk", grad_att, value_rows, preferred_element_type=jnp.float32
    )
    grad_scores = (
        attn_probs * (grad_probs - jnp.sum(attn_probs * grad_probs, axis=-1, keepdims=True))
    ).astype(BF16)
    grad_query = jnp.einsum(
        "hqk,khe->qhe", grad_scores, key_rows, preferred_element_type=jnp.float32
    ) * head_dim ** (-0.5)
    grad_key = jnp.einsum(
        "hqk,qhe->khe", grad_scores, queries, preferred_element_type=jnp.float32
    ) * head_dim ** (-0.5)
    grad_qkv = jnp.concatenate(
        [
            grad_query.reshape(row_count, model_width),
            grad_key.reshape(row_count, model_width),
            grad_value.reshape(row_count, model_width),
        ],
        axis=1,
    ).astype(BF16)
    grad_wqkv = jnp.dot(normed.T, grad_qkv, preferred_element_type=jnp.float32)
    back_in, gain_one = norm_back(
        stream,
        scale_one,
        gain_pair[0],
        jnp.dot(grad_qkv, w_qkv.T, preferred_element_type=jnp.float32),
    )
    return (
        grad_mid + back_in,
        (grad_wqkv, grad_out, grad_up, grad_down),
        jnp.stack([gain_one, gain_two]),
    )


def spectral_terms(output, target, length, present_row, frame_count):
    row_count, model_width = output.shape
    bin_count = model_width // 8
    spectra = output.reshape(row_count, 4, 2, bin_count)
    real_part = spectra[:, :, 0]
    imag_part = spectra[:, :, 1]
    magnitude = jnp.sqrt(real_part * real_part + imag_part * imag_part + 0.01)
    differ = magnitude - target.reshape(row_count, 4, bin_count)
    smooth_err = jnp.sqrt(differ * differ + 0.01)
    weight = (jnp.arange(row_count) < length).astype(jnp.float32)[:, None, None] * present_row[
        None, :, None
    ]
    loss_slope = weight * differ / smooth_err / magnitude / frame_count
    grad_spec = jnp.stack([loss_slope * real_part, loss_slope * imag_part], axis=2).reshape(
        row_count, model_width
    )
    return (jnp.sum(smooth_err * weight), grad_spec)


def pipelined_body(
    x_in,
    targets,
    valid_len,
    present_stems,
    w_master,
    norm_gains,
    gain_m,
    gain_v,
    l_stats,
    r_stats,
    l_roots,
    r_roots,
    step_count,
):
    model_width = x_in.shape[1]
    block_size = model_width // 4
    sections = lax.axis_size("section")
    section_idx = lax.axis_index("section")
    half_way = sections // 2
    groups = lax.axis_size("dp")
    group_idx = lax.axis_index("dp")
    micro_count = valid_len.shape[0] // groups
    seg_len = x_in.shape[0] // micro_count
    own_blocks = w_master.shape[1]
    own_gain = norm_gains.shape[2]
    full_w, full_g = (
        lax.all_gather(w_master.astype(BF16), "dp", axis=1, tiled=True),
        lax.all_gather(norm_gains.astype(BF16), "dp", axis=2, tiled=True),
    )
    matrices = split_matrices(full_w[0], model_width)
    gain_pair = full_g[0].astype(jnp.float32)
    lengths = lax.dynamic_slice_in_dim(valid_len, group_idx * micro_count, micro_count)
    stem_flags = lax.dynamic_slice_in_dim(
        present_stems, group_idx * micro_count, micro_count
    ).astype(jnp.float32)
    frame_count = jnp.sum(valid_len).astype(jnp.float32)
    decoder = section_idx >= half_way
    encoder = section_idx < half_way
    is_last = section_idx == sections - 1
    act_shape = (micro_count, seg_len, model_width)

    def forward_step(step_idx, loop_state):
        in_rows, kept_prev, skip_store, loss_grads, loss_sum, sq_sums = loop_state
        micro_idx = step_idx - section_idx
        active = (micro_idx >= 0) & (micro_idx < micro_count)
        slot_idx = jnp.clip(micro_idx, 0, micro_count - 1)
        fresh_rows = lax.dynamic_slice_in_dim(x_in, slot_idx * seg_len, seg_len, 0)
        previous = jnp.where(section_idx == 0, fresh_rows, in_rows)
        stream = previous.astype(jnp.float32) + jnp.where(
            decoder, skip_store[slot_idx].astype(jnp.float32), 0.0
        )
        length = lengths[slot_idx]
        target = lax.dynamic_slice_in_dim(targets, slot_idx * seg_len, seg_len, 0)

        def forward_compute_fn(operand):
            output, branch_attn, branch_ffn, kept_vals = layer_forward(
                stream, matrices, gain_pair, length
            )
            valid = (jnp.arange(seg_len) < length).astype(jnp.float32)[:, None]
            squares = jnp.stack(
                [
                    jnp.sum(valid * stream * stream),
                    jnp.sum(valid * branch_attn * branch_attn),
                    jnp.sum(valid * branch_ffn * branch_ffn),
                ]
            )
            seg_loss, grad_spec = spectral_terms(
                output, target, length, stem_flags[slot_idx], frame_count
            )
            return (output, squares, seg_loss, grad_spec)

        def forward_spare_fn(operand):
            empty = jnp.zeros((seg_len, model_width), jnp.float32)
            return (empty, jnp.zeros((3,), jnp.float32), jnp.zeros((), jnp.float32), empty)

        output, squares, seg_loss, grad_spec = lax.cond(
            active, forward_compute_fn, forward_spare_fn, 0
        )
        kept_prev = kept_prev.at[slot_idx].set(jnp.where(active, previous, kept_prev[slot_idx]))
        loss_grads = loss_grads.at[slot_idx].set(
            jnp.where(active & is_last, grad_spec, loss_grads[slot_idx])
        )
        loss_sum = loss_sum + jnp.where(is_last, seg_loss, 0.0)
        sq_sums = sq_sums + squares
        sent_rows = output.astype(BF16)
        in_rows = from_behind(sent_rows, "section", 1)
        from_encoder = from_behind(sent_rows, "section", half_way)
        recv_idx = step_idx - section_idx + half_way
        usable = decoder & (recv_idx >= 0) & (recv_idx < micro_count)
        recv_slot = jnp.clip(recv_idx, 0, micro_count - 1)
        skip_store = skip_store.at[recv_slot].set(
            jnp.where(usable, from_encoder, skip_store[recv_slot])
        )
        return (in_rows, kept_prev, skip_store, loss_grads, loss_sum, sq_sums)

    start_state = (
        jnp.zeros((seg_len, model_width), BF16),
        jnp.zeros(act_shape, BF16),
        jnp.zeros(act_shape, BF16),
        jnp.zeros(act_shape, jnp.float32),
        jnp.zeros((), jnp.float32),
        jnp.zeros((3,), jnp.float32),
    )
    unused_rows, kept_prev, skip_store, loss_grads, loss_sum, sq_sums = lax.fori_loop(
        0, micro_count + sections - 1, forward_step, start_state
    )

    def backward_step(step_idx, loop_state):
        in_grads, skip_grad_store, grad_mats, grad_gains = loop_state
        micro_idx = step_idx - (sections - 1 - section_idx)
        active = (micro_idx >= 0) & (micro_idx < micro_count)
        slot_idx = jnp.clip(micro_idx, 0, micro_count - 1)
        upstream = jnp.where(
            is_last,
            loss_grads[slot_idx],
            in_grads.astype(jnp.float32)
            + jnp.where(encoder, skip_grad_store[slot_idx].astype(jnp.float32), 0.0),
        )
        stream = kept_prev[slot_idx].astype(jnp.float32) + jnp.where(
            decoder, skip_store[slot_idx].astype(jnp.float32), 0.0
        )
        length = lengths[slot_idx]

        def backward_compute_fn(operand):
            return layer_backward(stream, matrices, gain_pair, length, upstream)

        def backward_spare_fn(operand):
            return (
                jnp.zeros_like(stream),
                tuple((jnp.zeros(mat.shape, jnp.float32) for mat in matrices)),
                jnp.zeros((2, model_width), jnp.float32),
            )

        grad_stream, layer_mats, layer_gains = lax.cond(
            active, backward_compute_fn, backward_spare_fn, 0
        )
        grad_mats = tuple((total + piece for total, piece in zip(grad_mats, layer_mats)))
        grad_gains = grad_gains + layer_gains
        grad_rows = grad_stream.astype(BF16)
        in_grads = from_behind(grad_rows, "section", -1)
        from_decoder = from_behind(grad_rows, "section", -half_way)
        recv_idx = micro_idx + half_way
        usable = encoder & (recv_idx >= 0) & (recv_idx < micro_count)
        recv_slot = jnp.clip(recv_idx, 0, micro_count - 1)
        skip_grad_store = skip_grad_store.at[recv_slot].set(
            jnp.where(usable, from_decoder, skip_grad_store[recv_slot])
        )
        return (in_grads, skip_grad_store, grad_mats, grad_gains)

    back_state = (
        jnp.zeros((seg_len, model_width), BF16),
        jnp.zeros(act_shape, BF16),
        tuple((jnp.zeros(mat.shape, jnp.float32) for mat in matrices)),
        jnp.zeros((2, model_width), jnp.float32),
    )
    unused_grads, unused_store, grad_mats, grad_gains = lax.fori_loop(
        0, micro_count + sections - 1, backward_step, back_state
    )
    grad_all = jnp.concatenate([to_blocks(mat, block_size) for mat in grad_mats], axis=0)
    summed_w, summed_g = lax.psum((grad_all, grad_gains), "dp")
    own_grad = lax.dynamic_slice_in_dim(summed_w, group_idx * own_blocks, own_blocks, 0)
    own_gain_grad = lax.dynamic_slice_in_dim(summed_g, group_idx * own_gain, own_gain, 1)
    own_square = jnp.sum(own_grad * own_grad) + jnp.sum(own_gain_grad * own_gain_grad)
    rows_local = jnp.zeros((sections, 3), jnp.float32).at[section_idx].set(sq_sums)
    total_square, loss_value, rows_total = lax.psum(
        (own_square, loss_sum / frame_count, rows_local), ("section", "dp")
    )
    grad_norm = jnp.sqrt(total_square)
    clip_limit = 0.00015 * math.sqrt(
        sections * (own_blocks * groups * block_size * block_size + 2 * model_width)
    )
    factor = clip_limit / jnp.maximum(grad_norm, clip_limit)
    grad_blocks = own_grad * factor
    square = (own_blocks, block_size, block_size)
    shaped = grad_blocks.reshape(square)
    highest = lax.Precision.HIGHEST
    l_new = 0.95 * l_stats[0].reshape(square) + 0.05 * jnp.einsum(
        "bij,bkj->bik", shaped, shaped, precision=highest
    )
    r_new = 0.95 * r_stats[0].reshape(square) + 0.05 * jnp.einsum(
        "bji,bjk->bik", shaped, shaped, precision=highest
    )
    left_side = jnp.einsum("bij,bjk->bik", l_roots[0].reshape(square), shaped, precision=highest)
    precond = jnp.einsum("bij,bjk->bik", left_side, r_roots[0].reshape(square), precision=highest)
    master = w_master[0]
    w_new = master - 0.5 * (precond.reshape(master.shape) + 0.01 * master)
    gain_grad = own_gain_grad * factor
    m_new = 0.9 * gain_m[0] + 0.1 * gain_grad
    v_new = 0.999 * gain_v[0] + 0.001 * gain_grad * gain_grad
    step_num = step_count[0].astype(jnp.float32)
    m_hat = m_new / (1.0 - jnp.power(0.9, step_num))
    v_hat = v_new / (1.0 - jnp.power(0.999, step_num))
    gains_new = norm_gains[0] - 0.5 * m_hat / (jnp.sqrt(v_hat) + 1e-08)
    rms = jnp.sqrt(rows_total[section_idx] / (frame_count * model_width)).reshape(1, 3)
    return (
        w_new[None],
        grad_blocks[None],
        l_new.reshape(master.shape)[None],
        r_new.reshape(master.shape)[None],
        gains_new[None],
        m_new[None],
        v_new[None],
        loss_value,
        grad_norm,
        rms,
    )


def layer_block(shape):
    return pl.BlockSpec((1,) + shape, lambda i: (i,) + (0,) * len(shape))


def whole_block(shape):
    return pl.BlockSpec(shape, lambda i: (0,) * len(shape))


def forward(layers, info, inverse, x_seg, target_seg, full_w, full_g):
    seg, width = x_seg.shape
    dim = width // HEADS
    part = width // 4
    half = layers // 2
    shapes = (
        (HEADS, seg, seg), (3 * HEADS, seg, dim), (seg, width), (seg, width), (4, seg, width), (4, seg, width)
    )
    kinds = (BF16, BF16, BF16, F32, BF16, BF16)
    return pl.pallas_call(
        functools.partial(forward_kernel, layers, half),
        grid=(layers,),
        in_specs=[
            pl.BlockSpec(memory_space=pltpu.SMEM),
            pl.BlockSpec(memory_space=pltpu.SMEM),
            whole_block((seg, width)),
            whole_block((seg, width // 2)),
            layer_block((48, part, width)),
            layer_block((2, width)),
        ],
        out_specs=[layer_block(s) for s in shapes]
        + [whole_block((layers, seg, width)), whole_block((seg, width)), whole_block((layers, 8, width))],
        out_shape=[jax.ShapeDtypeStruct((layers,) + s, k) for s, k in zip(shapes, kinds)]
        + [
            jax.ShapeDtypeStruct((layers, seg, width), BF16),
            jax.ShapeDtypeStruct((seg, width), F32),
            jax.ShapeDtypeStruct((layers, 8, width), F32),
        ],
        scratch_shapes=[pltpu.VMEM((HEADS, seg, dim), BF16), pltpu.VMEM((seg, width), F32)],
        compiler_params=pltpu.CompilerParams(vmem_limit_bytes=VMEM_LIMIT),
    )(info, inverse, x_seg, target_seg, full_w, full_g)


def backward(layers, loss_grad, full_w, full_g, sent, saved):
    seg, width = loss_grad.shape
    dim = width // HEADS
    part = width // 4
    half = layers // 2

    def from_end(array):
        shape = array.shape[1:]
        return pl.BlockSpec((1,) + shape, lambda i: (layers - 1 - i,) + (0,) * len(shape))

    return pl.pallas_call(
        functools.partial(backward_kernel, layers, half),
        grid=(layers,),
        in_specs=[
            whole_block((seg, width)),
            from_end(full_w),
            from_end(full_g),
            whole_block((layers, seg, width)),
        ]
        + [from_end(a) for a in saved],
        out_specs=[
            pl.BlockSpec((1, 48, part, width), lambda i: (layers - 1 - i, 0, 0, 0)),
            pl.BlockSpec((1, 8, width), lambda i: (layers - 1 - i, 0, 0)),
        ],
        out_shape=[
            jax.ShapeDtypeStruct((layers, 48, part, width), BF16),
            jax.ShapeDtypeStruct((layers, 8, width), F32),
        ],
        scratch_shapes=[
            pltpu.VMEM((layers, seg, width), BF16),
            pltpu.VMEM((seg, width), BF16),
            pltpu.VMEM((4, seg, width), BF16),
            pltpu.VMEM((seg, width), BF16),
            pltpu.VMEM((seg, width), F32),
            pltpu.VMEM((seg, width), BF16),
            pltpu.VMEM((HEADS, seg, dim), BF16),
            pltpu.VMEM((3 * HEADS, seg, dim), BF16),
            pltpu.VMEM((3, seg, width), BF16),
        ],
        compiler_params=pltpu.CompilerParams(vmem_limit_bytes=VMEM_LIMIT),
    )(loss_grad, full_w, full_g, sent, *saved)


def body(
    x_in, targets, valid_len, present_stems, w_master, norm_gains, gain_m, gain_v,
    l_stats, r_stats, l_roots, r_roots, step_count,
):
    width = x_in.shape[1]
    part = width // 4
    layers = lax.axis_size("section")
    section_idx = lax.axis_index("section")
    groups = lax.axis_size("dp")
    group_idx = lax.axis_index("dp")
    micro = valid_len.shape[0] // groups
    seg = x_in.shape[0] // micro
    own_blocks = w_master.shape[1]
    own_gain = norm_gains.shape[2]
    own_w = (
        w_master[0].astype(BF16).reshape(own_blocks // 4, 4, part, part).transpose(0, 2, 1, 3)
        .reshape(own_blocks // 4, part, width)
    )
    full_w = lax.all_gather(own_w, ("section", "dp"), axis=0, tiled=True).reshape(
        layers, -1, part, width
    )
    full_g = lax.all_gather(
        lax.all_gather(norm_gains[0], "dp", axis=1, tiled=True), "section", axis=0
    ).astype(BF16).astype(F32)
    slot = jnp.minimum(section_idx, micro - 1)
    used = (section_idx < micro).astype(jnp.int32)
    at = group_idx * micro + slot
    info = jnp.concatenate([valid_len[at][None] * used, present_stems[at] * used])
    frame_count = jnp.sum(valid_len).astype(F32)
    x_seg = lax.dynamic_slice_in_dim(x_in, slot * seg, seg, 0)
    target_seg = lax.dynamic_slice_in_dim(targets, slot * seg, seg, 0)
    *saved, sent, loss_grad, stats = forward(
        layers, info, (1.0 / frame_count)[None], x_seg, target_seg, full_w, full_g
    )
    grads, gain_grads = backward(layers, loss_grad, full_w, full_g, sent, saved)
    own_quads = lax.psum_scatter(
        grads.reshape(-1, part, width), ("section", "dp"), scatter_dimension=0, tiled=True
    ).astype(F32)
    own_grad = (
        own_quads.reshape(own_blocks // 4, part, 4, part).transpose(0, 2, 1, 3)
        .reshape(own_blocks, part * part)
    )
    summed_g, sums = lax.psum((gain_grads[:, :2], jnp.sum(stats, axis=2)), ("section", "dp"))
    own_gain_grad = lax.dynamic_slice(
        summed_g, (section_idx, 0, group_idx * own_gain), (1, 2, own_gain)
    )[0]
    own_square = jnp.sum(own_grad * own_grad) + jnp.sum(own_gain_grad * own_gain_grad)
    total_square = lax.psum(own_square, ("section", "dp"))
    loss_value = sums[0, 3] / frame_count
    grad_norm = jnp.sqrt(total_square)
    clip_limit = 0.00015 * math.sqrt(layers * (own_blocks * groups * part * part + 2 * width))
    factor = clip_limit / jnp.maximum(grad_norm, clip_limit)
    grad_blocks = own_grad * factor
    square = (own_blocks, part, part)
    shaped = grad_blocks.reshape(square)
    highest = lax.Precision.HIGHEST
    l_new = 0.95 * l_stats[0].reshape(square) + 0.05 * jnp.einsum(
        "bij,bkj->bik", shaped, shaped, precision=highest
    )
    r_new = 0.95 * r_stats[0].reshape(square) + 0.05 * jnp.einsum(
        "bji,bjk->bik", shaped, shaped, precision=highest
    )
    left_side = jnp.einsum("bij,bjk->bik", l_roots[0].reshape(square), shaped, precision=highest)
    precond = jnp.einsum("bij,bjk->bik", left_side, r_roots[0].reshape(square), precision=highest)
    master = w_master[0]
    w_new = master - 0.5 * (precond.reshape(master.shape) + 0.01 * master)
    gain_grad = own_gain_grad * factor
    m_new = 0.9 * gain_m[0] + 0.1 * gain_grad
    v_new = 0.999 * gain_v[0] + 0.001 * gain_grad * gain_grad
    step_num = step_count[0].astype(F32)
    m_hat = m_new / (1.0 - jnp.power(0.9, step_num))
    v_hat = v_new / (1.0 - jnp.power(0.999, step_num))
    gains_new = norm_gains[0] - 0.5 * m_hat / (jnp.sqrt(v_hat) + 1e-08)
    rms = jnp.sqrt(sums[section_idx, :3] / (frame_count * width)).reshape(1, 3)
    return (
        w_new[None],
        grad_blocks[None],
        l_new.reshape(master.shape)[None],
        r_new.reshape(master.shape)[None],
        gains_new[None],
        m_new[None],
        v_new[None],
        loss_value,
        grad_norm,
        rms,
    )


def solution(mesh):
    def step(*args):
        layers, groups = mesh.shape["section"], mesh.shape["dp"]
        micro, own_blocks = args[2].shape[0] // groups, args[4].shape[1]
        if micro <= layers and own_blocks % 4 == 0:
            return body(*args)
        return pipelined_body(*args)

    block = P("section", "dp", None)
    gain = P("section", None, "dp")
    return jax.shard_map(
        step,
        mesh=mesh,
        in_specs=(
            P("dp", None), P("dp", None), P(), P(), block, gain, gain, gain, block, block, block, block, P(),
        ),
        out_specs=(block, block, block, block, gain, gain, gain, P(), P(), P("section", None)),
        check_vma=False,
    )
```

```python
import functools
import math

import jax
import jax.numpy as jnp
from jax import lax
from jax.experimental import pallas as pl
from jax.experimental.pallas import tpu as pltpu
from jax.sharding import PartitionSpec as P

HEADS = 8
F32 = jnp.float32
BF16 = jnp.bfloat16
VMEM_LIMIT = 60 * 1024 * 1024


def dot_nn(a, b):
    return lax.dot_general(a, b, (((1,), (0,)), ((), ())), preferred_element_type=F32)


def dot_nt(a, b):
    return lax.dot_general(a, b, (((1,), (1,)), ((), ())), preferred_element_type=F32)


def dot_tn(a, b):
    return lax.dot_general(a, b, (((0,), (0,)), ((), ())), preferred_element_type=F32)


def gelu_parts(x):
    ax = jnp.abs(x)
    bell = jnp.exp(-0.5 * x * x)
    t = 1.0 / (1.0 + (0.3275911 * 0.7071067811865476) * ax)
    poly = t * (
        0.5 * 0.254829592
        + t
        * (
            0.5 * -0.284496736
            + t * (0.5 * 1.421413741 + t * (0.5 * -1.453152027 + t * (0.5 * 1.061405429)))
        )
    )
    tail = poly * bell
    cdf = jnp.where(x >= 0.0, 1.0 - tail, tail)
    return x * cdf, cdf + x * bell * 0.3989422804014327


def stack_quads(w_ref, first, step, number):
    return jnp.concatenate([w_ref[0, first + step * i] for i in range(number)], axis=0)


MESH = pl.DeviceIdType.MESH


def mesh_place():
    section = lax.axis_index("section")
    group = lax.axis_index("dp")
    core = lax.rem(section, 2)
    y = lax.rem(group, 2)
    z = group // 2
    z_peers = (z, z + 1 - 2 * lax.rem(z, 2), lax.rem(z + 2, 4), 3 - z)
    return section, group, core, y, z_peers


def remote(source, target, send_sem, recv_sem, section, group):
    return pltpu.make_async_remote_copy(
        src_ref=source, dst_ref=target, send_sem=send_sem, recv_sem=recv_sem,
        device_id=(section, group), device_id_type=MESH,
    )


def greet(places):
    barrier = pltpu.get_barrier_semaphore()
    for place in places:
        pl.semaphore_signal(barrier, inc=1, device_id=place, device_id_type=MESH)
    pl.semaphore_wait(barrier, len(places))


class Gather:
    def __init__(self, own_ref, gain_ref, w_ref, gains_ref, sems):
        self.own, self.gain, self.w, self.gains = own_ref, gain_ref, w_ref, gains_ref
        self.spread, self.z_sems, self.y_sems, self.core_sems, self.gain_sems, self.local = sems
        self.section, self.group, self.core, self.y, self.z_peers = mesh_place()
        self.quads = own_ref.shape[0] // 2
        self.others = [lax.rem(self.section + k, 4) for k in range(1, 4)]
        self.places = [(o, self.group) for o in self.others] + [
            (self.section, lax.rem(self.group + k, 8)) for k in range(1, 8)
        ]

    def piece(self, layer, group):
        return self.w.at[layer, pl.ds(group * 2 * self.quads + self.quads * self.core, self.quads)]

    def spread_copy(self, k):
        peer = self.others[k]
        half = lax.rem(peer, 2) * self.quads
        return remote(
            self.own.at[pl.ds(half, self.quads)],
            self.w.at[self.section, pl.ds(self.group * 2 * self.quads + half, self.quads)],
            self.spread.at[0, k], self.spread.at[1, k], peer, self.group,
        )

    def spread_wait(self, layer):
        for k in range(3):
            @pl.when(lax.rem(layer + k + 1, 4) == self.section)
            def _():
                ref = self.piece(layer, self.group)
                remote(ref, ref, self.spread.at[0, k], self.spread.at[1, k], self.others[0], self.group).wait_recv()

    def z_copy(self, layer, k):
        ref = self.piece(layer, self.group)
        return remote(
            ref, ref, self.z_sems.at[0, layer, k], self.z_sems.at[1, layer, k],
            self.section, self.z_peers[k] * 2 + self.y,
        )

    def z_landed(self, layer, k):
        ref = self.piece(layer, self.z_peers[k] * 2 + self.y)
        return remote(
            ref, ref, self.z_sems.at[0, layer, k], self.z_sems.at[1, layer, k],
            self.section, self.z_peers[k] * 2 + self.y,
        )

    def y_copy(self, layer, k, mine=True):
        y = self.y if mine else 1 - self.y
        ref = self.piece(layer, self.z_peers[k] * 2 + y)
        return remote(
            ref, ref, self.y_sems.at[0, layer, k], self.y_sems.at[1, layer, k],
            self.section, self.group + 1 - 2 * self.y,
        )

    def core_copy(self, layer, k, mine=True):
        y = self.y if k < 4 else 1 - self.y
        core = self.core if mine else 1 - self.core
        at = (self.z_peers[k % 4] * 2 + y) * 2 * self.quads + self.quads * core
        ref = self.w.at[layer, pl.ds(at, self.quads)]
        return remote(
            ref, ref, self.core_sems.at[0, layer, k], self.core_sems.at[1, layer, k],
            self.section + 1 - 2 * self.core, self.group,
        )

    def gain_copy(self, k):
        if k < 7:
            peer = lax.rem(self.group + k + 1, 8)
            return remote(
                self.gain, self.gains.at[self.section, self.group],
                self.gain_sems.at[0, k], self.gain_sems.at[1, k], self.section, peer,
            )
        ref = self.gains.at[self.section]
        return remote(
            ref, ref, self.gain_sems.at[0, k], self.gain_sems.at[1, k], self.others[k - 7], self.group
        )

    def gain_landed(self, k):
        if k < 7:
            ref = self.gains.at[self.section, lax.rem(self.group - k - 1 + 8, 8)]
        else:
            ref = self.gains.at[lax.rem(self.section - (k - 6) + 4, 4)]
        return remote(ref, ref, self.gain_sems.at[0, k], self.gain_sems.at[1, k], self.section, self.group)

    def begin(self):
        greet(self.places)
        for k in range(3):
            self.spread_copy(k).start()
        for k in range(7):
            self.gain_copy(k).start()
        half = self.core * self.quads
        self.w[self.section, pl.ds(self.group * 2 * self.quads + half, self.quads)] = self.own[
            pl.ds(half, self.quads)
        ]
        self.gains[self.section, self.group] = self.gain[...]

    def share_gains(self):
        for k in range(7):
            self.gain_landed(k).wait_recv()
        for k in range(7, 10):
            self.gain_copy(k).start()

    def wait_gains(self):
        for k in range(7, 10):
            self.gain_landed(k).wait_recv()

    def kick(self, layer):
        self.spread_wait(layer)
        for k in range(1, 4):
            self.z_copy(layer, k).start()
        self.y_copy(layer, 0).start()
        self.core_copy(layer, 0).start()

    def serve(self, layer, step):
        if step < 4:
            self.z_landed(layer, step).wait_recv()
            self.y_copy(layer, step).start()
            self.core_copy(layer, step).start()
        else:
            self.y_copy(layer, step - 4, False).wait_recv()
            self.core_copy(layer, step).start()

    def finish(self, layer):
        for k in range(8):
            self.core_copy(layer, k, False).wait_recv()

    def end(self, layers):
        for k in range(3):
            self.spread_copy(k).wait_send()
        for k in range(10):
            self.gain_copy(k).wait_send()

        def per_layer(layer, _):
            for k in range(1, 4):
                self.z_copy(layer, k).wait_send()
            for k in range(4):
                self.y_copy(layer, k).wait_send()
            for k in range(8):
                self.core_copy(layer, k).wait_send()
            return 0

        lax.fori_loop(0, layers, per_layer, 0)


def forward_kernel(
    layers, half, info_ref, scale_ref, x_ref, target_ref, own_ref, own_gain_ref,
    probs_ref, heads_ref, att_ref, middle_ref, hidden_ref, slope_ref, sent_ref, loss_grad_ref, stats_ref,
    full_ref, gains_out_ref, hold_ref, out_ref, w_all_ref, gains_ref, *sems,
):
    seg, width = x_ref.shape
    dim = width // HEADS
    part = width // 4
    layer = pl.program_id(0)
    rows = 256
    chunks = seg // rows
    length = info_ref[0]
    gather = Gather(own_ref, own_gain_ref, w_all_ref, gains_ref, sems)
    w_ref = w_all_ref.at[pl.ds(layer, 1)]

    def keep_copy(index):
        return pltpu.make_async_copy(w_all_ref.at[index], full_ref.at[index], gather.local.at[index])

    @pl.when(layer == 0)
    def _():
        gather.begin()
        sent_ref[0] = x_ref[...]
        stats_ref[...] = jnp.zeros_like(stats_ref)
        gather.kick(0)
        gather.share_gains()
        for step in range(1, 4):
            gather.serve(0, step)
        gather.kick(1)
        for step in range(4, 8):
            gather.serve(0, step)
        gather.wait_gains()

    gather.finish(layer)
    keep_copy(layer).start()
    more = layer + 1 < layers

    def serve(step):
        @pl.when(more)
        def _():
            gather.serve(layer + 1, step)
        if step == 3:
            @pl.when(layer + 2 < layers)
            def _():
                gather.kick(layer + 2)

    def stream_of(at):
        prev = sent_ref[layer, at].astype(F32)
        skip = sent_ref[jnp.maximum(layer + 1 - half, 0), at].astype(F32)
        return prev + jnp.where(layer >= half, skip, 0.0)

    def gain_row(which):
        return jnp.concatenate(
            [gains_ref[layer, g, which : which + 1, : width // 8] for g in range(8)], axis=1
        ).astype(BF16).astype(F32)

    gain_one = gain_row(0)
    gain_two = gain_row(1)

    def qkv_step(i, _):
        at = pl.ds(pl.multiple_of(i * rows, rows), rows)
        stream = stream_of(at)
        factor = lax.rsqrt(jnp.mean(stream * stream, axis=-1, keepdims=True) + 1e-06)
        normed = (stream * factor * gain_one).astype(BF16)
        for t in range(3):
            qkv = dot_nn(normed, stack_quads(w_ref, t, 3, 4)).astype(BF16)
            for h in range(HEADS):
                heads_ref[0, t * HEADS + h, at] = qkv[:, h * dim : (h + 1) * dim]
        return 0

    lax.fori_loop(0, chunks, qkv_step, 0)
    frames = lax.broadcasted_iota(jnp.int32, (1, seg), 1)
    masking = jnp.where(frames < length, 0.0, -1e30).astype(F32)

    def head_step(h, _):
        keys = heads_ref[0, HEADS + h]
        values = heads_ref[0, 2 * HEADS + h]
        for i in range(chunks):
            at = pl.ds(i * rows, rows)
            scores = dot_nt(heads_ref[0, h, at], keys) * dim ** (-0.5) + masking
            top = jnp.max(scores, axis=-1, keepdims=True)
            expd = jnp.exp(scores - top)
            probs = (expd * (1.0 / jnp.sum(expd, axis=-1, keepdims=True))).astype(BF16)
            probs_ref[0, h, at] = probs
            hold_ref[h, at] = dot_nn(probs, values).astype(BF16)
        for step in range(1, 8):
            @pl.when(h == step)
            def _():
                serve(step)
        return 0

    lax.fori_loop(0, HEADS, head_step, 0)

    def ffn_step(i, _):
        at = pl.ds(pl.multiple_of(i * rows, rows), rows)
        attended = jnp.concatenate([hold_ref[h, at] for h in range(HEADS)], axis=1)
        att_ref[0, at] = attended
        branch_attn = dot_nn(attended, stack_quads(w_ref, 12, 1, 4))
        stream = stream_of(at)
        middle = stream + branch_attn
        middle_ref[0, at] = middle
        factor = lax.rsqrt(jnp.mean(middle * middle, axis=-1, keepdims=True) + 1e-06)
        normed = (middle * factor * gain_two).astype(BF16)
        branch_ffn = jnp.zeros((rows, width), F32)
        for c in range(4):
            pre_act = dot_nn(normed, stack_quads(w_ref, 16 + c, 4, 4))
            hidden, slope = gelu_parts(pre_act)
            hidden = hidden.astype(BF16)
            hidden_ref[0, c, at] = hidden
            slope_ref[0, c, at] = slope.astype(BF16)
            branch_ffn = branch_ffn + dot_nn(hidden, stack_quads(w_ref, 32 + 4 * c, 1, 4))
        output = middle + branch_ffn
        out_ref[at] = output
        sent_ref[jnp.minimum(layer + 1, layers - 1), at] = jnp.where(
            layer + 1 < layers, output.astype(BF16), sent_ref[layers - 1, at]
        )
        valid = (lax.broadcasted_iota(jnp.int32, (rows, 1), 0) + i * rows < length).astype(F32)
        for k, value in enumerate((stream, branch_attn, branch_ffn)):
            stats_ref[layer, k : k + 1] += jnp.sum(valid * value * value, axis=0, keepdims=True)
        return 0

    lax.fori_loop(0, chunks, ffn_step, 0)

    @pl.when(layer == layers - 1)
    def _():
        bins = width // 8
        lane = lax.broadcasted_iota(jnp.int32, (1, width), 1)
        is_real = lax.rem(lane, 2 * bins) < bins
        stem = lane // (2 * bins)
        present = jnp.zeros((1, width), F32)
        for k in range(4):
            present = jnp.where(stem == k, info_ref[1 + k].astype(F32), present)
        inverse = scale_ref[0]

        def loss_step(i, _):
            at = pl.ds(pl.multiple_of(i * rows, rows), rows)
            output = out_ref[at]
            square = output * output
            other = jnp.where(
                is_real, pltpu.roll(square, width - bins, 1), pltpu.roll(square, bins, 1)
            )
            magnitude = jnp.sqrt(square + other + 0.01)
            goal = target_ref[at]
            goal = jnp.concatenate(
                [goal[:, (k // 2) * bins : (k // 2 + 1) * bins] for k in range(8)], axis=1
            )
            differ = magnitude - goal
            smooth = jnp.sqrt(differ * differ + 0.01)
            valid = (lax.broadcasted_iota(jnp.int32, (rows, 1), 0) + i * rows < length).astype(F32)
            weight = valid * present
            loss_grad_ref[at] = weight * differ * output * inverse / (smooth * magnitude)
            stats_ref[0, 3:4] += jnp.sum(
                jnp.where(is_real, weight * smooth, 0.0), axis=0, keepdims=True
            )
            return 0

        lax.fori_loop(0, chunks, loss_step, 0)
        gains_out_ref[...] = gains_ref[...]
        gather.end(layers)
        for k in range(layers):
            keep_copy(k).wait()


def norm_reverse(value, gain, grad):
    factor = lax.rsqrt(jnp.mean(value * value, axis=-1, keepdims=True) + 1e-06)
    scaled = grad * gain
    mean = jnp.mean(value * scaled, axis=-1, keepdims=True)
    unit = value * factor
    back = factor * scaled - unit * (factor * factor * mean)
    return back, jnp.sum(grad * unit, axis=0, keepdims=True), (unit * gain).astype(BF16)


def backward_kernel(
    layers, half, loss_grad_ref, w_ref, gain_ref, sent_ref,
    probs_ref, heads_ref, att_ref, middle_ref, hidden_ref, slope_ref,
    grads_ref, gain_grad_ref,
    sends_ref, dffn_ref, dpre_ref, normed_ref, dmid_ref, datt_ref, dhold_ref, dheads_ref, dqkv_ref,
):
    seg, width = loss_grad_ref.shape
    dim = width // HEADS
    part = width // 4
    layer = layers - 1 - pl.program_id(0)
    rows = 256
    chunks = seg // rows
    gain_one = gain_ref[0, 0:1]
    gain_two = gain_ref[0, 1:2]
    gain_grad_ref[...] = jnp.zeros_like(gain_grad_ref)

    @pl.when(layer == layers - 1)
    def _():
        sends_ref[...] = jnp.zeros_like(sends_ref)

    def put_grad(first, step, value):
        for r in range(4):
            grads_ref[0, first + step * r] = value[r * part : (r + 1) * part].astype(grads_ref.dtype)

    def ffn_step(i, _):
        at = pl.ds(pl.multiple_of(i * rows, rows), rows)
        later = sends_ref[jnp.minimum(layer + 1, layers - 1), at].astype(F32)
        skip = sends_ref[jnp.minimum(layer + half, layers - 1), at].astype(F32)
        upstream = jnp.where(
            layer == layers - 1, loss_grad_ref[at], later + jnp.where(layer + half < layers, skip, 0.0)
        )
        dffn = upstream.astype(BF16)
        dffn_ref[at] = dffn
        dnormed = jnp.zeros((rows, width), F32)
        for c in range(4):
            dhidden = dot_nt(dffn, stack_quads(w_ref, 32 + 4 * c, 1, 4))
            dpre = (dhidden * slope_ref[0, c, at].astype(F32)).astype(BF16)
            dpre_ref[c, at] = dpre
            dnormed = dnormed + dot_nt(dpre, stack_quads(w_ref, 16 + c, 4, 4))
        back, gain_grad, normed = norm_reverse(middle_ref[0, at], gain_two, dnormed)
        gain_grad_ref[0, 1:2] += gain_grad
        normed_ref[at] = normed
        dmid = upstream + back
        dmid_ref[at] = dmid
        datt = dmid.astype(BF16)
        datt_ref[at] = datt
        dattended = dot_nt(datt, stack_quads(w_ref, 12, 1, 4)).astype(BF16)
        for h in range(HEADS):
            dhold_ref[h, at] = dattended[:, h * dim : (h + 1) * dim]
        return 0

    lax.fori_loop(0, chunks, ffn_step, 0)

    def ffn_grad_step(c, _):
        put_grad(32 + 4 * c, 1, dot_tn(hidden_ref[0, c], dffn_ref[...]))
        put_grad(16 + c, 4, dot_tn(normed_ref[...], dpre_ref[c]))
        return 0

    lax.fori_loop(0, 4, ffn_grad_step, 0)
    put_grad(12, 1, dot_tn(att_ref[0], datt_ref[...]))

    def head_step(h, _):
        queries = heads_ref[0, h]
        keys = heads_ref[0, HEADS + h]
        values = heads_ref[0, 2 * HEADS + h]
        dkeys = jnp.zeros((seg, dim), F32)
        dvalues = jnp.zeros((seg, dim), F32)
        for i in range(chunks):
            at = pl.ds(i * rows, rows)
            probs = probs_ref[0, h, at]
            dhold = dhold_ref[h, at]
            dprobs = dot_nt(dhold, values)
            wide = probs.astype(F32)
            dot_sum = jnp.sum(wide * dprobs, axis=-1, keepdims=True)
            dscores = (wide * (dprobs - dot_sum)).astype(BF16)
            dheads_ref[h, at] = (dot_nn(dscores, keys) * dim ** (-0.5)).astype(BF16)
            dvalues = dvalues + dot_tn(probs, dhold)
            dkeys = dkeys + dot_tn(dscores, heads_ref[0, h, at])
        dheads_ref[HEADS + h] = (dkeys * dim ** (-0.5)).astype(BF16)
        dheads_ref[2 * HEADS + h] = dvalues.astype(BF16)
        return 0

    lax.fori_loop(0, HEADS, head_step, 0)

    def qkv_step(i, _):
        at = pl.ds(pl.multiple_of(i * rows, rows), rows)
        dnormed = jnp.zeros((rows, width), F32)
        for t in range(3):
            dqkv = jnp.concatenate([dheads_ref[t * HEADS + h, at] for h in range(HEADS)], axis=1)
            dqkv_ref[t, at] = dqkv
            dnormed = dnormed + dot_nt(dqkv, stack_quads(w_ref, t, 3, 4))
        prev = sent_ref[layer, at].astype(F32)
        skip = sent_ref[jnp.maximum(layer + 1 - half, 0), at].astype(F32)
        stream = prev + jnp.where(layer >= half, skip, 0.0)
        back, gain_grad, normed = norm_reverse(stream, gain_one, dnormed)
        gain_grad_ref[0, 0:1] += gain_grad
        normed_ref[at] = normed
        sends_ref[layer, at] = (dmid_ref[at] + back).astype(BF16)
        return 0

    lax.fori_loop(0, chunks, qkv_step, 0)

    def qkv_grad_step(t, _):
        put_grad(t, 3, dot_tn(normed_ref[...], dqkv_ref[t]))
        return 0

    lax.fori_loop(0, 3, qkv_grad_step, 0)


FF = 1536


def from_behind(value, axis, by):
    peers = lax.axis_size(axis)
    pairs = [(i, i + by) for i in range(peers) if 0 <= i + by < peers]
    return lax.ppermute(value, axis, pairs)


def unblock(blocks, row_count, col_count, block_size):
    return (
        blocks.reshape(row_count // block_size, col_count // block_size, block_size, block_size)
        .transpose(0, 2, 1, 3)
        .reshape(row_count, col_count)
    )


def to_blocks(matrix, block_size):
    row_count, col_count = matrix.shape
    return (
        matrix.reshape(row_count // block_size, block_size, col_count // block_size, block_size)
        .transpose(0, 2, 1, 3)
        .reshape(-1, block_size * block_size)
    )


def split_matrices(blocks, model_width):
    block_size = model_width // 4
    shapes = (
        (model_width, 3 * model_width),
        (model_width, model_width),
        (model_width, FF),
        (FF, model_width),
    )
    result = []
    offset = 0
    for row_count, col_count in shapes:
        number = row_count * col_count // (block_size * block_size)
        result.append(unblock(blocks[offset : offset + number], row_count, col_count, block_size))
        offset = offset + number
    return result


def rms_norm(stream, gain):
    factor = lax.rsqrt(jnp.mean(stream * stream, axis=-1, keepdims=True) + 1e-06)
    return (stream * factor * gain, factor)


def norm_back(stream, factor, gain, grad):
    scaled = grad * gain
    grad_in = factor * scaled - stream * factor**3 * jnp.mean(
        stream * scaled, axis=-1, keepdims=True
    )
    return (grad_in, jnp.sum(grad * stream * factor, axis=0))


def gelu_slope(pre_act):
    return (
        0.5 * (1.0 + lax.erf(pre_act * 0.7071067811865476))
        + pre_act * jnp.exp(-0.5 * pre_act * pre_act) * 0.3989422804014327
    )


def layer_forward(stream, matrices, gain_pair, length):
    w_qkv, w_out, w_up, w_down = matrices
    row_count, model_width = stream.shape
    head_dim = model_width // HEADS
    frames = jnp.arange(row_count)
    norm_one, scale_one = rms_norm(stream, gain_pair[0])
    normed = norm_one.astype(BF16)
    qkv_all = jnp.dot(normed, w_qkv, preferred_element_type=jnp.float32).astype(BF16)
    queries = qkv_all[:, :model_width].reshape(row_count, HEADS, head_dim)
    key_rows = qkv_all[:, model_width : 2 * model_width].reshape(row_count, HEADS, head_dim)
    value_rows = qkv_all[:, 2 * model_width :].reshape(row_count, HEADS, head_dim)
    masking = jnp.where(frames < length, 0.0, -1e30).astype(jnp.float32)
    scores = jnp.einsum(
        "qhe,khe->hqk", queries, key_rows, preferred_element_type=jnp.float32
    ) * head_dim ** (-0.5)
    attn_probs = jax.nn.softmax(scores + masking[None, None, :], axis=-1)
    probs_low = attn_probs.astype(BF16)
    attended = (
        jnp.einsum("hqk,khe->qhe", probs_low, value_rows, preferred_element_type=jnp.float32)
        .reshape(row_count, model_width)
        .astype(BF16)
    )
    branch_attn = jnp.dot(attended, w_out, preferred_element_type=jnp.float32)
    middle = stream + branch_attn
    norm_two, scale_two = rms_norm(middle, gain_pair[1])
    normed_two = norm_two.astype(BF16)
    pre_act = jnp.dot(normed_two, w_up, preferred_element_type=jnp.float32)
    hidden = jax.nn.gelu(pre_act, approximate=False).astype(BF16)
    branch_ffn = jnp.dot(hidden, w_down, preferred_element_type=jnp.float32)
    kept_vals = (
        scale_one,
        normed,
        queries,
        key_rows,
        value_rows,
        attn_probs,
        probs_low,
        attended,
        middle,
        scale_two,
        normed_two,
        pre_act,
        hidden,
    )
    return (middle + branch_ffn, branch_attn, branch_ffn, kept_vals)


def layer_backward(stream, matrices, gain_pair, length, upstream):
    w_qkv, w_out, w_up, w_down = matrices
    row_count, model_width = stream.shape
    head_dim = model_width // HEADS
    output, branch_attn, branch_ffn, kept_vals = layer_forward(stream, matrices, gain_pair, length)
    (
        scale_one,
        normed,
        queries,
        key_rows,
        value_rows,
        attn_probs,
        probs_low,
        attended,
        middle,
        scale_two,
        normed_two,
        pre_act,
        hidden,
    ) = kept_vals
    grad_ffn = upstream.astype(BF16)
    grad_down = jnp.dot(hidden.T, grad_ffn, preferred_element_type=jnp.float32)
    grad_hidden = jnp.dot(grad_ffn, w_down.T, preferred_element_type=jnp.float32)
    grad_pre = (grad_hidden * gelu_slope(pre_act)).astype(BF16)
    grad_up = jnp.dot(normed_two.T, grad_pre, preferred_element_type=jnp.float32)
    back_mid, gain_two = norm_back(
        middle,
        scale_two,
        gain_pair[1],
        jnp.dot(grad_pre, w_up.T, preferred_element_type=jnp.float32),
    )
    grad_mid = upstream + back_mid
    grad_branch = grad_mid.astype(BF16)
    grad_out = jnp.dot(attended.T, grad_branch, preferred_element_type=jnp.float32)
    grad_att = (
        jnp.dot(grad_branch, w_out.T, preferred_element_type=jnp.float32)
        .astype(BF16)
        .reshape(row_count, HEADS, head_dim)
    )
    grad_value = jnp.einsum("hqk,qhe->khe", probs_low, grad_att, preferred_element_type=jnp.float32)
    grad_probs = jnp.einsum(
        "qhe,khe->hqk", grad_att, value_rows, preferred_element_type=jnp.float32
    )
    grad_scores = (
        attn_probs * (grad_probs - jnp.sum(attn_probs * grad_probs, axis=-1, keepdims=True))
    ).astype(BF16)
    grad_query = jnp.einsum(
        "hqk,khe->qhe", grad_scores, key_rows, preferred_element_type=jnp.float32
    ) * head_dim ** (-0.5)
    grad_key = jnp.einsum(
        "hqk,qhe->khe", grad_scores, queries, preferred_element_type=jnp.float32
    ) * head_dim ** (-0.5)
    grad_qkv = jnp.concatenate(
        [
            grad_query.reshape(row_count, model_width),
            grad_key.reshape(row_count, model_width),
            grad_value.reshape(row_count, model_width),
        ],
        axis=1,
    ).astype(BF16)
    grad_wqkv = jnp.dot(normed.T, grad_qkv, preferred_element_type=jnp.float32)
    back_in, gain_one = norm_back(
        stream,
        scale_one,
        gain_pair[0],
        jnp.dot(grad_qkv, w_qkv.T, preferred_element_type=jnp.float32),
    )
    return (
        grad_mid + back_in,
        (grad_wqkv, grad_out, grad_up, grad_down),
        jnp.stack([gain_one, gain_two]),
    )


def spectral_terms(output, target, length, present_row, frame_count):
    row_count, model_width = output.shape
    bin_count = model_width // 8
    spectra = output.reshape(row_count, 4, 2, bin_count)
    real_part = spectra[:, :, 0]
    imag_part = spectra[:, :, 1]
    magnitude = jnp.sqrt(real_part * real_part + imag_part * imag_part + 0.01)
    differ = magnitude - target.reshape(row_count, 4, bin_count)
    smooth_err = jnp.sqrt(differ * differ + 0.01)
    weight = (jnp.arange(row_count) < length).astype(jnp.float32)[:, None, None] * present_row[
        None, :, None
    ]
    loss_slope = weight * differ / smooth_err / magnitude / frame_count
    grad_spec = jnp.stack([loss_slope * real_part, loss_slope * imag_part], axis=2).reshape(
        row_count, model_width
    )
    return (jnp.sum(smooth_err * weight), grad_spec)


def pipelined_body(
    x_in,
    targets,
    valid_len,
    present_stems,
    w_master,
    norm_gains,
    gain_m,
    gain_v,
    l_stats,
    r_stats,
    l_roots,
    r_roots,
    step_count,
):
    model_width = x_in.shape[1]
    block_size = model_width // 4
    sections = lax.axis_size("section")
    section_idx = lax.axis_index("section")
    half_way = sections // 2
    groups = lax.axis_size("dp")
    group_idx = lax.axis_index("dp")
    micro_count = valid_len.shape[0] // groups
    seg_len = x_in.shape[0] // micro_count
    own_blocks = w_master.shape[1]
    own_gain = norm_gains.shape[2]
    full_w, full_g = (
        lax.all_gather(w_master.astype(BF16), "dp", axis=1, tiled=True),
        lax.all_gather(norm_gains.astype(BF16), "dp", axis=2, tiled=True),
    )
    matrices = split_matrices(full_w[0], model_width)
    gain_pair = full_g[0].astype(jnp.float32)
    lengths = lax.dynamic_slice_in_dim(valid_len, group_idx * micro_count, micro_count)
    stem_flags = lax.dynamic_slice_in_dim(
        present_stems, group_idx * micro_count, micro_count
    ).astype(jnp.float32)
    frame_count = jnp.sum(valid_len).astype(jnp.float32)
    decoder = section_idx >= half_way
    encoder = section_idx < half_way
    is_last = section_idx == sections - 1
    act_shape = (micro_count, seg_len, model_width)

    def forward_step(step_idx, loop_state):
        in_rows, kept_prev, skip_store, loss_grads, loss_sum, sq_sums = loop_state
        micro_idx = step_idx - section_idx
        active = (micro_idx >= 0) & (micro_idx < micro_count)
        slot_idx = jnp.clip(micro_idx, 0, micro_count - 1)
        fresh_rows = lax.dynamic_slice_in_dim(x_in, slot_idx * seg_len, seg_len, 0)
        previous = jnp.where(section_idx == 0, fresh_rows, in_rows)
        stream = previous.astype(jnp.float32) + jnp.where(
            decoder, skip_store[slot_idx].astype(jnp.float32), 0.0
        )
        length = lengths[slot_idx]
        target = lax.dynamic_slice_in_dim(targets, slot_idx * seg_len, seg_len, 0)

        def forward_compute_fn(operand):
            output, branch_attn, branch_ffn, kept_vals = layer_forward(
                stream, matrices, gain_pair, length
            )
            valid = (jnp.arange(seg_len) < length).astype(jnp.float32)[:, None]
            squares = jnp.stack(
                [
                    jnp.sum(valid * stream * stream),
                    jnp.sum(valid * branch_attn * branch_attn),
                    jnp.sum(valid * branch_ffn * branch_ffn),
                ]
            )
            seg_loss, grad_spec = spectral_terms(
                output, target, length, stem_flags[slot_idx], frame_count
            )
            return (output, squares, seg_loss, grad_spec)

        def forward_spare_fn(operand):
            empty = jnp.zeros((seg_len, model_width), jnp.float32)
            return (empty, jnp.zeros((3,), jnp.float32), jnp.zeros((), jnp.float32), empty)

        output, squares, seg_loss, grad_spec = lax.cond(
            active, forward_compute_fn, forward_spare_fn, 0
        )
        kept_prev = kept_prev.at[slot_idx].set(jnp.where(active, previous, kept_prev[slot_idx]))
        loss_grads = loss_grads.at[slot_idx].set(
            jnp.where(active & is_last, grad_spec, loss_grads[slot_idx])
        )
        loss_sum = loss_sum + jnp.where(is_last, seg_loss, 0.0)
        sq_sums = sq_sums + squares
        sent_rows = output.astype(BF16)
        in_rows = from_behind(sent_rows, "section", 1)
        from_encoder = from_behind(sent_rows, "section", half_way)
        recv_idx = step_idx - section_idx + half_way
        usable = decoder & (recv_idx >= 0) & (recv_idx < micro_count)
        recv_slot = jnp.clip(recv_idx, 0, micro_count - 1)
        skip_store = skip_store.at[recv_slot].set(
            jnp.where(usable, from_encoder, skip_store[recv_slot])
        )
        return (in_rows, kept_prev, skip_store, loss_grads, loss_sum, sq_sums)

    start_state = (
        jnp.zeros((seg_len, model_width), BF16),
        jnp.zeros(act_shape, BF16),
        jnp.zeros(act_shape, BF16),
        jnp.zeros(act_shape, jnp.float32),
        jnp.zeros((), jnp.float32),
        jnp.zeros((3,), jnp.float32),
    )
    unused_rows, kept_prev, skip_store, loss_grads, loss_sum, sq_sums = lax.fori_loop(
        0, micro_count + sections - 1, forward_step, start_state
    )

    def backward_step(step_idx, loop_state):
        in_grads, skip_grad_store, grad_mats, grad_gains = loop_state
        micro_idx = step_idx - (sections - 1 - section_idx)
        active = (micro_idx >= 0) & (micro_idx < micro_count)
        slot_idx = jnp.clip(micro_idx, 0, micro_count - 1)
        upstream = jnp.where(
            is_last,
            loss_grads[slot_idx],
            in_grads.astype(jnp.float32)
            + jnp.where(encoder, skip_grad_store[slot_idx].astype(jnp.float32), 0.0),
        )
        stream = kept_prev[slot_idx].astype(jnp.float32) + jnp.where(
            decoder, skip_store[slot_idx].astype(jnp.float32), 0.0
        )
        length = lengths[slot_idx]

        def backward_compute_fn(operand):
            return layer_backward(stream, matrices, gain_pair, length, upstream)

        def backward_spare_fn(operand):
            return (
                jnp.zeros_like(stream),
                tuple((jnp.zeros(mat.shape, jnp.float32) for mat in matrices)),
                jnp.zeros((2, model_width), jnp.float32),
            )

        grad_stream, layer_mats, layer_gains = lax.cond(
            active, backward_compute_fn, backward_spare_fn, 0
        )
        grad_mats = tuple((total + piece for total, piece in zip(grad_mats, layer_mats)))
        grad_gains = grad_gains + layer_gains
        grad_rows = grad_stream.astype(BF16)
        in_grads = from_behind(grad_rows, "section", -1)
        from_decoder = from_behind(grad_rows, "section", -half_way)
        recv_idx = micro_idx + half_way
        usable = encoder & (recv_idx >= 0) & (recv_idx < micro_count)
        recv_slot = jnp.clip(recv_idx, 0, micro_count - 1)
        skip_grad_store = skip_grad_store.at[recv_slot].set(
            jnp.where(usable, from_decoder, skip_grad_store[recv_slot])
        )
        return (in_grads, skip_grad_store, grad_mats, grad_gains)

    back_state = (
        jnp.zeros((seg_len, model_width), BF16),
        jnp.zeros(act_shape, BF16),
        tuple((jnp.zeros(mat.shape, jnp.float32) for mat in matrices)),
        jnp.zeros((2, model_width), jnp.float32),
    )
    unused_grads, unused_store, grad_mats, grad_gains = lax.fori_loop(
        0, micro_count + sections - 1, backward_step, back_state
    )
    grad_all = jnp.concatenate([to_blocks(mat, block_size) for mat in grad_mats], axis=0)
    summed_w, summed_g = lax.psum((grad_all, grad_gains), "dp")
    own_grad = lax.dynamic_slice_in_dim(summed_w, group_idx * own_blocks, own_blocks, 0)
    own_gain_grad = lax.dynamic_slice_in_dim(summed_g, group_idx * own_gain, own_gain, 1)
    own_square = jnp.sum(own_grad * own_grad) + jnp.sum(own_gain_grad * own_gain_grad)
    rows_local = jnp.zeros((sections, 3), jnp.float32).at[section_idx].set(sq_sums)
    total_square, loss_value, rows_total = lax.psum(
        (own_square, loss_sum / frame_count, rows_local), ("section", "dp")
    )
    grad_norm = jnp.sqrt(total_square)
    clip_limit = 0.00015 * math.sqrt(
        sections * (own_blocks * groups * block_size * block_size + 2 * model_width)
    )
    factor = clip_limit / jnp.maximum(grad_norm, clip_limit)
    grad_blocks = own_grad * factor
    square = (own_blocks, block_size, block_size)
    shaped = grad_blocks.reshape(square)
    highest = lax.Precision.HIGHEST
    l_new = 0.95 * l_stats[0].reshape(square) + 0.05 * jnp.einsum(
        "bij,bkj->bik", shaped, shaped, precision=highest
    )
    r_new = 0.95 * r_stats[0].reshape(square) + 0.05 * jnp.einsum(
        "bji,bjk->bik", shaped, shaped, precision=highest
    )
    left_side = jnp.einsum("bij,bjk->bik", l_roots[0].reshape(square), shaped, precision=highest)
    precond = jnp.einsum("bij,bjk->bik", left_side, r_roots[0].reshape(square), precision=highest)
    master = w_master[0]
    w_new = master - 0.5 * (precond.reshape(master.shape) + 0.01 * master)
    gain_grad = own_gain_grad * factor
    m_new = 0.9 * gain_m[0] + 0.1 * gain_grad
    v_new = 0.999 * gain_v[0] + 0.001 * gain_grad * gain_grad
    step_num = step_count[0].astype(jnp.float32)
    m_hat = m_new / (1.0 - jnp.power(0.9, step_num))
    v_hat = v_new / (1.0 - jnp.power(0.999, step_num))
    gains_new = norm_gains[0] - 0.5 * m_hat / (jnp.sqrt(v_hat) + 1e-08)
    rms = jnp.sqrt(rows_total[section_idx] / (frame_count * model_width)).reshape(1, 3)
    return (
        w_new[None],
        grad_blocks[None],
        l_new.reshape(master.shape)[None],
        r_new.reshape(master.shape)[None],
        gains_new[None],
        m_new[None],
        v_new[None],
        loss_value,
        grad_norm,
        rms,
    )


def layer_block(shape):
    return pl.BlockSpec((1,) + shape, lambda i: (i,) + (0,) * len(shape))


def whole_block(shape):
    return pl.BlockSpec(shape, lambda i: (0,) * len(shape))


def forward(layers, info, inverse, x_seg, target_seg, own_w, own_gain):
    seg, width = x_seg.shape
    dim = width // HEADS
    part = width // 4
    half = layers // 2
    shapes = (
        (HEADS, seg, seg), (3 * HEADS, seg, dim), (seg, width), (seg, width), (4, seg, width), (4, seg, width)
    )
    kinds = (BF16, BF16, BF16, F32, BF16, BF16)
    return pl.pallas_call(
        functools.partial(forward_kernel, layers, half),
        grid=(layers,),
        in_specs=[
            pl.BlockSpec(memory_space=pltpu.SMEM),
            pl.BlockSpec(memory_space=pltpu.SMEM),
            whole_block((seg, width)),
            whole_block((seg, width // 2)),
            pl.BlockSpec(memory_space=pltpu.VMEM),
            pl.BlockSpec(memory_space=pltpu.VMEM),
        ],
        out_specs=[layer_block(s) for s in shapes]
        + [whole_block((layers, seg, width)), whole_block((seg, width)), whole_block((layers, 8, width))]
        + [pl.BlockSpec(memory_space=pl.ANY), pl.BlockSpec(memory_space=pltpu.VMEM)],
        out_shape=[jax.ShapeDtypeStruct((layers,) + s, k) for s, k in zip(shapes, kinds)]
        + [
            jax.ShapeDtypeStruct((layers, seg, width), BF16),
            jax.ShapeDtypeStruct((seg, width), F32),
            jax.ShapeDtypeStruct((layers, 8, width), F32),
            jax.ShapeDtypeStruct((layers, 48, part, width), BF16),
            jax.ShapeDtypeStruct((layers, 8, 8, 128), F32),
        ],
        scratch_shapes=[
            pltpu.VMEM((HEADS, seg, dim), BF16),
            pltpu.VMEM((seg, width), F32),
            pltpu.VMEM((layers, 48, part, width), BF16),
            pltpu.VMEM((layers, 8, 8, 128), F32),
            pltpu.SemaphoreType.DMA((2, 3)),
            pltpu.SemaphoreType.DMA((2, layers, 4)),
            pltpu.SemaphoreType.DMA((2, layers, 4)),
            pltpu.SemaphoreType.DMA((2, layers, 8)),
            pltpu.SemaphoreType.DMA((2, 10)),
            pltpu.SemaphoreType.DMA((layers,)),
        ],
        compiler_params=pltpu.CompilerParams(
            vmem_limit_bytes=VMEM_LIMIT, collective_id=0, has_side_effects=True
        ),
    )(info, inverse, x_seg, target_seg, own_w, own_gain)


def backward(layers, loss_grad, full_w, full_g, sent, saved):
    seg, width = loss_grad.shape
    dim = width // HEADS
    part = width // 4
    half = layers // 2

    def from_end(array):
        shape = array.shape[1:]
        return pl.BlockSpec((1,) + shape, lambda i: (layers - 1 - i,) + (0,) * len(shape))

    return pl.pallas_call(
        functools.partial(backward_kernel, layers, half),
        grid=(layers,),
        in_specs=[
            whole_block((seg, width)),
            from_end(full_w),
            from_end(full_g),
            whole_block((layers, seg, width)),
        ]
        + [from_end(a) for a in saved],
        out_specs=[
            pl.BlockSpec((1, 48, part, width), lambda i: (layers - 1 - i, 0, 0, 0)),
            pl.BlockSpec((1, 8, width), lambda i: (layers - 1 - i, 0, 0)),
        ],
        out_shape=[
            jax.ShapeDtypeStruct((layers, 48, part, width), BF16),
            jax.ShapeDtypeStruct((layers, 8, width), F32),
        ],
        scratch_shapes=[
            pltpu.VMEM((layers, seg, width), BF16),
            pltpu.VMEM((seg, width), BF16),
            pltpu.VMEM((4, seg, width), BF16),
            pltpu.VMEM((seg, width), BF16),
            pltpu.VMEM((seg, width), F32),
            pltpu.VMEM((seg, width), BF16),
            pltpu.VMEM((HEADS, seg, dim), BF16),
            pltpu.VMEM((3 * HEADS, seg, dim), BF16),
            pltpu.VMEM((3, seg, width), BF16),
        ],
        compiler_params=pltpu.CompilerParams(vmem_limit_bytes=VMEM_LIMIT),
    )(loss_grad, full_w, full_g, sent, *saved)


def body(
    x_in, targets, valid_len, present_stems, w_master, norm_gains, gain_m, gain_v,
    l_stats, r_stats, l_roots, r_roots, step_count,
):
    width = x_in.shape[1]
    part = width // 4
    layers = lax.axis_size("section")
    section_idx = lax.axis_index("section")
    groups = lax.axis_size("dp")
    group_idx = lax.axis_index("dp")
    micro = valid_len.shape[0] // groups
    seg = x_in.shape[0] // micro
    own_blocks = w_master.shape[1]
    own_gain = norm_gains.shape[2]
    own_w = (
        w_master[0].astype(BF16).reshape(own_blocks // 4, 4, part, part).transpose(0, 2, 1, 3)
        .reshape(own_blocks // 4, part, width)
    )
    gain_tile = jnp.zeros((8, 128), F32).at[:2, :own_gain].set(norm_gains[0])
    slot = jnp.minimum(section_idx, micro - 1)
    used = (section_idx < micro).astype(jnp.int32)
    at = group_idx * micro + slot
    info = jnp.concatenate([valid_len[at][None] * used, present_stems[at] * used])
    frame_count = jnp.sum(valid_len).astype(F32)
    x_seg = lax.dynamic_slice_in_dim(x_in, slot * seg, seg, 0)
    target_seg = lax.dynamic_slice_in_dim(targets, slot * seg, seg, 0)
    *saved, sent, loss_grad, stats, full_w, tiles = forward(
        layers, info, (1.0 / frame_count)[None], x_seg, target_seg, own_w, gain_tile
    )
    full_g = (
        tiles[:, :, :2, :own_gain].transpose(0, 2, 1, 3).reshape(layers, 2, width).astype(BF16).astype(F32)
    )
    grads, gain_grads = backward(layers, loss_grad, full_w, full_g, sent, saved)
    own_quads = lax.psum_scatter(
        grads.reshape(-1, part, width), ("section", "dp"), scatter_dimension=0, tiled=True
    ).astype(F32)
    own_grad = (
        own_quads.reshape(own_blocks // 4, part, 4, part).transpose(0, 2, 1, 3)
        .reshape(own_blocks, part * part)
    )
    summed_g, sums = lax.psum((gain_grads[:, :2], jnp.sum(stats, axis=2)), ("section", "dp"))
    own_gain_grad = lax.dynamic_slice(
        summed_g, (section_idx, 0, group_idx * own_gain), (1, 2, own_gain)
    )[0]
    own_square = jnp.sum(own_grad * own_grad) + jnp.sum(own_gain_grad * own_gain_grad)
    total_square = lax.psum(own_square, ("section", "dp"))
    loss_value = sums[0, 3] / frame_count
    grad_norm = jnp.sqrt(total_square)
    clip_limit = 0.00015 * math.sqrt(layers * (own_blocks * groups * part * part + 2 * width))
    factor = clip_limit / jnp.maximum(grad_norm, clip_limit)
    grad_blocks = own_grad * factor
    square = (own_blocks, part, part)
    shaped = grad_blocks.reshape(square)
    highest = lax.Precision.HIGHEST
    l_new = 0.95 * l_stats[0].reshape(square) + 0.05 * jnp.einsum(
        "bij,bkj->bik", shaped, shaped, precision=highest
    )
    r_new = 0.95 * r_stats[0].reshape(square) + 0.05 * jnp.einsum(
        "bji,bjk->bik", shaped, shaped, precision=highest
    )
    left_side = jnp.einsum("bij,bjk->bik", l_roots[0].reshape(square), shaped, precision=highest)
    precond = jnp.einsum("bij,bjk->bik", left_side, r_roots[0].reshape(square), precision=highest)
    master = w_master[0]
    w_new = master - 0.5 * (precond.reshape(master.shape) + 0.01 * master)
    gain_grad = own_gain_grad * factor
    m_new = 0.9 * gain_m[0] + 0.1 * gain_grad
    v_new = 0.999 * gain_v[0] + 0.001 * gain_grad * gain_grad
    step_num = step_count[0].astype(F32)
    m_hat = m_new / (1.0 - jnp.power(0.9, step_num))
    v_hat = v_new / (1.0 - jnp.power(0.999, step_num))
    gains_new = norm_gains[0] - 0.5 * m_hat / (jnp.sqrt(v_hat) + 1e-08)
    rms = jnp.sqrt(sums[section_idx, :3] / (frame_count * width)).reshape(1, 3)
    return (
        w_new[None],
        grad_blocks[None],
        l_new.reshape(master.shape)[None],
        r_new.reshape(master.shape)[None],
        gains_new[None],
        m_new[None],
        v_new[None],
        loss_value,
        grad_norm,
        rms,
    )


def solution(mesh):
    def step(*args):
        layers, groups = mesh.shape["section"], mesh.shape["dp"]
        micro, own_blocks = args[2].shape[0] // groups, args[4].shape[1]
        if micro <= layers == 4 and groups == 8 and own_blocks == 24:
            return body(*args)
        return pipelined_body(*args)

    block = P("section", "dp", None)
    gain = P("section", None, "dp")
    return jax.shard_map(
        step,
        mesh=mesh,
        in_specs=(
            P("dp", None), P("dp", None), P(), P(), block, gain, gain, gain, block, block, block, block, P(),
        ),
        out_specs=(block, block, block, block, gain, gain, gain, P(), P(), P("section", None)),
        check_vma=False,
    )
```

```python
import functools
import math

import jax
import jax.numpy as jnp
from jax import lax
from jax.experimental import pallas as pl
from jax.experimental.pallas import tpu as pltpu
from jax.sharding import PartitionSpec as P

HEADS = 8
F32 = jnp.float32
BF16 = jnp.bfloat16
VMEM_LIMIT = 61 * 1024 * 1024


def dot_nn(a, b):
    return lax.dot_general(a, b, (((1,), (0,)), ((), ())), preferred_element_type=F32)


def dot_nt(a, b):
    return lax.dot_general(a, b, (((1,), (1,)), ((), ())), preferred_element_type=F32)


def dot_tn(a, b):
    return lax.dot_general(a, b, (((0,), (0,)), ((), ())), preferred_element_type=F32)


def gelu_parts(x):
    ax = jnp.abs(x)
    bell = jnp.exp(-0.5 * x * x)
    t = 1.0 / (1.0 + (0.3275911 * 0.7071067811865476) * ax)
    poly = t * (
        0.5 * 0.254829592
        + t
        * (
            0.5 * -0.284496736
            + t * (0.5 * 1.421413741 + t * (0.5 * -1.453152027 + t * (0.5 * 1.061405429)))
        )
    )
    tail = poly * bell
    cdf = jnp.where(x >= 0.0, 1.0 - tail, tail)
    return x * cdf, cdf + x * bell * 0.3989422804014327


def stack_quads(w_ref, first, step, number):
    return jnp.concatenate([w_ref[0, first + step * i] for i in range(number)], axis=0)


MESH = pl.DeviceIdType.MESH


def mesh_place():
    section = lax.axis_index("section")
    group = lax.axis_index("dp")
    core = lax.rem(section, 2)
    y = lax.rem(group, 2)
    z = group // 2
    z_peers = (z, z + 1 - 2 * lax.rem(z, 2), lax.rem(z + 2, 4), 3 - z)
    return section, group, core, y, z_peers


def remote(source, target, send_sem, recv_sem, section, group):
    return pltpu.make_async_remote_copy(
        src_ref=source, dst_ref=target, send_sem=send_sem, recv_sem=recv_sem,
        device_id=(section, group), device_id_type=MESH,
    )


def greet(places):
    barrier = pltpu.get_barrier_semaphore()
    for place in places:
        pl.semaphore_signal(barrier, inc=1, device_id=place, device_id_type=MESH)
    pl.semaphore_wait(barrier, len(places))


class Gather:
    def __init__(self, own_ref, gain_ref, w_ref, gains_ref, sems):
        self.own, self.gain, self.w, self.gains = own_ref, gain_ref, w_ref, gains_ref
        self.spread, self.z_sems, self.y_sems, self.core_sems, self.gain_sems, self.local = sems
        self.section, self.group, self.core, self.y, self.z_peers = mesh_place()
        self.quads = own_ref.shape[0] // 2
        self.others = [lax.rem(self.section + k, 4) for k in range(1, 4)]
        self.places = [(o, self.group) for o in self.others] + [
            (self.section, lax.rem(self.group + k, 8)) for k in range(1, 8)
        ]

    def piece(self, layer, group):
        return self.w.at[layer, pl.ds(group * 2 * self.quads + self.quads * self.core, self.quads)]

    def spread_copy(self, k):
        peer = self.others[k]
        half = lax.rem(peer, 2) * self.quads
        return remote(
            self.own.at[pl.ds(half, self.quads)],
            self.w.at[self.section, pl.ds(self.group * 2 * self.quads + half, self.quads)],
            self.spread.at[0, k], self.spread.at[1, k], peer, self.group,
        )

    def spread_wait(self, layer):
        for k in range(3):
            @pl.when(lax.rem(layer + k + 1, 4) == self.section)
            def _():
                ref = self.piece(layer, self.group)
                remote(ref, ref, self.spread.at[0, k], self.spread.at[1, k], self.others[0], self.group).wait_recv()

    def z_copy(self, layer, k):
        ref = self.piece(layer, self.group)
        return remote(
            ref, ref, self.z_sems.at[0, layer, k], self.z_sems.at[1, layer, k],
            self.section, self.z_peers[k] * 2 + self.y,
        )

    def z_landed(self, layer, k):
        ref = self.piece(layer, self.z_peers[k] * 2 + self.y)
        return remote(
            ref, ref, self.z_sems.at[0, layer, k], self.z_sems.at[1, layer, k],
            self.section, self.z_peers[k] * 2 + self.y,
        )

    def y_copy(self, layer, k, mine=True):
        y = self.y if mine else 1 - self.y
        ref = self.piece(layer, self.z_peers[k] * 2 + y)
        return remote(
            ref, ref, self.y_sems.at[0, layer, k], self.y_sems.at[1, layer, k],
            self.section, self.group + 1 - 2 * self.y,
        )

    def core_copy(self, layer, k, mine=True):
        y = self.y if k < 4 else 1 - self.y
        core = self.core if mine else 1 - self.core
        at = (self.z_peers[k % 4] * 2 + y) * 2 * self.quads + self.quads * core
        ref = self.w.at[layer, pl.ds(at, self.quads)]
        return remote(
            ref, ref, self.core_sems.at[0, layer, k], self.core_sems.at[1, layer, k],
            self.section + 1 - 2 * self.core, self.group,
        )

    def gain_copy(self, k):
        if k < 7:
            peer = lax.rem(self.group + k + 1, 8)
            return remote(
                self.gain, self.gains.at[self.section, self.group],
                self.gain_sems.at[0, k], self.gain_sems.at[1, k], self.section, peer,
            )
        ref = self.gains.at[self.section]
        return remote(
            ref, ref, self.gain_sems.at[0, k], self.gain_sems.at[1, k], self.others[k - 7], self.group
        )

    def gain_landed(self, k):
        if k < 7:
            ref = self.gains.at[self.section, lax.rem(self.group - k - 1 + 8, 8)]
        else:
            ref = self.gains.at[lax.rem(self.section - (k - 6) + 4, 4)]
        return remote(ref, ref, self.gain_sems.at[0, k], self.gain_sems.at[1, k], self.section, self.group)

    def begin(self):
        greet(self.places)
        for k in range(3):
            self.spread_copy(k).start()
        for k in range(7):
            self.gain_copy(k).start()
        half = self.core * self.quads
        self.w[self.section, pl.ds(self.group * 2 * self.quads + half, self.quads)] = self.own[
            pl.ds(half, self.quads)
        ]
        self.gains[self.section, self.group] = self.gain[...]

    def share_gains(self):
        for k in range(7):
            self.gain_landed(k).wait_recv()
        for k in range(7, 10):
            self.gain_copy(k).start()

    def wait_gains(self):
        for k in range(7, 10):
            self.gain_landed(k).wait_recv()

    def kick(self, layer):
        self.spread_wait(layer)
        for k in range(1, 4):
            self.z_copy(layer, k).start()
        self.y_copy(layer, 0).start()
        self.core_copy(layer, 0).start()

    def serve(self, layer, step):
        if step < 4:
            self.z_landed(layer, step).wait_recv()
            self.y_copy(layer, step).start()
            self.core_copy(layer, step).start()
        else:
            self.y_copy(layer, step - 4, False).wait_recv()
            self.core_copy(layer, step).start()

    def finish(self, layer):
        for k in range(8):
            self.core_copy(layer, k, False).wait_recv()

    def end(self, layers):
        for k in range(3):
            self.spread_copy(k).wait_send()
        for k in range(10):
            self.gain_copy(k).wait_send()

        def per_layer(layer, _):
            for k in range(1, 4):
                self.z_copy(layer, k).wait_send()
            for k in range(4):
                self.y_copy(layer, k).wait_send()
            for k in range(8):
                self.core_copy(layer, k).wait_send()
            return 0

        lax.fori_loop(0, layers, per_layer, 0)


def forward_kernel(
    layers, half, info_ref, scale_ref, x_ref, target_ref, own_ref, own_gain_ref,
    probs_ref, heads_ref, att_ref, middle_ref, hidden_ref, slope_ref, sent_ref, loss_grad_ref, stats_ref,
    full_ref, gains_out_ref, hold_ref, out_ref, w_all_ref, gains_ref, *sems,
):
    seg, width = x_ref.shape
    dim = width // HEADS
    part = width // 4
    layer = pl.program_id(0)
    rows = 256
    chunks = seg // rows
    length = info_ref[0]
    gather = Gather(own_ref, own_gain_ref, w_all_ref, gains_ref, sems)
    w_ref = w_all_ref.at[pl.ds(layer, 1)]

    def keep_copy(index):
        return pltpu.make_async_copy(w_all_ref.at[index], full_ref.at[index], gather.local.at[index])

    @pl.when(layer == 0)
    def _():
        gather.begin()
        sent_ref[0] = x_ref[...]
        stats_ref[...] = jnp.zeros_like(stats_ref)
        gather.kick(0)
        gather.share_gains()
        for step in range(1, 4):
            gather.serve(0, step)
        gather.kick(1)
        for step in range(4, 8):
            gather.serve(0, step)
        gather.wait_gains()

    gather.finish(layer)
    keep_copy(layer).start()
    more = layer + 1 < layers

    def serve(step):
        @pl.when(more)
        def _():
            gather.serve(layer + 1, step)
        if step == 3:
            @pl.when(layer + 2 < layers)
            def _():
                gather.kick(layer + 2)

    def stream_of(at):
        prev = sent_ref[layer, at].astype(F32)
        skip = sent_ref[jnp.maximum(layer + 1 - half, 0), at].astype(F32)
        return prev + jnp.where(layer >= half, skip, 0.0)

    def gain_row(which):
        return jnp.concatenate(
            [gains_ref[layer, g, which : which + 1, : width // 8] for g in range(8)], axis=1
        ).astype(BF16).astype(F32)

    gain_one = gain_row(0)
    gain_two = gain_row(1)

    def qkv_step(i, _):
        at = pl.ds(pl.multiple_of(i * rows, rows), rows)
        stream = stream_of(at)
        factor = lax.rsqrt(jnp.mean(stream * stream, axis=-1, keepdims=True) + 1e-06)
        normed = (stream * factor * gain_one).astype(BF16)
        for t in range(3):
            qkv = dot_nn(normed, stack_quads(w_ref, t, 3, 4)).astype(BF16)
            for h in range(HEADS):
                heads_ref[0, t * HEADS + h, at] = qkv[:, h * dim : (h + 1) * dim]
        return 0

    lax.fori_loop(0, chunks, qkv_step, 0)
    frames = lax.broadcasted_iota(jnp.int32, (1, seg), 1)
    masking = jnp.where(frames < length, 0.0, -1e30).astype(F32)

    def head_step(h, _):
        keys = heads_ref[0, HEADS + h]
        values = heads_ref[0, 2 * HEADS + h]
        for i in range(chunks):
            at = pl.ds(i * rows, rows)
            scores = dot_nt(heads_ref[0, h, at], keys) * dim ** (-0.5) + masking
            top = jnp.max(scores, axis=-1, keepdims=True)
            expd = jnp.exp(scores - top)
            probs = (expd * (1.0 / jnp.sum(expd, axis=-1, keepdims=True))).astype(BF16)
            probs_ref[0, h, at] = probs
            hold_ref[h, at] = dot_nn(probs, values).astype(BF16)
        for step in range(1, 8):
            @pl.when(h == step)
            def _():
                serve(step)
        return 0

    lax.fori_loop(0, HEADS, head_step, 0)

    def ffn_step(i, _):
        at = pl.ds(pl.multiple_of(i * rows, rows), rows)
        attended = jnp.concatenate([hold_ref[h, at] for h in range(HEADS)], axis=1)
        att_ref[0, at] = attended
        branch_attn = dot_nn(attended, stack_quads(w_ref, 12, 1, 4))
        stream = stream_of(at)
        middle = stream + branch_attn
        middle_ref[0, at] = middle
        factor = lax.rsqrt(jnp.mean(middle * middle, axis=-1, keepdims=True) + 1e-06)
        normed = (middle * factor * gain_two).astype(BF16)
        branch_ffn = jnp.zeros((rows, width), F32)
        for c in range(4):
            pre_act = dot_nn(normed, stack_quads(w_ref, 16 + c, 4, 4))
            hidden, slope = gelu_parts(pre_act)
            hidden = hidden.astype(BF16)
            hidden_ref[0, c, at] = hidden
            slope_ref[0, c, at] = slope.astype(BF16)
            branch_ffn = branch_ffn + dot_nn(hidden, stack_quads(w_ref, 32 + 4 * c, 1, 4))
        output = middle + branch_ffn
        out_ref[at] = output
        sent_ref[jnp.minimum(layer + 1, layers - 1), at] = jnp.where(
            layer + 1 < layers, output.astype(BF16), sent_ref[layers - 1, at]
        )
        valid = (lax.broadcasted_iota(jnp.int32, (rows, 1), 0) + i * rows < length).astype(F32)
        for k, value in enumerate((stream, branch_attn, branch_ffn)):
            stats_ref[layer, k : k + 1] += jnp.sum(valid * value * value, axis=0, keepdims=True)
        return 0

    lax.fori_loop(0, chunks, ffn_step, 0)

    @pl.when(layer == layers - 1)
    def _():
        bins = width // 8
        lane = lax.broadcasted_iota(jnp.int32, (1, width), 1)
        is_real = lax.rem(lane, 2 * bins) < bins
        stem = lane // (2 * bins)
        present = jnp.zeros((1, width), F32)
        for k in range(4):
            present = jnp.where(stem == k, info_ref[1 + k].astype(F32), present)
        inverse = scale_ref[0]

        def loss_step(i, _):
            at = pl.ds(pl.multiple_of(i * rows, rows), rows)
            output = out_ref[at]
            square = output * output
            other = jnp.where(
                is_real, pltpu.roll(square, width - bins, 1), pltpu.roll(square, bins, 1)
            )
            magnitude = jnp.sqrt(square + other + 0.01)
            goal = target_ref[at]
            goal = jnp.concatenate(
                [goal[:, (k // 2) * bins : (k // 2 + 1) * bins] for k in range(8)], axis=1
            )
            differ = magnitude - goal
            smooth = jnp.sqrt(differ * differ + 0.01)
            valid = (lax.broadcasted_iota(jnp.int32, (rows, 1), 0) + i * rows < length).astype(F32)
            weight = valid * present
            loss_grad_ref[at] = weight * differ * output * inverse / (smooth * magnitude)
            stats_ref[0, 3:4] += jnp.sum(
                jnp.where(is_real, weight * smooth, 0.0), axis=0, keepdims=True
            )
            return 0

        lax.fori_loop(0, chunks, loss_step, 0)
        gains_out_ref[...] = gains_ref[...]
        gather.end(layers)
        for k in range(layers):
            keep_copy(k).wait()


class Scatter:
    def __init__(self, refs, sems):
        self.grads, self.core_in, self.y_in, self.z_in, self.last_out, self.last_in = refs
        self.core_sems, self.y_sems, self.z_sems, self.last_sems = sems
        self.section, self.group, self.core, self.y, self.z_peers = mesh_place()
        self.x = self.section // 2
        self.quads = self.grads.shape[3] // 2
        self.mine = pl.ds(self.core * self.quads, self.quads)
        self.theirs = pl.ds((1 - self.core) * self.quads, self.quads)

    def core_copy(self, layer, late):
        slot = lax.rem(layer, 2)
        zs = pl.ds(0, 1) if late else pl.ds(1, 3)
        return remote(
            self.grads.at[slot, zs, :, self.theirs], self.core_in.at[slot, zs],
            self.core_sems.at[0, slot, int(late)], self.core_sems.at[1, slot, int(late)],
            self.section + 1 - 2 * self.core, self.group,
        )

    def y_copy(self, layer, k):
        slot = lax.rem(layer, 2)
        return remote(
            self.grads.at[slot, self.z_peers[k], 1 - self.y, self.mine], self.y_in.at[slot, k],
            self.y_sems.at[0, slot, k], self.y_sems.at[1, slot, k],
            self.section, self.group + 1 - 2 * self.y,
        )

    def z_copy(self, layer, k):
        slot = lax.rem(layer, 2)
        return remote(
            self.grads.at[slot, self.z_peers[k], self.y, self.mine], self.z_in.at[layer, k - 1],
            self.z_sems.at[0, layer, k - 1], self.z_sems.at[1, layer, k - 1],
            self.section, self.z_peers[k] * 2 + self.y,
        )

    def last_copy(self, layer):
        slot = lax.rem(layer, 2)
        place = lax.rem(self.section - layer + 4, 4) - 1
        place = jnp.maximum(place, 0)
        return remote(
            self.last_out.at[slot], self.last_in.at[place],
            self.last_sems.at[0, slot], self.last_sems.at[1, place], layer, self.group,
        )

    def last_landed(self, place):
        return remote(
            self.last_in.at[place], self.last_in.at[place],
            self.last_sems.at[0, 0], self.last_sems.at[1, place], self.section, self.group,
        )

    def for_part(self, late, act):
        for k in (1, 2, 3, 0):
            @pl.when((self.z_peers[k] == 0) == late)
            def _():
                act(k)

    def add_core(self, layer, late):
        slot = lax.rem(layer, 2)
        self.core_copy(layer, late).wait_recv()

        def add(i, _):
            z, y = i // 2, lax.rem(i, 2)
            for q in range(self.quads):
                at = self.core * self.quads + q
                self.grads[slot, z, y, at] = self.grads[slot, z, y, at] + self.core_in[slot, z, y, q]
            return 0

        lax.fori_loop(0 if late else 2, 2 if late else 8, add, 0)
        self.for_part(late, lambda k: self.y_copy(layer, k).start())

    def add_y(self, layer, k):
        slot = lax.rem(layer, 2)
        self.y_copy(layer, k).wait_recv()
        for q in range(self.quads):
            at = self.core * self.quads + q
            z = self.z_peers[k]
            self.grads[slot, z, self.y, at] = self.grads[slot, z, self.y, at] + self.y_in[slot, k, q]
        if k:
            self.z_copy(layer, k).start()

    def add_y_if(self, layer, k, late):
        @pl.when((self.z_peers[k] == 0) == late)
        def _():
            self.add_y(layer, k)

    def add_z(self, layer, result_ref):
        slot = lax.rem(layer, 2)
        for k in range(1, 4):
            self.z_copy(layer, k).wait_recv()
        for q in range(self.quads):
            at = self.core * self.quads + q
            total = self.grads[slot, self.z_peers[0], self.y, at].astype(F32)
            for k in range(3):
                total = total + self.z_in[layer, k, q].astype(F32)

            @pl.when(layer == self.section)
            def _():
                result_ref[at] = total

            @pl.when(layer != self.section)
            def _():
                self.last_out[slot, q] = total.astype(BF16)

        @pl.when(layer != self.section)
        def _():
            self.last_copy(layer).start()

    def wait_sends(self, layer):
        for late in (False, True):
            self.core_copy(layer, late).wait_send()
        for k in range(4):
            self.y_copy(layer, k).wait_send()
        for k in range(1, 4):
            self.z_copy(layer, k).wait_send()

        @pl.when(layer != self.section)
        def _():
            self.last_copy(layer).wait_send()

    def collect(self, result_ref):
        for place in range(3):
            self.last_landed(place).wait_recv()
        for q in range(self.quads):
            mine = self.core * self.quads + q
            theirs = (1 - self.core) * self.quads + q
            result_ref[mine] = result_ref[mine] + self.last_in[1, q].astype(F32)
            result_ref[theirs] = self.last_in[0, q].astype(F32) + self.last_in[2, q].astype(F32)


class Totals:
    def __init__(self, refs, sems):
        self.stage_in, self.z_in, self.norm_section, self.norm_group = refs
        self.stage_sems, self.z_sems, self.section_sems, self.group_sems = sems
        self.section, self.group, self.core, self.y, self.z_peers = mesh_place()

    def stage_copy(self, k):
        peer = (
            (self.section + 1 - 2 * self.core, self.group),
            (self.section, self.group + 1 - 2 * self.y),
            (lax.rem(self.section + 2, 4), self.group),
        )[k]
        return remote(
            self.stage_in.at[2 * k], self.stage_in.at[2 * k + 1],
            self.stage_sems.at[0, k], self.stage_sems.at[1, k], *peer,
        )

    def z_copy(self, k):
        z = self.z_peers[0]
        return remote(
            self.z_in.at[z], self.z_in.at[z], self.z_sems.at[0, k - 1], self.z_sems.at[1, k - 1],
            self.section, self.z_peers[k] * 2 + self.y,
        )

    def z_landed(self, k):
        z = self.z_peers[k]
        return remote(
            self.z_in.at[z], self.z_in.at[z], self.z_sems.at[0, k - 1], self.z_sems.at[1, k - 1],
            self.section, self.z_peers[k] * 2 + self.y,
        )

    def begin(self, tile):
        self.stage_in[0] = tile
        self.stage_copy(0).start()

    def after_core(self):
        self.stage_copy(0).wait_recv()
        self.stage_in[2] = self.stage_in[0] + self.stage_in[1]
        self.stage_copy(1).start()

    def after_y(self):
        self.stage_copy(1).wait_recv()
        self.z_in[self.z_peers[0]] = self.stage_in[2] + self.stage_in[3]
        for k in range(1, 4):
            self.z_copy(k).start()

    def after_z(self):
        for k in range(1, 4):
            self.z_landed(k).wait_recv()
        self.stage_in[4] = self.z_in[0] + self.z_in[1] + self.z_in[2] + self.z_in[3]
        self.stage_copy(2).start()

    def after_x(self):
        self.stage_copy(2).wait_recv()
        return self.stage_in[4] + self.stage_in[5]

    def norm_copy(self, k):
        if k < 3:
            peer = (lax.rem(self.section + k + 1, 4), self.group)
            ref = self.norm_section.at[self.section]
            return remote(ref, ref, self.section_sems.at[0, k], self.section_sems.at[1, k], *peer)
        k = k - 3
        peer = (self.section, lax.rem(self.group + k + 1, 8))
        ref = self.norm_group.at[self.group]
        return remote(ref, ref, self.group_sems.at[0, k], self.group_sems.at[1, k], *peer)

    def norm_landed(self, k):
        if k < 3:
            ref = self.norm_section.at[lax.rem(self.section - k - 1 + 4, 4)]
            return remote(
                ref, ref, self.section_sems.at[0, k], self.section_sems.at[1, k], self.section, self.group
            )
        k = k - 3
        ref = self.norm_group.at[lax.rem(self.group - k - 1 + 8, 8)]
        return remote(ref, ref, self.group_sems.at[0, k], self.group_sems.at[1, k], self.section, self.group)

    def norm(self, value):
        self.norm_section[self.section] = value
        for k in range(3):
            self.norm_copy(k).start()
        for k in range(3):
            self.norm_landed(k).wait_recv()
        total = self.norm_section[0]
        for k in range(1, 4):
            total = total + self.norm_section[k]
        self.norm_group[self.group] = total
        for k in range(3, 10):
            self.norm_copy(k).start()
        for k in range(3, 10):
            self.norm_landed(k).wait_recv()
        total = self.norm_group[0]
        for k in range(1, 8):
            total = total + self.norm_group[k]
        return total

    def end(self):
        for k in range(3):
            self.stage_copy(k).wait_send()
        for k in range(1, 4):
            self.z_copy(k).wait_send()
        for k in range(10):
            self.norm_copy(k).wait_send()


def norm_reverse(value, gain, grad):
    factor = lax.rsqrt(jnp.mean(value * value, axis=-1, keepdims=True) + 1e-06)
    scaled = grad * gain
    mean = jnp.mean(value * scaled, axis=-1, keepdims=True)
    unit = value * factor
    back = factor * scaled - unit * (factor * factor * mean)
    return back, jnp.sum(grad * unit, axis=0, keepdims=True), (unit * gain).astype(BF16)


def backward_kernel(
    layers, half, loss_grad_ref, w_ref, gain_ref, sent_ref,
    probs_ref, heads_ref, att_ref, middle_ref, hidden_ref, slope_ref, stats_ref,
    result_ref, totals_ref, square_ref,
    sends_ref, dffn_ref, dpre_ref, normed_ref, dmid_ref, datt_ref, dhold_ref, dheads_ref, dqkv_ref,
    gain_grad_ref, *comm_refs,
):
    seg, width = loss_grad_ref.shape
    dim = width // HEADS
    part = width // 4
    layer = layers - 1 - pl.program_id(0)
    rows = 256
    chunks = seg // rows
    gain_one = gain_ref[0, 0:1]
    gain_two = gain_ref[0, 1:2]
    scatter = Scatter(comm_refs[:6], comm_refs[10:14])
    totals = Totals(comm_refs[6:10], comm_refs[14:])
    grads_ref = comm_refs[0]
    slot = lax.rem(layer, 2)

    @pl.when(layer == layers - 1)
    def _():
        section, group = scatter.section, scatter.group
        greet(
            [(lax.rem(section + k, 4), group) for k in range(1, 4)]
            + [(section, lax.rem(group + k, 8)) for k in range(1, 8)]
        )
        sends_ref[...] = jnp.zeros_like(sends_ref)
        gain_grad_ref[...] = jnp.zeros_like(gain_grad_ref)

    def put_grad(first, step, value):
        for r in range(4):
            quad = first + step * r
            owner = quad // 6
            grads_ref[slot, owner // 2, lax.rem(owner, 2), lax.rem(quad, 6)] = value[
                r * part : (r + 1) * part
            ].astype(BF16)

    def before(act):
        @pl.when(layer < layers - 1)
        def _():
            act(layer + 1)

    def ffn_step(i, _):
        at = pl.ds(pl.multiple_of(i * rows, rows), rows)
        later = sends_ref[jnp.minimum(layer + 1, layers - 1), at].astype(F32)
        skip = sends_ref[jnp.minimum(layer + half, layers - 1), at].astype(F32)
        upstream = jnp.where(
            layer == layers - 1, loss_grad_ref[at], later + jnp.where(layer + half < layers, skip, 0.0)
        )
        dffn = upstream.astype(BF16)
        dffn_ref[at] = dffn
        dnormed = jnp.zeros((rows, width), F32)
        for c in range(4):
            dhidden = dot_nt(dffn, stack_quads(w_ref, 32 + 4 * c, 1, 4))
            dpre = (dhidden * slope_ref[0, c, at].astype(F32)).astype(BF16)
            dpre_ref[c, at] = dpre
            dnormed = dnormed + dot_nt(dpre, stack_quads(w_ref, 16 + c, 4, 4))
        back, gain_grad, normed = norm_reverse(middle_ref[0, at], gain_two, dnormed)
        gain_grad_ref[layer, 1:2] += gain_grad
        normed_ref[at] = normed
        dmid = upstream + back
        dmid_ref[at] = dmid
        datt = dmid.astype(BF16)
        datt_ref[at] = datt
        dattended = dot_nt(datt, stack_quads(w_ref, 12, 1, 4)).astype(BF16)
        for h in range(HEADS):
            dhold_ref[h, at] = dattended[:, h * dim : (h + 1) * dim]

        @pl.when(i == 0)
        def _():
            before(lambda at: scatter.add_core(at, True))

        return 0

    lax.fori_loop(0, chunks, ffn_step, 0)
    before(lambda at: scatter.for_part(True, lambda k: scatter.add_y(at, k)))

    @pl.when(layer < layers - 2)
    def _():
        scatter.wait_sends(layer + 2)

    def ffn_grad_step(c, _):
        put_grad(32 + 4 * c, 1, dot_tn(hidden_ref[0, c], dffn_ref[...]))
        put_grad(16 + c, 4, dot_tn(normed_ref[...], dpre_ref[c]))
        return 0

    lax.fori_loop(0, 4, ffn_grad_step, 0)
    put_grad(12, 1, dot_tn(att_ref[0], datt_ref[...]))
    scatter.core_copy(layer, False).start()

    def head_step(h, _):
        queries = heads_ref[0, h]
        keys = heads_ref[0, HEADS + h]
        values = heads_ref[0, 2 * HEADS + h]
        dkeys = jnp.zeros((seg, dim), F32)
        dvalues = jnp.zeros((seg, dim), F32)
        for i in range(chunks):
            at = pl.ds(i * rows, rows)
            probs = probs_ref[0, h, at]
            dhold = dhold_ref[h, at]
            dprobs = dot_nt(dhold, values)
            wide = probs.astype(F32)
            dot_sum = jnp.sum(wide * dprobs, axis=-1, keepdims=True)
            dscores = (wide * (dprobs - dot_sum)).astype(BF16)
            dheads_ref[h, at] = (dot_nn(dscores, keys) * dim ** (-0.5)).astype(BF16)
            dvalues = dvalues + dot_tn(probs, dhold)
            dkeys = dkeys + dot_tn(dscores, heads_ref[0, h, at])
        dheads_ref[HEADS + h] = (dkeys * dim ** (-0.5)).astype(BF16)
        dheads_ref[2 * HEADS + h] = dvalues.astype(BF16)

        @pl.when(h == 1)
        def _():
            scatter.add_core(layer, False)

        for k, after in ((1, 5), (2, 6), (3, 7)):
            @pl.when(h == after)
            def _():
                scatter.add_y_if(layer, k, False)

        return 0

    lax.fori_loop(0, HEADS, head_step, 0)

    def qkv_step(i, _):
        at = pl.ds(pl.multiple_of(i * rows, rows), rows)
        dnormed = jnp.zeros((rows, width), F32)
        for t in range(3):
            dqkv = jnp.concatenate([dheads_ref[t * HEADS + h, at] for h in range(HEADS)], axis=1)
            dqkv_ref[t, at] = dqkv
            dnormed = dnormed + dot_nt(dqkv, stack_quads(w_ref, t, 3, 4))
        prev = sent_ref[layer, at].astype(F32)
        skip = sent_ref[jnp.maximum(layer + 1 - half, 0), at].astype(F32)
        stream = prev + jnp.where(layer >= half, skip, 0.0)
        back, gain_grad, normed = norm_reverse(stream, gain_one, dnormed)
        gain_grad_ref[layer, 0:1] += gain_grad
        normed_ref[at] = normed
        sends_ref[layer, at] = (dmid_ref[at] + back).astype(BF16)
        return 0

    lax.fori_loop(0, chunks, qkv_step, 0)

    def qkv_grad_step(t, _):
        put_grad(t, 3, dot_tn(normed_ref[...], dqkv_ref[t]))
        return 0

    lax.fori_loop(0, 3, qkv_grad_step, 0)
    scatter.add_y_if(layer, 0, False)
    scatter.core_copy(layer, True).start()
    before(lambda at: scatter.add_z(at, result_ref))

    @pl.when(layer == 0)
    def _():
        lane = lax.broadcasted_iota(jnp.int32, (1, width), 1)
        rows_out = [gain_grad_ref[k // 2, k % 2 : k % 2 + 1] for k in range(2 * layers)]
        for k in range(layers):
            row = jnp.zeros((1, width), F32)
            for i in range(4):
                value = jnp.sum(stats_ref[k, i : i + 1], axis=1, keepdims=True)
                row = jnp.where(lane == i, value, row)
            rows_out.append(row)
        rows_out.append(jnp.zeros((16 - 3 * layers, width), F32))
        totals.begin(jnp.concatenate(rows_out, axis=0))
        scatter.add_core(0, True)
        totals.after_core()
        scatter.for_part(True, lambda k: scatter.add_y(0, k))
        totals.after_y()
        scatter.add_z(0, result_ref)
        totals.after_z()
        scatter.collect(result_ref)
        square = jnp.zeros((8, width), F32)
        for q in range(6):
            value = result_ref[q]
            square = square + jnp.sum((value * value).reshape(part // 8, 8, width), axis=0)
        folded = square[:, :128] + square[:, 128:256] + square[:, 256:]
        square_ref[...] = totals.norm(folded)
        totals_ref[...] = totals.after_x()
        scatter.wait_sends(1)
        scatter.wait_sends(0)
        totals.end()


FF = 1536


def from_behind(value, axis, by):
    peers = lax.axis_size(axis)
    pairs = [(i, i + by) for i in range(peers) if 0 <= i + by < peers]
    return lax.ppermute(value, axis, pairs)


def unblock(blocks, row_count, col_count, block_size):
    return (
        blocks.reshape(row_count // block_size, col_count // block_size, block_size, block_size)
        .transpose(0, 2, 1, 3)
        .reshape(row_count, col_count)
    )


def to_blocks(matrix, block_size):
    row_count, col_count = matrix.shape
    return (
        matrix.reshape(row_count // block_size, block_size, col_count // block_size, block_size)
        .transpose(0, 2, 1, 3)
        .reshape(-1, block_size * block_size)
    )


def split_matrices(blocks, model_width):
    block_size = model_width // 4
    shapes = (
        (model_width, 3 * model_width),
        (model_width, model_width),
        (model_width, FF),
        (FF, model_width),
    )
    result = []
    offset = 0
    for row_count, col_count in shapes:
        number = row_count * col_count // (block_size * block_size)
        result.append(unblock(blocks[offset : offset + number], row_count, col_count, block_size))
        offset = offset + number
    return result


def rms_norm(stream, gain):
    factor = lax.rsqrt(jnp.mean(stream * stream, axis=-1, keepdims=True) + 1e-06)
    return (stream * factor * gain, factor)


def norm_back(stream, factor, gain, grad):
    scaled = grad * gain
    grad_in = factor * scaled - stream * factor**3 * jnp.mean(
        stream * scaled, axis=-1, keepdims=True
    )
    return (grad_in, jnp.sum(grad * stream * factor, axis=0))


def gelu_slope(pre_act):
    return (
        0.5 * (1.0 + lax.erf(pre_act * 0.7071067811865476))
        + pre_act * jnp.exp(-0.5 * pre_act * pre_act) * 0.3989422804014327
    )


def layer_forward(stream, matrices, gain_pair, length):
    w_qkv, w_out, w_up, w_down = matrices
    row_count, model_width = stream.shape
    head_dim = model_width // HEADS
    frames = jnp.arange(row_count)
    norm_one, scale_one = rms_norm(stream, gain_pair[0])
    normed = norm_one.astype(BF16)
    qkv_all = jnp.dot(normed, w_qkv, preferred_element_type=jnp.float32).astype(BF16)
    queries = qkv_all[:, :model_width].reshape(row_count, HEADS, head_dim)
    key_rows = qkv_all[:, model_width : 2 * model_width].reshape(row_count, HEADS, head_dim)
    value_rows = qkv_all[:, 2 * model_width :].reshape(row_count, HEADS, head_dim)
    masking = jnp.where(frames < length, 0.0, -1e30).astype(jnp.float32)
    scores = jnp.einsum(
        "qhe,khe->hqk", queries, key_rows, preferred_element_type=jnp.float32
    ) * head_dim ** (-0.5)
    attn_probs = jax.nn.softmax(scores + masking[None, None, :], axis=-1)
    probs_low = attn_probs.astype(BF16)
    attended = (
        jnp.einsum("hqk,khe->qhe", probs_low, value_rows, preferred_element_type=jnp.float32)
        .reshape(row_count, model_width)
        .astype(BF16)
    )
    branch_attn = jnp.dot(attended, w_out, preferred_element_type=jnp.float32)
    middle = stream + branch_attn
    norm_two, scale_two = rms_norm(middle, gain_pair[1])
    normed_two = norm_two.astype(BF16)
    pre_act = jnp.dot(normed_two, w_up, preferred_element_type=jnp.float32)
    hidden = jax.nn.gelu(pre_act, approximate=False).astype(BF16)
    branch_ffn = jnp.dot(hidden, w_down, preferred_element_type=jnp.float32)
    kept_vals = (
        scale_one,
        normed,
        queries,
        key_rows,
        value_rows,
        attn_probs,
        probs_low,
        attended,
        middle,
        scale_two,
        normed_two,
        pre_act,
        hidden,
    )
    return (middle + branch_ffn, branch_attn, branch_ffn, kept_vals)


def layer_backward(stream, matrices, gain_pair, length, upstream):
    w_qkv, w_out, w_up, w_down = matrices
    row_count, model_width = stream.shape
    head_dim = model_width // HEADS
    output, branch_attn, branch_ffn, kept_vals = layer_forward(stream, matrices, gain_pair, length)
    (
        scale_one,
        normed,
        queries,
        key_rows,
        value_rows,
        attn_probs,
        probs_low,
        attended,
        middle,
        scale_two,
        normed_two,
        pre_act,
        hidden,
    ) = kept_vals
    grad_ffn = upstream.astype(BF16)
    grad_down = jnp.dot(hidden.T, grad_ffn, preferred_element_type=jnp.float32)
    grad_hidden = jnp.dot(grad_ffn, w_down.T, preferred_element_type=jnp.float32)
    grad_pre = (grad_hidden * gelu_slope(pre_act)).astype(BF16)
    grad_up = jnp.dot(normed_two.T, grad_pre, preferred_element_type=jnp.float32)
    back_mid, gain_two = norm_back(
        middle,
        scale_two,
        gain_pair[1],
        jnp.dot(grad_pre, w_up.T, preferred_element_type=jnp.float32),
    )
    grad_mid = upstream + back_mid
    grad_branch = grad_mid.astype(BF16)
    grad_out = jnp.dot(attended.T, grad_branch, preferred_element_type=jnp.float32)
    grad_att = (
        jnp.dot(grad_branch, w_out.T, preferred_element_type=jnp.float32)
        .astype(BF16)
        .reshape(row_count, HEADS, head_dim)
    )
    grad_value = jnp.einsum("hqk,qhe->khe", probs_low, grad_att, preferred_element_type=jnp.float32)
    grad_probs = jnp.einsum(
        "qhe,khe->hqk", grad_att, value_rows, preferred_element_type=jnp.float32
    )
    grad_scores = (
        attn_probs * (grad_probs - jnp.sum(attn_probs * grad_probs, axis=-1, keepdims=True))
    ).astype(BF16)
    grad_query = jnp.einsum(
        "hqk,khe->qhe", grad_scores, key_rows, preferred_element_type=jnp.float32
    ) * head_dim ** (-0.5)
    grad_key = jnp.einsum(
        "hqk,qhe->khe", grad_scores, queries, preferred_element_type=jnp.float32
    ) * head_dim ** (-0.5)
    grad_qkv = jnp.concatenate(
        [
            grad_query.reshape(row_count, model_width),
            grad_key.reshape(row_count, model_width),
            grad_value.reshape(row_count, model_width),
        ],
        axis=1,
    ).astype(BF16)
    grad_wqkv = jnp.dot(normed.T, grad_qkv, preferred_element_type=jnp.float32)
    back_in, gain_one = norm_back(
        stream,
        scale_one,
        gain_pair[0],
        jnp.dot(grad_qkv, w_qkv.T, preferred_element_type=jnp.float32),
    )
    return (
        grad_mid + back_in,
        (grad_wqkv, grad_out, grad_up, grad_down),
        jnp.stack([gain_one, gain_two]),
    )


def spectral_terms(output, target, length, present_row, frame_count):
    row_count, model_width = output.shape
    bin_count = model_width // 8
    spectra = output.reshape(row_count, 4, 2, bin_count)
    real_part = spectra[:, :, 0]
    imag_part = spectra[:, :, 1]
    magnitude = jnp.sqrt(real_part * real_part + imag_part * imag_part + 0.01)
    differ = magnitude - target.reshape(row_count, 4, bin_count)
    smooth_err = jnp.sqrt(differ * differ + 0.01)
    weight = (jnp.arange(row_count) < length).astype(jnp.float32)[:, None, None] * present_row[
        None, :, None
    ]
    loss_slope = weight * differ / smooth_err / magnitude / frame_count
    grad_spec = jnp.stack([loss_slope * real_part, loss_slope * imag_part], axis=2).reshape(
        row_count, model_width
    )
    return (jnp.sum(smooth_err * weight), grad_spec)


def pipelined_body(
    x_in,
    targets,
    valid_len,
    present_stems,
    w_master,
    norm_gains,
    gain_m,
    gain_v,
    l_stats,
    r_stats,
    l_roots,
    r_roots,
    step_count,
):
    model_width = x_in.shape[1]
    block_size = model_width // 4
    sections = lax.axis_size("section")
    section_idx = lax.axis_index("section")
    half_way = sections // 2
    groups = lax.axis_size("dp")
    group_idx = lax.axis_index("dp")
    micro_count = valid_len.shape[0] // groups
    seg_len = x_in.shape[0] // micro_count
    own_blocks = w_master.shape[1]
    own_gain = norm_gains.shape[2]
    full_w, full_g = (
        lax.all_gather(w_master.astype(BF16), "dp", axis=1, tiled=True),
        lax.all_gather(norm_gains.astype(BF16), "dp", axis=2, tiled=True),
    )
    matrices = split_matrices(full_w[0], model_width)
    gain_pair = full_g[0].astype(jnp.float32)
    lengths = lax.dynamic_slice_in_dim(valid_len, group_idx * micro_count, micro_count)
    stem_flags = lax.dynamic_slice_in_dim(
        present_stems, group_idx * micro_count, micro_count
    ).astype(jnp.float32)
    frame_count = jnp.sum(valid_len).astype(jnp.float32)
    decoder = section_idx >= half_way
    encoder = section_idx < half_way
    is_last = section_idx == sections - 1
    act_shape = (micro_count, seg_len, model_width)

    def forward_step(step_idx, loop_state):
        in_rows, kept_prev, skip_store, loss_grads, loss_sum, sq_sums = loop_state
        micro_idx = step_idx - section_idx
        active = (micro_idx >= 0) & (micro_idx < micro_count)
        slot_idx = jnp.clip(micro_idx, 0, micro_count - 1)
        fresh_rows = lax.dynamic_slice_in_dim(x_in, slot_idx * seg_len, seg_len, 0)
        previous = jnp.where(section_idx == 0, fresh_rows, in_rows)
        stream = previous.astype(jnp.float32) + jnp.where(
            decoder, skip_store[slot_idx].astype(jnp.float32), 0.0
        )
        length = lengths[slot_idx]
        target = lax.dynamic_slice_in_dim(targets, slot_idx * seg_len, seg_len, 0)

        def forward_compute_fn(operand):
            output, branch_attn, branch_ffn, kept_vals = layer_forward(
                stream, matrices, gain_pair, length
            )
            valid = (jnp.arange(seg_len) < length).astype(jnp.float32)[:, None]
            squares = jnp.stack(
                [
                    jnp.sum(valid * stream * stream),
                    jnp.sum(valid * branch_attn * branch_attn),
                    jnp.sum(valid * branch_ffn * branch_ffn),
                ]
            )
            seg_loss, grad_spec = spectral_terms(
                output, target, length, stem_flags[slot_idx], frame_count
            )
            return (output, squares, seg_loss, grad_spec)

        def forward_spare_fn(operand):
            empty = jnp.zeros((seg_len, model_width), jnp.float32)
            return (empty, jnp.zeros((3,), jnp.float32), jnp.zeros((), jnp.float32), empty)

        output, squares, seg_loss, grad_spec = lax.cond(
            active, forward_compute_fn, forward_spare_fn, 0
        )
        kept_prev = kept_prev.at[slot_idx].set(jnp.where(active, previous, kept_prev[slot_idx]))
        loss_grads = loss_grads.at[slot_idx].set(
            jnp.where(active & is_last, grad_spec, loss_grads[slot_idx])
        )
        loss_sum = loss_sum + jnp.where(is_last, seg_loss, 0.0)
        sq_sums = sq_sums + squares
        sent_rows = output.astype(BF16)
        in_rows = from_behind(sent_rows, "section", 1)
        from_encoder = from_behind(sent_rows, "section", half_way)
        recv_idx = step_idx - section_idx + half_way
        usable = decoder & (recv_idx >= 0) & (recv_idx < micro_count)
        recv_slot = jnp.clip(recv_idx, 0, micro_count - 1)
        skip_store = skip_store.at[recv_slot].set(
            jnp.where(usable, from_encoder, skip_store[recv_slot])
        )
        return (in_rows, kept_prev, skip_store, loss_grads, loss_sum, sq_sums)

    start_state = (
        jnp.zeros((seg_len, model_width), BF16),
        jnp.zeros(act_shape, BF16),
        jnp.zeros(act_shape, BF16),
        jnp.zeros(act_shape, jnp.float32),
        jnp.zeros((), jnp.float32),
        jnp.zeros((3,), jnp.float32),
    )
    unused_rows, kept_prev, skip_store, loss_grads, loss_sum, sq_sums = lax.fori_loop(
        0, micro_count + sections - 1, forward_step, start_state
    )

    def backward_step(step_idx, loop_state):
        in_grads, skip_grad_store, grad_mats, grad_gains = loop_state
        micro_idx = step_idx - (sections - 1 - section_idx)
        active = (micro_idx >= 0) & (micro_idx < micro_count)
        slot_idx = jnp.clip(micro_idx, 0, micro_count - 1)
        upstream = jnp.where(
            is_last,
            loss_grads[slot_idx],
            in_grads.astype(jnp.float32)
            + jnp.where(encoder, skip_grad_store[slot_idx].astype(jnp.float32), 0.0),
        )
        stream = kept_prev[slot_idx].astype(jnp.float32) + jnp.where(
            decoder, skip_store[slot_idx].astype(jnp.float32), 0.0
        )
        length = lengths[slot_idx]

        def backward_compute_fn(operand):
            return layer_backward(stream, matrices, gain_pair, length, upstream)

        def backward_spare_fn(operand):
            return (
                jnp.zeros_like(stream),
                tuple((jnp.zeros(mat.shape, jnp.float32) for mat in matrices)),
                jnp.zeros((2, model_width), jnp.float32),
            )

        grad_stream, layer_mats, layer_gains = lax.cond(
            active, backward_compute_fn, backward_spare_fn, 0
        )
        grad_mats = tuple((total + piece for total, piece in zip(grad_mats, layer_mats)))
        grad_gains = grad_gains + layer_gains
        grad_rows = grad_stream.astype(BF16)
        in_grads = from_behind(grad_rows, "section", -1)
        from_decoder = from_behind(grad_rows, "section", -half_way)
        recv_idx = micro_idx + half_way
        usable = encoder & (recv_idx >= 0) & (recv_idx < micro_count)
        recv_slot = jnp.clip(recv_idx, 0, micro_count - 1)
        skip_grad_store = skip_grad_store.at[recv_slot].set(
            jnp.where(usable, from_decoder, skip_grad_store[recv_slot])
        )
        return (in_grads, skip_grad_store, grad_mats, grad_gains)

    back_state = (
        jnp.zeros((seg_len, model_width), BF16),
        jnp.zeros(act_shape, BF16),
        tuple((jnp.zeros(mat.shape, jnp.float32) for mat in matrices)),
        jnp.zeros((2, model_width), jnp.float32),
    )
    unused_grads, unused_store, grad_mats, grad_gains = lax.fori_loop(
        0, micro_count + sections - 1, backward_step, back_state
    )
    grad_all = jnp.concatenate([to_blocks(mat, block_size) for mat in grad_mats], axis=0)
    summed_w, summed_g = lax.psum((grad_all, grad_gains), "dp")
    own_grad = lax.dynamic_slice_in_dim(summed_w, group_idx * own_blocks, own_blocks, 0)
    own_gain_grad = lax.dynamic_slice_in_dim(summed_g, group_idx * own_gain, own_gain, 1)
    own_square = jnp.sum(own_grad * own_grad) + jnp.sum(own_gain_grad * own_gain_grad)
    rows_local = jnp.zeros((sections, 3), jnp.float32).at[section_idx].set(sq_sums)
    total_square, loss_value, rows_total = lax.psum(
        (own_square, loss_sum / frame_count, rows_local), ("section", "dp")
    )
    grad_norm = jnp.sqrt(total_square)
    clip_limit = 0.00015 * math.sqrt(
        sections * (own_blocks * groups * block_size * block_size + 2 * model_width)
    )
    factor = clip_limit / jnp.maximum(grad_norm, clip_limit)
    grad_blocks = own_grad * factor
    square = (own_blocks, block_size, block_size)
    shaped = grad_blocks.reshape(square)
    highest = lax.Precision.HIGHEST
    l_new = 0.95 * l_stats[0].reshape(square) + 0.05 * jnp.einsum(
        "bij,bkj->bik", shaped, shaped, precision=highest
    )
    r_new = 0.95 * r_stats[0].reshape(square) + 0.05 * jnp.einsum(
        "bji,bjk->bik", shaped, shaped, precision=highest
    )
    left_side = jnp.einsum("bij,bjk->bik", l_roots[0].reshape(square), shaped, precision=highest)
    precond = jnp.einsum("bij,bjk->bik", left_side, r_roots[0].reshape(square), precision=highest)
    master = w_master[0]
    w_new = master - 0.5 * (precond.reshape(master.shape) + 0.01 * master)
    gain_grad = own_gain_grad * factor
    m_new = 0.9 * gain_m[0] + 0.1 * gain_grad
    v_new = 0.999 * gain_v[0] + 0.001 * gain_grad * gain_grad
    step_num = step_count[0].astype(jnp.float32)
    m_hat = m_new / (1.0 - jnp.power(0.9, step_num))
    v_hat = v_new / (1.0 - jnp.power(0.999, step_num))
    gains_new = norm_gains[0] - 0.5 * m_hat / (jnp.sqrt(v_hat) + 1e-08)
    rms = jnp.sqrt(rows_total[section_idx] / (frame_count * model_width)).reshape(1, 3)
    return (
        w_new[None],
        grad_blocks[None],
        l_new.reshape(master.shape)[None],
        r_new.reshape(master.shape)[None],
        gains_new[None],
        m_new[None],
        v_new[None],
        loss_value,
        grad_norm,
        rms,
    )


def layer_block(shape):
    return pl.BlockSpec((1,) + shape, lambda i: (i,) + (0,) * len(shape))


def whole_block(shape):
    return pl.BlockSpec(shape, lambda i: (0,) * len(shape))


def forward(layers, info, inverse, x_seg, target_seg, own_w, own_gain):
    seg, width = x_seg.shape
    dim = width // HEADS
    part = width // 4
    half = layers // 2
    shapes = (
        (HEADS, seg, seg), (3 * HEADS, seg, dim), (seg, width), (seg, width), (4, seg, width), (4, seg, width)
    )
    kinds = (BF16, BF16, BF16, F32, BF16, BF16)
    return pl.pallas_call(
        functools.partial(forward_kernel, layers, half),
        grid=(layers,),
        in_specs=[
            pl.BlockSpec(memory_space=pltpu.SMEM),
            pl.BlockSpec(memory_space=pltpu.SMEM),
            whole_block((seg, width)),
            whole_block((seg, width // 2)),
            pl.BlockSpec(memory_space=pltpu.VMEM),
            pl.BlockSpec(memory_space=pltpu.VMEM),
        ],
        out_specs=[layer_block(s) for s in shapes]
        + [whole_block((layers, seg, width)), whole_block((seg, width)), whole_block((layers, 8, width))]
        + [pl.BlockSpec(memory_space=pl.ANY), pl.BlockSpec(memory_space=pltpu.VMEM)],
        out_shape=[jax.ShapeDtypeStruct((layers,) + s, k) for s, k in zip(shapes, kinds)]
        + [
            jax.ShapeDtypeStruct((layers, seg, width), BF16),
            jax.ShapeDtypeStruct((seg, width), F32),
            jax.ShapeDtypeStruct((layers, 8, width), F32),
            jax.ShapeDtypeStruct((layers, 48, part, width), BF16),
            jax.ShapeDtypeStruct((layers, 8, 8, 128), F32),
        ],
        scratch_shapes=[
            pltpu.VMEM((HEADS, seg, dim), BF16),
            pltpu.VMEM((seg, width), F32),
            pltpu.VMEM((layers, 48, part, width), BF16),
            pltpu.VMEM((layers, 8, 8, 128), F32),
            pltpu.SemaphoreType.DMA((2, 3)),
            pltpu.SemaphoreType.DMA((2, layers, 4)),
            pltpu.SemaphoreType.DMA((2, layers, 4)),
            pltpu.SemaphoreType.DMA((2, layers, 8)),
            pltpu.SemaphoreType.DMA((2, 10)),
            pltpu.SemaphoreType.DMA((layers,)),
        ],
        compiler_params=pltpu.CompilerParams(
            vmem_limit_bytes=VMEM_LIMIT, collective_id=0, has_side_effects=True
        ),
    )(info, inverse, x_seg, target_seg, own_w, own_gain)


def backward(layers, loss_grad, full_w, full_g, sent, saved, stats):
    seg, width = loss_grad.shape
    dim = width // HEADS
    part = width // 4
    half = layers // 2

    def from_end(array):
        shape = array.shape[1:]
        return pl.BlockSpec((1,) + shape, lambda i: (layers - 1 - i,) + (0,) * len(shape))

    return pl.pallas_call(
        functools.partial(backward_kernel, layers, half),
        grid=(layers,),
        in_specs=[
            whole_block((seg, width)),
            from_end(full_w),
            from_end(full_g),
            whole_block((layers, seg, width)),
        ]
        + [from_end(a) for a in saved]
        + [pl.BlockSpec(memory_space=pltpu.VMEM)],
        out_specs=[pl.BlockSpec(memory_space=pltpu.VMEM)] * 3,
        out_shape=[
            jax.ShapeDtypeStruct((6, part, width), F32),
            jax.ShapeDtypeStruct((16, width), F32),
            jax.ShapeDtypeStruct((8, 128), F32),
        ],
        scratch_shapes=[
            pltpu.VMEM((layers, seg, width), BF16),
            pltpu.VMEM((seg, width), BF16),
            pltpu.VMEM((4, seg, width), BF16),
            pltpu.VMEM((seg, width), BF16),
            pltpu.VMEM((seg, width), F32),
            pltpu.VMEM((seg, width), BF16),
            pltpu.VMEM((HEADS, seg, dim), BF16),
            pltpu.VMEM((3 * HEADS, seg, dim), BF16),
            pltpu.VMEM((3, seg, width), BF16),
            pltpu.VMEM((layers, 8, width), F32),
            pltpu.VMEM((2, 4, 2, 6, part, width), BF16),
            pltpu.VMEM((2, 4, 2, 3, part, width), BF16),
            pltpu.VMEM((2, 4, 3, part, width), BF16),
            pltpu.VMEM((layers, 3, 3, part, width), BF16),
            pltpu.VMEM((2, 3, part, width), BF16),
            pltpu.VMEM((3, 3, part, width), BF16),
            pltpu.VMEM((6, 16, width), F32),
            pltpu.VMEM((4, 16, width), F32),
            pltpu.VMEM((4, 8, 128), F32),
            pltpu.VMEM((8, 8, 128), F32),
            pltpu.SemaphoreType.DMA((2, 2, 2)),
            pltpu.SemaphoreType.DMA((2, 2, 4)),
            pltpu.SemaphoreType.DMA((2, layers, 3)),
            pltpu.SemaphoreType.DMA((2, 3)),
            pltpu.SemaphoreType.DMA((2, 3)),
            pltpu.SemaphoreType.DMA((2, 3)),
            pltpu.SemaphoreType.DMA((2, 3)),
            pltpu.SemaphoreType.DMA((2, 7)),
        ],
        compiler_params=pltpu.CompilerParams(
            vmem_limit_bytes=VMEM_LIMIT, collective_id=1, has_side_effects=True
        ),
    )(loss_grad, full_w, full_g, sent, *saved, stats)


def body(
    x_in, targets, valid_len, present_stems, w_master, norm_gains, gain_m, gain_v,
    l_stats, r_stats, l_roots, r_roots, step_count,
):
    width = x_in.shape[1]
    part = width // 4
    layers = lax.axis_size("section")
    section_idx = lax.axis_index("section")
    groups = lax.axis_size("dp")
    group_idx = lax.axis_index("dp")
    micro = valid_len.shape[0] // groups
    seg = x_in.shape[0] // micro
    own_blocks = w_master.shape[1]
    own_gain = norm_gains.shape[2]
    own_w = (
        w_master[0].astype(BF16).reshape(own_blocks // 4, 4, part, part).transpose(0, 2, 1, 3)
        .reshape(own_blocks // 4, part, width)
    )
    gain_tile = jnp.zeros((8, 128), F32).at[:2, :own_gain].set(norm_gains[0])
    slot = jnp.minimum(section_idx, micro - 1)
    used = (section_idx < micro).astype(jnp.int32)
    at = group_idx * micro + slot
    info = jnp.concatenate([valid_len[at][None] * used, present_stems[at] * used])
    frame_count = jnp.sum(valid_len).astype(F32)
    x_seg = lax.dynamic_slice_in_dim(x_in, slot * seg, seg, 0)
    target_seg = lax.dynamic_slice_in_dim(targets, slot * seg, seg, 0)
    *saved, sent, loss_grad, stats, full_w, tiles = forward(
        layers, info, (1.0 / frame_count)[None], x_seg, target_seg, own_w, gain_tile
    )
    full_g = (
        tiles[:, :, :2, :own_gain].transpose(0, 2, 1, 3).reshape(layers, 2, width).astype(BF16).astype(F32)
    )
    own_quads, tile, squares = backward(layers, loss_grad, full_w, full_g, sent, saved, stats)
    own_grad = (
        own_quads.reshape(own_blocks // 4, part, 4, part).transpose(0, 2, 1, 3)
        .reshape(own_blocks, part * part)
    )
    summed_g = tile[: 2 * layers].reshape(layers, 2, width)
    sums = tile[2 * layers : 3 * layers, :4]
    own_gain_grad = lax.dynamic_slice(
        summed_g, (section_idx, 0, group_idx * own_gain), (1, 2, own_gain)
    )[0]
    total_square = jnp.sum(squares) + jnp.sum(summed_g * summed_g)
    loss_value = sums[0, 3] / frame_count
    grad_norm = jnp.sqrt(total_square)
    clip_limit = 0.00015 * math.sqrt(layers * (own_blocks * groups * part * part + 2 * width))
    factor = clip_limit / jnp.maximum(grad_norm, clip_limit)
    grad_blocks = own_grad * factor
    square = (own_blocks, part, part)
    shaped = grad_blocks.reshape(square)
    highest = lax.Precision.HIGHEST
    l_new = 0.95 * l_stats[0].reshape(square) + 0.05 * jnp.einsum(
        "bij,bkj->bik", shaped, shaped, precision=highest
    )
    r_new = 0.95 * r_stats[0].reshape(square) + 0.05 * jnp.einsum(
        "bji,bjk->bik", shaped, shaped, precision=highest
    )
    left_side = jnp.einsum("bij,bjk->bik", l_roots[0].reshape(square), shaped, precision=highest)
    precond = jnp.einsum("bij,bjk->bik", left_side, r_roots[0].reshape(square), precision=highest)
    master = w_master[0]
    w_new = master - 0.5 * (precond.reshape(master.shape) + 0.01 * master)
    gain_grad = own_gain_grad * factor
    m_new = 0.9 * gain_m[0] + 0.1 * gain_grad
    v_new = 0.999 * gain_v[0] + 0.001 * gain_grad * gain_grad
    step_num = step_count[0].astype(F32)
    m_hat = m_new / (1.0 - jnp.power(0.9, step_num))
    v_hat = v_new / (1.0 - jnp.power(0.999, step_num))
    gains_new = norm_gains[0] - 0.5 * m_hat / (jnp.sqrt(v_hat) + 1e-08)
    rms = jnp.sqrt(sums[section_idx, :3] / (frame_count * width)).reshape(1, 3)
    return (
        w_new[None],
        grad_blocks[None],
        l_new.reshape(master.shape)[None],
        r_new.reshape(master.shape)[None],
        gains_new[None],
        m_new[None],
        v_new[None],
        loss_value,
        grad_norm,
        rms,
    )


def solution(mesh):
    def step(*args):
        layers, groups = mesh.shape["section"], mesh.shape["dp"]
        micro, own_blocks = args[2].shape[0] // groups, args[4].shape[1]
        if micro <= layers == 4 and groups == 8 and own_blocks == 24:
            return body(*args)
        return pipelined_body(*args)

    block = P("section", "dp", None)
    gain = P("section", None, "dp")
    return jax.shard_map(
        step,
        mesh=mesh,
        in_specs=(
            P("dp", None), P("dp", None), P(), P(), block, gain, gain, gain, block, block, block, block, P(),
        ),
        out_specs=(block, block, block, block, gain, gain, gain, P(), P(), P("section", None)),
        check_vma=False,
    )
```

```python
import functools
import math

import jax
import jax.numpy as jnp
from jax import lax
from jax.experimental import pallas as pl
from jax.experimental.pallas import tpu as pltpu
from jax.sharding import PartitionSpec as P

HEADS = 8
F32 = jnp.float32
BF16 = jnp.bfloat16
VMEM_LIMIT = 61 * 1024 * 1024


def dot_nn(a, b):
    return lax.dot_general(a, b, (((1,), (0,)), ((), ())), preferred_element_type=F32)


def dot_nt(a, b):
    return lax.dot_general(a, b, (((1,), (1,)), ((), ())), preferred_element_type=F32)


def dot_tn(a, b):
    return lax.dot_general(a, b, (((0,), (0,)), ((), ())), preferred_element_type=F32)


def gelu_parts(x):
    ax = jnp.abs(x)
    bell = jnp.exp(-0.5 * x * x)
    t = 1.0 / (1.0 + (0.3275911 * 0.7071067811865476) * ax)
    poly = t * (
        0.5 * 0.254829592
        + t
        * (
            0.5 * -0.284496736
            + t * (0.5 * 1.421413741 + t * (0.5 * -1.453152027 + t * (0.5 * 1.061405429)))
        )
    )
    tail = poly * bell
    cdf = jnp.where(x >= 0.0, 1.0 - tail, tail)
    return x * cdf, cdf + x * bell * 0.3989422804014327


def stack_quads(w_ref, first, step, number):
    return jnp.concatenate([w_ref[0, first + step * i] for i in range(number)], axis=0)


MESH = pl.DeviceIdType.MESH


def mesh_place():
    section = lax.axis_index("section")
    group = lax.axis_index("dp")
    core = lax.rem(section, 2)
    y = lax.rem(group, 2)
    z = group // 2
    z_peers = (z, z + 1 - 2 * lax.rem(z, 2), lax.rem(z + 2, 4), 3 - z)
    return section, group, core, y, z_peers


def remote(source, target, send_sem, recv_sem, section, group):
    return pltpu.make_async_remote_copy(
        src_ref=source, dst_ref=target, send_sem=send_sem, recv_sem=recv_sem,
        device_id=(section, group), device_id_type=MESH,
    )


def greet(places):
    barrier = pltpu.get_barrier_semaphore()
    for place in places:
        pl.semaphore_signal(barrier, inc=1, device_id=place, device_id_type=MESH)
    pl.semaphore_wait(barrier, len(places))


class Gather:
    def __init__(self, own_ref, gain_ref, w_ref, gains_ref, sems):
        self.own, self.gain, self.w, self.gains = own_ref, gain_ref, w_ref, gains_ref
        self.spread, self.z_sems, self.y_sems, self.core_sems, self.gain_sems, self.local = sems
        self.section, self.group, self.core, self.y, self.z_peers = mesh_place()
        self.quads = own_ref.shape[0] // 2
        self.others = [lax.rem(self.section + k, 4) for k in range(1, 4)]
        self.places = [(o, self.group) for o in self.others] + [
            (self.section, lax.rem(self.group + k, 8)) for k in range(1, 8)
        ]

    def piece(self, layer, group):
        return self.w.at[layer, pl.ds(group * 2 * self.quads + self.quads * self.core, self.quads)]

    def spread_copy(self, k):
        peer = self.others[k]
        half = lax.rem(peer, 2) * self.quads
        return remote(
            self.own.at[pl.ds(half, self.quads)],
            self.w.at[self.section, pl.ds(self.group * 2 * self.quads + half, self.quads)],
            self.spread.at[0, k], self.spread.at[1, k], peer, self.group,
        )

    def spread_wait(self, layer):
        for k in range(3):
            @pl.when(lax.rem(layer + k + 1, 4) == self.section)
            def _():
                ref = self.piece(layer, self.group)
                remote(ref, ref, self.spread.at[0, k], self.spread.at[1, k], self.others[0], self.group).wait_recv()

    def z_copy(self, layer, k):
        ref = self.piece(layer, self.group)
        return remote(
            ref, ref, self.z_sems.at[0, layer, k], self.z_sems.at[1, layer, k],
            self.section, self.z_peers[k] * 2 + self.y,
        )

    def z_landed(self, layer, k):
        ref = self.piece(layer, self.z_peers[k] * 2 + self.y)
        return remote(
            ref, ref, self.z_sems.at[0, layer, k], self.z_sems.at[1, layer, k],
            self.section, self.z_peers[k] * 2 + self.y,
        )

    def y_copy(self, layer, k, mine=True):
        y = self.y if mine else 1 - self.y
        ref = self.piece(layer, self.z_peers[k] * 2 + y)
        return remote(
            ref, ref, self.y_sems.at[0, layer, k], self.y_sems.at[1, layer, k],
            self.section, self.group + 1 - 2 * self.y,
        )

    def core_copy(self, layer, k, mine=True):
        y = self.y if k < 4 else 1 - self.y
        core = self.core if mine else 1 - self.core
        at = (self.z_peers[k % 4] * 2 + y) * 2 * self.quads + self.quads * core
        ref = self.w.at[layer, pl.ds(at, self.quads)]
        return remote(
            ref, ref, self.core_sems.at[0, layer, k], self.core_sems.at[1, layer, k],
            self.section + 1 - 2 * self.core, self.group,
        )

    def gain_copy(self, k):
        if k < 7:
            peer = lax.rem(self.group + k + 1, 8)
            return remote(
                self.gain, self.gains.at[self.section, self.group],
                self.gain_sems.at[0, k], self.gain_sems.at[1, k], self.section, peer,
            )
        ref = self.gains.at[self.section]
        return remote(
            ref, ref, self.gain_sems.at[0, k], self.gain_sems.at[1, k], self.others[k - 7], self.group
        )

    def gain_landed(self, k):
        if k < 7:
            ref = self.gains.at[self.section, lax.rem(self.group - k - 1 + 8, 8)]
        else:
            ref = self.gains.at[lax.rem(self.section - (k - 6) + 4, 4)]
        return remote(ref, ref, self.gain_sems.at[0, k], self.gain_sems.at[1, k], self.section, self.group)

    def begin(self):
        greet(self.places)
        for k in range(3):
            self.spread_copy(k).start()
        for k in range(7):
            self.gain_copy(k).start()
        half = self.core * self.quads
        self.w[self.section, pl.ds(self.group * 2 * self.quads + half, self.quads)] = self.own[
            pl.ds(half, self.quads)
        ]
        self.gains[self.section, self.group] = self.gain[...]

    def share_gains(self):
        for k in range(7):
            self.gain_landed(k).wait_recv()
        for k in range(7, 10):
            self.gain_copy(k).start()

    def wait_gains(self):
        for k in range(7, 10):
            self.gain_landed(k).wait_recv()

    def kick(self, layer):
        self.spread_wait(layer)
        for k in range(1, 4):
            self.z_copy(layer, k).start()
        self.y_copy(layer, 0).start()
        self.core_copy(layer, 0).start()

    def serve(self, layer, step):
        if step < 4:
            self.z_landed(layer, step).wait_recv()
            self.y_copy(layer, step).start()
            self.core_copy(layer, step).start()
        else:
            self.y_copy(layer, step - 4, False).wait_recv()
            self.core_copy(layer, step).start()

    def finish(self, layer):
        for k in range(8):
            self.core_copy(layer, k, False).wait_recv()

    def end(self, layers):
        for k in range(3):
            self.spread_copy(k).wait_send()
        for k in range(10):
            self.gain_copy(k).wait_send()

        def per_layer(layer, _):
            for k in range(1, 4):
                self.z_copy(layer, k).wait_send()
            for k in range(4):
                self.y_copy(layer, k).wait_send()
            for k in range(8):
                self.core_copy(layer, k).wait_send()
            return 0

        lax.fori_loop(0, layers, per_layer, 0)


def forward_kernel(
    layers, half, info_ref, scale_ref, x_ref, target_ref, own_ref, own_gain_ref,
    probs_ref, heads_ref, att_ref, middle_ref, hidden_ref, slope_ref, sent_ref, loss_grad_ref, stats_ref,
    full_ref, gains_out_ref, hold_ref, out_ref, w_all_ref, gains_ref, *sems,
):
    seg, width = x_ref.shape
    dim = width // HEADS
    part = width // 4
    layer = pl.program_id(0)
    rows = 256
    chunks = seg // rows
    length = info_ref[0]
    gather = Gather(own_ref, own_gain_ref, w_all_ref, gains_ref, sems)
    w_ref = w_all_ref.at[pl.ds(layer, 1)]

    def keep_copy(index):
        return pltpu.make_async_copy(w_all_ref.at[index], full_ref.at[index], gather.local.at[index])

    @pl.when(layer == 0)
    def _():
        gather.begin()
        sent_ref[0] = x_ref[...]
        stats_ref[...] = jnp.zeros_like(stats_ref)
        gather.kick(0)
        gather.share_gains()
        for step in range(1, 4):
            gather.serve(0, step)
        gather.kick(1)
        for step in range(4, 8):
            gather.serve(0, step)
        gather.wait_gains()

    gather.finish(layer)
    keep_copy(layer).start()
    more = layer + 1 < layers

    def serve(step):
        @pl.when(more)
        def _():
            gather.serve(layer + 1, step)
        if step == 3:
            @pl.when(layer + 2 < layers)
            def _():
                gather.kick(layer + 2)

    def stream_of(at):
        prev = sent_ref[layer, at].astype(F32)
        skip = sent_ref[jnp.maximum(layer + 1 - half, 0), at].astype(F32)
        return prev + jnp.where(layer >= half, skip, 0.0)

    def gain_row(which):
        return jnp.concatenate(
            [gains_ref[layer, g, which : which + 1, : width // 8] for g in range(8)], axis=1
        ).astype(BF16).astype(F32)

    gain_one = gain_row(0)
    gain_two = gain_row(1)

    def qkv_step(i, _):
        at = pl.ds(pl.multiple_of(i * rows, rows), rows)
        stream = stream_of(at)
        factor = lax.rsqrt(jnp.mean(stream * stream, axis=-1, keepdims=True) + 1e-06)
        normed = (stream * factor * gain_one).astype(BF16)
        for t in range(3):
            qkv = dot_nn(normed, stack_quads(w_ref, t, 3, 4)).astype(BF16)
            for h in range(HEADS):
                heads_ref[0, t * HEADS + h, at] = qkv[:, h * dim : (h + 1) * dim]
        return 0

    lax.fori_loop(0, chunks, qkv_step, 0)
    frames = lax.broadcasted_iota(jnp.int32, (1, seg), 1)
    masking = jnp.where(frames < length, 0.0, -1e30).astype(F32)

    def head_step(h, _):
        keys = heads_ref[0, HEADS + h]
        values = heads_ref[0, 2 * HEADS + h]
        for i in range(chunks):
            at = pl.ds(i * rows, rows)
            scores = dot_nt(heads_ref[0, h, at], keys) * dim ** (-0.5) + masking
            top = jnp.max(scores, axis=-1, keepdims=True)
            expd = jnp.exp(scores - top)
            probs = (expd * (1.0 / jnp.sum(expd, axis=-1, keepdims=True))).astype(BF16)
            probs_ref[0, h, at] = probs
            hold_ref[h, at] = dot_nn(probs, values).astype(BF16)
        for step, after in ((1, 1), (2, 4), (3, 7)):
            @pl.when(h == after)
            def _():
                serve(step)
        return 0

    lax.fori_loop(0, HEADS, head_step, 0)

    def ffn_step(i, _):
        at = pl.ds(pl.multiple_of(i * rows, rows), rows)
        attended = jnp.concatenate([hold_ref[h, at] for h in range(HEADS)], axis=1)
        att_ref[0, at] = attended
        branch_attn = dot_nn(attended, stack_quads(w_ref, 12, 1, 4))
        stream = stream_of(at)
        middle = stream + branch_attn
        middle_ref[0, at] = middle
        factor = lax.rsqrt(jnp.mean(middle * middle, axis=-1, keepdims=True) + 1e-06)
        normed = (middle * factor * gain_two).astype(BF16)
        branch_ffn = jnp.zeros((rows, width), F32)
        for c in range(4):
            pre_act = dot_nn(normed, stack_quads(w_ref, 16 + c, 4, 4))
            hidden, slope = gelu_parts(pre_act)
            hidden = hidden.astype(BF16)
            hidden_ref[0, c, at] = hidden
            slope_ref[0, c, at] = slope.astype(BF16)
            branch_ffn = branch_ffn + dot_nn(hidden, stack_quads(w_ref, 32 + 4 * c, 1, 4))
        output = middle + branch_ffn
        out_ref[at] = output
        sent_ref[jnp.minimum(layer + 1, layers - 1), at] = jnp.where(
            layer + 1 < layers, output.astype(BF16), sent_ref[layers - 1, at]
        )
        valid = (lax.broadcasted_iota(jnp.int32, (rows, 1), 0) + i * rows < length).astype(F32)
        for k, value in enumerate((stream, branch_attn, branch_ffn)):
            stats_ref[layer, k : k + 1] += jnp.sum(valid * value * value, axis=0, keepdims=True)

        @pl.when(i == 0)
        def _():
            serve(4)

        return 0

    lax.fori_loop(0, chunks, ffn_step, 0)
    for step in range(5, 8):
        serve(step)

    @pl.when(layer == layers - 1)
    def _():
        bins = width // 8
        lane = lax.broadcasted_iota(jnp.int32, (1, width), 1)
        is_real = lax.rem(lane, 2 * bins) < bins
        stem = lane // (2 * bins)
        present = jnp.zeros((1, width), F32)
        for k in range(4):
            present = jnp.where(stem == k, info_ref[1 + k].astype(F32), present)
        inverse = scale_ref[0]

        def loss_step(i, _):
            at = pl.ds(pl.multiple_of(i * rows, rows), rows)
            output = out_ref[at]
            square = output * output
            other = jnp.where(
                is_real, pltpu.roll(square, width - bins, 1), pltpu.roll(square, bins, 1)
            )
            magnitude = jnp.sqrt(square + other + 0.01)
            goal = target_ref[at]
            goal = jnp.concatenate(
                [goal[:, (k // 2) * bins : (k // 2 + 1) * bins] for k in range(8)], axis=1
            )
            differ = magnitude - goal
            smooth = jnp.sqrt(differ * differ + 0.01)
            valid = (lax.broadcasted_iota(jnp.int32, (rows, 1), 0) + i * rows < length).astype(F32)
            weight = valid * present
            loss_grad_ref[at] = weight * differ * output * inverse / (smooth * magnitude)
            stats_ref[0, 3:4] += jnp.sum(
                jnp.where(is_real, weight * smooth, 0.0), axis=0, keepdims=True
            )
            return 0

        lax.fori_loop(0, chunks, loss_step, 0)
        gains_out_ref[...] = gains_ref[...]
        gather.end(layers)
        for k in range(layers):
            keep_copy(k).wait()


class Scatter:
    def __init__(self, refs, sems):
        self.grads, self.core_in, self.y_in, self.z_in, self.last_out, self.last_in = refs
        self.core_sems, self.y_sems, self.z_sems, self.last_sems = sems
        self.section, self.group, self.core, self.y, self.z_peers = mesh_place()
        self.x = self.section // 2
        self.quads = self.grads.shape[3] // 2
        self.mine = pl.ds(self.core * self.quads, self.quads)
        self.theirs = pl.ds((1 - self.core) * self.quads, self.quads)

    def core_copy(self, layer, late):
        slot = lax.rem(layer, 2)
        zs = pl.ds(0, 1) if late else pl.ds(1, 3)
        return remote(
            self.grads.at[slot, zs, :, self.theirs], self.core_in.at[slot, zs],
            self.core_sems.at[0, slot, int(late)], self.core_sems.at[1, slot, int(late)],
            self.section + 1 - 2 * self.core, self.group,
        )

    def y_copy(self, layer, k):
        slot = lax.rem(layer, 2)
        return remote(
            self.grads.at[slot, self.z_peers[k], 1 - self.y, self.mine], self.y_in.at[slot, k],
            self.y_sems.at[0, slot, k], self.y_sems.at[1, slot, k],
            self.section, self.group + 1 - 2 * self.y,
        )

    def z_copy(self, layer, k):
        slot = lax.rem(layer, 2)
        return remote(
            self.grads.at[slot, self.z_peers[k], self.y, self.mine], self.z_in.at[layer, k - 1],
            self.z_sems.at[0, layer, k - 1], self.z_sems.at[1, layer, k - 1],
            self.section, self.z_peers[k] * 2 + self.y,
        )

    def last_copy(self, layer):
        slot = lax.rem(layer, 2)
        place = lax.rem(self.section - layer + 4, 4) - 1
        place = jnp.maximum(place, 0)
        return remote(
            self.last_out.at[slot], self.last_in.at[place],
            self.last_sems.at[0, slot], self.last_sems.at[1, place], layer, self.group,
        )

    def last_landed(self, place):
        return remote(
            self.last_in.at[place], self.last_in.at[place],
            self.last_sems.at[0, 0], self.last_sems.at[1, place], self.section, self.group,
        )

    def for_part(self, late, act):
        for k in (1, 2, 3, 0):
            @pl.when((self.z_peers[k] == 0) == late)
            def _():
                act(k)

    def add_core(self, layer, late):
        slot = lax.rem(layer, 2)
        self.core_copy(layer, late).wait_recv()

        def add(i, _):
            z, y = i // 2, lax.rem(i, 2)
            for q in range(self.quads):
                at = self.core * self.quads + q
                self.grads[slot, z, y, at] = self.grads[slot, z, y, at] + self.core_in[slot, z, y, q]
            return 0

        lax.fori_loop(0 if late else 2, 2 if late else 8, add, 0)
        self.for_part(late, lambda k: self.y_copy(layer, k).start())

    def add_y(self, layer, k):
        slot = lax.rem(layer, 2)
        self.y_copy(layer, k).wait_recv()
        for q in range(self.quads):
            at = self.core * self.quads + q
            z = self.z_peers[k]
            self.grads[slot, z, self.y, at] = self.grads[slot, z, self.y, at] + self.y_in[slot, k, q]
        if k:
            self.z_copy(layer, k).start()

    def add_y_if(self, layer, k, late):
        @pl.when((self.z_peers[k] == 0) == late)
        def _():
            self.add_y(layer, k)

    def add_z(self, layer, result_ref):
        slot = lax.rem(layer, 2)
        for k in range(1, 4):
            self.z_copy(layer, k).wait_recv()
        for q in range(self.quads):
            at = self.core * self.quads + q
            total = self.grads[slot, self.z_peers[0], self.y, at].astype(F32)
            for k in range(3):
                total = total + self.z_in[layer, k, q].astype(F32)

            @pl.when(layer == self.section)
            def _():
                result_ref[at] = total

            @pl.when(layer != self.section)
            def _():
                self.last_out[slot, q] = total.astype(BF16)

        @pl.when(layer != self.section)
        def _():
            self.last_copy(layer).start()

    def wait_sends(self, layer):
        for late in (False, True):
            self.core_copy(layer, late).wait_send()
        for k in range(4):
            self.y_copy(layer, k).wait_send()
        for k in range(1, 4):
            self.z_copy(layer, k).wait_send()

        @pl.when(layer != self.section)
        def _():
            self.last_copy(layer).wait_send()

    def collect(self, result_ref):
        for place in range(3):
            self.last_landed(place).wait_recv()
        for q in range(self.quads):
            mine = self.core * self.quads + q
            theirs = (1 - self.core) * self.quads + q
            result_ref[mine] = result_ref[mine] + self.last_in[1, q].astype(F32)
            result_ref[theirs] = self.last_in[0, q].astype(F32) + self.last_in[2, q].astype(F32)


class Totals:
    def __init__(self, refs, sems):
        self.stage_in, self.z_in, self.norm_section, self.norm_group = refs
        self.stage_sems, self.z_sems, self.section_sems, self.group_sems = sems
        self.section, self.group, self.core, self.y, self.z_peers = mesh_place()

    def stage_copy(self, k):
        peer = (
            (self.section + 1 - 2 * self.core, self.group),
            (self.section, self.group + 1 - 2 * self.y),
            (lax.rem(self.section + 2, 4), self.group),
        )[k]
        return remote(
            self.stage_in.at[2 * k], self.stage_in.at[2 * k + 1],
            self.stage_sems.at[0, k], self.stage_sems.at[1, k], *peer,
        )

    def z_copy(self, k):
        z = self.z_peers[0]
        return remote(
            self.z_in.at[z], self.z_in.at[z], self.z_sems.at[0, k - 1], self.z_sems.at[1, k - 1],
            self.section, self.z_peers[k] * 2 + self.y,
        )

    def z_landed(self, k):
        z = self.z_peers[k]
        return remote(
            self.z_in.at[z], self.z_in.at[z], self.z_sems.at[0, k - 1], self.z_sems.at[1, k - 1],
            self.section, self.z_peers[k] * 2 + self.y,
        )

    def begin(self, tile):
        self.stage_in[0] = tile
        self.stage_copy(0).start()

    def after_core(self):
        self.stage_copy(0).wait_recv()
        self.stage_in[2] = self.stage_in[0] + self.stage_in[1]
        self.stage_copy(1).start()

    def after_y(self):
        self.stage_copy(1).wait_recv()
        self.z_in[self.z_peers[0]] = self.stage_in[2] + self.stage_in[3]
        for k in range(1, 4):
            self.z_copy(k).start()

    def after_z(self):
        for k in range(1, 4):
            self.z_landed(k).wait_recv()
        self.stage_in[4] = self.z_in[0] + self.z_in[1] + self.z_in[2] + self.z_in[3]
        self.stage_copy(2).start()

    def after_x(self):
        self.stage_copy(2).wait_recv()
        return self.stage_in[4] + self.stage_in[5]

    def norm_copy(self, k):
        if k < 3:
            peer = (lax.rem(self.section + k + 1, 4), self.group)
            ref = self.norm_section.at[self.section]
            return remote(ref, ref, self.section_sems.at[0, k], self.section_sems.at[1, k], *peer)
        k = k - 3
        peer = (self.section, lax.rem(self.group + k + 1, 8))
        ref = self.norm_group.at[self.group]
        return remote(ref, ref, self.group_sems.at[0, k], self.group_sems.at[1, k], *peer)

    def norm_landed(self, k):
        if k < 3:
            ref = self.norm_section.at[lax.rem(self.section - k - 1 + 4, 4)]
            return remote(
                ref, ref, self.section_sems.at[0, k], self.section_sems.at[1, k], self.section, self.group
            )
        k = k - 3
        ref = self.norm_group.at[lax.rem(self.group - k - 1 + 8, 8)]
        return remote(ref, ref, self.group_sems.at[0, k], self.group_sems.at[1, k], self.section, self.group)

    def norm(self, value):
        self.norm_section[self.section] = value
        for k in range(3):
            self.norm_copy(k).start()
        for k in range(3):
            self.norm_landed(k).wait_recv()
        total = self.norm_section[0]
        for k in range(1, 4):
            total = total + self.norm_section[k]
        self.norm_group[self.group] = total
        for k in range(3, 10):
            self.norm_copy(k).start()
        for k in range(3, 10):
            self.norm_landed(k).wait_recv()
        total = self.norm_group[0]
        for k in range(1, 8):
            total = total + self.norm_group[k]
        return total

    def end(self):
        for k in range(3):
            self.stage_copy(k).wait_send()
        for k in range(1, 4):
            self.z_copy(k).wait_send()
        for k in range(10):
            self.norm_copy(k).wait_send()


def norm_reverse(value, gain, grad):
    factor = lax.rsqrt(jnp.mean(value * value, axis=-1, keepdims=True) + 1e-06)
    scaled = grad * gain
    mean = jnp.mean(value * scaled, axis=-1, keepdims=True)
    unit = value * factor
    back = factor * scaled - unit * (factor * factor * mean)
    return back, jnp.sum(grad * unit, axis=0, keepdims=True), (unit * gain).astype(BF16)


def backward_kernel(
    layers, half, loss_grad_ref, w_ref, gain_ref, sent_ref,
    probs_ref, heads_ref, att_ref, middle_ref, hidden_ref, slope_ref, stats_ref,
    result_ref, totals_ref, square_ref,
    sends_ref, dffn_ref, dpre_ref, normed_ref, dmid_ref, datt_ref, dhold_ref, dheads_ref, dqkv_ref,
    gain_grad_ref, *comm_refs,
):
    seg, width = loss_grad_ref.shape
    dim = width // HEADS
    part = width // 4
    layer = layers - 1 - pl.program_id(0)
    rows = 256
    chunks = seg // rows
    gain_one = gain_ref[0, 0:1]
    gain_two = gain_ref[0, 1:2]
    scatter = Scatter(comm_refs[:6], comm_refs[10:14])
    totals = Totals(comm_refs[6:10], comm_refs[14:])
    grads_ref = comm_refs[0]
    slot = lax.rem(layer, 2)

    @pl.when(layer == layers - 1)
    def _():
        section, group = scatter.section, scatter.group
        greet(
            [(lax.rem(section + k, 4), group) for k in range(1, 4)]
            + [(section, lax.rem(group + k, 8)) for k in range(1, 8)]
        )
        sends_ref[...] = jnp.zeros_like(sends_ref)
        gain_grad_ref[...] = jnp.zeros_like(gain_grad_ref)

    def put_grad(first, step, value):
        for r in range(4):
            quad = first + step * r
            owner = quad // 6
            grads_ref[slot, owner // 2, lax.rem(owner, 2), lax.rem(quad, 6)] = value[
                r * part : (r + 1) * part
            ].astype(BF16)

    def before(act):
        @pl.when(layer < layers - 1)
        def _():
            act(layer + 1)

    def ffn_step(i, _):
        at = pl.ds(pl.multiple_of(i * rows, rows), rows)
        later = sends_ref[jnp.minimum(layer + 1, layers - 1), at].astype(F32)
        skip = sends_ref[jnp.minimum(layer + half, layers - 1), at].astype(F32)
        upstream = jnp.where(
            layer == layers - 1, loss_grad_ref[at], later + jnp.where(layer + half < layers, skip, 0.0)
        )
        dffn = upstream.astype(BF16)
        dffn_ref[at] = dffn
        dnormed = jnp.zeros((rows, width), F32)
        for c in range(4):
            dhidden = dot_nt(dffn, stack_quads(w_ref, 32 + 4 * c, 1, 4))
            dpre = (dhidden * slope_ref[0, c, at].astype(F32)).astype(BF16)
            dpre_ref[c, at] = dpre
            dnormed = dnormed + dot_nt(dpre, stack_quads(w_ref, 16 + c, 4, 4))
        back, gain_grad, normed = norm_reverse(middle_ref[0, at], gain_two, dnormed)
        gain_grad_ref[layer, 1:2] += gain_grad
        normed_ref[at] = normed
        dmid = upstream + back
        dmid_ref[at] = dmid
        datt = dmid.astype(BF16)
        datt_ref[at] = datt
        dattended = dot_nt(datt, stack_quads(w_ref, 12, 1, 4)).astype(BF16)
        for h in range(HEADS):
            dhold_ref[h, at] = dattended[:, h * dim : (h + 1) * dim]

        @pl.when(i == 0)
        def _():
            before(lambda at: scatter.add_core(at, True))
            before(lambda at: scatter.add_y_if(at, 2, False))

        @pl.when(i == 1)
        def _():
            before(lambda at: scatter.add_y_if(at, 3, False))

        return 0

    lax.fori_loop(0, chunks, ffn_step, 0)

    @pl.when(layer < layers - 2)
    def _():
        scatter.wait_sends(layer + 2)

    def ffn_grad_step(c, _):
        put_grad(32 + 4 * c, 1, dot_tn(hidden_ref[0, c], dffn_ref[...]))
        put_grad(16 + c, 4, dot_tn(normed_ref[...], dpre_ref[c]))
        return 0

    lax.fori_loop(0, 4, ffn_grad_step, 0)
    put_grad(12, 1, dot_tn(att_ref[0], datt_ref[...]))
    scatter.core_copy(layer, False).start()
    before(lambda at: scatter.add_y_if(at, 0, False))
    before(lambda at: scatter.for_part(True, lambda k: scatter.add_y(at, k)))

    def head_step(h, _):
        queries = heads_ref[0, h]
        keys = heads_ref[0, HEADS + h]
        values = heads_ref[0, 2 * HEADS + h]
        dkeys = jnp.zeros((seg, dim), F32)
        dvalues = jnp.zeros((seg, dim), F32)
        for i in range(chunks):
            at = pl.ds(i * rows, rows)
            probs = probs_ref[0, h, at]
            dhold = dhold_ref[h, at]
            dprobs = dot_nt(dhold, values)
            wide = probs.astype(F32)
            dot_sum = jnp.sum(wide * dprobs, axis=-1, keepdims=True)
            dscores = (wide * (dprobs - dot_sum)).astype(BF16)
            dheads_ref[h, at] = (dot_nn(dscores, keys) * dim ** (-0.5)).astype(BF16)
            dvalues = dvalues + dot_tn(probs, dhold)
            dkeys = dkeys + dot_tn(dscores, heads_ref[0, h, at])
        dheads_ref[HEADS + h] = (dkeys * dim ** (-0.5)).astype(BF16)
        dheads_ref[2 * HEADS + h] = dvalues.astype(BF16)

        @pl.when(h == 3)
        def _():
            scatter.add_core(layer, False)

        return 0

    lax.fori_loop(0, HEADS, head_step, 0)

    def qkv_step(i, _):
        at = pl.ds(pl.multiple_of(i * rows, rows), rows)
        dnormed = jnp.zeros((rows, width), F32)
        for t in range(3):
            dqkv = jnp.concatenate([dheads_ref[t * HEADS + h, at] for h in range(HEADS)], axis=1)
            dqkv_ref[t, at] = dqkv
            dnormed = dnormed + dot_nt(dqkv, stack_quads(w_ref, t, 3, 4))
        prev = sent_ref[layer, at].astype(F32)
        skip = sent_ref[jnp.maximum(layer + 1 - half, 0), at].astype(F32)
        stream = prev + jnp.where(layer >= half, skip, 0.0)
        back, gain_grad, normed = norm_reverse(stream, gain_one, dnormed)
        gain_grad_ref[layer, 0:1] += gain_grad
        normed_ref[at] = normed
        sends_ref[layer, at] = (dmid_ref[at] + back).astype(BF16)
        return 0

    lax.fori_loop(0, chunks, qkv_step, 0)

    def qkv_grad_step(t, _):
        put_grad(t, 3, dot_tn(normed_ref[...], dqkv_ref[t]))
        return 0

    lax.fori_loop(0, 3, qkv_grad_step, 0)
    scatter.core_copy(layer, True).start()
    before(lambda at: scatter.add_z(at, result_ref))
    scatter.add_y_if(layer, 1, False)

    @pl.when(layer == 0)
    def _():
        lane = lax.broadcasted_iota(jnp.int32, (1, width), 1)
        rows_out = [gain_grad_ref[k // 2, k % 2 : k % 2 + 1] for k in range(2 * layers)]
        for k in range(layers):
            row = jnp.zeros((1, width), F32)
            for i in range(4):
                value = jnp.sum(stats_ref[k, i : i + 1], axis=1, keepdims=True)
                row = jnp.where(lane == i, value, row)
            rows_out.append(row)
        rows_out.append(jnp.zeros((16 - 3 * layers, width), F32))
        totals.begin(jnp.concatenate(rows_out, axis=0))
        scatter.add_core(0, True)
        scatter.add_y_if(0, 2, False)
        totals.after_core()
        scatter.add_y_if(0, 3, False)
        scatter.add_y_if(0, 0, False)
        scatter.for_part(True, lambda k: scatter.add_y(0, k))
        totals.after_y()
        scatter.add_z(0, result_ref)
        totals.after_z()
        scatter.collect(result_ref)
        square = jnp.zeros((8, width), F32)
        for q in range(6):
            value = result_ref[q]
            square = square + jnp.sum((value * value).reshape(part // 8, 8, width), axis=0)
        folded = square[:, :128] + square[:, 128:256] + square[:, 256:]
        square_ref[...] = totals.norm(folded)
        totals_ref[...] = totals.after_x()
        scatter.wait_sends(1)
        scatter.wait_sends(0)
        totals.end()


FF = 1536


def from_behind(value, axis, by):
    peers = lax.axis_size(axis)
    pairs = [(i, i + by) for i in range(peers) if 0 <= i + by < peers]
    return lax.ppermute(value, axis, pairs)


def unblock(blocks, row_count, col_count, block_size):
    return (
        blocks.reshape(row_count // block_size, col_count // block_size, block_size, block_size)
        .transpose(0, 2, 1, 3)
        .reshape(row_count, col_count)
    )


def to_blocks(matrix, block_size):
    row_count, col_count = matrix.shape
    return (
        matrix.reshape(row_count // block_size, block_size, col_count // block_size, block_size)
        .transpose(0, 2, 1, 3)
        .reshape(-1, block_size * block_size)
    )


def split_matrices(blocks, model_width):
    block_size = model_width // 4
    shapes = (
        (model_width, 3 * model_width),
        (model_width, model_width),
        (model_width, FF),
        (FF, model_width),
    )
    result = []
    offset = 0
    for row_count, col_count in shapes:
        number = row_count * col_count // (block_size * block_size)
        result.append(unblock(blocks[offset : offset + number], row_count, col_count, block_size))
        offset = offset + number
    return result


def rms_norm(stream, gain):
    factor = lax.rsqrt(jnp.mean(stream * stream, axis=-1, keepdims=True) + 1e-06)
    return (stream * factor * gain, factor)


def norm_back(stream, factor, gain, grad):
    scaled = grad * gain
    grad_in = factor * scaled - stream * factor**3 * jnp.mean(
        stream * scaled, axis=-1, keepdims=True
    )
    return (grad_in, jnp.sum(grad * stream * factor, axis=0))


def gelu_slope(pre_act):
    return (
        0.5 * (1.0 + lax.erf(pre_act * 0.7071067811865476))
        + pre_act * jnp.exp(-0.5 * pre_act * pre_act) * 0.3989422804014327
    )


def layer_forward(stream, matrices, gain_pair, length):
    w_qkv, w_out, w_up, w_down = matrices
    row_count, model_width = stream.shape
    head_dim = model_width // HEADS
    frames = jnp.arange(row_count)
    norm_one, scale_one = rms_norm(stream, gain_pair[0])
    normed = norm_one.astype(BF16)
    qkv_all = jnp.dot(normed, w_qkv, preferred_element_type=jnp.float32).astype(BF16)
    queries = qkv_all[:, :model_width].reshape(row_count, HEADS, head_dim)
    key_rows = qkv_all[:, model_width : 2 * model_width].reshape(row_count, HEADS, head_dim)
    value_rows = qkv_all[:, 2 * model_width :].reshape(row_count, HEADS, head_dim)
    masking = jnp.where(frames < length, 0.0, -1e30).astype(jnp.float32)
    scores = jnp.einsum(
        "qhe,khe->hqk", queries, key_rows, preferred_element_type=jnp.float32
    ) * head_dim ** (-0.5)
    attn_probs = jax.nn.softmax(scores + masking[None, None, :], axis=-1)
    probs_low = attn_probs.astype(BF16)
    attended = (
        jnp.einsum("hqk,khe->qhe", probs_low, value_rows, preferred_element_type=jnp.float32)
        .reshape(row_count, model_width)
        .astype(BF16)
    )
    branch_attn = jnp.dot(attended, w_out, preferred_element_type=jnp.float32)
    middle = stream + branch_attn
    norm_two, scale_two = rms_norm(middle, gain_pair[1])
    normed_two = norm_two.astype(BF16)
    pre_act = jnp.dot(normed_two, w_up, preferred_element_type=jnp.float32)
    hidden = jax.nn.gelu(pre_act, approximate=False).astype(BF16)
    branch_ffn = jnp.dot(hidden, w_down, preferred_element_type=jnp.float32)
    kept_vals = (
        scale_one,
        normed,
        queries,
        key_rows,
        value_rows,
        attn_probs,
        probs_low,
        attended,
        middle,
        scale_two,
        normed_two,
        pre_act,
        hidden,
    )
    return (middle + branch_ffn, branch_attn, branch_ffn, kept_vals)


def layer_backward(stream, matrices, gain_pair, length, upstream):
    w_qkv, w_out, w_up, w_down = matrices
    row_count, model_width = stream.shape
    head_dim = model_width // HEADS
    output, branch_attn, branch_ffn, kept_vals = layer_forward(stream, matrices, gain_pair, length)
    (
        scale_one,
        normed,
        queries,
        key_rows,
        value_rows,
        attn_probs,
        probs_low,
        attended,
        middle,
        scale_two,
        normed_two,
        pre_act,
        hidden,
    ) = kept_vals
    grad_ffn = upstream.astype(BF16)
    grad_down = jnp.dot(hidden.T, grad_ffn, preferred_element_type=jnp.float32)
    grad_hidden = jnp.dot(grad_ffn, w_down.T, preferred_element_type=jnp.float32)
    grad_pre = (grad_hidden * gelu_slope(pre_act)).astype(BF16)
    grad_up = jnp.dot(normed_two.T, grad_pre, preferred_element_type=jnp.float32)
    back_mid, gain_two = norm_back(
        middle,
        scale_two,
        gain_pair[1],
        jnp.dot(grad_pre, w_up.T, preferred_element_type=jnp.float32),
    )
    grad_mid = upstream + back_mid
    grad_branch = grad_mid.astype(BF16)
    grad_out = jnp.dot(attended.T, grad_branch, preferred_element_type=jnp.float32)
    grad_att = (
        jnp.dot(grad_branch, w_out.T, preferred_element_type=jnp.float32)
        .astype(BF16)
        .reshape(row_count, HEADS, head_dim)
    )
    grad_value = jnp.einsum("hqk,qhe->khe", probs_low, grad_att, preferred_element_type=jnp.float32)
    grad_probs = jnp.einsum(
        "qhe,khe->hqk", grad_att, value_rows, preferred_element_type=jnp.float32
    )
    grad_scores = (
        attn_probs * (grad_probs - jnp.sum(attn_probs * grad_probs, axis=-1, keepdims=True))
    ).astype(BF16)
    grad_query = jnp.einsum(
        "hqk,khe->qhe", grad_scores, key_rows, preferred_element_type=jnp.float32
    ) * head_dim ** (-0.5)
    grad_key = jnp.einsum(
        "hqk,qhe->khe", grad_scores, queries, preferred_element_type=jnp.float32
    ) * head_dim ** (-0.5)
    grad_qkv = jnp.concatenate(
        [
            grad_query.reshape(row_count, model_width),
            grad_key.reshape(row_count, model_width),
            grad_value.reshape(row_count, model_width),
        ],
        axis=1,
    ).astype(BF16)
    grad_wqkv = jnp.dot(normed.T, grad_qkv, preferred_element_type=jnp.float32)
    back_in, gain_one = norm_back(
        stream,
        scale_one,
        gain_pair[0],
        jnp.dot(grad_qkv, w_qkv.T, preferred_element_type=jnp.float32),
    )
    return (
        grad_mid + back_in,
        (grad_wqkv, grad_out, grad_up, grad_down),
        jnp.stack([gain_one, gain_two]),
    )


def spectral_terms(output, target, length, present_row, frame_count):
    row_count, model_width = output.shape
    bin_count = model_width // 8
    spectra = output.reshape(row_count, 4, 2, bin_count)
    real_part = spectra[:, :, 0]
    imag_part = spectra[:, :, 1]
    magnitude = jnp.sqrt(real_part * real_part + imag_part * imag_part + 0.01)
    differ = magnitude - target.reshape(row_count, 4, bin_count)
    smooth_err = jnp.sqrt(differ * differ + 0.01)
    weight = (jnp.arange(row_count) < length).astype(jnp.float32)[:, None, None] * present_row[
        None, :, None
    ]
    loss_slope = weight * differ / smooth_err / magnitude / frame_count
    grad_spec = jnp.stack([loss_slope * real_part, loss_slope * imag_part], axis=2).reshape(
        row_count, model_width
    )
    return (jnp.sum(smooth_err * weight), grad_spec)


def pipelined_body(
    x_in,
    targets,
    valid_len,
    present_stems,
    w_master,
    norm_gains,
    gain_m,
    gain_v,
    l_stats,
    r_stats,
    l_roots,
    r_roots,
    step_count,
):
    model_width = x_in.shape[1]
    block_size = model_width // 4
    sections = lax.axis_size("section")
    section_idx = lax.axis_index("section")
    half_way = sections // 2
    groups = lax.axis_size("dp")
    group_idx = lax.axis_index("dp")
    micro_count = valid_len.shape[0] // groups
    seg_len = x_in.shape[0] // micro_count
    own_blocks = w_master.shape[1]
    own_gain = norm_gains.shape[2]
    full_w, full_g = (
        lax.all_gather(w_master.astype(BF16), "dp", axis=1, tiled=True),
        lax.all_gather(norm_gains.astype(BF16), "dp", axis=2, tiled=True),
    )
    matrices = split_matrices(full_w[0], model_width)
    gain_pair = full_g[0].astype(jnp.float32)
    lengths = lax.dynamic_slice_in_dim(valid_len, group_idx * micro_count, micro_count)
    stem_flags = lax.dynamic_slice_in_dim(
        present_stems, group_idx * micro_count, micro_count
    ).astype(jnp.float32)
    frame_count = jnp.sum(valid_len).astype(jnp.float32)
    decoder = section_idx >= half_way
    encoder = section_idx < half_way
    is_last = section_idx == sections - 1
    act_shape = (micro_count, seg_len, model_width)

    def forward_step(step_idx, loop_state):
        in_rows, kept_prev, skip_store, loss_grads, loss_sum, sq_sums = loop_state
        micro_idx = step_idx - section_idx
        active = (micro_idx >= 0) & (micro_idx < micro_count)
        slot_idx = jnp.clip(micro_idx, 0, micro_count - 1)
        fresh_rows = lax.dynamic_slice_in_dim(x_in, slot_idx * seg_len, seg_len, 0)
        previous = jnp.where(section_idx == 0, fresh_rows, in_rows)
        stream = previous.astype(jnp.float32) + jnp.where(
            decoder, skip_store[slot_idx].astype(jnp.float32), 0.0
        )
        length = lengths[slot_idx]
        target = lax.dynamic_slice_in_dim(targets, slot_idx * seg_len, seg_len, 0)

        def forward_compute_fn(operand):
            output, branch_attn, branch_ffn, kept_vals = layer_forward(
                stream, matrices, gain_pair, length
            )
            valid = (jnp.arange(seg_len) < length).astype(jnp.float32)[:, None]
            squares = jnp.stack(
                [
                    jnp.sum(valid * stream * stream),
                    jnp.sum(valid * branch_attn * branch_attn),
                    jnp.sum(valid * branch_ffn * branch_ffn),
                ]
            )
            seg_loss, grad_spec = spectral_terms(
                output, target, length, stem_flags[slot_idx], frame_count
            )
            return (output, squares, seg_loss, grad_spec)

        def forward_spare_fn(operand):
            empty = jnp.zeros((seg_len, model_width), jnp.float32)
            return (empty, jnp.zeros((3,), jnp.float32), jnp.zeros((), jnp.float32), empty)

        output, squares, seg_loss, grad_spec = lax.cond(
            active, forward_compute_fn, forward_spare_fn, 0
        )
        kept_prev = kept_prev.at[slot_idx].set(jnp.where(active, previous, kept_prev[slot_idx]))
        loss_grads = loss_grads.at[slot_idx].set(
            jnp.where(active & is_last, grad_spec, loss_grads[slot_idx])
        )
        loss_sum = loss_sum + jnp.where(is_last, seg_loss, 0.0)
        sq_sums = sq_sums + squares
        sent_rows = output.astype(BF16)
        in_rows = from_behind(sent_rows, "section", 1)
        from_encoder = from_behind(sent_rows, "section", half_way)
        recv_idx = step_idx - section_idx + half_way
        usable = decoder & (recv_idx >= 0) & (recv_idx < micro_count)
        recv_slot = jnp.clip(recv_idx, 0, micro_count - 1)
        skip_store = skip_store.at[recv_slot].set(
            jnp.where(usable, from_encoder, skip_store[recv_slot])
        )
        return (in_rows, kept_prev, skip_store, loss_grads, loss_sum, sq_sums)

    start_state = (
        jnp.zeros((seg_len, model_width), BF16),
        jnp.zeros(act_shape, BF16),
        jnp.zeros(act_shape, BF16),
        jnp.zeros(act_shape, jnp.float32),
        jnp.zeros((), jnp.float32),
        jnp.zeros((3,), jnp.float32),
    )
    unused_rows, kept_prev, skip_store, loss_grads, loss_sum, sq_sums = lax.fori_loop(
        0, micro_count + sections - 1, forward_step, start_state
    )

    def backward_step(step_idx, loop_state):
        in_grads, skip_grad_store, grad_mats, grad_gains = loop_state
        micro_idx = step_idx - (sections - 1 - section_idx)
        active = (micro_idx >= 0) & (micro_idx < micro_count)
        slot_idx = jnp.clip(micro_idx, 0, micro_count - 1)
        upstream = jnp.where(
            is_last,
            loss_grads[slot_idx],
            in_grads.astype(jnp.float32)
            + jnp.where(encoder, skip_grad_store[slot_idx].astype(jnp.float32), 0.0),
        )
        stream = kept_prev[slot_idx].astype(jnp.float32) + jnp.where(
            decoder, skip_store[slot_idx].astype(jnp.float32), 0.0
        )
        length = lengths[slot_idx]

        def backward_compute_fn(operand):
            return layer_backward(stream, matrices, gain_pair, length, upstream)

        def backward_spare_fn(operand):
            return (
                jnp.zeros_like(stream),
                tuple((jnp.zeros(mat.shape, jnp.float32) for mat in matrices)),
                jnp.zeros((2, model_width), jnp.float32),
            )

        grad_stream, layer_mats, layer_gains = lax.cond(
            active, backward_compute_fn, backward_spare_fn, 0
        )
        grad_mats = tuple((total + piece for total, piece in zip(grad_mats, layer_mats)))
        grad_gains = grad_gains + layer_gains
        grad_rows = grad_stream.astype(BF16)
        in_grads = from_behind(grad_rows, "section", -1)
        from_decoder = from_behind(grad_rows, "section", -half_way)
        recv_idx = micro_idx + half_way
        usable = encoder & (recv_idx >= 0) & (recv_idx < micro_count)
        recv_slot = jnp.clip(recv_idx, 0, micro_count - 1)
        skip_grad_store = skip_grad_store.at[recv_slot].set(
            jnp.where(usable, from_decoder, skip_grad_store[recv_slot])
        )
        return (in_grads, skip_grad_store, grad_mats, grad_gains)

    back_state = (
        jnp.zeros((seg_len, model_width), BF16),
        jnp.zeros(act_shape, BF16),
        tuple((jnp.zeros(mat.shape, jnp.float32) for mat in matrices)),
        jnp.zeros((2, model_width), jnp.float32),
    )
    unused_grads, unused_store, grad_mats, grad_gains = lax.fori_loop(
        0, micro_count + sections - 1, backward_step, back_state
    )
    grad_all = jnp.concatenate([to_blocks(mat, block_size) for mat in grad_mats], axis=0)
    summed_w, summed_g = lax.psum((grad_all, grad_gains), "dp")
    own_grad = lax.dynamic_slice_in_dim(summed_w, group_idx * own_blocks, own_blocks, 0)
    own_gain_grad = lax.dynamic_slice_in_dim(summed_g, group_idx * own_gain, own_gain, 1)
    own_square = jnp.sum(own_grad * own_grad) + jnp.sum(own_gain_grad * own_gain_grad)
    rows_local = jnp.zeros((sections, 3), jnp.float32).at[section_idx].set(sq_sums)
    total_square, loss_value, rows_total = lax.psum(
        (own_square, loss_sum / frame_count, rows_local), ("section", "dp")
    )
    grad_norm = jnp.sqrt(total_square)
    clip_limit = 0.00015 * math.sqrt(
        sections * (own_blocks * groups * block_size * block_size + 2 * model_width)
    )
    factor = clip_limit / jnp.maximum(grad_norm, clip_limit)
    grad_blocks = own_grad * factor
    square = (own_blocks, block_size, block_size)
    shaped = grad_blocks.reshape(square)
    highest = lax.Precision.HIGHEST
    l_new = 0.95 * l_stats[0].reshape(square) + 0.05 * jnp.einsum(
        "bij,bkj->bik", shaped, shaped, precision=highest
    )
    r_new = 0.95 * r_stats[0].reshape(square) + 0.05 * jnp.einsum(
        "bji,bjk->bik", shaped, shaped, precision=highest
    )
    left_side = jnp.einsum("bij,bjk->bik", l_roots[0].reshape(square), shaped, precision=highest)
    precond = jnp.einsum("bij,bjk->bik", left_side, r_roots[0].reshape(square), precision=highest)
    master = w_master[0]
    w_new = master - 0.5 * (precond.reshape(master.shape) + 0.01 * master)
    gain_grad = own_gain_grad * factor
    m_new = 0.9 * gain_m[0] + 0.1 * gain_grad
    v_new = 0.999 * gain_v[0] + 0.001 * gain_grad * gain_grad
    step_num = step_count[0].astype(jnp.float32)
    m_hat = m_new / (1.0 - jnp.power(0.9, step_num))
    v_hat = v_new / (1.0 - jnp.power(0.999, step_num))
    gains_new = norm_gains[0] - 0.5 * m_hat / (jnp.sqrt(v_hat) + 1e-08)
    rms = jnp.sqrt(rows_total[section_idx] / (frame_count * model_width)).reshape(1, 3)
    return (
        w_new[None],
        grad_blocks[None],
        l_new.reshape(master.shape)[None],
        r_new.reshape(master.shape)[None],
        gains_new[None],
        m_new[None],
        v_new[None],
        loss_value,
        grad_norm,
        rms,
    )


def layer_block(shape):
    return pl.BlockSpec((1,) + shape, lambda i: (i,) + (0,) * len(shape))


def whole_block(shape):
    return pl.BlockSpec(shape, lambda i: (0,) * len(shape))


def forward(layers, info, inverse, x_seg, target_seg, own_w, own_gain):
    seg, width = x_seg.shape
    dim = width // HEADS
    part = width // 4
    half = layers // 2
    shapes = (
        (HEADS, seg, seg), (3 * HEADS, seg, dim), (seg, width), (seg, width), (4, seg, width), (4, seg, width)
    )
    kinds = (BF16, BF16, BF16, F32, BF16, BF16)
    return pl.pallas_call(
        functools.partial(forward_kernel, layers, half),
        grid=(layers,),
        in_specs=[
            pl.BlockSpec(memory_space=pltpu.SMEM),
            pl.BlockSpec(memory_space=pltpu.SMEM),
            whole_block((seg, width)),
            whole_block((seg, width // 2)),
            pl.BlockSpec(memory_space=pltpu.VMEM),
            pl.BlockSpec(memory_space=pltpu.VMEM),
        ],
        out_specs=[layer_block(s) for s in shapes]
        + [whole_block((layers, seg, width)), whole_block((seg, width)), whole_block((layers, 8, width))]
        + [pl.BlockSpec(memory_space=pl.ANY), pl.BlockSpec(memory_space=pltpu.VMEM)],
        out_shape=[jax.ShapeDtypeStruct((layers,) + s, k) for s, k in zip(shapes, kinds)]
        + [
            jax.ShapeDtypeStruct((layers, seg, width), BF16),
            jax.ShapeDtypeStruct((seg, width), F32),
            jax.ShapeDtypeStruct((layers, 8, width), F32),
            jax.ShapeDtypeStruct((layers, 48, part, width), BF16),
            jax.ShapeDtypeStruct((layers, 8, 8, 128), F32),
        ],
        scratch_shapes=[
            pltpu.VMEM((HEADS, seg, dim), BF16),
            pltpu.VMEM((seg, width), F32),
            pltpu.VMEM((layers, 48, part, width), BF16),
            pltpu.VMEM((layers, 8, 8, 128), F32),
            pltpu.SemaphoreType.DMA((2, 3)),
            pltpu.SemaphoreType.DMA((2, layers, 4)),
            pltpu.SemaphoreType.DMA((2, layers, 4)),
            pltpu.SemaphoreType.DMA((2, layers, 8)),
            pltpu.SemaphoreType.DMA((2, 10)),
            pltpu.SemaphoreType.DMA((layers,)),
        ],
        compiler_params=pltpu.CompilerParams(
            vmem_limit_bytes=VMEM_LIMIT, collective_id=0, has_side_effects=True
        ),
    )(info, inverse, x_seg, target_seg, own_w, own_gain)


def backward(layers, loss_grad, full_w, full_g, sent, saved, stats):
    seg, width = loss_grad.shape
    dim = width // HEADS
    part = width // 4
    half = layers // 2

    def from_end(array):
        shape = array.shape[1:]
        return pl.BlockSpec((1,) + shape, lambda i: (layers - 1 - i,) + (0,) * len(shape))

    return pl.pallas_call(
        functools.partial(backward_kernel, layers, half),
        grid=(layers,),
        in_specs=[
            whole_block((seg, width)),
            from_end(full_w),
            from_end(full_g),
            whole_block((layers, seg, width)),
        ]
        + [from_end(a) for a in saved]
        + [pl.BlockSpec(memory_space=pltpu.VMEM)],
        out_specs=[pl.BlockSpec(memory_space=pltpu.VMEM)] * 3,
        out_shape=[
            jax.ShapeDtypeStruct((6, part, width), F32),
            jax.ShapeDtypeStruct((16, width), F32),
            jax.ShapeDtypeStruct((8, 128), F32),
        ],
        scratch_shapes=[
            pltpu.VMEM((layers, seg, width), BF16),
            pltpu.VMEM((seg, width), BF16),
            pltpu.VMEM((4, seg, width), BF16),
            pltpu.VMEM((seg, width), BF16),
            pltpu.VMEM((seg, width), F32),
            pltpu.VMEM((seg, width), BF16),
            pltpu.VMEM((HEADS, seg, dim), BF16),
            pltpu.VMEM((3 * HEADS, seg, dim), BF16),
            pltpu.VMEM((3, seg, width), BF16),
            pltpu.VMEM((layers, 8, width), F32),
            pltpu.VMEM((2, 4, 2, 6, part, width), BF16),
            pltpu.VMEM((2, 4, 2, 3, part, width), BF16),
            pltpu.VMEM((2, 4, 3, part, width), BF16),
            pltpu.VMEM((layers, 3, 3, part, width), BF16),
            pltpu.VMEM((2, 3, part, width), BF16),
            pltpu.VMEM((3, 3, part, width), BF16),
            pltpu.VMEM((6, 16, width), F32),
            pltpu.VMEM((4, 16, width), F32),
            pltpu.VMEM((4, 8, 128), F32),
            pltpu.VMEM((8, 8, 128), F32),
            pltpu.SemaphoreType.DMA((2, 2, 2)),
            pltpu.SemaphoreType.DMA((2, 2, 4)),
            pltpu.SemaphoreType.DMA((2, layers, 3)),
            pltpu.SemaphoreType.DMA((2, 3)),
            pltpu.SemaphoreType.DMA((2, 3)),
            pltpu.SemaphoreType.DMA((2, 3)),
            pltpu.SemaphoreType.DMA((2, 3)),
            pltpu.SemaphoreType.DMA((2, 7)),
        ],
        compiler_params=pltpu.CompilerParams(
            vmem_limit_bytes=VMEM_LIMIT, collective_id=1, has_side_effects=True
        ),
    )(loss_grad, full_w, full_g, sent, *saved, stats)


def flat_rows(array):
    blocks, area = array.shape
    return (
        array.reshape(blocks // 8, 8, area // 128, 128).transpose(0, 2, 1, 3).reshape(-1, 128)
    )


def from_flat_rows(rows, blocks):
    return (
        rows.reshape(blocks // 8, -1, 8, 128).transpose(0, 2, 1, 3).reshape(blocks, -1)
    )


def load_block(rows_ref, base, block_ref):
    lane = lax.broadcasted_iota(jnp.int32, (24, 128), 1)
    a, b, c = (rows_ref[pl.ds(base + 8 * m, 24, stride=24), :] for m in range(3))
    block_ref[pl.ds(0, 24, stride=4), :] = a
    block_ref[pl.ds(1, 24, stride=4), :] = jnp.where(lane < 32, pltpu.roll(a, 32, 1), pltpu.roll(b, 32, 1))
    block_ref[pl.ds(2, 24, stride=4), :] = jnp.where(lane < 64, pltpu.roll(b, 64, 1), pltpu.roll(c, 64, 1))
    block_ref[pl.ds(3, 24, stride=4), :] = pltpu.roll(c, 96, 1)


def flat_parts(block_ref):
    lane = lax.broadcasted_iota(jnp.int32, (24, 128), 1)
    a, b, c, d = (block_ref[pl.ds(r, 24, stride=4), :] for r in range(4))
    b, c, d = pltpu.roll(b, 96, 1), pltpu.roll(c, 64, 1), pltpu.roll(d, 32, 1)
    return jnp.where(lane < 96, a, b), jnp.where(lane < 64, b, c), jnp.where(lane < 32, c, d)


def split(value):
    high = value.astype(BF16)
    return high, (value - high.astype(F32)).astype(BF16)


def dot_split(dot, left, right):
    return dot(left[0], right[0]) + (dot(left[0], right[1]) + dot(left[1], right[0]))


def update_kernel(
    layers, limit, step_ref, square_ref, tile_ref, quads_ref, w_ref, l_ref, r_ref, lroot_ref, rroot_ref,
    gain_ref, gain_m_ref, gain_v_ref,
    w_out, grad_out, l_out, r_out, gain_out, m_out, v_out, norm_out,
    block_ref,
):
    part, width = quads_ref.shape[1:]
    gains = tile_ref[: 2 * layers]
    norm = jnp.sqrt(jnp.sum(square_ref[...], keepdims=True) + jnp.sum(gains * gains, keepdims=True))
    factor = limit / jnp.maximum(norm, limit)

    def quad_step(q, _):
        for c in range(4):
            base = 4 * q + c
            load_block(lroot_ref, base, block_ref.at[0])
            load_block(rroot_ref, base, block_ref.at[1])
            grad = quads_ref[q, :, part * c : part * (c + 1)] * factor
            pair = split(grad)
            left = dot_split(dot_nn, split(block_ref[0, :, :part]), pair)
            pre = dot_split(dot_nn, split(left), split(block_ref[1, :, :part]))
            for i, value in enumerate((
                grad, pre, dot_split(dot_nt, pair, pair), dot_split(dot_tn, pair, pair)
            )):
                block_ref[2 + i, :, :part] = value
            parts = [flat_parts(block_ref.at[2 + i]) for i in range(4)]
            for m in range(3):
                at = (pl.ds(base + 8 * m, 24, stride=24), slice(None))
                grad_out[at] = parts[0][m]
                master = w_ref[at]
                w_out[at] = master - 0.5 * (parts[1][m] + 0.01 * master)
                l_out[at] = 0.95 * l_ref[at] + 0.05 * parts[2][m]
                r_out[at] = 0.95 * r_ref[at] + 0.05 * parts[3][m]
        return 0

    lax.fori_loop(0, 2, quad_step, 0)

    @pl.when(pl.program_id(0) == 0)
    def _():
        section, group = lax.axis_index("section"), lax.axis_index("dp")
        share = gain_ref.shape[1]
        row = tile_ref[:2]
        for k in range(1, layers):
            row = jnp.where(section == k, tile_ref[2 * k : 2 * k + 2], row)
        own = row[:, :share]
        for g in range(1, width // share):
            own = jnp.where(group == g, row[:, g * share : (g + 1) * share], own)
        grad = own * factor
        m_new = 0.9 * gain_m_ref[...] + 0.1 * grad
        v_new = 0.999 * gain_v_ref[...] + 0.001 * grad * grad
        step = jnp.full((1, 1), step_ref[0], jnp.int32).astype(F32)
        m_hat = m_new / (1.0 - jnp.exp(step * math.log(0.9)))
        v_hat = v_new / (1.0 - jnp.exp(step * math.log(0.999)))
        gain_out[...] = gain_ref[...] - 0.5 * m_hat / (jnp.sqrt(v_hat) + 1e-08)
        m_out[...] = m_new
        v_out[...] = v_new
        norm_out[...] = jnp.broadcast_to(norm, norm_out.shape)


def update(layers, limit, step_count, squares, tile, quads, flats, gains):
    blocks = 4 * quads.shape[0]
    part, width = quads.shape[1:]
    rows = flats[0].shape[0]
    whole = [pl.BlockSpec(memory_space=pltpu.VMEM)]
    flat = [pl.BlockSpec((rows // 3, 128), lambda i: (i, 0))]
    share = gains[0].shape
    return pl.pallas_call(
        functools.partial(update_kernel, layers, limit),
        grid=(3,),
        in_specs=[pl.BlockSpec(memory_space=pltpu.SMEM)] + whole * 2
        + [pl.BlockSpec((2, part, width), lambda i: (i, 0, 0))] + flat * 5 + whole * 3,
        out_specs=flat * 4 + whole * 4,
        out_shape=[jax.ShapeDtypeStruct((rows, 128), F32)] * 4
        + [jax.ShapeDtypeStruct(share, F32)] * 3 + [jax.ShapeDtypeStruct((8, 128), F32)],
        scratch_shapes=[pltpu.VMEM((6, part, 128), F32)],
        compiler_params=pltpu.CompilerParams(vmem_limit_bytes=VMEM_LIMIT),
    )(step_count, squares, tile, quads, *flats, *gains)


def body(
    x_in, targets, valid_len, present_stems, w_master, norm_gains, gain_m, gain_v,
    l_stats, r_stats, l_roots, r_roots, step_count,
):
    width = x_in.shape[1]
    part = width // 4
    layers = lax.axis_size("section")
    section_idx = lax.axis_index("section")
    groups = lax.axis_size("dp")
    group_idx = lax.axis_index("dp")
    micro = valid_len.shape[0] // groups
    seg = x_in.shape[0] // micro
    own_blocks = w_master.shape[1]
    own_gain = norm_gains.shape[2]
    own_w = (
        w_master[0].astype(BF16).reshape(own_blocks // 4, 4, part, part).transpose(0, 2, 1, 3)
        .reshape(own_blocks // 4, part, width)
    )
    gain_tile = jnp.zeros((8, 128), F32).at[:2, :own_gain].set(norm_gains[0])
    slot = jnp.minimum(section_idx, micro - 1)
    used = (section_idx < micro).astype(jnp.int32)
    at = group_idx * micro + slot
    info = jnp.concatenate([valid_len[at][None] * used, present_stems[at] * used])
    frame_count = jnp.sum(valid_len).astype(F32)
    x_seg = lax.dynamic_slice_in_dim(x_in, slot * seg, seg, 0)
    target_seg = lax.dynamic_slice_in_dim(targets, slot * seg, seg, 0)
    *saved, sent, loss_grad, stats, full_w, tiles = forward(
        layers, info, (1.0 / frame_count)[None], x_seg, target_seg, own_w, gain_tile
    )
    full_g = (
        tiles[:, :, :2, :own_gain].transpose(0, 2, 1, 3).reshape(layers, 2, width).astype(BF16).astype(F32)
    )
    own_quads, tile, squares = backward(layers, loss_grad, full_w, full_g, sent, saved, stats)
    sums = tile[2 * layers : 3 * layers, :4]
    loss_value = sums[0, 3] / frame_count
    clip_limit = 0.00015 * math.sqrt(layers * (own_blocks * groups * part * part + 2 * width))
    flats = [flat_rows(a[0]) for a in (w_master, l_stats, r_stats, l_roots, r_roots)]
    *news, gains_new, m_new, v_new, norms = update(
        layers, clip_limit, step_count, squares, tile, own_quads, flats,
        (norm_gains[0], gain_m[0], gain_v[0]),
    )
    w_new, grad_blocks, l_new, r_new = (from_flat_rows(a, own_blocks) for a in news)
    grad_norm = norms[0, 0]
    rms = jnp.sqrt(sums[section_idx, :3] / (frame_count * width)).reshape(1, 3)
    return (
        w_new[None],
        grad_blocks[None],
        l_new[None],
        r_new[None],
        gains_new[None],
        m_new[None],
        v_new[None],
        loss_value,
        grad_norm,
        rms,
    )


def solution(mesh):
    def step(*args):
        layers, groups = mesh.shape["section"], mesh.shape["dp"]
        micro, own_blocks = args[2].shape[0] // groups, args[4].shape[1]
        if micro <= layers == 4 and groups == 8 and own_blocks == 24:
            return body(*args)
        return pipelined_body(*args)

    block = P("section", "dp", None)
    gain = P("section", None, "dp")
    return jax.shard_map(
        step,
        mesh=mesh,
        in_specs=(
            P("dp", None), P("dp", None), P(), P(), block, gain, gain, gain, block, block, block, block, P(),
        ),
        out_specs=(block, block, block, block, gain, gain, gain, P(), P(), P("section", None)),
        check_vma=False,
    )
```

```python
import functools
import math

import jax
import jax.numpy as jnp
from jax import lax
from jax.experimental import pallas as pl
from jax.experimental.pallas import tpu as pltpu
from jax.sharding import PartitionSpec as P

HEADS = 8
F32 = jnp.float32
BF16 = jnp.bfloat16
VMEM_LIMIT = 61 * 1024 * 1024


def dot_nn(a, b):
    return lax.dot_general(a, b, (((1,), (0,)), ((), ())), preferred_element_type=F32)


def dot_nt(a, b):
    return lax.dot_general(a, b, (((1,), (1,)), ((), ())), preferred_element_type=F32)


def dot_tn(a, b):
    return lax.dot_general(a, b, (((0,), (0,)), ((), ())), preferred_element_type=F32)


def gelu_parts(x):
    ax = jnp.abs(x)
    bell = jnp.exp(-0.5 * x * x)
    t = 1.0 / (1.0 + (0.3275911 * 0.7071067811865476) * ax)
    poly = t * (
        0.5 * 0.254829592
        + t
        * (
            0.5 * -0.284496736
            + t * (0.5 * 1.421413741 + t * (0.5 * -1.453152027 + t * (0.5 * 1.061405429)))
        )
    )
    tail = poly * bell
    cdf = jnp.where(x >= 0.0, 1.0 - tail, tail)
    return x * cdf, cdf + x * bell * 0.3989422804014327


def stack_quads(w_ref, first, step, number):
    part = w_ref.shape[2] // 4
    if step == 1:
        return w_ref[0, first * part : (first + number) * part]
    return jnp.concatenate(
        [w_ref[0, (first + step * i) * part : (first + step * i + 1) * part] for i in range(number)], axis=0
    )


MESH = pl.DeviceIdType.MESH


def mesh_place():
    section = lax.axis_index("section")
    group = lax.axis_index("dp")
    core = lax.rem(section, 2)
    y = lax.rem(group, 2)
    z = group // 2
    z_peers = (z, z + 1 - 2 * lax.rem(z, 2), lax.rem(z + 2, 4), 3 - z)
    return section, group, core, y, z_peers


def remote(source, target, send_sem, recv_sem, section, group):
    return pltpu.make_async_remote_copy(
        src_ref=source, dst_ref=target, send_sem=send_sem, recv_sem=recv_sem,
        device_id=(section, group), device_id_type=MESH,
    )


def greet(places):
    barrier = pltpu.get_barrier_semaphore()
    for place in places:
        pl.semaphore_signal(barrier, inc=1, device_id=place, device_id_type=MESH)
    pl.semaphore_wait(barrier, len(places))


class Slabs:
    def __init__(self, rows):
        self.section, self.group, self.core, self.y, self.z_peers = mesh_place()
        self.x = self.section // 2
        self.rows, self.half = rows, rows // 2
        self.edge = self.half * 5 // 18
        self.slab = self.half - self.edge

    def slab_of(self, x, core):
        return pl.ds(pl.multiple_of(self.half * core + self.edge * x, 16), self.slab)

    def edge_of(self, x, core):
        return pl.ds(pl.multiple_of(self.half * core + self.slab * x, 16), self.edge)

    def half_of(self, core):
        return pl.ds(pl.multiple_of(self.half * core, 16), self.half)

    def x_peer(self):
        return lax.rem(self.section + 2, 4), self.group

    def y_peer(self):
        return self.section, self.group + 1 - 2 * self.y

    def z_peer(self, k):
        return self.section, self.z_peers[k] * 2 + self.y

    def core_peer(self):
        return self.section + 1 - 2 * self.core, self.group

    def greet_all(self):
        greet(
            [(lax.rem(self.section + k, 4), self.group) for k in range(1, 4)]
            + [(self.section, lax.rem(self.group + k, 8)) for k in range(1, 8)]
        )


class Gather(Slabs):
    def __init__(self, own_ref, gain_ref, w_ref, gains_ref, sems):
        super().__init__(own_ref.shape[0])
        self.own, self.gain, self.w, self.gains = own_ref, gain_ref, w_ref, gains_ref
        self.spread, self.z_sems, self.y_sems, self.x_sems, self.core_sems, self.gain_sems, self.local = sems
        self.others = [lax.rem(self.section + k, 4) for k in range(1, 4)]

    def chunk(self, k):
        y = self.y if k < 4 else 1 - self.y
        return self.z_peers[k % 4] * 2 + y

    def at(self, layer, group, rows):
        return self.w.at[layer, pl.ds(pl.multiple_of(group * self.rows + rows.start, 16), rows.size)]

    def spread_copy(self, k):
        peer = self.others[k]
        rows = self.slab_of(peer // 2, lax.rem(peer, 2))
        return remote(
            self.own.at[rows], self.at(self.section, self.group, rows),
            self.spread.at[0, k], self.spread.at[1, k], peer, self.group,
        )

    def spread_wait(self, layer):
        ref = self.at(layer, self.group, self.slab_of(self.x, self.core))
        for k in range(3):
            @pl.when(lax.rem(layer + k + 1, 4) == self.section)
            def _():
                remote(ref, ref, self.spread.at[0, k], self.spread.at[1, k], self.others[0], self.group).wait_recv()

    def z_copy(self, layer, k, landed=False):
        ref = self.at(layer, self.chunk(k) if landed else self.group, self.slab_of(self.x, self.core))
        return remote(ref, ref, self.z_sems.at[0, layer, k], self.z_sems.at[1, layer, k], *self.z_peer(k))

    def y_copy(self, layer, k, landed=False):
        ref = self.at(layer, self.chunk(k + 4 if landed else k), self.slab_of(self.x, self.core))
        return remote(ref, ref, self.y_sems.at[0, layer, k], self.y_sems.at[1, layer, k], *self.y_peer())

    def x_copy(self, layer, k, landed=False):
        ref = self.at(layer, self.chunk(k), self.edge_of(1 - self.x if landed else self.x, self.core))
        return remote(ref, ref, self.x_sems.at[0, layer, k], self.x_sems.at[1, layer, k], *self.x_peer())

    def core_copy(self, layer, k, landed=False):
        ref = self.at(layer, self.chunk(k), self.half_of(1 - self.core if landed else self.core))
        return remote(ref, ref, self.core_sems.at[0, layer, k], self.core_sems.at[1, layer, k], *self.core_peer())

    def gain_copy(self, k):
        if k < 7:
            peer = lax.rem(self.group + k + 1, 8)
            return remote(
                self.gain, self.gains.at[self.section, self.group],
                self.gain_sems.at[0, k], self.gain_sems.at[1, k], self.section, peer,
            )
        ref = self.gains.at[self.section]
        return remote(
            ref, ref, self.gain_sems.at[0, k], self.gain_sems.at[1, k], self.others[k - 7], self.group
        )

    def gain_landed(self, k):
        if k < 7:
            ref = self.gains.at[self.section, lax.rem(self.group - k - 1 + 8, 8)]
        else:
            ref = self.gains.at[lax.rem(self.section - (k - 6) + 4, 4)]
        return remote(ref, ref, self.gain_sems.at[0, k], self.gain_sems.at[1, k], self.section, self.group)

    def begin(self):
        self.greet_all()
        for k in range(3):
            self.spread_copy(k).start()
        for k in range(7):
            self.gain_copy(k).start()
        rows = self.slab_of(self.x, self.core)
        self.w[self.section, pl.ds(pl.multiple_of(self.group * self.rows + rows.start, 16), rows.size)] = self.own[rows]
        self.gains[self.section, self.group] = self.gain[...]

    def share_gains(self):
        for k in range(7):
            self.gain_landed(k).wait_recv()
        for k in range(7, 10):
            self.gain_copy(k).start()

    def wait_gains(self):
        for k in range(7, 10):
            self.gain_landed(k).wait_recv()

    def kick(self, layer):
        self.spread_wait(layer)
        for k in range(1, 4):
            self.z_copy(layer, k).start()
        self.y_copy(layer, 0).start()
        self.x_copy(layer, 0).start()

    def serve_z(self, layer, k):
        self.z_copy(layer, k, True).wait_recv()
        self.y_copy(layer, k).start()
        self.x_copy(layer, k).start()

    def serve_y(self, layer, k):
        self.y_copy(layer, k, True).wait_recv()
        self.x_copy(layer, k + 4).start()

    def serve_x(self, layer, k):
        self.x_copy(layer, k, True).wait_recv()
        self.core_copy(layer, k).start()

    def finish(self, layer):
        for k in range(8):
            self.core_copy(layer, k, True).wait_recv()

    def end(self, layers):
        for k in range(3):
            self.spread_copy(k).wait_send()
        for k in range(10):
            self.gain_copy(k).wait_send()

        def per_layer(layer, _):
            for k in range(1, 4):
                self.z_copy(layer, k).wait_send()
            for k in range(4):
                self.y_copy(layer, k).wait_send()
            for k in range(8):
                self.x_copy(layer, k).wait_send()
                self.core_copy(layer, k).wait_send()
            return 0

        lax.fori_loop(0, layers, per_layer, 0)


def forward_kernel(
    layers, half, info_ref, scale_ref, x_ref, target_ref, own_ref, own_gain_ref,
    probs_ref, heads_ref, att_ref, middle_ref, hidden_ref, slope_ref, sent_ref, loss_grad_ref, stats_ref,
    full_ref, gains_out_ref, hold_ref, out_ref, w_all_ref, gains_ref, *sems,
):
    seg, width = x_ref.shape
    dim = width // HEADS
    part = width // 4
    layer = pl.program_id(0)
    rows = 256
    chunks = seg // rows
    length = info_ref[0]
    gather = Gather(own_ref, own_gain_ref, w_all_ref, gains_ref, sems)
    w_ref = w_all_ref.at[pl.ds(layer, 1)]

    def keep_copy(index):
        return pltpu.make_async_copy(w_all_ref.at[index], full_ref.at[index], gather.local.at[index])

    @pl.when(layer == 0)
    def _():
        gather.begin()
        sent_ref[0] = x_ref[...]
        stats_ref[...] = jnp.zeros_like(stats_ref)
        gather.kick(0)
        gather.share_gains()
        gather.serve_z(0, 1)
        gather.serve_z(0, 2)
        gather.serve_x(0, 0)
        gather.serve_x(0, 1)
        gather.serve_z(0, 3)
        gather.kick(1)
        gather.wait_gains()
        gather.serve_y(0, 0)
        gather.serve_x(0, 2)
        gather.serve_y(0, 1)
        gather.serve_y(0, 2)
        gather.serve_x(0, 3)
        gather.serve_y(0, 3)
        for k in range(4, 8):
            gather.serve_x(0, k)

    gather.finish(layer)
    keep_copy(layer).start()
    more = layer + 1 < layers

    def serve(here, *steps):
        @pl.when(more & here)
        def _():
            for kind, k in steps:
                getattr(gather, kind)(layer + 1, k)

    def kick(here):
        @pl.when((layer + 2 < layers) & here)
        def _():
            gather.kick(layer + 2)

    def stream_of(at):
        prev = sent_ref[layer, at].astype(F32)
        skip = sent_ref[jnp.maximum(layer + 1 - half, 0), at].astype(F32)
        return prev + jnp.where(layer >= half, skip, 0.0)

    def gain_row(which):
        return jnp.concatenate(
            [gains_ref[layer, g, which : which + 1, : width // 8] for g in range(8)], axis=1
        ).astype(BF16).astype(F32)

    gain_one = gain_row(0)
    gain_two = gain_row(1)

    def qkv_step(i, _):
        at = pl.ds(pl.multiple_of(i * rows, rows), rows)
        stream = stream_of(at)
        factor = lax.rsqrt(jnp.mean(stream * stream, axis=-1, keepdims=True) + 1e-06)
        normed = (stream * factor * gain_one).astype(BF16)
        for t in range(3):
            qkv = dot_nn(normed, stack_quads(w_ref, t, 3, 4)).astype(BF16)
            for h in range(HEADS):
                heads_ref[0, t * HEADS + h, at] = qkv[:, h * dim : (h + 1) * dim]
        return 0

    lax.fori_loop(0, chunks, qkv_step, 0)
    frames = lax.broadcasted_iota(jnp.int32, (1, seg), 1)
    masking = jnp.where(frames < length, 0.0, -1e30).astype(F32)

    def head_step(h, _):
        keys = heads_ref[0, HEADS + h]
        values = heads_ref[0, 2 * HEADS + h]
        for i in range(chunks):
            at = pl.ds(i * rows, rows)
            scores = dot_nt(heads_ref[0, h, at], keys) * dim ** (-0.5) + masking
            top = jnp.max(scores, axis=-1, keepdims=True)
            expd = jnp.exp(scores - top)
            probs = (expd * (1.0 / jnp.sum(expd, axis=-1, keepdims=True))).astype(BF16)
            probs_ref[0, h, at] = probs
            hold_ref[h, at] = dot_nn(probs, values).astype(BF16)
        serve(h == 1, ("serve_z", 1), ("serve_z", 2))
        serve(h == 3, ("serve_z", 3), ("serve_x", 0))
        kick(h == 3)
        serve(h == 5, ("serve_x", 1), ("serve_y", 0))
        serve(h == 7, ("serve_x", 2), ("serve_y", 1))
        return 0

    lax.fori_loop(0, HEADS, head_step, 0)

    def ffn_step(i, _):
        at = pl.ds(pl.multiple_of(i * rows, rows), rows)
        attended = jnp.concatenate([hold_ref[h, at] for h in range(HEADS)], axis=1)
        att_ref[0, at] = attended
        branch_attn = dot_nn(attended, stack_quads(w_ref, 12, 1, 4))
        stream = stream_of(at)
        middle = stream + branch_attn
        middle_ref[0, at] = middle
        factor = lax.rsqrt(jnp.mean(middle * middle, axis=-1, keepdims=True) + 1e-06)
        normed = (middle * factor * gain_two).astype(BF16)
        branch_ffn = jnp.zeros((rows, width), F32)
        for c in range(4):
            pre_act = dot_nn(normed, stack_quads(w_ref, 16 + c, 4, 4))
            hidden, slope = gelu_parts(pre_act)
            hidden = hidden.astype(BF16)
            hidden_ref[0, c, at] = hidden
            slope_ref[0, c, at] = slope.astype(BF16)
            branch_ffn = branch_ffn + dot_nn(hidden, stack_quads(w_ref, 32 + 4 * c, 1, 4))
        output = middle + branch_ffn
        out_ref[at] = output
        sent_ref[jnp.minimum(layer + 1, layers - 1), at] = jnp.where(
            layer + 1 < layers, output.astype(BF16), sent_ref[layers - 1, at]
        )
        valid = (lax.broadcasted_iota(jnp.int32, (rows, 1), 0) + i * rows < length).astype(F32)
        for k, value in enumerate((stream, branch_attn, branch_ffn)):
            stats_ref[layer, k : k + 1] += jnp.sum(valid * value * value, axis=0, keepdims=True)

        serve(i == 0, ("serve_x", 3), ("serve_y", 2), ("serve_y", 3), ("serve_x", 4))
        return 0

    lax.fori_loop(0, chunks, ffn_step, 0)
    serve(True, ("serve_x", 5), ("serve_x", 6), ("serve_x", 7))

    @pl.when(layer == layers - 1)
    def _():
        bins = width // 8
        lane = lax.broadcasted_iota(jnp.int32, (1, width), 1)
        is_real = lax.rem(lane, 2 * bins) < bins
        stem = lane // (2 * bins)
        present = jnp.zeros((1, width), F32)
        for k in range(4):
            present = jnp.where(stem == k, info_ref[1 + k].astype(F32), present)
        inverse = scale_ref[0]

        def loss_step(i, _):
            at = pl.ds(pl.multiple_of(i * rows, rows), rows)
            output = out_ref[at]
            square = output * output
            other = jnp.where(
                is_real, pltpu.roll(square, width - bins, 1), pltpu.roll(square, bins, 1)
            )
            magnitude = jnp.sqrt(square + other + 0.01)
            goal = target_ref[at]
            goal = jnp.concatenate(
                [goal[:, (k // 2) * bins : (k // 2 + 1) * bins] for k in range(8)], axis=1
            )
            differ = magnitude - goal
            smooth = jnp.sqrt(differ * differ + 0.01)
            valid = (lax.broadcasted_iota(jnp.int32, (rows, 1), 0) + i * rows < length).astype(F32)
            weight = valid * present
            loss_grad_ref[at] = weight * differ * output * inverse / (smooth * magnitude)
            stats_ref[0, 3:4] += jnp.sum(
                jnp.where(is_real, weight * smooth, 0.0), axis=0, keepdims=True
            )
            return 0

        lax.fori_loop(0, chunks, loss_step, 0)
        gains_out_ref[...] = gains_ref[...]
        gather.end(layers)
        for k in range(layers):
            keep_copy(k).wait()


class Scatter(Slabs):
    def __init__(self, refs, sems):
        self.grads, self.core_in, self.x_in, self.y_in, self.z_in, self.last_out, self.last_in = refs
        super().__init__(self.grads.shape[3])
        self.core_sems, self.x_sems, self.y_sems, self.z_sems, self.last_sems = sems
        self.mine = self.slab_of(self.x, self.core)

    def core_copy(self, layer, late):
        slot = lax.rem(layer, 2)
        zs = pl.ds(0, 1) if late else pl.ds(1, 3)
        return remote(
            self.grads.at[slot, zs, :, self.half_of(1 - self.core)], self.core_in.at[slot, zs],
            self.core_sems.at[0, slot, int(late)], self.core_sems.at[1, slot, int(late)], *self.core_peer(),
        )

    def x_copy(self, layer, k):
        slot = lax.rem(layer, 2)
        return remote(
            self.grads.at[slot, self.z_peers[k], :, self.edge_of(1 - self.x, self.core)], self.x_in.at[slot, k],
            self.x_sems.at[0, slot, k], self.x_sems.at[1, slot, k], *self.x_peer(),
        )

    def y_copy(self, layer, k):
        slot = lax.rem(layer, 2)
        return remote(
            self.grads.at[slot, self.z_peers[k], 1 - self.y, self.mine], self.y_in.at[slot, k],
            self.y_sems.at[0, slot, k], self.y_sems.at[1, slot, k], *self.y_peer(),
        )

    def z_copy(self, layer, k):
        slot = lax.rem(layer, 2)
        return remote(
            self.grads.at[slot, self.z_peers[k], self.y, self.mine], self.z_in.at[layer, k - 1],
            self.z_sems.at[0, layer, k - 1], self.z_sems.at[1, layer, k - 1], *self.z_peer(k),
        )

    def last_copy(self, layer):
        slot = lax.rem(layer, 2)
        place = jnp.maximum(lax.rem(self.section - layer + 4, 4) - 1, 0)
        return remote(
            self.last_out.at[slot], self.last_in.at[place],
            self.last_sems.at[0, slot], self.last_sems.at[1, place], layer, self.group,
        )

    def last_landed(self, place):
        return remote(
            self.last_in.at[place], self.last_in.at[place],
            self.last_sems.at[0, 0], self.last_sems.at[1, place], self.section, self.group,
        )

    def for_part(self, late, act):
        for k in (1, 2, 3, 0):
            @pl.when((self.z_peers[k] == 0) == late)
            def _():
                act(k)

    def add_core(self, layer, late):
        slot = lax.rem(layer, 2)
        self.core_copy(layer, late).wait_recv()
        rows = self.half_of(self.core)

        def add(i, _):
            z, y = i // 2, lax.rem(i, 2)
            self.grads[slot, z, y, rows] = self.grads[slot, z, y, rows] + self.core_in[slot, z, y]
            return 0

        lax.fori_loop(0 if late else 2, 2 if late else 8, add, 0)
        self.for_part(late, lambda k: self.x_copy(layer, k).start())

    def add_x(self, layer, k, late):
        @pl.when((self.z_peers[k] == 0) == late)
        def _():
            slot = lax.rem(layer, 2)
            self.x_copy(layer, k).wait_recv()
            rows = self.edge_of(self.x, self.core)
            z = self.z_peers[k]
            for y in range(2):
                self.grads[slot, z, y, rows] = self.grads[slot, z, y, rows] + self.x_in[slot, k, y]
            self.y_copy(layer, k).start()

    def add_y(self, layer, k, late):
        @pl.when((self.z_peers[k] == 0) == late)
        def _():
            slot = lax.rem(layer, 2)
            self.y_copy(layer, k).wait_recv()
            z = self.z_peers[k]
            self.grads[slot, z, self.y, self.mine] = self.grads[slot, z, self.y, self.mine] + self.y_in[slot, k]
            if k:
                self.z_copy(layer, k).start()

    def add_z(self, layer, result_ref):
        slot = lax.rem(layer, 2)
        for k in range(1, 4):
            self.z_copy(layer, k).wait_recv()
        total = self.grads[slot, self.z_peers[0], self.y, self.mine].astype(F32)
        for k in range(3):
            total = total + self.z_in[layer, k].astype(F32)

        @pl.when(layer == self.section)
        def _():
            result_ref[...] = jnp.zeros_like(result_ref)
            result_ref[self.mine] = total

        @pl.when(layer != self.section)
        def _():
            self.last_out[slot] = total.astype(BF16)
            self.last_copy(layer).start()

    def wait_sends(self, layer):
        for late in (False, True):
            self.core_copy(layer, late).wait_send()
        for k in range(4):
            self.x_copy(layer, k).wait_send()
            self.y_copy(layer, k).wait_send()
        for k in range(1, 4):
            self.z_copy(layer, k).wait_send()

        @pl.when(layer != self.section)
        def _():
            self.last_copy(layer).wait_send()

    def collect(self, result_ref):
        for place in (0, 2, 1):
            self.last_landed(place).wait_recv()
            peer = lax.rem(self.section + place + 1, 4)
            rows = self.slab_of(peer // 2, lax.rem(peer, 2))
            result_ref[rows] = result_ref[rows] + self.last_in[place].astype(F32)


class Totals:
    def __init__(self, refs, sems):
        self.stage_in, self.z_in, self.norm_section, self.norm_group = refs
        self.stage_sems, self.z_sems, self.section_sems, self.group_sems = sems
        self.section, self.group, self.core, self.y, self.z_peers = mesh_place()

    def stage_copy(self, k):
        peer = (
            (self.section + 1 - 2 * self.core, self.group),
            (self.section, self.group + 1 - 2 * self.y),
            (lax.rem(self.section + 2, 4), self.group),
        )[k]
        return remote(
            self.stage_in.at[2 * k], self.stage_in.at[2 * k + 1],
            self.stage_sems.at[0, k], self.stage_sems.at[1, k], *peer,
        )

    def z_copy(self, k):
        z = self.z_peers[0]
        return remote(
            self.z_in.at[z], self.z_in.at[z], self.z_sems.at[0, k - 1], self.z_sems.at[1, k - 1],
            self.section, self.z_peers[k] * 2 + self.y,
        )

    def z_landed(self, k):
        z = self.z_peers[k]
        return remote(
            self.z_in.at[z], self.z_in.at[z], self.z_sems.at[0, k - 1], self.z_sems.at[1, k - 1],
            self.section, self.z_peers[k] * 2 + self.y,
        )

    def begin(self, tile):
        self.stage_in[0] = tile
        self.stage_copy(0).start()

    def after_core(self):
        self.stage_copy(0).wait_recv()
        self.stage_in[2] = self.stage_in[0] + self.stage_in[1]
        self.stage_copy(1).start()

    def after_y(self):
        self.stage_copy(1).wait_recv()
        self.z_in[self.z_peers[0]] = self.stage_in[2] + self.stage_in[3]
        for k in range(1, 4):
            self.z_copy(k).start()

    def after_z(self):
        for k in range(1, 4):
            self.z_landed(k).wait_recv()
        self.stage_in[4] = self.z_in[0] + self.z_in[1] + self.z_in[2] + self.z_in[3]
        self.stage_copy(2).start()

    def after_x(self):
        self.stage_copy(2).wait_recv()
        return self.stage_in[4] + self.stage_in[5]

    def norm_copy(self, k):
        if k < 3:
            peer = (lax.rem(self.section + k + 1, 4), self.group)
            ref = self.norm_section.at[self.section]
            return remote(ref, ref, self.section_sems.at[0, k], self.section_sems.at[1, k], *peer)
        k = k - 3
        peer = (self.section, lax.rem(self.group + k + 1, 8))
        ref = self.norm_group.at[self.group]
        return remote(ref, ref, self.group_sems.at[0, k], self.group_sems.at[1, k], *peer)

    def norm_landed(self, k):
        if k < 3:
            ref = self.norm_section.at[lax.rem(self.section - k - 1 + 4, 4)]
            return remote(
                ref, ref, self.section_sems.at[0, k], self.section_sems.at[1, k], self.section, self.group
            )
        k = k - 3
        ref = self.norm_group.at[lax.rem(self.group - k - 1 + 8, 8)]
        return remote(ref, ref, self.group_sems.at[0, k], self.group_sems.at[1, k], self.section, self.group)

    def norm(self, value):
        self.norm_section[self.section] = value
        for k in range(3):
            self.norm_copy(k).start()
        for k in range(3):
            self.norm_landed(k).wait_recv()
        total = self.norm_section[0]
        for k in range(1, 4):
            total = total + self.norm_section[k]
        self.norm_group[self.group] = total
        for k in range(3, 10):
            self.norm_copy(k).start()
        for k in range(3, 10):
            self.norm_landed(k).wait_recv()
        total = self.norm_group[0]
        for k in range(1, 8):
            total = total + self.norm_group[k]
        return total

    def end(self):
        for k in range(3):
            self.stage_copy(k).wait_send()
        for k in range(1, 4):
            self.z_copy(k).wait_send()
        for k in range(10):
            self.norm_copy(k).wait_send()


def norm_reverse(value, gain, grad):
    factor = lax.rsqrt(jnp.mean(value * value, axis=-1, keepdims=True) + 1e-06)
    scaled = grad * gain
    mean = jnp.mean(value * scaled, axis=-1, keepdims=True)
    unit = value * factor
    back = factor * scaled - unit * (factor * factor * mean)
    return back, jnp.sum(grad * unit, axis=0, keepdims=True), (unit * gain).astype(BF16)


def backward_kernel(
    layers, half, loss_grad_ref, w_ref, gain_ref, sent_ref,
    probs_ref, heads_ref, att_ref, middle_ref, hidden_ref, slope_ref, stats_ref,
    result_ref, totals_ref, square_ref,
    sends_ref, dffn_ref, dpre_ref, normed_ref, dmid_ref, datt_ref, dhold_ref, dheads_ref, dqkv_ref,
    gain_grad_ref, *comm_refs,
):
    seg, width = loss_grad_ref.shape
    dim = width // HEADS
    part = width // 4
    layer = layers - 1 - pl.program_id(0)
    rows = 256
    chunks = seg // rows
    gain_one = gain_ref[0, 0:1]
    gain_two = gain_ref[0, 1:2]
    scatter = Scatter(comm_refs[:7], comm_refs[11:16])
    totals = Totals(comm_refs[7:11], comm_refs[16:])
    grads_ref = comm_refs[0]
    slot = lax.rem(layer, 2)

    @pl.when(layer == layers - 1)
    def _():
        scatter.greet_all()
        sends_ref[...] = jnp.zeros_like(sends_ref)
        gain_grad_ref[...] = jnp.zeros_like(gain_grad_ref)

    def put_grad(first, step, value):
        for r in range(4):
            quad = first + step * r
            owner = quad // 6
            at = pl.ds(pl.multiple_of(lax.rem(quad, 6) * part, part), part)
            grads_ref[slot, owner // 2, lax.rem(owner, 2), at] = value[r * part : (r + 1) * part].astype(BF16)

    def before(act):
        @pl.when(layer < layers - 1)
        def _():
            act(layer + 1)

    def ffn_step(i, _):
        at = pl.ds(pl.multiple_of(i * rows, rows), rows)
        later = sends_ref[jnp.minimum(layer + 1, layers - 1), at].astype(F32)
        skip = sends_ref[jnp.minimum(layer + half, layers - 1), at].astype(F32)
        upstream = jnp.where(
            layer == layers - 1, loss_grad_ref[at], later + jnp.where(layer + half < layers, skip, 0.0)
        )
        dffn = upstream.astype(BF16)
        dffn_ref[at] = dffn
        dnormed = jnp.zeros((rows, width), F32)
        for c in range(4):
            dhidden = dot_nt(dffn, stack_quads(w_ref, 32 + 4 * c, 1, 4))
            dpre = (dhidden * slope_ref[0, c, at].astype(F32)).astype(BF16)
            dpre_ref[c, at] = dpre
            dnormed = dnormed + dot_nt(dpre, stack_quads(w_ref, 16 + c, 4, 4))
        back, gain_grad, normed = norm_reverse(middle_ref[0, at], gain_two, dnormed)
        gain_grad_ref[layer, 1:2] += gain_grad
        normed_ref[at] = normed
        dmid = upstream + back
        dmid_ref[at] = dmid
        datt = dmid.astype(BF16)
        datt_ref[at] = datt
        dattended = dot_nt(datt, stack_quads(w_ref, 12, 1, 4)).astype(BF16)
        for h in range(HEADS):
            dhold_ref[h, at] = dattended[:, h * dim : (h + 1) * dim]

        @pl.when(i == 0)
        def _():
            before(lambda at: scatter.add_core(at, True))
            before(lambda at: scatter.add_x(at, 3, False))

        @pl.when(i == 1)
        def _():
            before(lambda at: scatter.add_x(at, 0, False))
            before(lambda at: scatter.add_y(at, 1, False))

        return 0

    lax.fori_loop(0, chunks, ffn_step, 0)

    @pl.when(layer < layers - 2)
    def _():
        scatter.wait_sends(layer + 2)

    def ffn_grad_step(c, _):
        put_grad(32 + 4 * c, 1, dot_tn(hidden_ref[0, c], dffn_ref[...]))
        put_grad(16 + c, 4, dot_tn(normed_ref[...], dpre_ref[c]))
        return 0

    lax.fori_loop(0, 4, ffn_grad_step, 0)
    put_grad(12, 1, dot_tn(att_ref[0], datt_ref[...]))
    scatter.core_copy(layer, False).start()

    @pl.when(layer < layers - 1)
    def _():
        for k in range(4):
            scatter.add_x(layer + 1, k, True)
        for k in (2, 3, 0):
            scatter.add_y(layer + 1, k, False)

    def head_step(h, _):
        queries = heads_ref[0, h]
        keys = heads_ref[0, HEADS + h]
        values = heads_ref[0, 2 * HEADS + h]
        dkeys = jnp.zeros((seg, dim), F32)
        dvalues = jnp.zeros((seg, dim), F32)
        for i in range(chunks):
            at = pl.ds(i * rows, rows)
            probs = probs_ref[0, h, at]
            dhold = dhold_ref[h, at]
            dprobs = dot_nt(dhold, values)
            wide = probs.astype(F32)
            dot_sum = jnp.sum(wide * dprobs, axis=-1, keepdims=True)
            dscores = (wide * (dprobs - dot_sum)).astype(BF16)
            dheads_ref[h, at] = (dot_nn(dscores, keys) * dim ** (-0.5)).astype(BF16)
            dvalues = dvalues + dot_tn(probs, dhold)
            dkeys = dkeys + dot_tn(dscores, heads_ref[0, h, at])
        dheads_ref[HEADS + h] = (dkeys * dim ** (-0.5)).astype(BF16)
        dheads_ref[2 * HEADS + h] = dvalues.astype(BF16)

        @pl.when(h == 3)
        def _():
            scatter.add_core(layer, False)

        @pl.when(h == 5)
        def _():
            for k in range(4):
                before(lambda at: scatter.add_y(at, k, True))

        @pl.when(h == 7)
        def _():
            scatter.add_x(layer, 1, False)

        return 0

    lax.fori_loop(0, HEADS, head_step, 0)

    def qkv_step(i, _):
        at = pl.ds(pl.multiple_of(i * rows, rows), rows)
        dnormed = jnp.zeros((rows, width), F32)
        for t in range(3):
            dqkv = jnp.concatenate([dheads_ref[t * HEADS + h, at] for h in range(HEADS)], axis=1)
            dqkv_ref[t, at] = dqkv
            dnormed = dnormed + dot_nt(dqkv, stack_quads(w_ref, t, 3, 4))
        prev = sent_ref[layer, at].astype(F32)
        skip = sent_ref[jnp.maximum(layer + 1 - half, 0), at].astype(F32)
        stream = prev + jnp.where(layer >= half, skip, 0.0)
        back, gain_grad, normed = norm_reverse(stream, gain_one, dnormed)
        gain_grad_ref[layer, 0:1] += gain_grad
        normed_ref[at] = normed
        sends_ref[layer, at] = (dmid_ref[at] + back).astype(BF16)
        return 0

    lax.fori_loop(0, chunks, qkv_step, 0)

    def qkv_grad_step(t, _):
        put_grad(t, 3, dot_tn(normed_ref[...], dqkv_ref[t]))
        return 0

    lax.fori_loop(0, 3, qkv_grad_step, 0)
    scatter.core_copy(layer, True).start()
    before(lambda at: scatter.add_z(at, result_ref))
    scatter.add_x(layer, 2, False)

    @pl.when(layer == 0)
    def _():
        lane = lax.broadcasted_iota(jnp.int32, (1, width), 1)
        rows_out = [gain_grad_ref[k // 2, k % 2 : k % 2 + 1] for k in range(2 * layers)]
        for k in range(layers):
            row = jnp.zeros((1, width), F32)
            for i in range(4):
                value = jnp.sum(stats_ref[k, i : i + 1], axis=1, keepdims=True)
                row = jnp.where(lane == i, value, row)
            rows_out.append(row)
        rows_out.append(jnp.zeros((16 - 3 * layers, width), F32))
        totals.begin(jnp.concatenate(rows_out, axis=0))
        scatter.add_core(0, True)
        scatter.add_y(0, 1, False)
        scatter.add_x(0, 3, False)
        totals.after_core()
        scatter.add_x(0, 0, False)
        scatter.add_y(0, 2, False)
        for k in range(4):
            scatter.add_x(0, k, True)
        scatter.add_y(0, 3, False)
        scatter.add_y(0, 0, False)
        for k in range(4):
            scatter.add_y(0, k, True)
        totals.after_y()
        scatter.add_z(0, result_ref)
        totals.after_z()
        scatter.collect(result_ref)
        square = jnp.zeros((8, width), F32)
        for q in range(6):
            value = result_ref[q * part : (q + 1) * part]
            square = square + jnp.sum((value * value).reshape(part // 8, 8, width), axis=0)
        folded = square[:, :128] + square[:, 128:256] + square[:, 256:]
        square_ref[...] = totals.norm(folded)
        totals_ref[...] = totals.after_x()
        scatter.wait_sends(1)
        scatter.wait_sends(0)
        totals.end()


FF = 1536


def from_behind(value, axis, by):
    peers = lax.axis_size(axis)
    pairs = [(i, i + by) for i in range(peers) if 0 <= i + by < peers]
    return lax.ppermute(value, axis, pairs)


def unblock(blocks, row_count, col_count, block_size):
    return (
        blocks.reshape(row_count // block_size, col_count // block_size, block_size, block_size)
        .transpose(0, 2, 1, 3)
        .reshape(row_count, col_count)
    )


def to_blocks(matrix, block_size):
    row_count, col_count = matrix.shape
    return (
        matrix.reshape(row_count // block_size, block_size, col_count // block_size, block_size)
        .transpose(0, 2, 1, 3)
        .reshape(-1, block_size * block_size)
    )


def split_matrices(blocks, model_width):
    block_size = model_width // 4
    shapes = (
        (model_width, 3 * model_width),
        (model_width, model_width),
        (model_width, FF),
        (FF, model_width),
    )
    result = []
    offset = 0
    for row_count, col_count in shapes:
        number = row_count * col_count // (block_size * block_size)
        result.append(unblock(blocks[offset : offset + number], row_count, col_count, block_size))
        offset = offset + number
    return result


def rms_norm(stream, gain):
    factor = lax.rsqrt(jnp.mean(stream * stream, axis=-1, keepdims=True) + 1e-06)
    return (stream * factor * gain, factor)


def norm_back(stream, factor, gain, grad):
    scaled = grad * gain
    grad_in = factor * scaled - stream * factor**3 * jnp.mean(
        stream * scaled, axis=-1, keepdims=True
    )
    return (grad_in, jnp.sum(grad * stream * factor, axis=0))


def gelu_slope(pre_act):
    return (
        0.5 * (1.0 + lax.erf(pre_act * 0.7071067811865476))
        + pre_act * jnp.exp(-0.5 * pre_act * pre_act) * 0.3989422804014327
    )


def layer_forward(stream, matrices, gain_pair, length):
    w_qkv, w_out, w_up, w_down = matrices
    row_count, model_width = stream.shape
    head_dim = model_width // HEADS
    frames = jnp.arange(row_count)
    norm_one, scale_one = rms_norm(stream, gain_pair[0])
    normed = norm_one.astype(BF16)
    qkv_all = jnp.dot(normed, w_qkv, preferred_element_type=jnp.float32).astype(BF16)
    queries = qkv_all[:, :model_width].reshape(row_count, HEADS, head_dim)
    key_rows = qkv_all[:, model_width : 2 * model_width].reshape(row_count, HEADS, head_dim)
    value_rows = qkv_all[:, 2 * model_width :].reshape(row_count, HEADS, head_dim)
    masking = jnp.where(frames < length, 0.0, -1e30).astype(jnp.float32)
    scores = jnp.einsum(
        "qhe,khe->hqk", queries, key_rows, preferred_element_type=jnp.float32
    ) * head_dim ** (-0.5)
    attn_probs = jax.nn.softmax(scores + masking[None, None, :], axis=-1)
    probs_low = attn_probs.astype(BF16)
    attended = (
        jnp.einsum("hqk,khe->qhe", probs_low, value_rows, preferred_element_type=jnp.float32)
        .reshape(row_count, model_width)
        .astype(BF16)
    )
    branch_attn = jnp.dot(attended, w_out, preferred_element_type=jnp.float32)
    middle = stream + branch_attn
    norm_two, scale_two = rms_norm(middle, gain_pair[1])
    normed_two = norm_two.astype(BF16)
    pre_act = jnp.dot(normed_two, w_up, preferred_element_type=jnp.float32)
    hidden = jax.nn.gelu(pre_act, approximate=False).astype(BF16)
    branch_ffn = jnp.dot(hidden, w_down, preferred_element_type=jnp.float32)
    kept_vals = (
        scale_one,
        normed,
        queries,
        key_rows,
        value_rows,
        attn_probs,
        probs_low,
        attended,
        middle,
        scale_two,
        normed_two,
        pre_act,
        hidden,
    )
    return (middle + branch_ffn, branch_attn, branch_ffn, kept_vals)


def layer_backward(stream, matrices, gain_pair, length, upstream):
    w_qkv, w_out, w_up, w_down = matrices
    row_count, model_width = stream.shape
    head_dim = model_width // HEADS
    output, branch_attn, branch_ffn, kept_vals = layer_forward(stream, matrices, gain_pair, length)
    (
        scale_one,
        normed,
        queries,
        key_rows,
        value_rows,
        attn_probs,
        probs_low,
        attended,
        middle,
        scale_two,
        normed_two,
        pre_act,
        hidden,
    ) = kept_vals
    grad_ffn = upstream.astype(BF16)
    grad_down = jnp.dot(hidden.T, grad_ffn, preferred_element_type=jnp.float32)
    grad_hidden = jnp.dot(grad_ffn, w_down.T, preferred_element_type=jnp.float32)
    grad_pre = (grad_hidden * gelu_slope(pre_act)).astype(BF16)
    grad_up = jnp.dot(normed_two.T, grad_pre, preferred_element_type=jnp.float32)
    back_mid, gain_two = norm_back(
        middle,
        scale_two,
        gain_pair[1],
        jnp.dot(grad_pre, w_up.T, preferred_element_type=jnp.float32),
    )
    grad_mid = upstream + back_mid
    grad_branch = grad_mid.astype(BF16)
    grad_out = jnp.dot(attended.T, grad_branch, preferred_element_type=jnp.float32)
    grad_att = (
        jnp.dot(grad_branch, w_out.T, preferred_element_type=jnp.float32)
        .astype(BF16)
        .reshape(row_count, HEADS, head_dim)
    )
    grad_value = jnp.einsum("hqk,qhe->khe", probs_low, grad_att, preferred_element_type=jnp.float32)
    grad_probs = jnp.einsum(
        "qhe,khe->hqk", grad_att, value_rows, preferred_element_type=jnp.float32
    )
    grad_scores = (
        attn_probs * (grad_probs - jnp.sum(attn_probs * grad_probs, axis=-1, keepdims=True))
    ).astype(BF16)
    grad_query = jnp.einsum(
        "hqk,khe->qhe", grad_scores, key_rows, preferred_element_type=jnp.float32
    ) * head_dim ** (-0.5)
    grad_key = jnp.einsum(
        "hqk,qhe->khe", grad_scores, queries, preferred_element_type=jnp.float32
    ) * head_dim ** (-0.5)
    grad_qkv = jnp.concatenate(
        [
            grad_query.reshape(row_count, model_width),
            grad_key.reshape(row_count, model_width),
            grad_value.reshape(row_count, model_width),
        ],
        axis=1,
    ).astype(BF16)
    grad_wqkv = jnp.dot(normed.T, grad_qkv, preferred_element_type=jnp.float32)
    back_in, gain_one = norm_back(
        stream,
        scale_one,
        gain_pair[0],
        jnp.dot(grad_qkv, w_qkv.T, preferred_element_type=jnp.float32),
    )
    return (
        grad_mid + back_in,
        (grad_wqkv, grad_out, grad_up, grad_down),
        jnp.stack([gain_one, gain_two]),
    )


def spectral_terms(output, target, length, present_row, frame_count):
    row_count, model_width = output.shape
    bin_count = model_width // 8
    spectra = output.reshape(row_count, 4, 2, bin_count)
    real_part = spectra[:, :, 0]
    imag_part = spectra[:, :, 1]
    magnitude = jnp.sqrt(real_part * real_part + imag_part * imag_part + 0.01)
    differ = magnitude - target.reshape(row_count, 4, bin_count)
    smooth_err = jnp.sqrt(differ * differ + 0.01)
    weight = (jnp.arange(row_count) < length).astype(jnp.float32)[:, None, None] * present_row[
        None, :, None
    ]
    loss_slope = weight * differ / smooth_err / magnitude / frame_count
    grad_spec = jnp.stack([loss_slope * real_part, loss_slope * imag_part], axis=2).reshape(
        row_count, model_width
    )
    return (jnp.sum(smooth_err * weight), grad_spec)


def pipelined_body(
    x_in,
    targets,
    valid_len,
    present_stems,
    w_master,
    norm_gains,
    gain_m,
    gain_v,
    l_stats,
    r_stats,
    l_roots,
    r_roots,
    step_count,
):
    model_width = x_in.shape[1]
    block_size = model_width // 4
    sections = lax.axis_size("section")
    section_idx = lax.axis_index("section")
    half_way = sections // 2
    groups = lax.axis_size("dp")
    group_idx = lax.axis_index("dp")
    micro_count = valid_len.shape[0] // groups
    seg_len = x_in.shape[0] // micro_count
    own_blocks = w_master.shape[1]
    own_gain = norm_gains.shape[2]
    full_w, full_g = (
        lax.all_gather(w_master.astype(BF16), "dp", axis=1, tiled=True),
        lax.all_gather(norm_gains.astype(BF16), "dp", axis=2, tiled=True),
    )
    matrices = split_matrices(full_w[0], model_width)
    gain_pair = full_g[0].astype(jnp.float32)
    lengths = lax.dynamic_slice_in_dim(valid_len, group_idx * micro_count, micro_count)
    stem_flags = lax.dynamic_slice_in_dim(
        present_stems, group_idx * micro_count, micro_count
    ).astype(jnp.float32)
    frame_count = jnp.sum(valid_len).astype(jnp.float32)
    decoder = section_idx >= half_way
    encoder = section_idx < half_way
    is_last = section_idx == sections - 1
    act_shape = (micro_count, seg_len, model_width)

    def forward_step(step_idx, loop_state):
        in_rows, kept_prev, skip_store, loss_grads, loss_sum, sq_sums = loop_state
        micro_idx = step_idx - section_idx
        active = (micro_idx >= 0) & (micro_idx < micro_count)
        slot_idx = jnp.clip(micro_idx, 0, micro_count - 1)
        fresh_rows = lax.dynamic_slice_in_dim(x_in, slot_idx * seg_len, seg_len, 0)
        previous = jnp.where(section_idx == 0, fresh_rows, in_rows)
        stream = previous.astype(jnp.float32) + jnp.where(
            decoder, skip_store[slot_idx].astype(jnp.float32), 0.0
        )
        length = lengths[slot_idx]
        target = lax.dynamic_slice_in_dim(targets, slot_idx * seg_len, seg_len, 0)

        def forward_compute_fn(operand):
            output, branch_attn, branch_ffn, kept_vals = layer_forward(
                stream, matrices, gain_pair, length
            )
            valid = (jnp.arange(seg_len) < length).astype(jnp.float32)[:, None]
            squares = jnp.stack(
                [
                    jnp.sum(valid * stream * stream),
                    jnp.sum(valid * branch_attn * branch_attn),
                    jnp.sum(valid * branch_ffn * branch_ffn),
                ]
            )
            seg_loss, grad_spec = spectral_terms(
                output, target, length, stem_flags[slot_idx], frame_count
            )
            return (output, squares, seg_loss, grad_spec)

        def forward_spare_fn(operand):
            empty = jnp.zeros((seg_len, model_width), jnp.float32)
            return (empty, jnp.zeros((3,), jnp.float32), jnp.zeros((), jnp.float32), empty)

        output, squares, seg_loss, grad_spec = lax.cond(
            active, forward_compute_fn, forward_spare_fn, 0
        )
        kept_prev = kept_prev.at[slot_idx].set(jnp.where(active, previous, kept_prev[slot_idx]))
        loss_grads = loss_grads.at[slot_idx].set(
            jnp.where(active & is_last, grad_spec, loss_grads[slot_idx])
        )
        loss_sum = loss_sum + jnp.where(is_last, seg_loss, 0.0)
        sq_sums = sq_sums + squares
        sent_rows = output.astype(BF16)
        in_rows = from_behind(sent_rows, "section", 1)
        from_encoder = from_behind(sent_rows, "section", half_way)
        recv_idx = step_idx - section_idx + half_way
        usable = decoder & (recv_idx >= 0) & (recv_idx < micro_count)
        recv_slot = jnp.clip(recv_idx, 0, micro_count - 1)
        skip_store = skip_store.at[recv_slot].set(
            jnp.where(usable, from_encoder, skip_store[recv_slot])
        )
        return (in_rows, kept_prev, skip_store, loss_grads, loss_sum, sq_sums)

    start_state = (
        jnp.zeros((seg_len, model_width), BF16),
        jnp.zeros(act_shape, BF16),
        jnp.zeros(act_shape, BF16),
        jnp.zeros(act_shape, jnp.float32),
        jnp.zeros((), jnp.float32),
        jnp.zeros((3,), jnp.float32),
    )
    unused_rows, kept_prev, skip_store, loss_grads, loss_sum, sq_sums = lax.fori_loop(
        0, micro_count + sections - 1, forward_step, start_state
    )

    def backward_step(step_idx, loop_state):
        in_grads, skip_grad_store, grad_mats, grad_gains = loop_state
        micro_idx = step_idx - (sections - 1 - section_idx)
        active = (micro_idx >= 0) & (micro_idx < micro_count)
        slot_idx = jnp.clip(micro_idx, 0, micro_count - 1)
        upstream = jnp.where(
            is_last,
            loss_grads[slot_idx],
            in_grads.astype(jnp.float32)
            + jnp.where(encoder, skip_grad_store[slot_idx].astype(jnp.float32), 0.0),
        )
        stream = kept_prev[slot_idx].astype(jnp.float32) + jnp.where(
            decoder, skip_store[slot_idx].astype(jnp.float32), 0.0
        )
        length = lengths[slot_idx]

        def backward_compute_fn(operand):
            return layer_backward(stream, matrices, gain_pair, length, upstream)

        def backward_spare_fn(operand):
            return (
                jnp.zeros_like(stream),
                tuple((jnp.zeros(mat.shape, jnp.float32) for mat in matrices)),
                jnp.zeros((2, model_width), jnp.float32),
            )

        grad_stream, layer_mats, layer_gains = lax.cond(
            active, backward_compute_fn, backward_spare_fn, 0
        )
        grad_mats = tuple((total + piece for total, piece in zip(grad_mats, layer_mats)))
        grad_gains = grad_gains + layer_gains
        grad_rows = grad_stream.astype(BF16)
        in_grads = from_behind(grad_rows, "section", -1)
        from_decoder = from_behind(grad_rows, "section", -half_way)
        recv_idx = micro_idx + half_way
        usable = encoder & (recv_idx >= 0) & (recv_idx < micro_count)
        recv_slot = jnp.clip(recv_idx, 0, micro_count - 1)
        skip_grad_store = skip_grad_store.at[recv_slot].set(
            jnp.where(usable, from_decoder, skip_grad_store[recv_slot])
        )
        return (in_grads, skip_grad_store, grad_mats, grad_gains)

    back_state = (
        jnp.zeros((seg_len, model_width), BF16),
        jnp.zeros(act_shape, BF16),
        tuple((jnp.zeros(mat.shape, jnp.float32) for mat in matrices)),
        jnp.zeros((2, model_width), jnp.float32),
    )
    unused_grads, unused_store, grad_mats, grad_gains = lax.fori_loop(
        0, micro_count + sections - 1, backward_step, back_state
    )
    grad_all = jnp.concatenate([to_blocks(mat, block_size) for mat in grad_mats], axis=0)
    summed_w, summed_g = lax.psum((grad_all, grad_gains), "dp")
    own_grad = lax.dynamic_slice_in_dim(summed_w, group_idx * own_blocks, own_blocks, 0)
    own_gain_grad = lax.dynamic_slice_in_dim(summed_g, group_idx * own_gain, own_gain, 1)
    own_square = jnp.sum(own_grad * own_grad) + jnp.sum(own_gain_grad * own_gain_grad)
    rows_local = jnp.zeros((sections, 3), jnp.float32).at[section_idx].set(sq_sums)
    total_square, loss_value, rows_total = lax.psum(
        (own_square, loss_sum / frame_count, rows_local), ("section", "dp")
    )
    grad_norm = jnp.sqrt(total_square)
    clip_limit = 0.00015 * math.sqrt(
        sections * (own_blocks * groups * block_size * block_size + 2 * model_width)
    )
    factor = clip_limit / jnp.maximum(grad_norm, clip_limit)
    grad_blocks = own_grad * factor
    square = (own_blocks, block_size, block_size)
    shaped = grad_blocks.reshape(square)
    highest = lax.Precision.HIGHEST
    l_new = 0.95 * l_stats[0].reshape(square) + 0.05 * jnp.einsum(
        "bij,bkj->bik", shaped, shaped, precision=highest
    )
    r_new = 0.95 * r_stats[0].reshape(square) + 0.05 * jnp.einsum(
        "bji,bjk->bik", shaped, shaped, precision=highest
    )
    left_side = jnp.einsum("bij,bjk->bik", l_roots[0].reshape(square), shaped, precision=highest)
    precond = jnp.einsum("bij,bjk->bik", left_side, r_roots[0].reshape(square), precision=highest)
    master = w_master[0]
    w_new = master - 0.5 * (precond.reshape(master.shape) + 0.01 * master)
    gain_grad = own_gain_grad * factor
    m_new = 0.9 * gain_m[0] + 0.1 * gain_grad
    v_new = 0.999 * gain_v[0] + 0.001 * gain_grad * gain_grad
    step_num = step_count[0].astype(jnp.float32)
    m_hat = m_new / (1.0 - jnp.power(0.9, step_num))
    v_hat = v_new / (1.0 - jnp.power(0.999, step_num))
    gains_new = norm_gains[0] - 0.5 * m_hat / (jnp.sqrt(v_hat) + 1e-08)
    rms = jnp.sqrt(rows_total[section_idx] / (frame_count * model_width)).reshape(1, 3)
    return (
        w_new[None],
        grad_blocks[None],
        l_new.reshape(master.shape)[None],
        r_new.reshape(master.shape)[None],
        gains_new[None],
        m_new[None],
        v_new[None],
        loss_value,
        grad_norm,
        rms,
    )


def layer_block(shape):
    return pl.BlockSpec((1,) + shape, lambda i: (i,) + (0,) * len(shape))


def whole_block(shape):
    return pl.BlockSpec(shape, lambda i: (0,) * len(shape))


def forward(layers, info, inverse, x_seg, target_seg, own_w, own_gain):
    seg, width = x_seg.shape
    dim = width // HEADS
    part = width // 4
    half = layers // 2
    shapes = (
        (HEADS, seg, seg), (3 * HEADS, seg, dim), (seg, width), (seg, width), (4, seg, width), (4, seg, width)
    )
    kinds = (BF16, BF16, BF16, F32, BF16, BF16)
    return pl.pallas_call(
        functools.partial(forward_kernel, layers, half),
        grid=(layers,),
        in_specs=[
            pl.BlockSpec(memory_space=pltpu.SMEM),
            pl.BlockSpec(memory_space=pltpu.SMEM),
            whole_block((seg, width)),
            whole_block((seg, width // 2)),
            pl.BlockSpec(memory_space=pltpu.VMEM),
            pl.BlockSpec(memory_space=pltpu.VMEM),
        ],
        out_specs=[layer_block(s) for s in shapes]
        + [whole_block((layers, seg, width)), whole_block((seg, width)), whole_block((layers, 8, width))]
        + [pl.BlockSpec(memory_space=pl.ANY), pl.BlockSpec(memory_space=pltpu.VMEM)],
        out_shape=[jax.ShapeDtypeStruct((layers,) + s, k) for s, k in zip(shapes, kinds)]
        + [
            jax.ShapeDtypeStruct((layers, seg, width), BF16),
            jax.ShapeDtypeStruct((seg, width), F32),
            jax.ShapeDtypeStruct((layers, 8, width), F32),
            jax.ShapeDtypeStruct((layers, 48 * part, width), BF16),
            jax.ShapeDtypeStruct((layers, 8, 8, 128), F32),
        ],
        scratch_shapes=[
            pltpu.VMEM((HEADS, seg, dim), BF16),
            pltpu.VMEM((seg, width), F32),
            pltpu.VMEM((layers, 48 * part, width), BF16),
            pltpu.VMEM((layers, 8, 8, 128), F32),
            pltpu.SemaphoreType.DMA((2, 3)),
            pltpu.SemaphoreType.DMA((2, layers, 4)),
            pltpu.SemaphoreType.DMA((2, layers, 4)),
            pltpu.SemaphoreType.DMA((2, layers, 8)),
            pltpu.SemaphoreType.DMA((2, layers, 8)),
            pltpu.SemaphoreType.DMA((2, 10)),
            pltpu.SemaphoreType.DMA((layers,)),
        ],
        compiler_params=pltpu.CompilerParams(
            vmem_limit_bytes=VMEM_LIMIT, collective_id=0, has_side_effects=True
        ),
    )(info, inverse, x_seg, target_seg, own_w, own_gain)


def backward(layers, loss_grad, full_w, full_g, sent, saved, stats):
    seg, width = loss_grad.shape
    dim = width // HEADS
    part = width // 4
    half = layers // 2

    def from_end(array):
        shape = array.shape[1:]
        return pl.BlockSpec((1,) + shape, lambda i: (layers - 1 - i,) + (0,) * len(shape))

    return pl.pallas_call(
        functools.partial(backward_kernel, layers, half),
        grid=(layers,),
        in_specs=[
            whole_block((seg, width)),
            from_end(full_w),
            from_end(full_g),
            whole_block((layers, seg, width)),
        ]
        + [from_end(a) for a in saved]
        + [pl.BlockSpec(memory_space=pltpu.VMEM)],
        out_specs=[pl.BlockSpec(memory_space=pltpu.VMEM)] * 3,
        out_shape=[
            jax.ShapeDtypeStruct((6 * part, width), F32),
            jax.ShapeDtypeStruct((16, width), F32),
            jax.ShapeDtypeStruct((8, 128), F32),
        ],
        scratch_shapes=[
            pltpu.VMEM((layers, seg, width), BF16),
            pltpu.VMEM((seg, width), BF16),
            pltpu.VMEM((4, seg, width), BF16),
            pltpu.VMEM((seg, width), BF16),
            pltpu.VMEM((seg, width), F32),
            pltpu.VMEM((seg, width), BF16),
            pltpu.VMEM((HEADS, seg, dim), BF16),
            pltpu.VMEM((3 * HEADS, seg, dim), BF16),
            pltpu.VMEM((3, seg, width), BF16),
            pltpu.VMEM((layers, 8, width), F32),
            pltpu.VMEM((2, 4, 2, 576, width), BF16),
            pltpu.VMEM((2, 4, 2, 288, width), BF16),
            pltpu.VMEM((2, 4, 2, 80, width), BF16),
            pltpu.VMEM((2, 4, 208, width), BF16),
            pltpu.VMEM((layers, 3, 208, width), BF16),
            pltpu.VMEM((2, 208, width), BF16),
            pltpu.VMEM((3, 208, width), BF16),
            pltpu.VMEM((6, 16, width), F32),
            pltpu.VMEM((4, 16, width), F32),
            pltpu.VMEM((4, 8, 128), F32),
            pltpu.VMEM((8, 8, 128), F32),
            pltpu.SemaphoreType.DMA((2, 2, 2)),
            pltpu.SemaphoreType.DMA((2, 2, 4)),
            pltpu.SemaphoreType.DMA((2, 2, 4)),
            pltpu.SemaphoreType.DMA((2, layers, 3)),
            pltpu.SemaphoreType.DMA((2, 3)),
            pltpu.SemaphoreType.DMA((2, 3)),
            pltpu.SemaphoreType.DMA((2, 3)),
            pltpu.SemaphoreType.DMA((2, 3)),
            pltpu.SemaphoreType.DMA((2, 7)),
        ],
        compiler_params=pltpu.CompilerParams(
            vmem_limit_bytes=VMEM_LIMIT, collective_id=1, has_side_effects=True
        ),
    )(loss_grad, full_w, full_g, sent, *saved, stats)


def flat_rows(array):
    blocks, area = array.shape
    return (
        array.reshape(blocks // 8, 8, area // 128, 128).transpose(0, 2, 1, 3).reshape(-1, 128)
    )


def from_flat_rows(rows, blocks):
    return (
        rows.reshape(blocks // 8, -1, 8, 128).transpose(0, 2, 1, 3).reshape(blocks, -1)
    )


def load_block(rows_ref, base, block_ref):
    lane = lax.broadcasted_iota(jnp.int32, (24, 128), 1)
    a, b, c = (rows_ref[pl.ds(base + 8 * m, 24, stride=24), :] for m in range(3))
    block_ref[pl.ds(0, 24, stride=4), :] = a
    block_ref[pl.ds(1, 24, stride=4), :] = jnp.where(lane < 32, pltpu.roll(a, 32, 1), pltpu.roll(b, 32, 1))
    block_ref[pl.ds(2, 24, stride=4), :] = jnp.where(lane < 64, pltpu.roll(b, 64, 1), pltpu.roll(c, 64, 1))
    block_ref[pl.ds(3, 24, stride=4), :] = pltpu.roll(c, 96, 1)


def flat_parts(block_ref):
    lane = lax.broadcasted_iota(jnp.int32, (24, 128), 1)
    a, b, c, d = (block_ref[pl.ds(r, 24, stride=4), :] for r in range(4))
    b, c, d = pltpu.roll(b, 96, 1), pltpu.roll(c, 64, 1), pltpu.roll(d, 32, 1)
    return jnp.where(lane < 96, a, b), jnp.where(lane < 64, b, c), jnp.where(lane < 32, c, d)


def split(value):
    high = value.astype(BF16)
    return high, (value - high.astype(F32)).astype(BF16)


def dot_split(dot, left, right):
    return dot(left[0], right[0]) + (dot(left[0], right[1]) + dot(left[1], right[0]))


def update_kernel(
    layers, limit, step_ref, square_ref, tile_ref, quads_ref, w_ref, l_ref, r_ref, lroot_ref, rroot_ref,
    gain_ref, gain_m_ref, gain_v_ref,
    w_out, grad_out, l_out, r_out, gain_out, m_out, v_out, norm_out,
    block_ref,
):
    part, width = quads_ref.shape[1:]
    gains = tile_ref[: 2 * layers]
    norm = jnp.sqrt(jnp.sum(square_ref[...], keepdims=True) + jnp.sum(gains * gains, keepdims=True))
    factor = limit / jnp.maximum(norm, limit)

    def quad_step(q, _):
        for c in range(4):
            base = 4 * q + c
            load_block(lroot_ref, base, block_ref.at[0])
            load_block(rroot_ref, base, block_ref.at[1])
            grad = quads_ref[q, :, part * c : part * (c + 1)] * factor
            pair = split(grad)
            left = dot_split(dot_nn, split(block_ref[0, :, :part]), pair)
            pre = dot_split(dot_nn, split(left), split(block_ref[1, :, :part]))
            for i, value in enumerate((
                grad, pre, dot_split(dot_nt, pair, pair), dot_split(dot_tn, pair, pair)
            )):
                block_ref[2 + i, :, :part] = value
            parts = [flat_parts(block_ref.at[2 + i]) for i in range(4)]
            for m in range(3):
                at = (pl.ds(base + 8 * m, 24, stride=24), slice(None))
                grad_out[at] = parts[0][m]
                master = w_ref[at]
                w_out[at] = master - 0.5 * (parts[1][m] + 0.01 * master)
                l_out[at] = 0.95 * l_ref[at] + 0.05 * parts[2][m]
                r_out[at] = 0.95 * r_ref[at] + 0.05 * parts[3][m]
        return 0

    lax.fori_loop(0, 2, quad_step, 0)

    @pl.when(pl.program_id(0) == 0)
    def _():
        section, group = lax.axis_index("section"), lax.axis_index("dp")
        share = gain_ref.shape[1]
        row = tile_ref[:2]
        for k in range(1, layers):
            row = jnp.where(section == k, tile_ref[2 * k : 2 * k + 2], row)
        own = row[:, :share]
        for g in range(1, width // share):
            own = jnp.where(group == g, row[:, g * share : (g + 1) * share], own)
        grad = own * factor
        m_new = 0.9 * gain_m_ref[...] + 0.1 * grad
        v_new = 0.999 * gain_v_ref[...] + 0.001 * grad * grad
        step = jnp.full((1, 1), step_ref[0], jnp.int32).astype(F32)
        m_hat = m_new / (1.0 - jnp.exp(step * math.log(0.9)))
        v_hat = v_new / (1.0 - jnp.exp(step * math.log(0.999)))
        gain_out[...] = gain_ref[...] - 0.5 * m_hat / (jnp.sqrt(v_hat) + 1e-08)
        m_out[...] = m_new
        v_out[...] = v_new
        norm_out[...] = jnp.broadcast_to(norm, norm_out.shape)


def update(layers, limit, step_count, squares, tile, quads, flats, gains):
    blocks = 4 * quads.shape[0]
    part, width = quads.shape[1:]
    rows = flats[0].shape[0]
    whole = [pl.BlockSpec(memory_space=pltpu.VMEM)]
    flat = [pl.BlockSpec((rows // 3, 128), lambda i: (i, 0))]
    share = gains[0].shape
    return pl.pallas_call(
        functools.partial(update_kernel, layers, limit),
        grid=(3,),
        in_specs=[pl.BlockSpec(memory_space=pltpu.SMEM)] + whole * 2
        + [pl.BlockSpec((2, part, width), lambda i: (i, 0, 0))] + flat * 5 + whole * 3,
        out_specs=flat * 4 + whole * 4,
        out_shape=[jax.ShapeDtypeStruct((rows, 128), F32)] * 4
        + [jax.ShapeDtypeStruct(share, F32)] * 3 + [jax.ShapeDtypeStruct((8, 128), F32)],
        scratch_shapes=[pltpu.VMEM((6, part, 128), F32)],
        compiler_params=pltpu.CompilerParams(vmem_limit_bytes=VMEM_LIMIT),
    )(step_count, squares, tile, quads, *flats, *gains)


def body(
    x_in, targets, valid_len, present_stems, w_master, norm_gains, gain_m, gain_v,
    l_stats, r_stats, l_roots, r_roots, step_count,
):
    width = x_in.shape[1]
    part = width // 4
    layers = lax.axis_size("section")
    section_idx = lax.axis_index("section")
    groups = lax.axis_size("dp")
    group_idx = lax.axis_index("dp")
    micro = valid_len.shape[0] // groups
    seg = x_in.shape[0] // micro
    own_blocks = w_master.shape[1]
    own_gain = norm_gains.shape[2]
    own_w = (
        w_master[0].astype(BF16).reshape(own_blocks // 4, 4, part, part).transpose(0, 2, 1, 3)
        .reshape(own_blocks // 4 * part, width)
    )
    gain_tile = jnp.zeros((8, 128), F32).at[:2, :own_gain].set(norm_gains[0])
    slot = jnp.minimum(section_idx, micro - 1)
    used = (section_idx < micro).astype(jnp.int32)
    at = group_idx * micro + slot
    info = jnp.concatenate([valid_len[at][None] * used, present_stems[at] * used])
    frame_count = jnp.sum(valid_len).astype(F32)
    x_seg = lax.dynamic_slice_in_dim(x_in, slot * seg, seg, 0)
    target_seg = lax.dynamic_slice_in_dim(targets, slot * seg, seg, 0)
    *saved, sent, loss_grad, stats, full_w, tiles = forward(
        layers, info, (1.0 / frame_count)[None], x_seg, target_seg, own_w, gain_tile
    )
    full_g = (
        tiles[:, :, :2, :own_gain].transpose(0, 2, 1, 3).reshape(layers, 2, width).astype(BF16).astype(F32)
    )
    own_quads, tile, squares = backward(layers, loss_grad, full_w, full_g, sent, saved, stats)
    sums = tile[2 * layers : 3 * layers, :4]
    loss_value = sums[0, 3] / frame_count
    clip_limit = 0.00015 * math.sqrt(layers * (own_blocks * groups * part * part + 2 * width))
    flats = [flat_rows(a[0]) for a in (w_master, l_stats, r_stats, l_roots, r_roots)]
    *news, gains_new, m_new, v_new, norms = update(
        layers, clip_limit, step_count, squares, tile, own_quads.reshape(-1, part, width), flats,
        (norm_gains[0], gain_m[0], gain_v[0]),
    )
    w_new, grad_blocks, l_new, r_new = (from_flat_rows(a, own_blocks) for a in news)
    grad_norm = norms[0, 0]
    rms = jnp.sqrt(sums[section_idx, :3] / (frame_count * width)).reshape(1, 3)
    return (
        w_new[None],
        grad_blocks[None],
        l_new[None],
        r_new[None],
        gains_new[None],
        m_new[None],
        v_new[None],
        loss_value,
        grad_norm,
        rms,
    )


def solution(mesh):
    def step(*args):
        layers, groups = mesh.shape["section"], mesh.shape["dp"]
        micro, own_blocks = args[2].shape[0] // groups, args[4].shape[1]
        if micro <= layers == 4 and groups == 8 and own_blocks == 24:
            return body(*args)
        return pipelined_body(*args)

    block = P("section", "dp", None)
    gain = P("section", None, "dp")
    return jax.shard_map(
        step,
        mesh=mesh,
        in_specs=(
            P("dp", None), P("dp", None), P(), P(), block, gain, gain, gain, block, block, block, block, P(),
        ),
        out_specs=(block, block, block, block, gain, gain, gain, P(), P(), P("section", None)),
        check_vma=False,
    )
```

```python
import functools
import math

import jax
import jax.numpy as jnp
from jax import lax
from jax.experimental import pallas as pl
from jax.experimental.pallas import tpu as pltpu
from jax.sharding import PartitionSpec as P

HEADS = 8
F32 = jnp.float32
BF16 = jnp.bfloat16
VMEM_LIMIT = 61 * 1024 * 1024


def dot_nn(a, b):
    return lax.dot_general(a, b, (((1,), (0,)), ((), ())), preferred_element_type=F32)


def dot_nt(a, b):
    return lax.dot_general(a, b, (((1,), (1,)), ((), ())), preferred_element_type=F32)


def dot_tn(a, b):
    return lax.dot_general(a, b, (((0,), (0,)), ((), ())), preferred_element_type=F32)


def gelu_parts(x):
    ax = jnp.abs(x)
    bell = jnp.exp(-0.5 * x * x)
    t = 1.0 / (1.0 + (0.3275911 * 0.7071067811865476) * ax)
    poly = t * (
        0.5 * 0.254829592
        + t
        * (
            0.5 * -0.284496736
            + t * (0.5 * 1.421413741 + t * (0.5 * -1.453152027 + t * (0.5 * 1.061405429)))
        )
    )
    tail = poly * bell
    cdf = jnp.where(x >= 0.0, 1.0 - tail, tail)
    return x * cdf, cdf + x * bell * 0.3989422804014327


def stack_quads(w_ref, first, step, number):
    part = w_ref.shape[2] // 4
    if step == 1:
        return w_ref[0, first * part : (first + number) * part]
    return jnp.concatenate(
        [w_ref[0, (first + step * i) * part : (first + step * i + 1) * part] for i in range(number)], axis=0
    )


def flat_rows(array):
    blocks, area = array.shape
    return (
        array.reshape(blocks // 8, 8, area // 128, 128).transpose(0, 2, 1, 3).reshape(-1, 128)
    )


def from_flat_rows(rows, blocks):
    return (
        rows.reshape(blocks // 8, -1, 8, 128).transpose(0, 2, 1, 3).reshape(blocks, -1)
    )


def load_block(rows_ref, base, block_ref):
    lane = lax.broadcasted_iota(jnp.int32, (24, 128), 1)
    a, b, c = (rows_ref[pl.ds(base + 8 * m, 24, stride=24), :] for m in range(3))
    block_ref[pl.ds(0, 24, stride=4), :] = a
    block_ref[pl.ds(1, 24, stride=4), :] = jnp.where(lane < 32, pltpu.roll(a, 32, 1), pltpu.roll(b, 32, 1))
    block_ref[pl.ds(2, 24, stride=4), :] = jnp.where(lane < 64, pltpu.roll(b, 64, 1), pltpu.roll(c, 64, 1))
    block_ref[pl.ds(3, 24, stride=4), :] = pltpu.roll(c, 96, 1)


def flat_parts(block_ref):
    lane = lax.broadcasted_iota(jnp.int32, (24, 128), 1)
    a, b, c, d = (block_ref[pl.ds(r, 24, stride=4), :] for r in range(4))
    b, c, d = pltpu.roll(b, 96, 1), pltpu.roll(c, 64, 1), pltpu.roll(d, 32, 1)
    return jnp.where(lane < 96, a, b), jnp.where(lane < 64, b, c), jnp.where(lane < 32, c, d)


MESH = pl.DeviceIdType.MESH


def mesh_place():
    section = lax.axis_index("section")
    group = lax.axis_index("dp")
    core = lax.rem(section, 2)
    y = lax.rem(group, 2)
    z = group // 2
    z_peers = (z, z + 1 - 2 * lax.rem(z, 2), lax.rem(z + 2, 4), 3 - z)
    return section, group, core, y, z_peers


def remote(source, target, send_sem, recv_sem, section, group):
    return pltpu.make_async_remote_copy(
        src_ref=source, dst_ref=target, send_sem=send_sem, recv_sem=recv_sem,
        device_id=(section, group), device_id_type=MESH,
    )


def greet(places):
    barrier = pltpu.get_barrier_semaphore()
    for place in places:
        pl.semaphore_signal(barrier, inc=1, device_id=place, device_id_type=MESH)
    pl.semaphore_wait(barrier, len(places))


class Slabs:
    def __init__(self, rows):
        self.section, self.group, self.core, self.y, self.z_peers = mesh_place()
        self.x = self.section // 2
        self.rows, self.half = rows, rows // 2
        self.edge = self.half * 5 // 18
        self.slab = self.half - self.edge

    def slab_of(self, x, core):
        return pl.ds(pl.multiple_of(self.half * core + self.edge * x, 16), self.slab)

    def edge_of(self, x, core):
        return pl.ds(pl.multiple_of(self.half * core + self.slab * x, 16), self.edge)

    def half_of(self, core):
        return pl.ds(pl.multiple_of(self.half * core, 16), self.half)

    def x_peer(self):
        return lax.rem(self.section + 2, 4), self.group

    def y_peer(self):
        return self.section, self.group + 1 - 2 * self.y

    def z_peer(self, k):
        return self.section, self.z_peers[k] * 2 + self.y

    def core_peer(self):
        return self.section + 1 - 2 * self.core, self.group

    def greet_all(self):
        greet(
            [(lax.rem(self.section + k, 4), self.group) for k in range(1, 4)]
            + [(self.section, lax.rem(self.group + k, 8)) for k in range(1, 8)]
        )


class Gather(Slabs):
    def __init__(self, own_ref, gain_ref, w_ref, gains_ref, sems):
        super().__init__(own_ref.shape[0])
        self.own, self.gain, self.w, self.gains = own_ref, gain_ref, w_ref, gains_ref
        self.spread, self.z_sems, self.y_sems, self.x_sems, self.core_sems, self.gain_sems, self.local = sems
        self.others = [lax.rem(self.section + k, 4) for k in range(1, 4)]

    def chunk(self, k):
        y = self.y if k < 4 else 1 - self.y
        return self.z_peers[k % 4] * 2 + y

    def at(self, layer, group, rows):
        return self.w.at[layer, pl.ds(pl.multiple_of(group * self.rows + rows.start, 16), rows.size)]

    def spread_copy(self, k):
        peer = self.others[k]
        rows = self.slab_of(peer // 2, lax.rem(peer, 2))
        return remote(
            self.own.at[rows], self.at(self.section, self.group, rows),
            self.spread.at[0, k], self.spread.at[1, k], peer, self.group,
        )

    def spread_wait(self, layer):
        ref = self.at(layer, self.group, self.slab_of(self.x, self.core))
        for k in range(3):
            @pl.when(lax.rem(layer + k + 1, 4) == self.section)
            def _():
                remote(ref, ref, self.spread.at[0, k], self.spread.at[1, k], self.others[0], self.group).wait_recv()

    def z_copy(self, layer, k, landed=False):
        ref = self.at(layer, self.chunk(k) if landed else self.group, self.slab_of(self.x, self.core))
        return remote(ref, ref, self.z_sems.at[0, layer, k], self.z_sems.at[1, layer, k], *self.z_peer(k))

    def y_copy(self, layer, k, landed=False):
        ref = self.at(layer, self.chunk(k + 4 if landed else k), self.slab_of(self.x, self.core))
        return remote(ref, ref, self.y_sems.at[0, layer, k], self.y_sems.at[1, layer, k], *self.y_peer())

    def x_copy(self, layer, k, landed=False):
        ref = self.at(layer, self.chunk(k), self.edge_of(1 - self.x if landed else self.x, self.core))
        return remote(ref, ref, self.x_sems.at[0, layer, k], self.x_sems.at[1, layer, k], *self.x_peer())

    def core_copy(self, layer, k, landed=False):
        ref = self.at(layer, self.chunk(k), self.half_of(1 - self.core if landed else self.core))
        return remote(ref, ref, self.core_sems.at[0, layer, k], self.core_sems.at[1, layer, k], *self.core_peer())

    def gain_copy(self, k):
        if k < 7:
            peer = lax.rem(self.group + k + 1, 8)
            return remote(
                self.gain, self.gains.at[self.section, self.group],
                self.gain_sems.at[0, k], self.gain_sems.at[1, k], self.section, peer,
            )
        ref = self.gains.at[self.section]
        return remote(
            ref, ref, self.gain_sems.at[0, k], self.gain_sems.at[1, k], self.others[k - 7], self.group
        )

    def gain_landed(self, k):
        if k < 7:
            ref = self.gains.at[self.section, lax.rem(self.group - k - 1 + 8, 8)]
        else:
            ref = self.gains.at[lax.rem(self.section - (k - 6) + 4, 4)]
        return remote(ref, ref, self.gain_sems.at[0, k], self.gain_sems.at[1, k], self.section, self.group)

    def begin(self):
        for k in range(3):
            self.spread_copy(k).start()
        for k in range(7):
            self.gain_copy(k).start()
        rows = self.slab_of(self.x, self.core)
        self.w[self.section, pl.ds(pl.multiple_of(self.group * self.rows + rows.start, 16), rows.size)] = self.own[rows]
        self.gains[self.section, self.group] = self.gain[...]

    def share_gains(self):
        for k in range(7):
            self.gain_landed(k).wait_recv()
        for k in range(7, 10):
            self.gain_copy(k).start()

    def wait_gains(self):
        for k in range(7, 10):
            self.gain_landed(k).wait_recv()

    def kick(self, layer):
        self.spread_wait(layer)
        for k in range(1, 4):
            self.z_copy(layer, k).start()
        self.y_copy(layer, 0).start()
        self.x_copy(layer, 0).start()

    def serve_z(self, layer, k):
        self.z_copy(layer, k, True).wait_recv()
        self.y_copy(layer, k).start()
        self.x_copy(layer, k).start()

    def serve_y(self, layer, k):
        self.y_copy(layer, k, True).wait_recv()
        self.x_copy(layer, k + 4).start()

    def serve_x(self, layer, k):
        self.x_copy(layer, k, True).wait_recv()
        self.core_copy(layer, k).start()

    def finish(self, layer):
        for k in range(8):
            self.core_copy(layer, k, True).wait_recv()

    def end(self, layers):
        for k in range(3):
            self.spread_copy(k).wait_send()
        for k in range(10):
            self.gain_copy(k).wait_send()

        def per_layer(layer, _):
            for k in range(1, 4):
                self.z_copy(layer, k).wait_send()
            for k in range(4):
                self.y_copy(layer, k).wait_send()
            for k in range(8):
                self.x_copy(layer, k).wait_send()
                self.core_copy(layer, k).wait_send()
            return 0

        lax.fori_loop(0, layers, per_layer, 0)


def segment_info(micro, length_ref, stems_ref):
    section, group = lax.axis_index("section"), lax.axis_index("dp")
    at = group * micro + jnp.minimum(section, micro - 1)
    used = (section < micro).astype(jnp.int32)
    frames = length_ref[0]
    for k in range(1, length_ref.shape[0]):
        frames = frames + length_ref[k]
    return length_ref[at] * used, [stems_ref[at, k] * used for k in range(4)], frames


def forward_kernel(
    layers, half, micro, length_ref, stems_ref, x_ref, target_ref, flat_ref, raw_gain_ref,
    probs_ref, heads_ref, att_ref, middle_ref, hidden_ref, slope_ref, sent_ref, loss_grad_ref, stats_ref,
    full_ref, gains_out_ref,
    hold_ref, out_ref, w_all_ref, gains_ref, own_ref, own_gain_ref, block_ref, *sems,
):
    seg, width = x_ref.shape
    dim = width // HEADS
    part = width // 4
    layer = pl.program_id(0)
    rows = 256
    chunks = seg // rows
    length, present_flags, frame_total = segment_info(micro, length_ref, stems_ref)
    gather = Gather(own_ref, own_gain_ref, w_all_ref, gains_ref, sems)
    w_ref = w_all_ref.at[pl.ds(layer, 1)]

    def own_step(q, _):
        for c in range(4):
            block = 4 * q + c
            load_block(flat_ref, (block // 8) * 576 + lax.rem(block, 8), block_ref.at[c])
        quad = jnp.concatenate([block_ref[c, :, :part] for c in range(4)], axis=1)
        own_ref[pl.ds(pl.multiple_of(q * part, part), part)] = quad.astype(BF16)
        return 0

    def keep_copy(index):
        return pltpu.make_async_copy(w_all_ref.at[index], full_ref.at[index], gather.local.at[index])

    @pl.when(layer == 0)
    def _():
        gather.greet_all()
        lax.fori_loop(0, flat_ref.shape[0] // 288, own_step, 0)
        own_gain_ref[...] = jnp.zeros_like(own_gain_ref)
        own_gain_ref[:2, : raw_gain_ref.shape[1]] = raw_gain_ref[...]
        gather.begin()
        sent_ref[0] = x_ref[...]
        stats_ref[...] = jnp.zeros_like(stats_ref)
        gather.kick(0)
        gather.share_gains()
        gather.serve_z(0, 1)
        gather.serve_z(0, 2)
        gather.serve_x(0, 0)
        gather.serve_x(0, 1)
        gather.serve_z(0, 3)
        gather.kick(1)
        gather.wait_gains()
        gather.serve_y(0, 0)
        gather.serve_x(0, 2)
        gather.serve_y(0, 1)
        gather.serve_y(0, 2)
        gather.serve_x(0, 3)
        gather.serve_y(0, 3)
        for k in range(4, 8):
            gather.serve_x(0, k)
        gather.serve_z(1, 1)
        gather.serve_z(1, 2)

    gather.finish(layer)
    keep_copy(layer).start()
    more = layer + 1 < layers

    def serve(here, *steps):
        @pl.when(more & here)
        def _():
            for kind, k in steps:
                getattr(gather, kind)(layer + 1, k)

    def ahead(here, *steps):
        @pl.when((layer + 2 < layers) & here)
        def _():
            for kind, *k in steps:
                getattr(gather, kind)(layer + 2, *k)

    def stream_of(at):
        prev = sent_ref[layer, at].astype(F32)
        skip = sent_ref[jnp.maximum(layer + 1 - half, 0), at].astype(F32)
        return prev + jnp.where(layer >= half, skip, 0.0)

    def gain_row(which):
        return jnp.concatenate(
            [gains_ref[layer, g, which : which + 1, : width // 8] for g in range(8)], axis=1
        ).astype(BF16).astype(F32)

    gain_one = gain_row(0)
    gain_two = gain_row(1)
    gains_out_ref[layer, 0:1] = gain_one
    gains_out_ref[layer, 1:2] = gain_two

    def qkv_step(i, _):
        at = pl.ds(pl.multiple_of(i * rows, rows), rows)
        stream = stream_of(at)
        factor = lax.rsqrt(jnp.mean(stream * stream, axis=-1, keepdims=True) + 1e-06)
        normed = (stream * factor * gain_one).astype(BF16)
        for t in range(3):
            qkv = dot_nn(normed, stack_quads(w_ref, t, 3, 4)).astype(BF16)
            for h in range(HEADS):
                heads_ref[0, t * HEADS + h, at] = qkv[:, h * dim : (h + 1) * dim]
        return 0

    lax.fori_loop(0, chunks, qkv_step, 0)
    frames = lax.broadcasted_iota(jnp.int32, (1, seg), 1)
    masking = jnp.where(frames < length, 0.0, -1e30).astype(F32)

    def head_step(h):
        keys = heads_ref[0, HEADS + h]
        values = heads_ref[0, 2 * HEADS + h]
        scores = dot_nt(heads_ref[0, h], keys) * dim ** (-0.5) + masking
        top = jnp.max(scores, axis=-1, keepdims=True)
        expd = jnp.exp(scores - top)
        probs = (expd * (1.0 / jnp.sum(expd, axis=-1, keepdims=True))).astype(BF16)
        probs_ref[0, h] = probs
        hold_ref[h] = dot_nn(probs, values).astype(BF16)

    for h in range(HEADS // 2):
        head_step(h)
    serve(True, ("serve_z", 3), ("serve_x", 0), ("serve_x", 1))
    ahead(True, ("kick",))
    for h in range(HEADS // 2, HEADS):
        head_step(h)
    serve(True, ("serve_y", 0), ("serve_x", 2), ("serve_y", 1))

    def ffn_step(i, _):
        at = pl.ds(pl.multiple_of(i * rows, rows), rows)
        attended = jnp.concatenate([hold_ref[h, at] for h in range(HEADS)], axis=1)
        att_ref[0, at] = attended
        branch_attn = dot_nn(attended, stack_quads(w_ref, 12, 1, 4))
        stream = stream_of(at)
        middle = stream + branch_attn
        middle_ref[0, at] = middle
        factor = lax.rsqrt(jnp.mean(middle * middle, axis=-1, keepdims=True) + 1e-06)
        normed = (middle * factor * gain_two).astype(BF16)
        branch_ffn = jnp.zeros((rows, width), F32)
        for c in range(4):
            pre_act = dot_nn(normed, stack_quads(w_ref, 16 + c, 4, 4))
            hidden, slope = gelu_parts(pre_act)
            hidden = hidden.astype(BF16)
            hidden_ref[0, c, at] = hidden
            slope_ref[0, c, at] = slope.astype(BF16)
            branch_ffn = branch_ffn + dot_nn(hidden, stack_quads(w_ref, 32 + 4 * c, 1, 4))
        output = middle + branch_ffn
        out_ref[at] = output
        sent_ref[jnp.minimum(layer + 1, layers - 1), at] = jnp.where(
            layer + 1 < layers, output.astype(BF16), sent_ref[layers - 1, at]
        )
        valid = (lax.broadcasted_iota(jnp.int32, (rows, 1), 0) + i * rows < length).astype(F32)
        for k, value in enumerate((stream, branch_attn, branch_ffn)):
            stats_ref[layer, k : k + 1] += jnp.sum(valid * value * value, axis=0, keepdims=True)

        ahead(i == 0, ("serve_z", 1))
        serve(i == 0, ("serve_x", 3), ("serve_x", 4), ("serve_y", 2))
        return 0

    lax.fori_loop(0, chunks, ffn_step, 0)
    ahead(True, ("serve_z", 2))
    serve(True, ("serve_y", 3), ("serve_x", 5), ("serve_x", 6), ("serve_x", 7))

    @pl.when(layer == layers - 1)
    def _():
        bins = width // 8
        lane = lax.broadcasted_iota(jnp.int32, (1, width), 1)
        is_real = lax.rem(lane, 2 * bins) < bins
        stem = lane // (2 * bins)
        present = jnp.zeros((1, width), F32)
        for k in range(4):
            present = jnp.where(stem == k, present_flags[k].astype(F32), present)
        inverse = 1.0 / jnp.full((1, 1), frame_total, jnp.int32).astype(F32)

        def loss_step(i, _):
            at = pl.ds(pl.multiple_of(i * rows, rows), rows)
            output = out_ref[at]
            square = output * output
            other = jnp.where(
                is_real, pltpu.roll(square, width - bins, 1), pltpu.roll(square, bins, 1)
            )
            magnitude = jnp.sqrt(square + other + 0.01)
            goal = target_ref[:, at].T
            goal = jnp.concatenate(
                [goal[:, (k // 2) * bins : (k // 2 + 1) * bins] for k in range(8)], axis=1
            )
            differ = magnitude - goal
            smooth = jnp.sqrt(differ * differ + 0.01)
            valid = (lax.broadcasted_iota(jnp.int32, (rows, 1), 0) + i * rows < length).astype(F32)
            weight = valid * present
            loss_grad_ref[at] = weight * differ * output * inverse / (smooth * magnitude)
            stats_ref[0, 3:4] += jnp.sum(
                jnp.where(is_real, weight * smooth, 0.0), axis=0, keepdims=True
            )
            return 0

        lax.fori_loop(0, chunks, loss_step, 0)
        gather.end(layers)
        for k in range(layers):
            keep_copy(k).wait()


class Scatter(Slabs):
    def __init__(self, refs, sems):
        self.grads, self.core_in, self.x_in, self.y_in, self.z_in, self.last_out, self.last_in = refs
        super().__init__(self.grads.shape[3])
        self.core_sems, self.x_sems, self.y_sems, self.z_sems, self.last_sems = sems
        self.mine = self.slab_of(self.x, self.core)

    def core_copy(self, layer, late):
        slot = lax.rem(layer, 2)
        zs = pl.ds(0, 1) if late else pl.ds(1, 3)
        return remote(
            self.grads.at[slot, zs, :, self.half_of(1 - self.core)], self.core_in.at[slot, zs],
            self.core_sems.at[0, slot, int(late)], self.core_sems.at[1, slot, int(late)], *self.core_peer(),
        )

    def x_copy(self, layer, k):
        slot = lax.rem(layer, 2)
        return remote(
            self.grads.at[slot, self.z_peers[k], :, self.edge_of(1 - self.x, self.core)], self.x_in.at[slot, k],
            self.x_sems.at[0, slot, k], self.x_sems.at[1, slot, k], *self.x_peer(),
        )

    def y_copy(self, layer, k):
        slot = lax.rem(layer, 2)
        return remote(
            self.grads.at[slot, self.z_peers[k], 1 - self.y, self.mine], self.y_in.at[slot, k],
            self.y_sems.at[0, slot, k], self.y_sems.at[1, slot, k], *self.y_peer(),
        )

    def z_copy(self, layer, k):
        slot = lax.rem(layer, 2)
        return remote(
            self.grads.at[slot, self.z_peers[k], self.y, self.mine], self.z_in.at[layer, k - 1],
            self.z_sems.at[0, layer, k - 1], self.z_sems.at[1, layer, k - 1], *self.z_peer(k),
        )

    def last_copy(self, layer):
        slot = lax.rem(layer, 2)
        place = jnp.maximum(lax.rem(self.section - layer + 4, 4) - 1, 0)
        return remote(
            self.last_out.at[slot], self.last_in.at[place],
            self.last_sems.at[0, slot], self.last_sems.at[1, place], layer, self.group,
        )

    def last_landed(self, place):
        return remote(
            self.last_in.at[place], self.last_in.at[place],
            self.last_sems.at[0, 0], self.last_sems.at[1, place], self.section, self.group,
        )

    def for_part(self, late, act):
        for k in (1, 2, 3, 0):
            @pl.when((self.z_peers[k] == 0) == late)
            def _():
                act(k)

    def add_core(self, layer, late):
        slot = lax.rem(layer, 2)
        self.core_copy(layer, late).wait_recv()
        rows = self.half_of(self.core)

        def add(i, _):
            z, y = i // 2, lax.rem(i, 2)
            self.grads[slot, z, y, rows] = self.grads[slot, z, y, rows] + self.core_in[slot, z, y]
            return 0

        lax.fori_loop(0 if late else 2, 2 if late else 8, add, 0)
        self.for_part(late, lambda k: self.x_copy(layer, k).start())

    def add_x(self, layer, k, late):
        @pl.when((self.z_peers[k] == 0) == late)
        def _():
            slot = lax.rem(layer, 2)
            self.x_copy(layer, k).wait_recv()
            rows = self.edge_of(self.x, self.core)
            z = self.z_peers[k]
            for y in range(2):
                self.grads[slot, z, y, rows] = self.grads[slot, z, y, rows] + self.x_in[slot, k, y]
            self.y_copy(layer, k).start()

    def add_y(self, layer, k, late):
        @pl.when((self.z_peers[k] == 0) == late)
        def _():
            slot = lax.rem(layer, 2)
            self.y_copy(layer, k).wait_recv()
            z = self.z_peers[k]
            self.grads[slot, z, self.y, self.mine] = self.grads[slot, z, self.y, self.mine] + self.y_in[slot, k]
            if k:
                self.z_copy(layer, k).start()

    def add_z(self, layer, result_ref):
        slot = lax.rem(layer, 2)
        for k in range(1, 4):
            self.z_copy(layer, k).wait_recv()
        total = self.grads[slot, self.z_peers[0], self.y, self.mine].astype(F32)
        for k in range(3):
            total = total + self.z_in[layer, k].astype(F32)

        @pl.when(layer == self.section)
        def _():
            result_ref[...] = jnp.zeros_like(result_ref)
            result_ref[self.mine] = total

        @pl.when(layer != self.section)
        def _():
            self.last_out[slot] = total.astype(BF16)
            self.last_copy(layer).start()

    def wait_sends(self, layer):
        for late in (False, True):
            self.core_copy(layer, late).wait_send()
        for k in range(4):
            self.x_copy(layer, k).wait_send()
            self.y_copy(layer, k).wait_send()
        for k in range(1, 4):
            self.z_copy(layer, k).wait_send()

        @pl.when(layer != self.section)
        def _():
            self.last_copy(layer).wait_send()

    def collect(self, result_ref):
        for place in (0, 2, 1):
            self.last_landed(place).wait_recv()
            peer = lax.rem(self.section + place + 1, 4)
            rows = self.slab_of(peer // 2, lax.rem(peer, 2))
            result_ref[rows] = result_ref[rows] + self.last_in[place].astype(F32)


class Totals:
    def __init__(self, refs, sems):
        self.stage_in, self.z_in, self.norm_section, self.norm_group = refs
        self.stage_sems, self.z_sems, self.section_sems, self.group_sems = sems
        self.section, self.group, self.core, self.y, self.z_peers = mesh_place()

    def stage_copy(self, k):
        peer = (
            (self.section + 1 - 2 * self.core, self.group),
            (self.section, self.group + 1 - 2 * self.y),
            (lax.rem(self.section + 2, 4), self.group),
        )[k]
        return remote(
            self.stage_in.at[2 * k], self.stage_in.at[2 * k + 1],
            self.stage_sems.at[0, k], self.stage_sems.at[1, k], *peer,
        )

    def z_copy(self, k):
        z = self.z_peers[0]
        return remote(
            self.z_in.at[z], self.z_in.at[z], self.z_sems.at[0, k - 1], self.z_sems.at[1, k - 1],
            self.section, self.z_peers[k] * 2 + self.y,
        )

    def z_landed(self, k):
        z = self.z_peers[k]
        return remote(
            self.z_in.at[z], self.z_in.at[z], self.z_sems.at[0, k - 1], self.z_sems.at[1, k - 1],
            self.section, self.z_peers[k] * 2 + self.y,
        )

    def begin(self, tile):
        self.stage_in[0] = tile
        self.stage_copy(0).start()

    def after_core(self):
        self.stage_copy(0).wait_recv()
        self.stage_in[2] = self.stage_in[0] + self.stage_in[1]
        self.stage_copy(1).start()

    def after_y(self):
        self.stage_copy(1).wait_recv()
        self.z_in[self.z_peers[0]] = self.stage_in[2] + self.stage_in[3]
        for k in range(1, 4):
            self.z_copy(k).start()

    def after_z(self):
        for k in range(1, 4):
            self.z_landed(k).wait_recv()
        self.stage_in[4] = self.z_in[0] + self.z_in[1] + self.z_in[2] + self.z_in[3]
        self.stage_copy(2).start()

    def after_x(self):
        self.stage_copy(2).wait_recv()
        return self.stage_in[4] + self.stage_in[5]

    def norm_copy(self, k):
        if k < 3:
            peer = (lax.rem(self.section + k + 1, 4), self.group)
            ref = self.norm_section.at[self.section]
            return remote(ref, ref, self.section_sems.at[0, k], self.section_sems.at[1, k], *peer)
        k = k - 3
        peer = (self.section, lax.rem(self.group + k + 1, 8))
        ref = self.norm_group.at[self.group]
        return remote(ref, ref, self.group_sems.at[0, k], self.group_sems.at[1, k], *peer)

    def norm_landed(self, k):
        if k < 3:
            ref = self.norm_section.at[lax.rem(self.section - k - 1 + 4, 4)]
            return remote(
                ref, ref, self.section_sems.at[0, k], self.section_sems.at[1, k], self.section, self.group
            )
        k = k - 3
        ref = self.norm_group.at[lax.rem(self.group - k - 1 + 8, 8)]
        return remote(ref, ref, self.group_sems.at[0, k], self.group_sems.at[1, k], self.section, self.group)

    def norm(self, value):
        self.norm_section[self.section] = value
        for k in range(3):
            self.norm_copy(k).start()
        for k in range(3):
            self.norm_landed(k).wait_recv()
        total = self.norm_section[0]
        for k in range(1, 4):
            total = total + self.norm_section[k]
        self.norm_group[self.group] = total
        for k in range(3, 10):
            self.norm_copy(k).start()
        for k in range(3, 10):
            self.norm_landed(k).wait_recv()
        total = self.norm_group[0]
        for k in range(1, 8):
            total = total + self.norm_group[k]
        return total

    def end(self):
        for k in range(3):
            self.stage_copy(k).wait_send()
        for k in range(1, 4):
            self.z_copy(k).wait_send()
        for k in range(10):
            self.norm_copy(k).wait_send()


def norm_reverse(value, gain, grad):
    factor = lax.rsqrt(jnp.mean(value * value, axis=-1, keepdims=True) + 1e-06)
    scaled = grad * gain
    mean = jnp.mean(value * scaled, axis=-1, keepdims=True)
    unit = value * factor
    back = factor * scaled - unit * (factor * factor * mean)
    return back, jnp.sum(grad * unit, axis=0, keepdims=True), (unit * gain).astype(BF16)


def backward_kernel(
    layers, half, loss_grad_ref, w_ref, gain_ref, sent_ref,
    probs_ref, heads_ref, att_ref, middle_ref, hidden_ref, slope_ref, stats_ref,
    result_ref, totals_ref, square_ref,
    sends_ref, dffn_ref, dpre_ref, normed_ref, dmid_ref, datt_ref, dhold_ref, dheads_ref, dqkv_ref,
    gain_grad_ref, *comm_refs,
):
    seg, width = loss_grad_ref.shape
    dim = width // HEADS
    part = width // 4
    layer = layers - 1 - pl.program_id(0)
    rows = 256
    chunks = seg // rows
    gain_one = gain_ref[0, 0:1]
    gain_two = gain_ref[0, 1:2]
    scatter = Scatter(comm_refs[:7], comm_refs[11:16])
    totals = Totals(comm_refs[7:11], comm_refs[16:])
    grads_ref = comm_refs[0]
    slot = lax.rem(layer, 2)

    @pl.when(layer == layers - 1)
    def _():
        scatter.greet_all()
        sends_ref[...] = jnp.zeros_like(sends_ref)
        gain_grad_ref[...] = jnp.zeros_like(gain_grad_ref)

    def put_grad(first, step, value):
        for r in range(4):
            quad = first + step * r
            owner = quad // 6
            at = pl.ds(pl.multiple_of(lax.rem(quad, 6) * part, part), part)
            grads_ref[slot, owner // 2, lax.rem(owner, 2), at] = value[r * part : (r + 1) * part].astype(BF16)

    def before(act):
        @pl.when(layer < layers - 1)
        def _():
            act(layer + 1)

    def ffn_step(i, _):
        at = pl.ds(pl.multiple_of(i * rows, rows), rows)
        later = sends_ref[jnp.minimum(layer + 1, layers - 1), at].astype(F32)
        skip = sends_ref[jnp.minimum(layer + half, layers - 1), at].astype(F32)
        upstream = jnp.where(
            layer == layers - 1, loss_grad_ref[at], later + jnp.where(layer + half < layers, skip, 0.0)
        )
        dffn = upstream.astype(BF16)
        dffn_ref[at] = dffn
        dnormed = jnp.zeros((rows, width), F32)
        for c in range(4):
            dhidden = dot_nt(dffn, stack_quads(w_ref, 32 + 4 * c, 1, 4))
            dpre = (dhidden * slope_ref[0, c, at].astype(F32)).astype(BF16)
            dpre_ref[c, at] = dpre
            dnormed = dnormed + dot_nt(dpre, stack_quads(w_ref, 16 + c, 4, 4))
        back, gain_grad, normed = norm_reverse(middle_ref[0, at], gain_two, dnormed)
        gain_grad_ref[layer, 1:2] += gain_grad
        normed_ref[at] = normed
        dmid = upstream + back
        dmid_ref[at] = dmid
        datt = dmid.astype(BF16)
        datt_ref[at] = datt
        dattended = dot_nt(datt, stack_quads(w_ref, 12, 1, 4)).astype(BF16)
        for h in range(HEADS):
            dhold_ref[h, at] = dattended[:, h * dim : (h + 1) * dim]

        @pl.when(i == 0)
        def _():
            before(lambda at: scatter.add_core(at, True))
            before(lambda at: scatter.add_x(at, 3, False))

        @pl.when(i == 1)
        def _():
            before(lambda at: scatter.add_x(at, 0, False))
            before(lambda at: scatter.add_y(at, 1, False))

        return 0

    lax.fori_loop(0, chunks, ffn_step, 0)

    @pl.when(layer < layers - 2)
    def _():
        scatter.wait_sends(layer + 2)

    def ffn_grad_step(c, _):
        put_grad(32 + 4 * c, 1, dot_tn(hidden_ref[0, c], dffn_ref[...]))
        put_grad(16 + c, 4, dot_tn(normed_ref[...], dpre_ref[c]))
        return 0

    for c in range(4):
        ffn_grad_step(c, 0)
    put_grad(12, 1, dot_tn(att_ref[0], datt_ref[...]))
    scatter.core_copy(layer, False).start()

    @pl.when(layer < layers - 1)
    def _():
        for k in range(4):
            scatter.add_x(layer + 1, k, True)
        for k in (2, 3, 0):
            scatter.add_y(layer + 1, k, False)

    def head_step(h):
        queries = heads_ref[0, h]
        keys = heads_ref[0, HEADS + h]
        probs = probs_ref[0, h]
        dhold = dhold_ref[h]
        dprobs = dot_nt(dhold, heads_ref[0, 2 * HEADS + h])
        wide = probs.astype(F32)
        dot_sum = jnp.sum(wide * dprobs, axis=-1, keepdims=True)
        dscores = (wide * (dprobs - dot_sum)).astype(BF16)
        dheads_ref[h] = (dot_nn(dscores, keys) * dim ** (-0.5)).astype(BF16)
        dheads_ref[HEADS + h] = (dot_tn(dscores, queries) * dim ** (-0.5)).astype(BF16)
        dheads_ref[2 * HEADS + h] = dot_tn(probs, dhold).astype(BF16)

    for h in range(HEADS // 2):
        head_step(h)

    @pl.when(layer < layers - 1)
    def _():
        for k in range(4):
            scatter.add_y(layer + 1, k, True)

    for h in range(HEADS // 2, HEADS):
        head_step(h)
    scatter.add_core(layer, False)

    def qkv_step(i, _):
        at = pl.ds(pl.multiple_of(i * rows, rows), rows)
        dnormed = jnp.zeros((rows, width), F32)
        for t in range(3):
            dqkv = jnp.concatenate([dheads_ref[t * HEADS + h, at] for h in range(HEADS)], axis=1)
            dqkv_ref[t, at] = dqkv
            dnormed = dnormed + dot_nt(dqkv, stack_quads(w_ref, t, 3, 4))
        prev = sent_ref[layer, at].astype(F32)
        skip = sent_ref[jnp.maximum(layer + 1 - half, 0), at].astype(F32)
        stream = prev + jnp.where(layer >= half, skip, 0.0)
        back, gain_grad, normed = norm_reverse(stream, gain_one, dnormed)
        gain_grad_ref[layer, 0:1] += gain_grad
        normed_ref[at] = normed
        sends_ref[layer, at] = (dmid_ref[at] + back).astype(BF16)
        return 0

    lax.fori_loop(0, chunks, qkv_step, 0)

    def qkv_grad_step(t, _):
        put_grad(t, 3, dot_tn(normed_ref[...], dqkv_ref[t]))
        return 0

    for t in range(3):
        qkv_grad_step(t, 0)
    scatter.core_copy(layer, True).start()
    before(lambda at: scatter.add_z(at, result_ref))
    scatter.add_x(layer, 1, False)
    scatter.add_x(layer, 2, False)

    @pl.when(layer == 0)
    def _():
        lane = lax.broadcasted_iota(jnp.int32, (1, width), 1)
        rows_out = [gain_grad_ref[k // 2, k % 2 : k % 2 + 1] for k in range(2 * layers)]
        for k in range(layers):
            row = jnp.zeros((1, width), F32)
            for i in range(4):
                value = jnp.sum(stats_ref[k, i : i + 1], axis=1, keepdims=True)
                row = jnp.where(lane == i, value, row)
            rows_out.append(row)
        rows_out.append(jnp.zeros((16 - 3 * layers, width), F32))
        totals.begin(jnp.concatenate(rows_out, axis=0))
        scatter.add_core(0, True)
        scatter.add_y(0, 1, False)
        scatter.add_x(0, 3, False)
        totals.after_core()
        scatter.add_x(0, 0, False)
        scatter.add_y(0, 2, False)
        for k in range(4):
            scatter.add_x(0, k, True)
        scatter.add_y(0, 3, False)
        scatter.add_y(0, 0, False)
        for k in range(4):
            scatter.add_y(0, k, True)
        totals.after_y()
        scatter.add_z(0, result_ref)
        totals.after_z()
        scatter.collect(result_ref)
        square = jnp.zeros((8, width), F32)
        for q in range(6):
            value = result_ref[q * part : (q + 1) * part]
            square = square + jnp.sum((value * value).reshape(part // 8, 8, width), axis=0)
        folded = square[:, :128] + square[:, 128:256] + square[:, 256:]
        square_ref[...] = totals.norm(folded)
        totals_ref[...] = totals.after_x()
        scatter.wait_sends(1)
        scatter.wait_sends(0)
        totals.end()


FF = 1536


def from_behind(value, axis, by):
    peers = lax.axis_size(axis)
    pairs = [(i, i + by) for i in range(peers) if 0 <= i + by < peers]
    return lax.ppermute(value, axis, pairs)


def unblock(blocks, row_count, col_count, block_size):
    return (
        blocks.reshape(row_count // block_size, col_count // block_size, block_size, block_size)
        .transpose(0, 2, 1, 3)
        .reshape(row_count, col_count)
    )


def to_blocks(matrix, block_size):
    row_count, col_count = matrix.shape
    return (
        matrix.reshape(row_count // block_size, block_size, col_count // block_size, block_size)
        .transpose(0, 2, 1, 3)
        .reshape(-1, block_size * block_size)
    )


def split_matrices(blocks, model_width):
    block_size = model_width // 4
    shapes = (
        (model_width, 3 * model_width),
        (model_width, model_width),
        (model_width, FF),
        (FF, model_width),
    )
    result = []
    offset = 0
    for row_count, col_count in shapes:
        number = row_count * col_count // (block_size * block_size)
        result.append(unblock(blocks[offset : offset + number], row_count, col_count, block_size))
        offset = offset + number
    return result


def rms_norm(stream, gain):
    factor = lax.rsqrt(jnp.mean(stream * stream, axis=-1, keepdims=True) + 1e-06)
    return (stream * factor * gain, factor)


def norm_back(stream, factor, gain, grad):
    scaled = grad * gain
    grad_in = factor * scaled - stream * factor**3 * jnp.mean(
        stream * scaled, axis=-1, keepdims=True
    )
    return (grad_in, jnp.sum(grad * stream * factor, axis=0))


def gelu_slope(pre_act):
    return (
        0.5 * (1.0 + lax.erf(pre_act * 0.7071067811865476))
        + pre_act * jnp.exp(-0.5 * pre_act * pre_act) * 0.3989422804014327
    )


def layer_forward(stream, matrices, gain_pair, length):
    w_qkv, w_out, w_up, w_down = matrices
    row_count, model_width = stream.shape
    head_dim = model_width // HEADS
    frames = jnp.arange(row_count)
    norm_one, scale_one = rms_norm(stream, gain_pair[0])
    normed = norm_one.astype(BF16)
    qkv_all = jnp.dot(normed, w_qkv, preferred_element_type=jnp.float32).astype(BF16)
    queries = qkv_all[:, :model_width].reshape(row_count, HEADS, head_dim)
    key_rows = qkv_all[:, model_width : 2 * model_width].reshape(row_count, HEADS, head_dim)
    value_rows = qkv_all[:, 2 * model_width :].reshape(row_count, HEADS, head_dim)
    masking = jnp.where(frames < length, 0.0, -1e30).astype(jnp.float32)
    scores = jnp.einsum(
        "qhe,khe->hqk", queries, key_rows, preferred_element_type=jnp.float32
    ) * head_dim ** (-0.5)
    attn_probs = jax.nn.softmax(scores + masking[None, None, :], axis=-1)
    probs_low = attn_probs.astype(BF16)
    attended = (
        jnp.einsum("hqk,khe->qhe", probs_low, value_rows, preferred_element_type=jnp.float32)
        .reshape(row_count, model_width)
        .astype(BF16)
    )
    branch_attn = jnp.dot(attended, w_out, preferred_element_type=jnp.float32)
    middle = stream + branch_attn
    norm_two, scale_two = rms_norm(middle, gain_pair[1])
    normed_two = norm_two.astype(BF16)
    pre_act = jnp.dot(normed_two, w_up, preferred_element_type=jnp.float32)
    hidden = jax.nn.gelu(pre_act, approximate=False).astype(BF16)
    branch_ffn = jnp.dot(hidden, w_down, preferred_element_type=jnp.float32)
    kept_vals = (
        scale_one,
        normed,
        queries,
        key_rows,
        value_rows,
        attn_probs,
        probs_low,
        attended,
        middle,
        scale_two,
        normed_two,
        pre_act,
        hidden,
    )
    return (middle + branch_ffn, branch_attn, branch_ffn, kept_vals)


def layer_backward(stream, matrices, gain_pair, length, upstream):
    w_qkv, w_out, w_up, w_down = matrices
    row_count, model_width = stream.shape
    head_dim = model_width // HEADS
    output, branch_attn, branch_ffn, kept_vals = layer_forward(stream, matrices, gain_pair, length)
    (
        scale_one,
        normed,
        queries,
        key_rows,
        value_rows,
        attn_probs,
        probs_low,
        attended,
        middle,
        scale_two,
        normed_two,
        pre_act,
        hidden,
    ) = kept_vals
    grad_ffn = upstream.astype(BF16)
    grad_down = jnp.dot(hidden.T, grad_ffn, preferred_element_type=jnp.float32)
    grad_hidden = jnp.dot(grad_ffn, w_down.T, preferred_element_type=jnp.float32)
    grad_pre = (grad_hidden * gelu_slope(pre_act)).astype(BF16)
    grad_up = jnp.dot(normed_two.T, grad_pre, preferred_element_type=jnp.float32)
    back_mid, gain_two = norm_back(
        middle,
        scale_two,
        gain_pair[1],
        jnp.dot(grad_pre, w_up.T, preferred_element_type=jnp.float32),
    )
    grad_mid = upstream + back_mid
    grad_branch = grad_mid.astype(BF16)
    grad_out = jnp.dot(attended.T, grad_branch, preferred_element_type=jnp.float32)
    grad_att = (
        jnp.dot(grad_branch, w_out.T, preferred_element_type=jnp.float32)
        .astype(BF16)
        .reshape(row_count, HEADS, head_dim)
    )
    grad_value = jnp.einsum("hqk,qhe->khe", probs_low, grad_att, preferred_element_type=jnp.float32)
    grad_probs = jnp.einsum(
        "qhe,khe->hqk", grad_att, value_rows, preferred_element_type=jnp.float32
    )
    grad_scores = (
        attn_probs * (grad_probs - jnp.sum(attn_probs * grad_probs, axis=-1, keepdims=True))
    ).astype(BF16)
    grad_query = jnp.einsum(
        "hqk,khe->qhe", grad_scores, key_rows, preferred_element_type=jnp.float32
    ) * head_dim ** (-0.5)
    grad_key = jnp.einsum(
        "hqk,qhe->khe", grad_scores, queries, preferred_element_type=jnp.float32
    ) * head_dim ** (-0.5)
    grad_qkv = jnp.concatenate(
        [
            grad_query.reshape(row_count, model_width),
            grad_key.reshape(row_count, model_width),
            grad_value.reshape(row_count, model_width),
        ],
        axis=1,
    ).astype(BF16)
    grad_wqkv = jnp.dot(normed.T, grad_qkv, preferred_element_type=jnp.float32)
    back_in, gain_one = norm_back(
        stream,
        scale_one,
        gain_pair[0],
        jnp.dot(grad_qkv, w_qkv.T, preferred_element_type=jnp.float32),
    )
    return (
        grad_mid + back_in,
        (grad_wqkv, grad_out, grad_up, grad_down),
        jnp.stack([gain_one, gain_two]),
    )


def spectral_terms(output, target, length, present_row, frame_count):
    row_count, model_width = output.shape
    bin_count = model_width // 8
    spectra = output.reshape(row_count, 4, 2, bin_count)
    real_part = spectra[:, :, 0]
    imag_part = spectra[:, :, 1]
    magnitude = jnp.sqrt(real_part * real_part + imag_part * imag_part + 0.01)
    differ = magnitude - target.reshape(row_count, 4, bin_count)
    smooth_err = jnp.sqrt(differ * differ + 0.01)
    weight = (jnp.arange(row_count) < length).astype(jnp.float32)[:, None, None] * present_row[
        None, :, None
    ]
    loss_slope = weight * differ / smooth_err / magnitude / frame_count
    grad_spec = jnp.stack([loss_slope * real_part, loss_slope * imag_part], axis=2).reshape(
        row_count, model_width
    )
    return (jnp.sum(smooth_err * weight), grad_spec)


def pipelined_body(
    x_in,
    targets,
    valid_len,
    present_stems,
    w_master,
    norm_gains,
    gain_m,
    gain_v,
    l_stats,
    r_stats,
    l_roots,
    r_roots,
    step_count,
):
    model_width = x_in.shape[1]
    block_size = model_width // 4
    sections = lax.axis_size("section")
    section_idx = lax.axis_index("section")
    half_way = sections // 2
    groups = lax.axis_size("dp")
    group_idx = lax.axis_index("dp")
    micro_count = valid_len.shape[0] // groups
    seg_len = x_in.shape[0] // micro_count
    own_blocks = w_master.shape[1]
    own_gain = norm_gains.shape[2]
    full_w, full_g = (
        lax.all_gather(w_master.astype(BF16), "dp", axis=1, tiled=True),
        lax.all_gather(norm_gains.astype(BF16), "dp", axis=2, tiled=True),
    )
    matrices = split_matrices(full_w[0], model_width)
    gain_pair = full_g[0].astype(jnp.float32)
    lengths = lax.dynamic_slice_in_dim(valid_len, group_idx * micro_count, micro_count)
    stem_flags = lax.dynamic_slice_in_dim(
        present_stems, group_idx * micro_count, micro_count
    ).astype(jnp.float32)
    frame_count = jnp.sum(valid_len).astype(jnp.float32)
    decoder = section_idx >= half_way
    encoder = section_idx < half_way
    is_last = section_idx == sections - 1
    act_shape = (micro_count, seg_len, model_width)

    def forward_step(step_idx, loop_state):
        in_rows, kept_prev, skip_store, loss_grads, loss_sum, sq_sums = loop_state
        micro_idx = step_idx - section_idx
        active = (micro_idx >= 0) & (micro_idx < micro_count)
        slot_idx = jnp.clip(micro_idx, 0, micro_count - 1)
        fresh_rows = lax.dynamic_slice_in_dim(x_in, slot_idx * seg_len, seg_len, 0)
        previous = jnp.where(section_idx == 0, fresh_rows, in_rows)
        stream = previous.astype(jnp.float32) + jnp.where(
            decoder, skip_store[slot_idx].astype(jnp.float32), 0.0
        )
        length = lengths[slot_idx]
        target = lax.dynamic_slice_in_dim(targets, slot_idx * seg_len, seg_len, 0)

        def forward_compute_fn(operand):
            output, branch_attn, branch_ffn, kept_vals = layer_forward(
                stream, matrices, gain_pair, length
            )
            valid = (jnp.arange(seg_len) < length).astype(jnp.float32)[:, None]
            squares = jnp.stack(
                [
                    jnp.sum(valid * stream * stream),
                    jnp.sum(valid * branch_attn * branch_attn),
                    jnp.sum(valid * branch_ffn * branch_ffn),
                ]
            )
            seg_loss, grad_spec = spectral_terms(
                output, target, length, stem_flags[slot_idx], frame_count
            )
            return (output, squares, seg_loss, grad_spec)

        def forward_spare_fn(operand):
            empty = jnp.zeros((seg_len, model_width), jnp.float32)
            return (empty, jnp.zeros((3,), jnp.float32), jnp.zeros((), jnp.float32), empty)

        output, squares, seg_loss, grad_spec = lax.cond(
            active, forward_compute_fn, forward_spare_fn, 0
        )
        kept_prev = kept_prev.at[slot_idx].set(jnp.where(active, previous, kept_prev[slot_idx]))
        loss_grads = loss_grads.at[slot_idx].set(
            jnp.where(active & is_last, grad_spec, loss_grads[slot_idx])
        )
        loss_sum = loss_sum + jnp.where(is_last, seg_loss, 0.0)
        sq_sums = sq_sums + squares
        sent_rows = output.astype(BF16)
        in_rows = from_behind(sent_rows, "section", 1)
        from_encoder = from_behind(sent_rows, "section", half_way)
        recv_idx = step_idx - section_idx + half_way
        usable = decoder & (recv_idx >= 0) & (recv_idx < micro_count)
        recv_slot = jnp.clip(recv_idx, 0, micro_count - 1)
        skip_store = skip_store.at[recv_slot].set(
            jnp.where(usable, from_encoder, skip_store[recv_slot])
        )
        return (in_rows, kept_prev, skip_store, loss_grads, loss_sum, sq_sums)

    start_state = (
        jnp.zeros((seg_len, model_width), BF16),
        jnp.zeros(act_shape, BF16),
        jnp.zeros(act_shape, BF16),
        jnp.zeros(act_shape, jnp.float32),
        jnp.zeros((), jnp.float32),
        jnp.zeros((3,), jnp.float32),
    )
    unused_rows, kept_prev, skip_store, loss_grads, loss_sum, sq_sums = lax.fori_loop(
        0, micro_count + sections - 1, forward_step, start_state
    )

    def backward_step(step_idx, loop_state):
        in_grads, skip_grad_store, grad_mats, grad_gains = loop_state
        micro_idx = step_idx - (sections - 1 - section_idx)
        active = (micro_idx >= 0) & (micro_idx < micro_count)
        slot_idx = jnp.clip(micro_idx, 0, micro_count - 1)
        upstream = jnp.where(
            is_last,
            loss_grads[slot_idx],
            in_grads.astype(jnp.float32)
            + jnp.where(encoder, skip_grad_store[slot_idx].astype(jnp.float32), 0.0),
        )
        stream = kept_prev[slot_idx].astype(jnp.float32) + jnp.where(
            decoder, skip_store[slot_idx].astype(jnp.float32), 0.0
        )
        length = lengths[slot_idx]

        def backward_compute_fn(operand):
            return layer_backward(stream, matrices, gain_pair, length, upstream)

        def backward_spare_fn(operand):
            return (
                jnp.zeros_like(stream),
                tuple((jnp.zeros(mat.shape, jnp.float32) for mat in matrices)),
                jnp.zeros((2, model_width), jnp.float32),
            )

        grad_stream, layer_mats, layer_gains = lax.cond(
            active, backward_compute_fn, backward_spare_fn, 0
        )
        grad_mats = tuple((total + piece for total, piece in zip(grad_mats, layer_mats)))
        grad_gains = grad_gains + layer_gains
        grad_rows = grad_stream.astype(BF16)
        in_grads = from_behind(grad_rows, "section", -1)
        from_decoder = from_behind(grad_rows, "section", -half_way)
        recv_idx = micro_idx + half_way
        usable = encoder & (recv_idx >= 0) & (recv_idx < micro_count)
        recv_slot = jnp.clip(recv_idx, 0, micro_count - 1)
        skip_grad_store = skip_grad_store.at[recv_slot].set(
            jnp.where(usable, from_decoder, skip_grad_store[recv_slot])
        )
        return (in_grads, skip_grad_store, grad_mats, grad_gains)

    back_state = (
        jnp.zeros((seg_len, model_width), BF16),
        jnp.zeros(act_shape, BF16),
        tuple((jnp.zeros(mat.shape, jnp.float32) for mat in matrices)),
        jnp.zeros((2, model_width), jnp.float32),
    )
    unused_grads, unused_store, grad_mats, grad_gains = lax.fori_loop(
        0, micro_count + sections - 1, backward_step, back_state
    )
    grad_all = jnp.concatenate([to_blocks(mat, block_size) for mat in grad_mats], axis=0)
    summed_w, summed_g = lax.psum((grad_all, grad_gains), "dp")
    own_grad = lax.dynamic_slice_in_dim(summed_w, group_idx * own_blocks, own_blocks, 0)
    own_gain_grad = lax.dynamic_slice_in_dim(summed_g, group_idx * own_gain, own_gain, 1)
    own_square = jnp.sum(own_grad * own_grad) + jnp.sum(own_gain_grad * own_gain_grad)
    rows_local = jnp.zeros((sections, 3), jnp.float32).at[section_idx].set(sq_sums)
    total_square, loss_value, rows_total = lax.psum(
        (own_square, loss_sum / frame_count, rows_local), ("section", "dp")
    )
    grad_norm = jnp.sqrt(total_square)
    clip_limit = 0.00015 * math.sqrt(
        sections * (own_blocks * groups * block_size * block_size + 2 * model_width)
    )
    factor = clip_limit / jnp.maximum(grad_norm, clip_limit)
    grad_blocks = own_grad * factor
    square = (own_blocks, block_size, block_size)
    shaped = grad_blocks.reshape(square)
    highest = lax.Precision.HIGHEST
    l_new = 0.95 * l_stats[0].reshape(square) + 0.05 * jnp.einsum(
        "bij,bkj->bik", shaped, shaped, precision=highest
    )
    r_new = 0.95 * r_stats[0].reshape(square) + 0.05 * jnp.einsum(
        "bji,bjk->bik", shaped, shaped, precision=highest
    )
    left_side = jnp.einsum("bij,bjk->bik", l_roots[0].reshape(square), shaped, precision=highest)
    precond = jnp.einsum("bij,bjk->bik", left_side, r_roots[0].reshape(square), precision=highest)
    master = w_master[0]
    w_new = master - 0.5 * (precond.reshape(master.shape) + 0.01 * master)
    gain_grad = own_gain_grad * factor
    m_new = 0.9 * gain_m[0] + 0.1 * gain_grad
    v_new = 0.999 * gain_v[0] + 0.001 * gain_grad * gain_grad
    step_num = step_count[0].astype(jnp.float32)
    m_hat = m_new / (1.0 - jnp.power(0.9, step_num))
    v_hat = v_new / (1.0 - jnp.power(0.999, step_num))
    gains_new = norm_gains[0] - 0.5 * m_hat / (jnp.sqrt(v_hat) + 1e-08)
    rms = jnp.sqrt(rows_total[section_idx] / (frame_count * model_width)).reshape(1, 3)
    return (
        w_new[None],
        grad_blocks[None],
        l_new.reshape(master.shape)[None],
        r_new.reshape(master.shape)[None],
        gains_new[None],
        m_new[None],
        v_new[None],
        loss_value,
        grad_norm,
        rms,
    )


def layer_block(shape):
    return pl.BlockSpec((1,) + shape, lambda i: (i,) + (0,) * len(shape))


def whole_block(shape):
    return pl.BlockSpec(shape, lambda i: (0,) * len(shape))


def forward(layers, micro, valid_len, present_stems, x_in, targets, flat_w, gain):
    width = x_in.shape[1]
    seg = x_in.shape[0] // micro
    dim = width // HEADS
    part = width // 4
    half = layers // 2
    shapes = (
        (HEADS, seg, seg), (3 * HEADS, seg, dim), (seg, width), (seg, width), (4, seg, width), (4, seg, width)
    )
    kinds = (BF16, BF16, BF16, F32, BF16, BF16)

    def slot():
        return jnp.minimum(lax.axis_index("section"), micro - 1)

    return pl.pallas_call(
        functools.partial(forward_kernel, layers, half, micro),
        grid=(layers,),
        in_specs=[
            pl.BlockSpec(memory_space=pltpu.SMEM),
            pl.BlockSpec(memory_space=pltpu.SMEM),
            pl.BlockSpec((seg, width), lambda i: (slot(), 0)),
            pl.BlockSpec((width // 2, seg), lambda i: (0, slot())),
            pl.BlockSpec(memory_space=pltpu.VMEM),
            pl.BlockSpec(memory_space=pltpu.VMEM),
        ],
        out_specs=[layer_block(s) for s in shapes]
        + [whole_block((layers, seg, width)), whole_block((seg, width)), whole_block((layers, 8, width))]
        + [pl.BlockSpec(memory_space=pl.ANY), whole_block((layers, 8, width))],
        out_shape=[jax.ShapeDtypeStruct((layers,) + s, k) for s, k in zip(shapes, kinds)]
        + [
            jax.ShapeDtypeStruct((layers, seg, width), BF16),
            jax.ShapeDtypeStruct((seg, width), F32),
            jax.ShapeDtypeStruct((layers, 8, width), F32),
            jax.ShapeDtypeStruct((layers, 48 * part, width), BF16),
            jax.ShapeDtypeStruct((layers, 8, width), F32),
        ],
        scratch_shapes=[
            pltpu.VMEM((HEADS, seg, dim), BF16),
            pltpu.VMEM((seg, width), F32),
            pltpu.VMEM((layers, 48 * part, width), BF16),
            pltpu.VMEM((layers, 8, 8, 128), F32),
            pltpu.VMEM((6 * part, width), BF16),
            pltpu.VMEM((8, 128), F32),
            pltpu.VMEM((4, part, 128), F32),
            pltpu.SemaphoreType.DMA((2, 3)),
            pltpu.SemaphoreType.DMA((2, layers, 4)),
            pltpu.SemaphoreType.DMA((2, layers, 4)),
            pltpu.SemaphoreType.DMA((2, layers, 8)),
            pltpu.SemaphoreType.DMA((2, layers, 8)),
            pltpu.SemaphoreType.DMA((2, 10)),
            pltpu.SemaphoreType.DMA((layers,)),
        ],
        compiler_params=pltpu.CompilerParams(
            vmem_limit_bytes=VMEM_LIMIT, collective_id=0, has_side_effects=True
        ),
    )(valid_len, present_stems, x_in, targets.T, flat_w, gain)


def backward(layers, loss_grad, full_w, full_g, sent, saved, stats):
    seg, width = loss_grad.shape
    dim = width // HEADS
    part = width // 4
    half = layers // 2

    def from_end(array):
        shape = array.shape[1:]
        return pl.BlockSpec((1,) + shape, lambda i: (layers - 1 - i,) + (0,) * len(shape))

    return pl.pallas_call(
        functools.partial(backward_kernel, layers, half),
        grid=(layers,),
        in_specs=[
            whole_block((seg, width)),
            from_end(full_w),
            from_end(full_g),
            whole_block((layers, seg, width)),
        ]
        + [from_end(a) for a in saved]
        + [pl.BlockSpec(memory_space=pltpu.VMEM)],
        out_specs=[pl.BlockSpec(memory_space=pltpu.VMEM)] * 3,
        out_shape=[
            jax.ShapeDtypeStruct((6 * part, width), F32),
            jax.ShapeDtypeStruct((16, width), F32),
            jax.ShapeDtypeStruct((8, 128), F32),
        ],
        scratch_shapes=[
            pltpu.VMEM((layers, seg, width), BF16),
            pltpu.VMEM((seg, width), BF16),
            pltpu.VMEM((4, seg, width), BF16),
            pltpu.VMEM((seg, width), BF16),
            pltpu.VMEM((seg, width), F32),
            pltpu.VMEM((seg, width), BF16),
            pltpu.VMEM((HEADS, seg, dim), BF16),
            pltpu.VMEM((3 * HEADS, seg, dim), BF16),
            pltpu.VMEM((3, seg, width), BF16),
            pltpu.VMEM((layers, 8, width), F32),
            pltpu.VMEM((2, 4, 2, 576, width), BF16),
            pltpu.VMEM((2, 4, 2, 288, width), BF16),
            pltpu.VMEM((2, 4, 2, 80, width), BF16),
            pltpu.VMEM((2, 4, 208, width), BF16),
            pltpu.VMEM((layers, 3, 208, width), BF16),
            pltpu.VMEM((2, 208, width), BF16),
            pltpu.VMEM((3, 208, width), BF16),
            pltpu.VMEM((6, 16, width), F32),
            pltpu.VMEM((4, 16, width), F32),
            pltpu.VMEM((4, 8, 128), F32),
            pltpu.VMEM((8, 8, 128), F32),
            pltpu.SemaphoreType.DMA((2, 2, 2)),
            pltpu.SemaphoreType.DMA((2, 2, 4)),
            pltpu.SemaphoreType.DMA((2, 2, 4)),
            pltpu.SemaphoreType.DMA((2, layers, 3)),
            pltpu.SemaphoreType.DMA((2, 3)),
            pltpu.SemaphoreType.DMA((2, 3)),
            pltpu.SemaphoreType.DMA((2, 3)),
            pltpu.SemaphoreType.DMA((2, 3)),
            pltpu.SemaphoreType.DMA((2, 7)),
        ],
        compiler_params=pltpu.CompilerParams(
            vmem_limit_bytes=VMEM_LIMIT, collective_id=1, has_side_effects=True
        ),
    )(loss_grad, full_w, full_g, sent, *saved, stats)


def split(value):
    high = value.astype(BF16)
    return high, (value - high.astype(F32)).astype(BF16)


def dot_split(dot, left, right):
    return dot(left[0], right[0]) + (dot(left[0], right[1]) + dot(left[1], right[0]))


def update_kernel(
    layers, limit, length_ref, step_ref, square_ref, tile_ref, quads_ref, w_ref, l_ref, r_ref, lroot_ref, rroot_ref,
    gain_ref, gain_m_ref, gain_v_ref,
    w_out, grad_out, l_out, r_out, gain_out, m_out, v_out, loss_out, norm_out, rms_out,
    block_ref,
):
    part, width = quads_ref.shape[1:]
    gains = tile_ref[: 2 * layers]
    norm = jnp.sqrt(jnp.sum(square_ref[...], keepdims=True) + jnp.sum(gains * gains, keepdims=True))
    factor = limit / jnp.maximum(norm, limit)

    def quad_step(q, _):
        for c in range(4):
            base = 4 * q + c
            load_block(lroot_ref, base, block_ref.at[0])
            load_block(rroot_ref, base, block_ref.at[1])
            grad = quads_ref[q, :, part * c : part * (c + 1)] * factor
            pair = split(grad)
            left = dot_split(dot_nn, split(block_ref[0, :, :part]), pair)
            pre = dot_split(dot_nn, split(left), split(block_ref[1, :, :part]))
            for i, value in enumerate((
                grad, pre, dot_split(dot_nt, pair, pair), dot_split(dot_tn, pair, pair)
            )):
                block_ref[2 + i, :, :part] = value
            parts = [flat_parts(block_ref.at[2 + i]) for i in range(4)]
            for m in range(3):
                at = (pl.ds(base + 8 * m, 24, stride=24), slice(None))
                grad_out[at] = parts[0][m]
                master = w_ref[at]
                w_out[at] = master - 0.5 * (parts[1][m] + 0.01 * master)
                l_out[at] = 0.95 * l_ref[at] + 0.05 * parts[2][m]
                r_out[at] = 0.95 * r_ref[at] + 0.05 * parts[3][m]
        return 0

    lax.fori_loop(0, 2, quad_step, 0)

    @pl.when(pl.program_id(0) == 0)
    def _():
        section, group = lax.axis_index("section"), lax.axis_index("dp")
        share = gain_ref.shape[1]
        row = tile_ref[:2]
        for k in range(1, layers):
            row = jnp.where(section == k, tile_ref[2 * k : 2 * k + 2], row)
        own = row[:, :share]
        for g in range(1, width // share):
            own = jnp.where(group == g, row[:, g * share : (g + 1) * share], own)
        grad = own * factor
        m_new = 0.9 * gain_m_ref[...] + 0.1 * grad
        v_new = 0.999 * gain_v_ref[...] + 0.001 * grad * grad
        step = jnp.full((1, 1), step_ref[0], jnp.int32).astype(F32)
        m_hat = m_new / (1.0 - jnp.exp(step * math.log(0.9)))
        v_hat = v_new / (1.0 - jnp.exp(step * math.log(0.999)))
        gain_out[...] = gain_ref[...] - 0.5 * m_hat / (jnp.sqrt(v_hat) + 1e-08)
        m_out[...] = m_new
        v_out[...] = v_new
        norm_out[...] = norm
        frames = length_ref[0]
        for k in range(1, length_ref.shape[0]):
            frames = frames + length_ref[k]
        frames = jnp.full((1, 1), frames, jnp.int32).astype(F32)
        loss_out[...] = tile_ref[2 * layers : 2 * layers + 1, 3:4] / frames
        squares = tile_ref[2 * layers : 2 * layers + 1, :3]
        for k in range(1, layers):
            squares = jnp.where(section == k, tile_ref[2 * layers + k : 2 * layers + k + 1, :3], squares)
        rms_out[...] = jnp.sqrt(squares / (frames * width))


def update(layers, limit, valid_len, step_count, squares, tile, quads, flats, gains):
    blocks = 4 * quads.shape[0]
    part, width = quads.shape[1:]
    rows = flats[0].shape[0]
    whole = [pl.BlockSpec(memory_space=pltpu.VMEM)]
    flat = [pl.BlockSpec((rows // 3, 128), lambda i: (i, 0))]
    share = gains[0].shape
    return pl.pallas_call(
        functools.partial(update_kernel, layers, limit),
        grid=(3,),
        in_specs=[pl.BlockSpec(memory_space=pltpu.SMEM)] * 2 + whole * 2
        + [pl.BlockSpec((2, part, width), lambda i: (i, 0, 0))] + flat * 5 + whole * 3,
        out_specs=flat * 4 + whole * 6,
        out_shape=[jax.ShapeDtypeStruct((rows, 128), F32)] * 4
        + [jax.ShapeDtypeStruct(share, F32)] * 3
        + [jax.ShapeDtypeStruct((1, 1), F32)] * 2 + [jax.ShapeDtypeStruct((1, 3), F32)],
        scratch_shapes=[pltpu.VMEM((6, part, 128), F32)],
        compiler_params=pltpu.CompilerParams(vmem_limit_bytes=VMEM_LIMIT),
    )(valid_len, step_count, squares, tile, quads, *flats, *gains)


def body(
    x_in, targets, valid_len, present_stems, w_master, norm_gains, gain_m, gain_v,
    l_stats, r_stats, l_roots, r_roots, step_count,
):
    width = x_in.shape[1]
    part = width // 4
    layers = lax.axis_size("section")
    groups = lax.axis_size("dp")
    micro = valid_len.shape[0] // groups
    own_blocks = w_master.shape[1]
    flats = [flat_rows(a[0]) for a in (w_master, l_stats, r_stats, l_roots, r_roots)]
    *saved, sent, loss_grad, stats, full_w, full_g = forward(
        layers, micro, valid_len, present_stems, x_in, targets, flats[0], norm_gains[0]
    )
    own_quads, tile, squares = backward(layers, loss_grad, full_w, full_g, sent, saved, stats)
    clip_limit = 0.00015 * math.sqrt(layers * (own_blocks * groups * part * part + 2 * width))
    *news, gains_new, m_new, v_new, loss_value, grad_norm, rms = update(
        layers, clip_limit, valid_len, step_count, squares, tile, own_quads.reshape(-1, part, width), flats,
        (norm_gains[0], gain_m[0], gain_v[0]),
    )
    w_new, grad_blocks, l_new, r_new = (from_flat_rows(a, own_blocks)[None] for a in news)
    return (
        w_new,
        grad_blocks,
        l_new,
        r_new,
        gains_new[None],
        m_new[None],
        v_new[None],
        loss_value.reshape(()),
        grad_norm.reshape(()),
        rms,
    )


def solution(mesh):
    def step(*args):
        layers, groups = mesh.shape["section"], mesh.shape["dp"]
        micro, own_blocks = args[2].shape[0] // groups, args[4].shape[1]
        if micro <= layers == 4 and groups == 8 and own_blocks == 24:
            return body(*args)
        return pipelined_body(*args)

    block = P("section", "dp", None)
    gain = P("section", None, "dp")
    return jax.shard_map(
        step,
        mesh=mesh,
        in_specs=(
            P("dp", None), P("dp", None), P(), P(), block, gain, gain, gain, block, block, block, block, P(),
        ),
        out_specs=(block, block, block, block, gain, gain, gain, P(), P(), P("section", None)),
        check_vma=False,
    )
```

```python
import functools
import math

import jax
import jax.numpy as jnp
from jax import lax
from jax.experimental import pallas as pl
from jax.experimental.pallas import tpu as pltpu
from jax.sharding import PartitionSpec as P

HEADS = 8
F32 = jnp.float32
BF16 = jnp.bfloat16
VMEM_LIMIT = 61 * 1024 * 1024


def dot_nn(a, b):
    return lax.dot_general(a, b, (((1,), (0,)), ((), ())), preferred_element_type=F32)


def dot_nt(a, b):
    return lax.dot_general(a, b, (((1,), (1,)), ((), ())), preferred_element_type=F32)


def dot_tn(a, b):
    return lax.dot_general(a, b, (((0,), (0,)), ((), ())), preferred_element_type=F32)


def gelu_parts(x):
    ax = jnp.abs(x)
    bell = jnp.exp(-0.5 * x * x)
    t = 1.0 / (1.0 + (0.3275911 * 0.7071067811865476) * ax)
    poly = t * (
        0.5 * 0.254829592
        + t
        * (
            0.5 * -0.284496736
            + t * (0.5 * 1.421413741 + t * (0.5 * -1.453152027 + t * (0.5 * 1.061405429)))
        )
    )
    tail = poly * bell
    cdf = jnp.where(x >= 0.0, 1.0 - tail, tail)
    return x * cdf, cdf + x * bell * 0.3989422804014327


def stack_quads(w_ref, first, step, number):
    part = w_ref.shape[2] // 4
    if step == 1:
        return w_ref[0, first * part : (first + number) * part]
    return jnp.concatenate(
        [w_ref[0, (first + step * i) * part : (first + step * i + 1) * part] for i in range(number)], axis=0
    )


def flat_rows(array):
    blocks, area = array.shape
    return (
        array.reshape(blocks // 8, 8, area // 128, 128).transpose(0, 2, 1, 3).reshape(-1, 128)
    )


def from_flat_rows(rows, blocks):
    return (
        rows.reshape(blocks // 8, -1, 8, 128).transpose(0, 2, 1, 3).reshape(blocks, -1)
    )


def load_block(rows_ref, base, block_ref):
    lane = lax.broadcasted_iota(jnp.int32, (24, 128), 1)
    a, b, c = (rows_ref[pl.ds(base + 8 * m, 24, stride=24), :] for m in range(3))
    block_ref[pl.ds(0, 24, stride=4), :] = a
    block_ref[pl.ds(1, 24, stride=4), :] = jnp.where(lane < 32, pltpu.roll(a, 32, 1), pltpu.roll(b, 32, 1))
    block_ref[pl.ds(2, 24, stride=4), :] = jnp.where(lane < 64, pltpu.roll(b, 64, 1), pltpu.roll(c, 64, 1))
    block_ref[pl.ds(3, 24, stride=4), :] = pltpu.roll(c, 96, 1)


def flat_parts(block_ref):
    lane = lax.broadcasted_iota(jnp.int32, (24, 128), 1)
    a, b, c, d = (block_ref[pl.ds(r, 24, stride=4), :] for r in range(4))
    b, c, d = pltpu.roll(b, 96, 1), pltpu.roll(c, 64, 1), pltpu.roll(d, 32, 1)
    return jnp.where(lane < 96, a, b), jnp.where(lane < 64, b, c), jnp.where(lane < 32, c, d)


MESH = pl.DeviceIdType.MESH


def mesh_place():
    section = lax.axis_index("section")
    group = lax.axis_index("dp")
    core = lax.rem(section, 2)
    y = lax.rem(group, 2)
    z = group // 2
    z_peers = (z, z + 1 - 2 * lax.rem(z, 2), lax.rem(z + 2, 4), 3 - z)
    return section, group, core, y, z_peers


def remote(source, target, send_sem, recv_sem, section, group):
    return pltpu.make_async_remote_copy(
        src_ref=source, dst_ref=target, send_sem=send_sem, recv_sem=recv_sem,
        device_id=(section, group), device_id_type=MESH,
    )


def greet(places):
    barrier = pltpu.get_barrier_semaphore()
    for place in places:
        pl.semaphore_signal(barrier, inc=1, device_id=place, device_id_type=MESH)
    pl.semaphore_wait(barrier, len(places))


class Slabs:
    def __init__(self, rows):
        self.section, self.group, self.core, self.y, self.z_peers = mesh_place()
        self.x = self.section // 2
        self.rows, self.half = rows, rows // 2
        self.edge = self.half * 5 // 18
        self.slab = self.half - self.edge

    def slab_of(self, x, core):
        return pl.ds(pl.multiple_of(self.half * core + self.edge * x, 16), self.slab)

    def edge_of(self, x, core):
        return pl.ds(pl.multiple_of(self.half * core + self.slab * x, 16), self.edge)

    def half_of(self, core):
        return pl.ds(pl.multiple_of(self.half * core, 16), self.half)

    def x_peer(self):
        return lax.rem(self.section + 2, 4), self.group

    def y_peer(self):
        return self.section, self.group + 1 - 2 * self.y

    def z_peer(self, k):
        return self.section, self.z_peers[k] * 2 + self.y

    def core_peer(self):
        return self.section + 1 - 2 * self.core, self.group

    def greet_all(self):
        greet(
            [(lax.rem(self.section + k, 4), self.group) for k in range(1, 4)]
            + [(self.section, lax.rem(self.group + k, 8)) for k in range(1, 8)]
        )


class Gather(Slabs):
    def __init__(self, own_ref, gain_ref, w_ref, gains_ref, sems):
        super().__init__(own_ref.shape[0])
        self.own, self.gain, self.w, self.gains = own_ref, gain_ref, w_ref, gains_ref
        self.spread, self.z_sems, self.y_sems, self.x_sems, self.core_sems, self.gain_sems, self.local = sems
        self.others = [lax.rem(self.section + k, 4) for k in range(1, 4)]

    def chunk(self, k):
        y = self.y if k < 4 else 1 - self.y
        return self.z_peers[k % 4] * 2 + y

    def at(self, layer, group, rows):
        return self.w.at[layer, pl.ds(pl.multiple_of(group * self.rows + rows.start, 16), rows.size)]

    def spread_copy(self, k):
        peer = self.others[k]
        rows = self.slab_of(peer // 2, lax.rem(peer, 2))
        return remote(
            self.own.at[rows], self.at(self.section, self.group, rows),
            self.spread.at[0, k], self.spread.at[1, k], peer, self.group,
        )

    def spread_wait(self, layer):
        ref = self.at(layer, self.group, self.slab_of(self.x, self.core))
        for k in range(3):
            @pl.when(lax.rem(layer + k + 1, 4) == self.section)
            def _():
                remote(ref, ref, self.spread.at[0, k], self.spread.at[1, k], self.others[0], self.group).wait_recv()

    def z_copy(self, layer, k, landed=False):
        ref = self.at(layer, self.chunk(k) if landed else self.group, self.slab_of(self.x, self.core))
        return remote(ref, ref, self.z_sems.at[0, layer, k], self.z_sems.at[1, layer, k], *self.z_peer(k))

    def y_copy(self, layer, k, landed=False):
        ref = self.at(layer, self.chunk(k + 4 if landed else k), self.slab_of(self.x, self.core))
        return remote(ref, ref, self.y_sems.at[0, layer, k], self.y_sems.at[1, layer, k], *self.y_peer())

    def x_copy(self, layer, k, landed=False):
        ref = self.at(layer, self.chunk(k), self.edge_of(1 - self.x if landed else self.x, self.core))
        return remote(ref, ref, self.x_sems.at[0, layer, k], self.x_sems.at[1, layer, k], *self.x_peer())

    def core_copy(self, layer, k, landed=False):
        ref = self.at(layer, self.chunk(k), self.half_of(1 - self.core if landed else self.core))
        return remote(ref, ref, self.core_sems.at[0, layer, k], self.core_sems.at[1, layer, k], *self.core_peer())

    def gain_copy(self, k):
        if k < 7:
            peer = lax.rem(self.group + k + 1, 8)
            return remote(
                self.gain, self.gains.at[self.section, self.group],
                self.gain_sems.at[0, k], self.gain_sems.at[1, k], self.section, peer,
            )
        ref = self.gains.at[self.section]
        return remote(
            ref, ref, self.gain_sems.at[0, k], self.gain_sems.at[1, k], self.others[k - 7], self.group
        )

    def gain_landed(self, k):
        if k < 7:
            ref = self.gains.at[self.section, lax.rem(self.group - k - 1 + 8, 8)]
        else:
            ref = self.gains.at[lax.rem(self.section - (k - 6) + 4, 4)]
        return remote(ref, ref, self.gain_sems.at[0, k], self.gain_sems.at[1, k], self.section, self.group)

    def begin(self):
        for k in range(3):
            self.spread_copy(k).start()
        for k in range(7):
            self.gain_copy(k).start()
        rows = self.slab_of(self.x, self.core)
        self.w[self.section, pl.ds(pl.multiple_of(self.group * self.rows + rows.start, 16), rows.size)] = self.own[rows]
        self.gains[self.section, self.group] = self.gain[...]

    def share_gains(self):
        for k in range(7):
            self.gain_landed(k).wait_recv()
        for k in range(7, 10):
            self.gain_copy(k).start()

    def wait_gains(self):
        for k in range(7, 10):
            self.gain_landed(k).wait_recv()

    def kick(self, layer):
        self.spread_wait(layer)
        for k in range(1, 4):
            self.z_copy(layer, k).start()
        self.y_copy(layer, 0).start()
        self.x_copy(layer, 0).start()

    def serve_z(self, layer, k):
        self.z_copy(layer, k, True).wait_recv()
        self.y_copy(layer, k).start()
        self.x_copy(layer, k).start()

    def serve_y(self, layer, k):
        self.y_copy(layer, k, True).wait_recv()
        self.x_copy(layer, k + 4).start()

    def serve_x(self, layer, k):
        self.x_copy(layer, k, True).wait_recv()
        self.core_copy(layer, k).start()

    def finish_first(self, layer):
        for k in range(8):
            @pl.when(self.z_peers[k % 4] == 0)
            def _():
                self.core_copy(layer, k, True).wait_recv()

    def finish_rest(self, layer):
        for k in range(8):
            @pl.when(self.z_peers[k % 4] != 0)
            def _():
                self.core_copy(layer, k, True).wait_recv()

    def end(self, layers):
        for k in range(3):
            self.spread_copy(k).wait_send()
        for k in range(10):
            self.gain_copy(k).wait_send()

        def per_layer(layer, _):
            for k in range(1, 4):
                self.z_copy(layer, k).wait_send()
            for k in range(4):
                self.y_copy(layer, k).wait_send()
            for k in range(8):
                self.x_copy(layer, k).wait_send()
                self.core_copy(layer, k).wait_send()
            return 0

        lax.fori_loop(0, layers, per_layer, 0)


def segment_info(micro, length_ref, stems_ref):
    section, group = lax.axis_index("section"), lax.axis_index("dp")
    at = group * micro + jnp.minimum(section, micro - 1)
    used = (section < micro).astype(jnp.int32)
    frames = length_ref[0]
    for k in range(1, length_ref.shape[0]):
        frames = frames + length_ref[k]
    return length_ref[at] * used, [stems_ref[at, k] * used for k in range(4)], frames


def forward_kernel(
    layers, half, micro, length_ref, stems_ref, x_ref, target_ref, flat_ref, raw_gain_ref,
    probs_ref, qkv_ref, att_ref, middle_ref, hidden_ref, slope_ref, sent_ref, loss_grad_ref, stats_ref,
    full_ref, gains_out_ref,
    out_ref, w_all_ref, gains_ref, own_ref, own_gain_ref, block_ref, *sems,
):
    seg, width = x_ref.shape
    dim = width // HEADS
    part = width // 4
    layer = pl.program_id(0)
    rows = 256
    chunks = seg // rows
    length, present_flags, frame_total = segment_info(micro, length_ref, stems_ref)
    gather = Gather(own_ref, own_gain_ref, w_all_ref, gains_ref, sems)
    w_ref = w_all_ref.at[pl.ds(layer, 1)]

    def own_step(q, _):
        for c in range(4):
            block = 4 * q + c
            load_block(flat_ref, (block // 8) * 576 + lax.rem(block, 8), block_ref.at[c])
        quad = jnp.concatenate([block_ref[c, :, :part] for c in range(4)], axis=1)
        own_ref[pl.ds(pl.multiple_of(q * part, part), part)] = quad.astype(BF16)
        return 0

    def keep_copy(index):
        return pltpu.make_async_copy(w_all_ref.at[index], full_ref.at[index], gather.local.at[index])

    @pl.when(layer == 0)
    def _():
        gather.greet_all()
        lax.fori_loop(0, flat_ref.shape[0] // 288, own_step, 0)
        own_gain_ref[...] = jnp.zeros_like(own_gain_ref)
        own_gain_ref[:2, : raw_gain_ref.shape[1]] = raw_gain_ref[...]
        gather.begin()
        sent_ref[0] = x_ref[...]
        stats_ref[...] = jnp.zeros_like(stats_ref)
        gather.kick(0)
        gather.share_gains()
        gather.serve_z(0, 1)
        gather.serve_z(0, 2)
        gather.serve_x(0, 0)
        gather.serve_x(0, 1)
        gather.serve_z(0, 3)
        gather.kick(1)
        gather.wait_gains()
        gather.serve_y(0, 0)
        gather.serve_x(0, 2)
        gather.serve_y(0, 1)
        gather.serve_y(0, 2)
        gather.serve_x(0, 3)
        gather.serve_y(0, 3)
        for k in range(4, 8):
            gather.serve_x(0, k)
        gather.serve_z(1, 1)
        gather.serve_y(1, 0)
        gather.serve_z(1, 2)

    @pl.when(layer > 0)
    def _():
        gather.serve_x(layer, 7)

    @pl.when(layer + 2 < layers)
    def _():
        gather.kick(layer + 2)

    gather.finish_first(layer)
    more = layer + 1 < layers

    def serve(here, *steps):
        @pl.when(more & here)
        def _():
            for kind, k in steps:
                getattr(gather, kind)(layer + 1, k)

    def ahead(here, *steps):
        @pl.when((layer + 2 < layers) & here)
        def _():
            for kind, *k in steps:
                getattr(gather, kind)(layer + 2, *k)

    def stream_of(at):
        prev = sent_ref[layer, at].astype(F32)
        skip = sent_ref[jnp.maximum(layer + 1 - half, 0), at].astype(F32)
        return prev + jnp.where(layer >= half, skip, 0.0)

    def gain_row(which):
        return jnp.concatenate(
            [gains_ref[layer, g, which : which + 1, : width // 8] for g in range(8)], axis=1
        ).astype(BF16).astype(F32)

    gain_one = gain_row(0)
    gain_two = gain_row(1)
    gains_out_ref[layer, 0:1] = gain_one
    gains_out_ref[layer, 1:2] = gain_two

    def qkv_step(i, _):
        at = pl.ds(pl.multiple_of(i * rows, rows), rows)
        stream = stream_of(at)
        factor = lax.rsqrt(jnp.mean(stream * stream, axis=-1, keepdims=True) + 1e-06)
        normed = (stream * factor * gain_one).astype(BF16)
        for t in range(3):
            qkv_ref[0, t, at] = dot_nn(normed, stack_quads(w_ref, t, 3, 4)).astype(BF16)
        return 0

    lax.fori_loop(0, chunks, qkv_step, 0)
    serve(layer == 0, ("serve_y", 1))
    serve(True, ("serve_x", 0), ("serve_x", 1))
    frames = lax.broadcasted_iota(jnp.int32, (1, seg), 1)
    masking = jnp.where(frames < length, 0.0, -1e30).astype(F32)

    def head_step(h):
        queries, keys, values = (qkv_ref[0, t, :, h * dim : (h + 1) * dim] for t in range(3))
        scores = dot_nt(queries, keys) * dim ** (-0.5) + masking
        top = jnp.max(scores, axis=-1, keepdims=True)
        expd = jnp.exp(scores - top)
        probs = (expd * (1.0 / jnp.sum(expd, axis=-1, keepdims=True))).astype(BF16)
        probs_ref[0, h] = probs
        return dot_nn(probs, values).astype(BF16)

    def put_heads(first):
        heads = [head_step(h) for h in range(first, first + HEADS // 2)]
        att_ref[0, :, first * dim : (first + HEADS // 2) * dim] = jnp.concatenate(heads, axis=1)

    put_heads(0)
    serve(True, ("serve_z", 3), ("serve_x", 2), ("serve_x", 4), ("serve_x", 5))
    put_heads(HEADS // 2)
    serve(True, ("serve_y", 2))
    ahead(True, ("serve_z", 1), ("serve_y", 0))
    gather.finish_rest(layer)
    keep_copy(layer).start()

    def ffn_step(i, _):
        at = pl.ds(pl.multiple_of(i * rows, rows), rows)
        branch_attn = dot_nn(att_ref[0, at], stack_quads(w_ref, 12, 1, 4))
        stream = stream_of(at)
        middle = stream + branch_attn
        middle_ref[0, at] = middle
        factor = lax.rsqrt(jnp.mean(middle * middle, axis=-1, keepdims=True) + 1e-06)
        normed = (middle * factor * gain_two).astype(BF16)
        branch_ffn = jnp.zeros((rows, width), F32)
        for c in range(4):
            pre_act = dot_nn(normed, stack_quads(w_ref, 16 + c, 4, 4))
            hidden, slope = gelu_parts(pre_act)
            hidden = hidden.astype(BF16)
            hidden_ref[0, c, at] = hidden
            slope_ref[0, c, at] = slope.astype(BF16)
            branch_ffn = branch_ffn + dot_nn(hidden, stack_quads(w_ref, 32 + 4 * c, 1, 4))
            if c == 1:
                serve(i == 1, ("serve_y", 3), ("serve_x", 6))
                ahead(i == 1, ("serve_z", 2))
        output = middle + branch_ffn
        out_ref[at] = output
        sent_ref[jnp.minimum(layer + 1, layers - 1), at] = jnp.where(
            layer + 1 < layers, output.astype(BF16), sent_ref[layers - 1, at]
        )
        valid = (lax.broadcasted_iota(jnp.int32, (rows, 1), 0) + i * rows < length).astype(F32)
        for k, value in enumerate((stream, branch_attn, branch_ffn)):
            stats_ref[layer, k : k + 1] += jnp.sum(valid * value * value, axis=0, keepdims=True)

        serve(i == 0, ("serve_x", 3))
        return 0

    lax.fori_loop(0, chunks, ffn_step, 0)
    ahead(True, ("serve_y", 1))

    @pl.when(layer == layers - 1)
    def _():
        bins = width // 8
        lane = lax.broadcasted_iota(jnp.int32, (1, width), 1)
        is_real = lax.rem(lane, 2 * bins) < bins
        stem = lane // (2 * bins)
        present = jnp.zeros((1, width), F32)
        for k in range(4):
            present = jnp.where(stem == k, present_flags[k].astype(F32), present)
        inverse = 1.0 / jnp.full((1, 1), frame_total, jnp.int32).astype(F32)

        def loss_step(i, _):
            at = pl.ds(pl.multiple_of(i * rows, rows), rows)
            output = out_ref[at]
            square = output * output
            other = jnp.where(
                is_real, pltpu.roll(square, width - bins, 1), pltpu.roll(square, bins, 1)
            )
            magnitude = jnp.sqrt(square + other + 0.01)
            goal = target_ref[:, at].T
            goal = jnp.concatenate(
                [goal[:, (k // 2) * bins : (k // 2 + 1) * bins] for k in range(8)], axis=1
            )
            differ = magnitude - goal
            smooth = jnp.sqrt(differ * differ + 0.01)
            valid = (lax.broadcasted_iota(jnp.int32, (rows, 1), 0) + i * rows < length).astype(F32)
            weight = valid * present
            loss_grad_ref[at] = weight * differ * output * inverse / (smooth * magnitude)
            stats_ref[0, 3:4] += jnp.sum(
                jnp.where(is_real, weight * smooth, 0.0), axis=0, keepdims=True
            )
            return 0

        lax.fori_loop(0, chunks, loss_step, 0)
        gather.end(layers)
        for k in range(layers):
            keep_copy(k).wait()


class Scatter(Slabs):
    def __init__(self, refs, sems):
        self.grads, self.core_in, self.x_in, self.y_in, self.stage, self.z_in, self.last_in = refs
        super().__init__(self.grads.shape[3])
        self.core_sems, self.x_sems, self.y_sems, self.z_sems, self.last_sems = sems
        self.mine = self.slab_of(self.x, self.core)

    def core_copy(self, layer, late):
        slot = lax.rem(layer, 2)
        zs = pl.ds(0, 1) if late else pl.ds(1, 3)
        return remote(
            self.grads.at[slot, zs, :, self.half_of(1 - self.core)], self.core_in.at[slot, zs],
            self.core_sems.at[0, slot, int(late)], self.core_sems.at[1, slot, int(late)], *self.core_peer(),
        )

    def x_copy(self, layer, k):
        slot = lax.rem(layer, 2)
        return remote(
            self.grads.at[slot, self.z_peers[k], :, self.edge_of(1 - self.x, self.core)], self.x_in.at[layer, k],
            self.x_sems.at[0, layer, k], self.x_sems.at[1, layer, k], *self.x_peer(),
        )

    def y_copy(self, layer, k):
        slot = lax.rem(layer, 2)
        return remote(
            self.grads.at[slot, self.z_peers[k], 1 - self.y, self.mine], self.y_in.at[layer, k],
            self.y_sems.at[0, layer, k], self.y_sems.at[1, layer, k], *self.y_peer(),
        )

    def z_copy(self, layer, k):
        return remote(
            self.stage.at[layer, k], self.z_in.at[layer, k - 1],
            self.z_sems.at[0, layer, k - 1], self.z_sems.at[1, layer, k - 1], *self.z_peer(k),
        )

    def last_copy(self, layer):
        place = jnp.maximum(lax.rem(self.section - layer + 4, 4) - 1, 0)
        return remote(
            self.stage.at[layer, 0], self.last_in.at[place],
            self.last_sems.at[0, layer], self.last_sems.at[1, place], layer, self.group,
        )

    def last_landed(self, place):
        return remote(
            self.last_in.at[place], self.last_in.at[place],
            self.last_sems.at[0, 0], self.last_sems.at[1, place], self.section, self.group,
        )

    def for_part(self, late, act):
        for k in (1, 2, 3, 0):
            @pl.when((self.z_peers[k] == 0) == late)
            def _():
                act(k)

    def add_core(self, layer, late):
        slot = lax.rem(layer, 2)
        self.core_copy(layer, late).wait_recv()
        rows = self.half_of(self.core)

        def add(i, _):
            z, y = i // 2, lax.rem(i, 2)
            self.grads[slot, z, y, rows] = self.grads[slot, z, y, rows] + self.core_in[slot, z, y]
            return 0

        lax.fori_loop(0 if late else 2, 2 if late else 8, add, 0)
        self.for_part(late, lambda k: self.x_copy(layer, k).start())

    def add_x(self, layer, k, late):
        @pl.when((self.z_peers[k] == 0) == late)
        def _():
            slot = lax.rem(layer, 2)
            self.x_copy(layer, k).wait_recv()
            rows = self.edge_of(self.x, self.core)
            inner = pl.ds(pl.multiple_of((self.slab - self.edge) * self.x, 16), self.edge)
            z = self.z_peers[k]
            self.grads[slot, z, 1 - self.y, rows] = (
                self.grads[slot, z, 1 - self.y, rows] + self.x_in[layer, k, 1 - self.y]
            )
            self.y_copy(layer, k).start()
            self.stage[layer, k] = self.grads[slot, z, self.y, self.mine]
            self.stage[layer, k, inner] = self.stage[layer, k, inner] + self.x_in[layer, k, self.y]

    def add_y(self, layer, k, late):
        @pl.when((self.z_peers[k] == 0) == late)
        def _():
            self.y_copy(layer, k).wait_recv()
            self.stage[layer, k] = self.stage[layer, k] + self.y_in[layer, k]
            if k:
                self.z_copy(layer, k).start()

    def add_z(self, layer, result_ref):
        for k in range(1, 4):
            self.z_copy(layer, k).wait_recv()
        total = self.stage[layer, 0].astype(F32)
        for k in range(3):
            total = total + self.z_in[layer, k].astype(F32)

        @pl.when(layer == self.section)
        def _():
            result_ref[...] = jnp.zeros_like(result_ref)
            result_ref[self.mine] = total

        @pl.when(layer != self.section)
        def _():
            self.stage[layer, 0] = total.astype(BF16)
            self.last_copy(layer).start()

    def wait_sends(self, layer):
        for late in (False, True):
            self.core_copy(layer, late).wait_send()
        for k in range(4):
            self.x_copy(layer, k).wait_send()
            self.y_copy(layer, k).wait_send()

    def end(self, layers):
        def per_layer(layer, _):
            for k in range(1, 4):
                self.z_copy(layer, k).wait_send()

            @pl.when(layer != self.section)
            def _():
                self.last_copy(layer).wait_send()

            return 0

        lax.fori_loop(0, layers, per_layer, 0)

    def collect(self, result_ref):
        for place in (0, 2, 1):
            self.last_landed(place).wait_recv()
            peer = lax.rem(self.section + place + 1, 4)
            rows = self.slab_of(peer // 2, lax.rem(peer, 2))
            result_ref[rows] = result_ref[rows] + self.last_in[place].astype(F32)


class Totals:
    def __init__(self, refs, sems):
        self.stage_in, self.z_in, self.norm_section, self.norm_group = refs
        self.stage_sems, self.z_sems, self.section_sems, self.group_sems = sems
        self.section, self.group, self.core, self.y, self.z_peers = mesh_place()

    def stage_copy(self, k):
        peer = (
            (self.section + 1 - 2 * self.core, self.group),
            (self.section, self.group + 1 - 2 * self.y),
            (lax.rem(self.section + 2, 4), self.group),
        )[k]
        return remote(
            self.stage_in.at[2 * k], self.stage_in.at[2 * k + 1],
            self.stage_sems.at[0, k], self.stage_sems.at[1, k], *peer,
        )

    def z_copy(self, k):
        z = self.z_peers[0]
        return remote(
            self.z_in.at[z], self.z_in.at[z], self.z_sems.at[0, k - 1], self.z_sems.at[1, k - 1],
            self.section, self.z_peers[k] * 2 + self.y,
        )

    def z_landed(self, k):
        z = self.z_peers[k]
        return remote(
            self.z_in.at[z], self.z_in.at[z], self.z_sems.at[0, k - 1], self.z_sems.at[1, k - 1],
            self.section, self.z_peers[k] * 2 + self.y,
        )

    def begin(self, tile):
        self.stage_in[0] = tile
        self.stage_copy(0).start()

    def after_core(self):
        self.stage_copy(0).wait_recv()
        self.stage_in[2] = self.stage_in[0] + self.stage_in[1]
        self.stage_copy(1).start()

    def after_y(self):
        self.stage_copy(1).wait_recv()
        self.z_in[self.z_peers[0]] = self.stage_in[2] + self.stage_in[3]
        for k in range(1, 4):
            self.z_copy(k).start()

    def after_z(self):
        for k in range(1, 4):
            self.z_landed(k).wait_recv()
        self.stage_in[4] = self.z_in[0] + self.z_in[1] + self.z_in[2] + self.z_in[3]
        self.stage_copy(2).start()

    def after_x(self):
        self.stage_copy(2).wait_recv()
        return self.stage_in[4] + self.stage_in[5]

    def norm_copy(self, k):
        if k < 3:
            peer = (lax.rem(self.section + k + 1, 4), self.group)
            ref = self.norm_section.at[self.section]
            return remote(ref, ref, self.section_sems.at[0, k], self.section_sems.at[1, k], *peer)
        k = k - 3
        peer = (self.section, lax.rem(self.group + k + 1, 8))
        ref = self.norm_group.at[self.group]
        return remote(ref, ref, self.group_sems.at[0, k], self.group_sems.at[1, k], *peer)

    def norm_landed(self, k):
        if k < 3:
            ref = self.norm_section.at[lax.rem(self.section - k - 1 + 4, 4)]
            return remote(
                ref, ref, self.section_sems.at[0, k], self.section_sems.at[1, k], self.section, self.group
            )
        k = k - 3
        ref = self.norm_group.at[lax.rem(self.group - k - 1 + 8, 8)]
        return remote(ref, ref, self.group_sems.at[0, k], self.group_sems.at[1, k], self.section, self.group)

    def norm(self, value):
        self.norm_section[self.section] = value
        for k in range(3):
            self.norm_copy(k).start()
        for k in range(3):
            self.norm_landed(k).wait_recv()
        total = self.norm_section[0]
        for k in range(1, 4):
            total = total + self.norm_section[k]
        self.norm_group[self.group] = total
        for k in range(3, 10):
            self.norm_copy(k).start()
        for k in range(3, 10):
            self.norm_landed(k).wait_recv()
        total = self.norm_group[0]
        for k in range(1, 8):
            total = total + self.norm_group[k]
        return total

    def end(self):
        for k in range(3):
            self.stage_copy(k).wait_send()
        for k in range(1, 4):
            self.z_copy(k).wait_send()
        for k in range(10):
            self.norm_copy(k).wait_send()


def norm_reverse(value, gain, grad):
    factor = lax.rsqrt(jnp.mean(value * value, axis=-1, keepdims=True) + 1e-06)
    scaled = grad * gain
    mean = jnp.mean(value * scaled, axis=-1, keepdims=True)
    unit = value * factor
    back = factor * scaled - unit * (factor * factor * mean)
    return back, jnp.sum(grad * unit, axis=0, keepdims=True), (unit * gain).astype(BF16)


def backward_kernel(
    layers, half, loss_grad_ref, w_ref, gain_ref, sent_ref,
    probs_ref, qkv_ref, att_ref, middle_ref, hidden_ref, slope_ref, stats_ref,
    result_ref, totals_ref, square_ref,
    sends_ref, dffn_ref, dpre_ref, normed_ref, dmid_ref, datt_ref, dhold_ref, dqkv_ref,
    gain_grad_ref, *comm_refs,
):
    seg, width = loss_grad_ref.shape
    dim = width // HEADS
    part = width // 4
    layer = layers - 1 - pl.program_id(0)
    rows = 256
    chunks = seg // rows
    gain_one = gain_ref[0, 0:1]
    gain_two = gain_ref[0, 1:2]
    scatter = Scatter(comm_refs[:7], comm_refs[11:16])
    totals = Totals(comm_refs[7:11], comm_refs[16:])
    grads_ref = comm_refs[0]
    slot = lax.rem(layer, 2)

    @pl.when(layer == layers - 1)
    def _():
        scatter.greet_all()
        sends_ref[...] = jnp.zeros_like(sends_ref)
        gain_grad_ref[...] = jnp.zeros_like(gain_grad_ref)

    def put_grad(first, step, value):
        for r in range(4):
            quad = first + step * r
            owner = quad // 6
            at = pl.ds(pl.multiple_of(lax.rem(quad, 6) * part, part), part)
            grads_ref[slot, owner // 2, lax.rem(owner, 2), at] = value[r * part : (r + 1) * part].astype(BF16)

    def serve(back, here, *steps):
        @pl.when((layer + back < layers) & here)
        def _():
            for kind, *args in steps:
                getattr(scatter, kind)(layer + back, *args)

    def ffn_step(i, _):
        at = pl.ds(pl.multiple_of(i * rows, rows), rows)
        later = sends_ref[jnp.minimum(layer + 1, layers - 1), at].astype(F32)
        skip = sends_ref[jnp.minimum(layer + half, layers - 1), at].astype(F32)
        upstream = jnp.where(
            layer == layers - 1, loss_grad_ref[at], later + jnp.where(layer + half < layers, skip, 0.0)
        )
        dffn = upstream.astype(BF16)
        dffn_ref[at] = dffn
        dnormed = jnp.zeros((rows, width), F32)
        for c in range(4):
            dhidden = dot_nt(dffn, stack_quads(w_ref, 32 + 4 * c, 1, 4))
            dpre = (dhidden * slope_ref[0, c, at].astype(F32)).astype(BF16)
            dpre_ref[c, at] = dpre
            dnormed = dnormed + dot_nt(dpre, stack_quads(w_ref, 16 + c, 4, 4))
        back, gain_grad, normed = norm_reverse(middle_ref[0, at], gain_two, dnormed)
        gain_grad_ref[layer, 1:2] += gain_grad
        normed_ref[at] = normed
        dmid = upstream + back
        dmid_ref[at] = dmid
        datt = dmid.astype(BF16)
        datt_ref[at] = datt
        dattended = dot_nt(datt, stack_quads(w_ref, 12, 1, 4)).astype(BF16)
        dhold_ref[at] = dattended

        serve(1, i == 1, ("add_x", 1, False), ("add_core", True))
        serve(2, i == 1, ("add_y", 3, False), ("add_y", 0, False))
        return 0

    lax.fori_loop(0, chunks, ffn_step, 0)

    @pl.when(layer < layers - 2)
    def _():
        scatter.wait_sends(layer + 2)

    def ffn_grad_step(c, _):
        put_grad(32 + 4 * c, 1, dot_tn(hidden_ref[0, c], dffn_ref[...]))
        put_grad(16 + c, 4, dot_tn(normed_ref[...], dpre_ref[c]))
        return 0

    for c in range(4):
        ffn_grad_step(c, 0)
    put_grad(12, 1, dot_tn(att_ref[0], datt_ref[...]))
    scatter.core_copy(layer, False).start()

    serve(1, True, ("add_x", 2, False))
    serve(2, True, *[("add_y", k, True) for k in range(4)])

    def head_step(h):
        queries, keys, values = (qkv_ref[0, t, :, h * dim : (h + 1) * dim] for t in range(3))
        probs = probs_ref[0, h]
        dhold = dhold_ref[:, h * dim : (h + 1) * dim]
        dprobs = dot_nt(dhold, values)
        wide = probs.astype(F32)
        dot_sum = jnp.sum(wide * dprobs, axis=-1, keepdims=True)
        dscores = (wide * (dprobs - dot_sum)).astype(BF16)
        return (
            (dot_nn(dscores, keys) * dim ** (-0.5)).astype(BF16),
            (dot_tn(dscores, queries) * dim ** (-0.5)).astype(BF16),
            dot_tn(probs, dhold).astype(BF16),
        )

    def put_heads(first, parts):
        for t in range(3):
            dqkv_ref[t, :, first * dim : (first + len(parts)) * dim] = jnp.concatenate([p[t] for p in parts], axis=1)

    put_heads(0, [head_step(h) for h in range(HEADS // 2)])

    serve(1, True, ("add_x", 3, False))

    put_heads(HEADS // 2, [head_step(h) for h in range(HEADS // 2, HEADS)])
    scatter.add_core(layer, False)
    serve(1, True, ("add_x", 0, False), ("add_y", 1, False))

    def qkv_step(i, _):
        at = pl.ds(pl.multiple_of(i * rows, rows), rows)
        dnormed = jnp.zeros((rows, width), F32)
        for t in range(3):
            dnormed = dnormed + dot_nt(dqkv_ref[t, at], stack_quads(w_ref, t, 3, 4))
        prev = sent_ref[layer, at].astype(F32)
        skip = sent_ref[jnp.maximum(layer + 1 - half, 0), at].astype(F32)
        stream = prev + jnp.where(layer >= half, skip, 0.0)
        back, gain_grad, normed = norm_reverse(stream, gain_one, dnormed)
        gain_grad_ref[layer, 0:1] += gain_grad
        normed_ref[at] = normed
        sends_ref[layer, at] = (dmid_ref[at] + back).astype(BF16)
        return 0

    lax.fori_loop(0, chunks, qkv_step, 0)

    def qkv_grad_step(t, _):
        put_grad(t, 3, dot_tn(normed_ref[...], dqkv_ref[t]))
        return 0

    for t in range(3):
        qkv_grad_step(t, 0)
    scatter.core_copy(layer, True).start()
    serve(1, True, *[("add_x", k, True) for k in range(4)], ("add_y", 2, False))
    serve(2, True, ("add_z", result_ref))

    @pl.when(layer == 0)
    def _():
        lane = lax.broadcasted_iota(jnp.int32, (1, width), 1)
        rows_out = [gain_grad_ref[k // 2, k % 2 : k % 2 + 1] for k in range(2 * layers)]
        for k in range(layers):
            row = jnp.zeros((1, width), F32)
            for i in range(4):
                value = jnp.sum(stats_ref[k, i : i + 1], axis=1, keepdims=True)
                row = jnp.where(lane == i, value, row)
            rows_out.append(row)
        rows_out.append(jnp.zeros((16 - 3 * layers, width), F32))
        totals.begin(jnp.concatenate(rows_out, axis=0))
        scatter.add_x(0, 1, False)
        scatter.add_core(0, True)
        scatter.add_y(1, 3, False)
        scatter.add_y(1, 0, False)
        totals.after_core()
        scatter.add_x(0, 2, False)
        for k in range(4):
            scatter.add_y(1, k, True)
        scatter.add_x(0, 3, False)
        totals.after_y()
        scatter.add_y(0, 1, False)
        scatter.add_x(0, 0, False)
        for k in range(4):
            scatter.add_x(0, k, True)
        scatter.add_y(0, 2, False)
        scatter.add_z(1, result_ref)
        scatter.add_y(0, 3, False)
        scatter.add_y(0, 0, False)
        for k in range(4):
            scatter.add_y(0, k, True)
        scatter.add_z(0, result_ref)
        totals.after_z()
        scatter.collect(result_ref)
        square = jnp.zeros((8, width), F32)
        for q in range(6):
            value = result_ref[q * part : (q + 1) * part]
            square = square + jnp.sum((value * value).reshape(part // 8, 8, width), axis=0)
        folded = square[:, :128] + square[:, 128:256] + square[:, 256:]
        square_ref[...] = totals.norm(folded)
        totals_ref[...] = totals.after_x()
        scatter.wait_sends(1)
        scatter.wait_sends(0)
        scatter.end(layers)
        totals.end()


FF = 1536


def from_behind(value, axis, by):
    peers = lax.axis_size(axis)
    pairs = [(i, i + by) for i in range(peers) if 0 <= i + by < peers]
    return lax.ppermute(value, axis, pairs)


def unblock(blocks, row_count, col_count, block_size):
    return (
        blocks.reshape(row_count // block_size, col_count // block_size, block_size, block_size)
        .transpose(0, 2, 1, 3)
        .reshape(row_count, col_count)
    )


def to_blocks(matrix, block_size):
    row_count, col_count = matrix.shape
    return (
        matrix.reshape(row_count // block_size, block_size, col_count // block_size, block_size)
        .transpose(0, 2, 1, 3)
        .reshape(-1, block_size * block_size)
    )


def split_matrices(blocks, model_width):
    block_size = model_width // 4
    shapes = (
        (model_width, 3 * model_width),
        (model_width, model_width),
        (model_width, FF),
        (FF, model_width),
    )
    result = []
    offset = 0
    for row_count, col_count in shapes:
        number = row_count * col_count // (block_size * block_size)
        result.append(unblock(blocks[offset : offset + number], row_count, col_count, block_size))
        offset = offset + number
    return result


def rms_norm(stream, gain):
    factor = lax.rsqrt(jnp.mean(stream * stream, axis=-1, keepdims=True) + 1e-06)
    return (stream * factor * gain, factor)


def norm_back(stream, factor, gain, grad):
    scaled = grad * gain
    grad_in = factor * scaled - stream * factor**3 * jnp.mean(
        stream * scaled, axis=-1, keepdims=True
    )
    return (grad_in, jnp.sum(grad * stream * factor, axis=0))


def gelu_slope(pre_act):
    return (
        0.5 * (1.0 + lax.erf(pre_act * 0.7071067811865476))
        + pre_act * jnp.exp(-0.5 * pre_act * pre_act) * 0.3989422804014327
    )


def layer_forward(stream, matrices, gain_pair, length):
    w_qkv, w_out, w_up, w_down = matrices
    row_count, model_width = stream.shape
    head_dim = model_width // HEADS
    frames = jnp.arange(row_count)
    norm_one, scale_one = rms_norm(stream, gain_pair[0])
    normed = norm_one.astype(BF16)
    qkv_all = jnp.dot(normed, w_qkv, preferred_element_type=jnp.float32).astype(BF16)
    queries = qkv_all[:, :model_width].reshape(row_count, HEADS, head_dim)
    key_rows = qkv_all[:, model_width : 2 * model_width].reshape(row_count, HEADS, head_dim)
    value_rows = qkv_all[:, 2 * model_width :].reshape(row_count, HEADS, head_dim)
    masking = jnp.where(frames < length, 0.0, -1e30).astype(jnp.float32)
    scores = jnp.einsum(
        "qhe,khe->hqk", queries, key_rows, preferred_element_type=jnp.float32
    ) * head_dim ** (-0.5)
    attn_probs = jax.nn.softmax(scores + masking[None, None, :], axis=-1)
    probs_low = attn_probs.astype(BF16)
    attended = (
        jnp.einsum("hqk,khe->qhe", probs_low, value_rows, preferred_element_type=jnp.float32)
        .reshape(row_count, model_width)
        .astype(BF16)
    )
    branch_attn = jnp.dot(attended, w_out, preferred_element_type=jnp.float32)
    middle = stream + branch_attn
    norm_two, scale_two = rms_norm(middle, gain_pair[1])
    normed_two = norm_two.astype(BF16)
    pre_act = jnp.dot(normed_two, w_up, preferred_element_type=jnp.float32)
    hidden = jax.nn.gelu(pre_act, approximate=False).astype(BF16)
    branch_ffn = jnp.dot(hidden, w_down, preferred_element_type=jnp.float32)
    kept_vals = (
        scale_one,
        normed,
        queries,
        key_rows,
        value_rows,
        attn_probs,
        probs_low,
        attended,
        middle,
        scale_two,
        normed_two,
        pre_act,
        hidden,
    )
    return (middle + branch_ffn, branch_attn, branch_ffn, kept_vals)


def layer_backward(stream, matrices, gain_pair, length, upstream):
    w_qkv, w_out, w_up, w_down = matrices
    row_count, model_width = stream.shape
    head_dim = model_width // HEADS
    output, branch_attn, branch_ffn, kept_vals = layer_forward(stream, matrices, gain_pair, length)
    (
        scale_one,
        normed,
        queries,
        key_rows,
        value_rows,
        attn_probs,
        probs_low,
        attended,
        middle,
        scale_two,
        normed_two,
        pre_act,
        hidden,
    ) = kept_vals
    grad_ffn = upstream.astype(BF16)
    grad_down = jnp.dot(hidden.T, grad_ffn, preferred_element_type=jnp.float32)
    grad_hidden = jnp.dot(grad_ffn, w_down.T, preferred_element_type=jnp.float32)
    grad_pre = (grad_hidden * gelu_slope(pre_act)).astype(BF16)
    grad_up = jnp.dot(normed_two.T, grad_pre, preferred_element_type=jnp.float32)
    back_mid, gain_two = norm_back(
        middle,
        scale_two,
        gain_pair[1],
        jnp.dot(grad_pre, w_up.T, preferred_element_type=jnp.float32),
    )
    grad_mid = upstream + back_mid
    grad_branch = grad_mid.astype(BF16)
    grad_out = jnp.dot(attended.T, grad_branch, preferred_element_type=jnp.float32)
    grad_att = (
        jnp.dot(grad_branch, w_out.T, preferred_element_type=jnp.float32)
        .astype(BF16)
        .reshape(row_count, HEADS, head_dim)
    )
    grad_value = jnp.einsum("hqk,qhe->khe", probs_low, grad_att, preferred_element_type=jnp.float32)
    grad_probs = jnp.einsum(
        "qhe,khe->hqk", grad_att, value_rows, preferred_element_type=jnp.float32
    )
    grad_scores = (
        attn_probs * (grad_probs - jnp.sum(attn_probs * grad_probs, axis=-1, keepdims=True))
    ).astype(BF16)
    grad_query = jnp.einsum(
        "hqk,khe->qhe", grad_scores, key_rows, preferred_element_type=jnp.float32
    ) * head_dim ** (-0.5)
    grad_key = jnp.einsum(
        "hqk,qhe->khe", grad_scores, queries, preferred_element_type=jnp.float32
    ) * head_dim ** (-0.5)
    grad_qkv = jnp.concatenate(
        [
            grad_query.reshape(row_count, model_width),
            grad_key.reshape(row_count, model_width),
            grad_value.reshape(row_count, model_width),
        ],
        axis=1,
    ).astype(BF16)
    grad_wqkv = jnp.dot(normed.T, grad_qkv, preferred_element_type=jnp.float32)
    back_in, gain_one = norm_back(
        stream,
        scale_one,
        gain_pair[0],
        jnp.dot(grad_qkv, w_qkv.T, preferred_element_type=jnp.float32),
    )
    return (
        grad_mid + back_in,
        (grad_wqkv, grad_out, grad_up, grad_down),
        jnp.stack([gain_one, gain_two]),
    )


def spectral_terms(output, target, length, present_row, frame_count):
    row_count, model_width = output.shape
    bin_count = model_width // 8
    spectra = output.reshape(row_count, 4, 2, bin_count)
    real_part = spectra[:, :, 0]
    imag_part = spectra[:, :, 1]
    magnitude = jnp.sqrt(real_part * real_part + imag_part * imag_part + 0.01)
    differ = magnitude - target.reshape(row_count, 4, bin_count)
    smooth_err = jnp.sqrt(differ * differ + 0.01)
    weight = (jnp.arange(row_count) < length).astype(jnp.float32)[:, None, None] * present_row[
        None, :, None
    ]
    loss_slope = weight * differ / smooth_err / magnitude / frame_count
    grad_spec = jnp.stack([loss_slope * real_part, loss_slope * imag_part], axis=2).reshape(
        row_count, model_width
    )
    return (jnp.sum(smooth_err * weight), grad_spec)


def pipelined_body(
    x_in,
    targets,
    valid_len,
    present_stems,
    w_master,
    norm_gains,
    gain_m,
    gain_v,
    l_stats,
    r_stats,
    l_roots,
    r_roots,
    step_count,
):
    model_width = x_in.shape[1]
    block_size = model_width // 4
    sections = lax.axis_size("section")
    section_idx = lax.axis_index("section")
    half_way = sections // 2
    groups = lax.axis_size("dp")
    group_idx = lax.axis_index("dp")
    micro_count = valid_len.shape[0] // groups
    seg_len = x_in.shape[0] // micro_count
    own_blocks = w_master.shape[1]
    own_gain = norm_gains.shape[2]
    full_w, full_g = (
        lax.all_gather(w_master.astype(BF16), "dp", axis=1, tiled=True),
        lax.all_gather(norm_gains.astype(BF16), "dp", axis=2, tiled=True),
    )
    matrices = split_matrices(full_w[0], model_width)
    gain_pair = full_g[0].astype(jnp.float32)
    lengths = lax.dynamic_slice_in_dim(valid_len, group_idx * micro_count, micro_count)
    stem_flags = lax.dynamic_slice_in_dim(
        present_stems, group_idx * micro_count, micro_count
    ).astype(jnp.float32)
    frame_count = jnp.sum(valid_len).astype(jnp.float32)
    decoder = section_idx >= half_way
    encoder = section_idx < half_way
    is_last = section_idx == sections - 1
    act_shape = (micro_count, seg_len, model_width)

    def forward_step(step_idx, loop_state):
        in_rows, kept_prev, skip_store, loss_grads, loss_sum, sq_sums = loop_state
        micro_idx = step_idx - section_idx
        active = (micro_idx >= 0) & (micro_idx < micro_count)
        slot_idx = jnp.clip(micro_idx, 0, micro_count - 1)
        fresh_rows = lax.dynamic_slice_in_dim(x_in, slot_idx * seg_len, seg_len, 0)
        previous = jnp.where(section_idx == 0, fresh_rows, in_rows)
        stream = previous.astype(jnp.float32) + jnp.where(
            decoder, skip_store[slot_idx].astype(jnp.float32), 0.0
        )
        length = lengths[slot_idx]
        target = lax.dynamic_slice_in_dim(targets, slot_idx * seg_len, seg_len, 0)

        def forward_compute_fn(operand):
            output, branch_attn, branch_ffn, kept_vals = layer_forward(
                stream, matrices, gain_pair, length
            )
            valid = (jnp.arange(seg_len) < length).astype(jnp.float32)[:, None]
            squares = jnp.stack(
                [
                    jnp.sum(valid * stream * stream),
                    jnp.sum(valid * branch_attn * branch_attn),
                    jnp.sum(valid * branch_ffn * branch_ffn),
                ]
            )
            seg_loss, grad_spec = spectral_terms(
                output, target, length, stem_flags[slot_idx], frame_count
            )
            return (output, squares, seg_loss, grad_spec)

        def forward_spare_fn(operand):
            empty = jnp.zeros((seg_len, model_width), jnp.float32)
            return (empty, jnp.zeros((3,), jnp.float32), jnp.zeros((), jnp.float32), empty)

        output, squares, seg_loss, grad_spec = lax.cond(
            active, forward_compute_fn, forward_spare_fn, 0
        )
        kept_prev = kept_prev.at[slot_idx].set(jnp.where(active, previous, kept_prev[slot_idx]))
        loss_grads = loss_grads.at[slot_idx].set(
            jnp.where(active & is_last, grad_spec, loss_grads[slot_idx])
        )
        loss_sum = loss_sum + jnp.where(is_last, seg_loss, 0.0)
        sq_sums = sq_sums + squares
        sent_rows = output.astype(BF16)
        in_rows = from_behind(sent_rows, "section", 1)
        from_encoder = from_behind(sent_rows, "section", half_way)
        recv_idx = step_idx - section_idx + half_way
        usable = decoder & (recv_idx >= 0) & (recv_idx < micro_count)
        recv_slot = jnp.clip(recv_idx, 0, micro_count - 1)
        skip_store = skip_store.at[recv_slot].set(
            jnp.where(usable, from_encoder, skip_store[recv_slot])
        )
        return (in_rows, kept_prev, skip_store, loss_grads, loss_sum, sq_sums)

    start_state = (
        jnp.zeros((seg_len, model_width), BF16),
        jnp.zeros(act_shape, BF16),
        jnp.zeros(act_shape, BF16),
        jnp.zeros(act_shape, jnp.float32),
        jnp.zeros((), jnp.float32),
        jnp.zeros((3,), jnp.float32),
    )
    unused_rows, kept_prev, skip_store, loss_grads, loss_sum, sq_sums = lax.fori_loop(
        0, micro_count + sections - 1, forward_step, start_state
    )

    def backward_step(step_idx, loop_state):
        in_grads, skip_grad_store, grad_mats, grad_gains = loop_state
        micro_idx = step_idx - (sections - 1 - section_idx)
        active = (micro_idx >= 0) & (micro_idx < micro_count)
        slot_idx = jnp.clip(micro_idx, 0, micro_count - 1)
        upstream = jnp.where(
            is_last,
            loss_grads[slot_idx],
            in_grads.astype(jnp.float32)
            + jnp.where(encoder, skip_grad_store[slot_idx].astype(jnp.float32), 0.0),
        )
        stream = kept_prev[slot_idx].astype(jnp.float32) + jnp.where(
            decoder, skip_store[slot_idx].astype(jnp.float32), 0.0
        )
        length = lengths[slot_idx]

        def backward_compute_fn(operand):
            return layer_backward(stream, matrices, gain_pair, length, upstream)

        def backward_spare_fn(operand):
            return (
                jnp.zeros_like(stream),
                tuple((jnp.zeros(mat.shape, jnp.float32) for mat in matrices)),
                jnp.zeros((2, model_width), jnp.float32),
            )

        grad_stream, layer_mats, layer_gains = lax.cond(
            active, backward_compute_fn, backward_spare_fn, 0
        )
        grad_mats = tuple((total + piece for total, piece in zip(grad_mats, layer_mats)))
        grad_gains = grad_gains + layer_gains
        grad_rows = grad_stream.astype(BF16)
        in_grads = from_behind(grad_rows, "section", -1)
        from_decoder = from_behind(grad_rows, "section", -half_way)
        recv_idx = micro_idx + half_way
        usable = encoder & (recv_idx >= 0) & (recv_idx < micro_count)
        recv_slot = jnp.clip(recv_idx, 0, micro_count - 1)
        skip_grad_store = skip_grad_store.at[recv_slot].set(
            jnp.where(usable, from_decoder, skip_grad_store[recv_slot])
        )
        return (in_grads, skip_grad_store, grad_mats, grad_gains)

    back_state = (
        jnp.zeros((seg_len, model_width), BF16),
        jnp.zeros(act_shape, BF16),
        tuple((jnp.zeros(mat.shape, jnp.float32) for mat in matrices)),
        jnp.zeros((2, model_width), jnp.float32),
    )
    unused_grads, unused_store, grad_mats, grad_gains = lax.fori_loop(
        0, micro_count + sections - 1, backward_step, back_state
    )
    grad_all = jnp.concatenate([to_blocks(mat, block_size) for mat in grad_mats], axis=0)
    summed_w, summed_g = lax.psum((grad_all, grad_gains), "dp")
    own_grad = lax.dynamic_slice_in_dim(summed_w, group_idx * own_blocks, own_blocks, 0)
    own_gain_grad = lax.dynamic_slice_in_dim(summed_g, group_idx * own_gain, own_gain, 1)
    own_square = jnp.sum(own_grad * own_grad) + jnp.sum(own_gain_grad * own_gain_grad)
    rows_local = jnp.zeros((sections, 3), jnp.float32).at[section_idx].set(sq_sums)
    total_square, loss_value, rows_total = lax.psum(
        (own_square, loss_sum / frame_count, rows_local), ("section", "dp")
    )
    grad_norm = jnp.sqrt(total_square)
    clip_limit = 0.00015 * math.sqrt(
        sections * (own_blocks * groups * block_size * block_size + 2 * model_width)
    )
    factor = clip_limit / jnp.maximum(grad_norm, clip_limit)
    grad_blocks = own_grad * factor
    square = (own_blocks, block_size, block_size)
    shaped = grad_blocks.reshape(square)
    highest = lax.Precision.HIGHEST
    l_new = 0.95 * l_stats[0].reshape(square) + 0.05 * jnp.einsum(
        "bij,bkj->bik", shaped, shaped, precision=highest
    )
    r_new = 0.95 * r_stats[0].reshape(square) + 0.05 * jnp.einsum(
        "bji,bjk->bik", shaped, shaped, precision=highest
    )
    left_side = jnp.einsum("bij,bjk->bik", l_roots[0].reshape(square), shaped, precision=highest)
    precond = jnp.einsum("bij,bjk->bik", left_side, r_roots[0].reshape(square), precision=highest)
    master = w_master[0]
    w_new = master - 0.5 * (precond.reshape(master.shape) + 0.01 * master)
    gain_grad = own_gain_grad * factor
    m_new = 0.9 * gain_m[0] + 0.1 * gain_grad
    v_new = 0.999 * gain_v[0] + 0.001 * gain_grad * gain_grad
    step_num = step_count[0].astype(jnp.float32)
    m_hat = m_new / (1.0 - jnp.power(0.9, step_num))
    v_hat = v_new / (1.0 - jnp.power(0.999, step_num))
    gains_new = norm_gains[0] - 0.5 * m_hat / (jnp.sqrt(v_hat) + 1e-08)
    rms = jnp.sqrt(rows_total[section_idx] / (frame_count * model_width)).reshape(1, 3)
    return (
        w_new[None],
        grad_blocks[None],
        l_new.reshape(master.shape)[None],
        r_new.reshape(master.shape)[None],
        gains_new[None],
        m_new[None],
        v_new[None],
        loss_value,
        grad_norm,
        rms,
    )


def layer_block(shape):
    return pl.BlockSpec((1,) + shape, lambda i: (i,) + (0,) * len(shape))


def whole_block(shape):
    return pl.BlockSpec(shape, lambda i: (0,) * len(shape))


def held_block(shape):
    return pl.BlockSpec(shape, lambda i: (0,) * len(shape), pipeline_mode=pl.Buffered(1))


def forward(layers, micro, valid_len, present_stems, x_in, targets, flat_w, gain):
    width = x_in.shape[1]
    seg = x_in.shape[0] // micro
    dim = width // HEADS
    part = width // 4
    half = layers // 2
    shapes = (
        (HEADS, seg, seg), (3, seg, width), (seg, width), (seg, width), (4, seg, width), (4, seg, width)
    )
    kinds = (BF16, BF16, BF16, F32, BF16, BF16)

    def slot():
        return jnp.minimum(lax.axis_index("section"), micro - 1)

    return pl.pallas_call(
        functools.partial(forward_kernel, layers, half, micro),
        grid=(layers,),
        in_specs=[
            pl.BlockSpec(memory_space=pltpu.SMEM),
            pl.BlockSpec(memory_space=pltpu.SMEM),
            pl.BlockSpec((seg, width), lambda i: (slot(), 0)),
            pl.BlockSpec((width // 2, seg), lambda i: (0, slot())),
            pl.BlockSpec(memory_space=pltpu.VMEM),
            pl.BlockSpec(memory_space=pltpu.VMEM),
        ],
        out_specs=[layer_block(s) for s in shapes]
        + [whole_block((layers, seg, width)), whole_block((seg, width)), whole_block((layers, 8, width))]
        + [pl.BlockSpec(memory_space=pl.ANY), whole_block((layers, 8, width))],
        out_shape=[jax.ShapeDtypeStruct((layers,) + s, k) for s, k in zip(shapes, kinds)]
        + [
            jax.ShapeDtypeStruct((layers, seg, width), BF16),
            jax.ShapeDtypeStruct((seg, width), F32),
            jax.ShapeDtypeStruct((layers, 8, width), F32),
            jax.ShapeDtypeStruct((layers, 48 * part, width), BF16),
            jax.ShapeDtypeStruct((layers, 8, width), F32),
        ],
        scratch_shapes=[
            pltpu.VMEM((seg, width), F32),
            pltpu.VMEM((layers, 48 * part, width), BF16),
            pltpu.VMEM((layers, 8, 8, 128), F32),
            pltpu.VMEM((6 * part, width), BF16),
            pltpu.VMEM((8, 128), F32),
            pltpu.VMEM((4, part, 128), F32),
            pltpu.SemaphoreType.DMA((2, 3)),
            pltpu.SemaphoreType.DMA((2, layers, 4)),
            pltpu.SemaphoreType.DMA((2, layers, 4)),
            pltpu.SemaphoreType.DMA((2, layers, 8)),
            pltpu.SemaphoreType.DMA((2, layers, 8)),
            pltpu.SemaphoreType.DMA((2, 10)),
            pltpu.SemaphoreType.DMA((layers,)),
        ],
        compiler_params=pltpu.CompilerParams(
            vmem_limit_bytes=VMEM_LIMIT, collective_id=0, has_side_effects=True
        ),
    )(valid_len, present_stems, x_in, targets.T, flat_w, gain)


def backward(layers, loss_grad, full_w, full_g, sent, saved, stats):
    seg, width = loss_grad.shape
    dim = width // HEADS
    part = width // 4
    half = layers // 2

    def from_end(array):
        shape = array.shape[1:]
        return pl.BlockSpec((1,) + shape, lambda i: (layers - 1 - i,) + (0,) * len(shape))

    return pl.pallas_call(
        functools.partial(backward_kernel, layers, half),
        grid=(layers,),
        in_specs=[
            held_block((seg, width)),
            from_end(full_w),
            from_end(full_g),
            held_block((layers, seg, width)),
        ]
        + [from_end(a) for a in saved]
        + [pl.BlockSpec(memory_space=pltpu.VMEM)],
        out_specs=[pl.BlockSpec(memory_space=pltpu.VMEM)] * 3,
        out_shape=[
            jax.ShapeDtypeStruct((6 * part, width), F32),
            jax.ShapeDtypeStruct((16, width), F32),
            jax.ShapeDtypeStruct((8, 128), F32),
        ],
        scratch_shapes=[
            pltpu.VMEM((layers, seg, width), BF16),
            pltpu.VMEM((seg, width), BF16),
            pltpu.VMEM((4, seg, width), BF16),
            pltpu.VMEM((seg, width), BF16),
            pltpu.VMEM((seg, width), F32),
            pltpu.VMEM((seg, width), BF16),
            pltpu.VMEM((seg, width), BF16),
            pltpu.VMEM((3, seg, width), BF16),
            pltpu.VMEM((layers, 8, width), F32),
            pltpu.VMEM((2, 4, 2, 576, width), BF16),
            pltpu.VMEM((2, 4, 2, 288, width), BF16),
            pltpu.VMEM((layers, 4, 2, 80, width), BF16),
            pltpu.VMEM((layers, 4, 208, width), BF16),
            pltpu.VMEM((layers, 4, 208, width), BF16),
            pltpu.VMEM((layers, 3, 208, width), BF16),
            pltpu.VMEM((3, 208, width), BF16),
            pltpu.VMEM((6, 16, width), F32),
            pltpu.VMEM((4, 16, width), F32),
            pltpu.VMEM((4, 8, 128), F32),
            pltpu.VMEM((8, 8, 128), F32),
            pltpu.SemaphoreType.DMA((2, 2, 2)),
            pltpu.SemaphoreType.DMA((2, layers, 4)),
            pltpu.SemaphoreType.DMA((2, layers, 4)),
            pltpu.SemaphoreType.DMA((2, layers, 3)),
            pltpu.SemaphoreType.DMA((2, layers)),
            pltpu.SemaphoreType.DMA((2, 3)),
            pltpu.SemaphoreType.DMA((2, 3)),
            pltpu.SemaphoreType.DMA((2, 3)),
            pltpu.SemaphoreType.DMA((2, 7)),
        ],
        compiler_params=pltpu.CompilerParams(
            vmem_limit_bytes=VMEM_LIMIT, collective_id=1, has_side_effects=True
        ),
    )(loss_grad, full_w, full_g, sent, *saved, stats)


def split(value):
    high = value.astype(BF16)
    return high, (value - high.astype(F32)).astype(BF16)


def dot_split(dot, left, right):
    return dot(left[0], right[0]) + (dot(left[0], right[1]) + dot(left[1], right[0]))


def update_kernel(
    layers, limit, length_ref, step_ref, square_ref, tile_ref, quads_ref, w_ref, l_ref, r_ref, lroot_ref, rroot_ref,
    gain_ref, gain_m_ref, gain_v_ref,
    w_out, grad_out, l_out, r_out, gain_out, m_out, v_out, loss_out, norm_out, rms_out,
    block_ref,
):
    part, width = quads_ref.shape[1:]
    gains = tile_ref[: 2 * layers]
    norm = jnp.sqrt(jnp.sum(square_ref[...], keepdims=True) + jnp.sum(gains * gains, keepdims=True))
    factor = limit / jnp.maximum(norm, limit)

    def quad_step(q, _):
        for c in range(4):
            base = 4 * q + c
            load_block(lroot_ref, base, block_ref.at[0])
            load_block(rroot_ref, base, block_ref.at[1])
            grad = quads_ref[q, :, part * c : part * (c + 1)] * factor
            pair = split(grad)
            left = dot_split(dot_nn, split(block_ref[0, :, :part]), pair)
            pre = dot_split(dot_nn, split(left), split(block_ref[1, :, :part]))
            for i, value in enumerate((
                grad, pre, dot_split(dot_nt, pair, pair), dot_split(dot_tn, pair, pair)
            )):
                block_ref[2 + i, :, :part] = value
            parts = [flat_parts(block_ref.at[2 + i]) for i in range(4)]
            for m in range(3):
                at = (pl.ds(base + 8 * m, 24, stride=24), slice(None))
                grad_out[at] = parts[0][m]
                master = w_ref[at]
                w_out[at] = master - 0.5 * (parts[1][m] + 0.01 * master)
                l_out[at] = 0.95 * l_ref[at] + 0.05 * parts[2][m]
                r_out[at] = 0.95 * r_ref[at] + 0.05 * parts[3][m]
        return 0

    lax.fori_loop(0, 2, quad_step, 0)

    @pl.when(pl.program_id(0) == 0)
    def _():
        section, group = lax.axis_index("section"), lax.axis_index("dp")
        share = gain_ref.shape[1]
        row = tile_ref[:2]
        for k in range(1, layers):
            row = jnp.where(section == k, tile_ref[2 * k : 2 * k + 2], row)
        own = row[:, :share]
        for g in range(1, width // share):
            own = jnp.where(group == g, row[:, g * share : (g + 1) * share], own)
        grad = own * factor
        m_new = 0.9 * gain_m_ref[...] + 0.1 * grad
        v_new = 0.999 * gain_v_ref[...] + 0.001 * grad * grad
        step = jnp.full((1, 1), step_ref[0], jnp.int32).astype(F32)
        m_hat = m_new / (1.0 - jnp.exp(step * math.log(0.9)))
        v_hat = v_new / (1.0 - jnp.exp(step * math.log(0.999)))
        gain_out[...] = gain_ref[...] - 0.5 * m_hat / (jnp.sqrt(v_hat) + 1e-08)
        m_out[...] = m_new
        v_out[...] = v_new
        norm_out[...] = norm
        frames = length_ref[0]
        for k in range(1, length_ref.shape[0]):
            frames = frames + length_ref[k]
        frames = jnp.full((1, 1), frames, jnp.int32).astype(F32)
        loss_out[...] = tile_ref[2 * layers : 2 * layers + 1, 3:4] / frames
        squares = tile_ref[2 * layers : 2 * layers + 1, :3]
        for k in range(1, layers):
            squares = jnp.where(section == k, tile_ref[2 * layers + k : 2 * layers + k + 1, :3], squares)
        rms_out[...] = jnp.sqrt(squares / (frames * width))


def update(layers, limit, valid_len, step_count, squares, tile, quads, flats, gains):
    blocks = 4 * quads.shape[0]
    part, width = quads.shape[1:]
    rows = flats[0].shape[0]
    whole = [pl.BlockSpec(memory_space=pltpu.VMEM)]
    flat = [pl.BlockSpec((rows // 3, 128), lambda i: (i, 0))]
    share = gains[0].shape
    return pl.pallas_call(
        functools.partial(update_kernel, layers, limit),
        grid=(3,),
        in_specs=[pl.BlockSpec(memory_space=pltpu.SMEM)] * 2 + whole * 2
        + [pl.BlockSpec((2, part, width), lambda i: (i, 0, 0))] + flat * 5 + whole * 3,
        out_specs=flat * 4 + whole * 6,
        out_shape=[jax.ShapeDtypeStruct((rows, 128), F32)] * 4
        + [jax.ShapeDtypeStruct(share, F32)] * 3
        + [jax.ShapeDtypeStruct((1, 1), F32)] * 2 + [jax.ShapeDtypeStruct((1, 3), F32)],
        scratch_shapes=[pltpu.VMEM((6, part, 128), F32)],
        compiler_params=pltpu.CompilerParams(vmem_limit_bytes=VMEM_LIMIT),
    )(valid_len, step_count, squares, tile, quads, *flats, *gains)


def body(
    x_in, targets, valid_len, present_stems, w_master, norm_gains, gain_m, gain_v,
    l_stats, r_stats, l_roots, r_roots, step_count,
):
    width = x_in.shape[1]
    part = width // 4
    layers = lax.axis_size("section")
    groups = lax.axis_size("dp")
    micro = valid_len.shape[0] // groups
    own_blocks = w_master.shape[1]
    flats = [flat_rows(a[0]) for a in (w_master, l_stats, r_stats, l_roots, r_roots)]
    *saved, sent, loss_grad, stats, full_w, full_g = forward(
        layers, micro, valid_len, present_stems, x_in, targets, flats[0], norm_gains[0]
    )
    own_quads, tile, squares = backward(layers, loss_grad, full_w, full_g, sent, saved, stats)
    clip_limit = 0.00015 * math.sqrt(layers * (own_blocks * groups * part * part + 2 * width))
    *news, gains_new, m_new, v_new, loss_value, grad_norm, rms = update(
        layers, clip_limit, valid_len, step_count, squares, tile, own_quads.reshape(-1, part, width), flats,
        (norm_gains[0], gain_m[0], gain_v[0]),
    )
    w_new, grad_blocks, l_new, r_new = (from_flat_rows(a, own_blocks)[None] for a in news)
    return (
        w_new,
        grad_blocks,
        l_new,
        r_new,
        gains_new[None],
        m_new[None],
        v_new[None],
        loss_value.reshape(()),
        grad_norm.reshape(()),
        rms,
    )


def solution(mesh):
    def step(*args):
        layers, groups = mesh.shape["section"], mesh.shape["dp"]
        micro, own_blocks = args[2].shape[0] // groups, args[4].shape[1]
        if micro <= layers == 4 and groups == 8 and own_blocks == 24:
            return body(*args)
        return pipelined_body(*args)

    block = P("section", "dp", None)
    gain = P("section", None, "dp")
    return jax.shard_map(
        step,
        mesh=mesh,
        in_specs=(
            P("dp", None), P("dp", None), P(), P(), block, gain, gain, gain, block, block, block, block, P(),
        ),
        out_specs=(block, block, block, block, gain, gain, gain, P(), P(), P("section", None)),
        check_vma=False,
    )
```

```python
import functools
import math

import jax
import jax.numpy as jnp
from jax import lax
from jax.experimental import pallas as pl
from jax.experimental.pallas import tpu as pltpu
from jax.sharding import PartitionSpec as P

HEADS = 8
F32 = jnp.float32
BF16 = jnp.bfloat16
VMEM_LIMIT = 61 * 1024 * 1024


def dot_nn(a, b):
    return lax.dot_general(a, b, (((1,), (0,)), ((), ())), preferred_element_type=F32)


def dot_nt(a, b):
    return lax.dot_general(a, b, (((1,), (1,)), ((), ())), preferred_element_type=F32)


def dot_tn(a, b):
    return lax.dot_general(a, b, (((0,), (0,)), ((), ())), preferred_element_type=F32)


def gelu_parts(x):
    ax = jnp.abs(x)
    bell = jnp.exp(-0.5 * x * x)
    t = 1.0 / (1.0 + (0.3275911 * 0.7071067811865476) * ax)
    poly = t * (
        0.5 * 0.254829592
        + t
        * (
            0.5 * -0.284496736
            + t * (0.5 * 1.421413741 + t * (0.5 * -1.453152027 + t * (0.5 * 1.061405429)))
        )
    )
    tail = poly * bell
    cdf = jnp.where(x >= 0.0, 1.0 - tail, tail)
    return x * cdf, cdf + x * bell * 0.3989422804014327


def stack_quads(w_ref, first, step, number):
    part = w_ref.shape[2] // 4
    if step == 1:
        return w_ref[0, first * part : (first + number) * part]
    return jnp.concatenate(
        [w_ref[0, (first + step * i) * part : (first + step * i + 1) * part] for i in range(number)], axis=0
    )


def flat_rows(array):
    blocks, area = array.shape
    return (
        array.reshape(blocks // 8, 8, area // 128, 128).transpose(0, 2, 1, 3).reshape(-1, 128)
    )


def from_flat_rows(rows, blocks):
    return (
        rows.reshape(blocks // 8, -1, 8, 128).transpose(0, 2, 1, 3).reshape(blocks, -1)
    )


def load_block(rows_ref, base, block_ref):
    lane = lax.broadcasted_iota(jnp.int32, (24, 128), 1)
    a, b, c = (rows_ref[pl.ds(base + 8 * m, 24, stride=24), :] for m in range(3))
    block_ref[pl.ds(0, 24, stride=4), :] = a
    block_ref[pl.ds(1, 24, stride=4), :] = jnp.where(lane < 32, pltpu.roll(a, 32, 1), pltpu.roll(b, 32, 1))
    block_ref[pl.ds(2, 24, stride=4), :] = jnp.where(lane < 64, pltpu.roll(b, 64, 1), pltpu.roll(c, 64, 1))
    block_ref[pl.ds(3, 24, stride=4), :] = pltpu.roll(c, 96, 1)


def flat_parts(block_ref):
    lane = lax.broadcasted_iota(jnp.int32, (24, 128), 1)
    a, b, c, d = (block_ref[pl.ds(r, 24, stride=4), :] for r in range(4))
    b, c, d = pltpu.roll(b, 96, 1), pltpu.roll(c, 64, 1), pltpu.roll(d, 32, 1)
    return jnp.where(lane < 96, a, b), jnp.where(lane < 64, b, c), jnp.where(lane < 32, c, d)


MESH = pl.DeviceIdType.MESH


def mesh_place():
    section = lax.axis_index("section")
    group = lax.axis_index("dp")
    core = lax.rem(section, 2)
    y = lax.rem(group, 2)
    z = group // 2
    z_peers = (z, z + 1 - 2 * lax.rem(z, 2), lax.rem(z + 2, 4), 3 - z)
    return section, group, core, y, z_peers


def remote(source, target, send_sem, recv_sem, section, group):
    return pltpu.make_async_remote_copy(
        src_ref=source, dst_ref=target, send_sem=send_sem, recv_sem=recv_sem,
        device_id=(section, group), device_id_type=MESH,
    )


def greet(places):
    barrier = pltpu.get_barrier_semaphore()
    for place in places:
        pl.semaphore_signal(barrier, inc=1, device_id=place, device_id_type=MESH)
    pl.semaphore_wait(barrier, len(places))


class Slabs:
    def __init__(self, rows):
        self.section, self.group, self.core, self.y, self.z_peers = mesh_place()
        self.x = self.section // 2
        self.rows, self.half = rows, rows // 2
        self.edge = self.half * 5 // 18
        self.slab = self.half - self.edge

    def slab_of(self, x, core):
        return pl.ds(pl.multiple_of(self.half * core + self.edge * x, 16), self.slab)

    def edge_of(self, x, core):
        return pl.ds(pl.multiple_of(self.half * core + self.slab * x, 16), self.edge)

    def half_of(self, core):
        return pl.ds(pl.multiple_of(self.half * core, 16), self.half)

    def x_peer(self):
        return lax.rem(self.section + 2, 4), self.group

    def y_peer(self):
        return self.section, self.group + 1 - 2 * self.y

    def z_peer(self, k):
        return self.section, self.z_peers[k] * 2 + self.y

    def core_peer(self):
        return self.section + 1 - 2 * self.core, self.group

    def greet_all(self):
        greet(
            [(lax.rem(self.section + k, 4), self.group) for k in range(1, 4)]
            + [(self.section, lax.rem(self.group + k, 8)) for k in range(1, 8)]
        )


class Gather(Slabs):
    def __init__(self, own_ref, gain_ref, w_ref, gains_ref, sems):
        super().__init__(own_ref.shape[0])
        self.own, self.gain, self.w, self.gains = own_ref, gain_ref, w_ref, gains_ref
        self.spread, self.z_sems, self.y_sems, self.x_sems, self.core_sems, self.gain_sems, self.local = sems
        self.others = [lax.rem(self.section + k, 4) for k in range(1, 4)]

    def chunk(self, k):
        y = self.y if k < 4 else 1 - self.y
        return self.z_peers[k % 4] * 2 + y

    def at(self, layer, group, rows):
        return self.w.at[layer, pl.ds(pl.multiple_of(group * self.rows + rows.start, 16), rows.size)]

    def spread_copy(self, k):
        peer = self.others[k]
        rows = self.slab_of(peer // 2, lax.rem(peer, 2))
        return remote(
            self.own.at[rows], self.at(self.section, self.group, rows),
            self.spread.at[0, k], self.spread.at[1, k], peer, self.group,
        )

    def spread_wait(self, layer):
        ref = self.at(layer, self.group, self.slab_of(self.x, self.core))
        for k in range(3):
            @pl.when(lax.rem(layer + k + 1, 4) == self.section)
            def _():
                remote(ref, ref, self.spread.at[0, k], self.spread.at[1, k], self.others[0], self.group).wait_recv()

    def z_copy(self, layer, k, landed=False):
        ref = self.at(layer, self.chunk(k) if landed else self.group, self.slab_of(self.x, self.core))
        return remote(ref, ref, self.z_sems.at[0, layer, k], self.z_sems.at[1, layer, k], *self.z_peer(k))

    def y_copy(self, layer, k, landed=False):
        ref = self.at(layer, self.chunk(k + 4 if landed else k), self.slab_of(self.x, self.core))
        return remote(ref, ref, self.y_sems.at[0, layer, k], self.y_sems.at[1, layer, k], *self.y_peer())

    def x_copy(self, layer, k, landed=False):
        ref = self.at(layer, self.chunk(k), self.edge_of(1 - self.x if landed else self.x, self.core))
        return remote(ref, ref, self.x_sems.at[0, layer, k], self.x_sems.at[1, layer, k], *self.x_peer())

    def core_copy(self, layer, k, landed=False):
        ref = self.at(layer, self.chunk(k), self.half_of(1 - self.core if landed else self.core))
        return remote(ref, ref, self.core_sems.at[0, layer, k], self.core_sems.at[1, layer, k], *self.core_peer())

    def gain_copy(self, k):
        if k < 7:
            peer = lax.rem(self.group + k + 1, 8)
            return remote(
                self.gain, self.gains.at[self.section, self.group],
                self.gain_sems.at[0, k], self.gain_sems.at[1, k], self.section, peer,
            )
        ref = self.gains.at[self.section]
        return remote(
            ref, ref, self.gain_sems.at[0, k], self.gain_sems.at[1, k], self.others[k - 7], self.group
        )

    def gain_landed(self, k):
        if k < 7:
            ref = self.gains.at[self.section, lax.rem(self.group - k - 1 + 8, 8)]
        else:
            ref = self.gains.at[lax.rem(self.section - (k - 6) + 4, 4)]
        return remote(ref, ref, self.gain_sems.at[0, k], self.gain_sems.at[1, k], self.section, self.group)

    def spread_own(self):
        for k in range(3):
            self.spread_copy(k).start()

    def begin(self):
        @pl.when(self.section == 0)
        def _():
            self.spread_own()

        for k in range(7):
            self.gain_copy(k).start()
        rows = self.slab_of(self.x, self.core)
        self.w[self.section, pl.ds(pl.multiple_of(self.group * self.rows + rows.start, 16), rows.size)] = self.own[rows]
        self.gains[self.section, self.group] = self.gain[...]

    def share_gains(self):
        for k in range(7):
            self.gain_landed(k).wait_recv()
        for k in range(7, 10):
            self.gain_copy(k).start()

    def wait_gains(self):
        for k in range(7, 10):
            self.gain_landed(k).wait_recv()

    def kick(self, layer):
        self.spread_wait(layer)
        for k in range(1, 4):
            self.z_copy(layer, k).start()
        self.y_copy(layer, 0).start()
        self.x_copy(layer, 0).start()

    def serve_z(self, layer, k):
        self.z_copy(layer, k, True).wait_recv()
        self.y_copy(layer, k).start()
        self.x_copy(layer, k).start()

    def serve_y(self, layer, k):
        self.y_copy(layer, k, True).wait_recv()
        self.x_copy(layer, k + 4).start()

    def serve_x(self, layer, k):
        self.x_copy(layer, k, True).wait_recv()
        self.core_copy(layer, k).start()

    def finish_first(self, layer):
        for k in range(8):
            @pl.when(self.z_peers[k % 4] == 0)
            def _():
                self.core_copy(layer, k, True).wait_recv()

    def finish_rest(self, layer):
        for k in range(8):
            @pl.when(self.z_peers[k % 4] != 0)
            def _():
                self.core_copy(layer, k, True).wait_recv()

    def end(self, layers):
        for k in range(3):
            self.spread_copy(k).wait_send()
        for k in range(10):
            self.gain_copy(k).wait_send()

        def per_layer(layer, _):
            for k in range(1, 4):
                self.z_copy(layer, k).wait_send()
            for k in range(4):
                self.y_copy(layer, k).wait_send()
            for k in range(8):
                self.x_copy(layer, k).wait_send()
                self.core_copy(layer, k).wait_send()
            return 0

        lax.fori_loop(0, layers, per_layer, 0)


def segment_info(micro, length_ref, stems_ref):
    section, group = lax.axis_index("section"), lax.axis_index("dp")
    at = group * micro + jnp.minimum(section, micro - 1)
    used = (section < micro).astype(jnp.int32)
    frames = length_ref[0]
    for k in range(1, length_ref.shape[0]):
        frames = frames + length_ref[k]
    return length_ref[at] * used, [stems_ref[at, k] * used for k in range(4)], frames


FIRST_POINTS = {"qkv": "z2 y1 x0 x1", "heads": "z3 x2 x4 x5", "attended": "y2", "ffn1": "x3", "ffn2": "y3 x6", "ffn3": "x7"}
POINTS = {"qkv": "x0 x1", "heads": "z3 x2 x4 x5", "attended": "y2", "ffn1": "x3", "ffn2": "y3 x6", "ffn3": "x7"}
AHEAD_POINTS = {"attended": "z1 y0", "ffn2": "z2", "ffn3": "y1"}


def forward_kernel(
    layers, half, micro, length_ref, stems_ref, x_ref, target_ref, flat_ref, raw_gain_ref,
    probs_ref, qkv_ref, att_ref, middle_ref, hidden_ref, slope_ref, sent_ref, loss_grad_ref, stats_ref,
    full_ref, gains_out_ref,
    out_ref, normed_ref, w_all_ref, gains_ref, own_ref, own_gain_ref, block_ref, *sems,
):
    seg, width = x_ref.shape
    dim = width // HEADS
    part = width // 4
    layer = pl.program_id(0)
    rows = 256
    chunks = seg // rows
    length, present_flags, frame_total = segment_info(micro, length_ref, stems_ref)
    gather = Gather(own_ref, own_gain_ref, w_all_ref, gains_ref, sems)
    w_ref = w_all_ref.at[pl.ds(layer, 1)]

    def own_step(q, _):
        for c in range(4):
            block = 4 * q + c
            load_block(flat_ref, (block // 8) * 576 + lax.rem(block, 8), block_ref.at[c])
        quad = jnp.concatenate([block_ref[c, :, :part] for c in range(4)], axis=1)
        own_ref[pl.ds(pl.multiple_of(q * part, part), part)] = quad.astype(BF16)
        return 0

    def keep_copy(index):
        return pltpu.make_async_copy(w_all_ref.at[index], full_ref.at[index], gather.local.at[index])

    @pl.when(layer == 0)
    def _():
        gather.greet_all()
        lax.fori_loop(0, flat_ref.shape[0] // 288, own_step, 0)
        own_gain_ref[...] = jnp.zeros_like(own_gain_ref)
        own_gain_ref[:2, : raw_gain_ref.shape[1]] = raw_gain_ref[...]
        gather.begin()
        sent_ref[0] = x_ref[...]
        stats_ref[...] = jnp.zeros_like(stats_ref)
        gather.kick(0)

        @pl.when(gather.section != 0)
        def _():
            gather.spread_own()

        gather.share_gains()
        gather.serve_z(0, 1)
        gather.serve_z(0, 2)
        gather.kick(1)
        gather.serve_x(0, 0)
        gather.serve_x(0, 1)
        gather.serve_z(0, 3)
        gather.wait_gains()
        gather.serve_y(0, 0)
        gather.serve_x(0, 2)
        gather.serve_y(0, 1)
        gather.serve_y(0, 2)
        gather.serve_x(0, 3)
        gather.serve_y(0, 3)
        for k in range(4, 8):
            gather.serve_x(0, k)
        gather.serve_z(1, 1)
        gather.serve_y(1, 0)

    @pl.when(layer + 2 < layers)
    def _():
        gather.kick(layer + 2)

    gather.finish_first(layer)
    more = layer + 1 < layers

    def serve(point):
        for here, steps, later in (
            (layer == 0, FIRST_POINTS.get(point, ""), ""),
            (layer > 0, POINTS.get(point, ""), ""),
            (layer >= 0, "", AHEAD_POINTS.get(point, "")),
        ):
            for names, back in ((steps, 1), (later, 2)):
                if names:
                    @pl.when((layer + back < layers) & here)
                    def _():
                        for name in names.split():
                            getattr(gather, "serve_" + name[0])(layer + back, int(name[1]))

    def stream_of(at):
        prev = sent_ref[layer, at].astype(F32)
        skip = sent_ref[jnp.maximum(layer + 1 - half, 0), at].astype(F32)
        return prev + jnp.where(layer >= half, skip, 0.0)

    def gain_row(which):
        return jnp.concatenate(
            [gains_ref[layer, g, which : which + 1, : width // 8] for g in range(8)], axis=1
        ).astype(BF16).astype(F32)

    gain_one = gain_row(0)
    gain_two = gain_row(1)
    gains_out_ref[layer, 0:1] = gain_one
    gains_out_ref[layer, 1:2] = gain_two

    first_stream = stream_of(slice(None))
    first_factor = lax.rsqrt(jnp.mean(first_stream * first_stream, axis=-1, keepdims=True) + 1e-06)
    first_normed = (first_stream * first_factor * gain_one).astype(BF16)
    for t in range(3):
        qkv_ref[0, t] = dot_nn(first_normed, stack_quads(w_ref, t, 3, 4)).astype(BF16)
    serve("qkv")
    frames = lax.broadcasted_iota(jnp.int32, (1, seg), 1)
    masking = jnp.where(frames < length, 0.0, -1e30).astype(F32)

    def head_step(h):
        queries, keys, values = (qkv_ref[0, t, :, h * dim : (h + 1) * dim] for t in range(3))
        scores = dot_nt(queries, keys) * dim ** (-0.5) + masking
        top = jnp.max(scores, axis=-1, keepdims=True)
        expd = jnp.exp(scores - top)
        probs = (expd * (1.0 / jnp.sum(expd, axis=-1, keepdims=True))).astype(BF16)
        probs_ref[0, h] = probs
        return dot_nn(probs, values).astype(BF16)

    def put_heads(first):
        heads = [head_step(h) for h in range(first, first + HEADS // 2)]
        att_ref[0, :, first * dim : (first + HEADS // 2) * dim] = jnp.concatenate(heads, axis=1)

    put_heads(0)
    serve("heads")
    put_heads(HEADS // 2)
    serve("attended")
    gather.finish_rest(layer)
    keep_copy(layer).start()

    valid = (lax.broadcasted_iota(jnp.int32, (seg, 1), 0) < length).astype(F32)

    def add_stat(k, value):
        stats_ref[layer, k : k + 1] = jnp.sum(valid * value * value, axis=0, keepdims=True)

    branch_attn = dot_nn(att_ref[0], stack_quads(w_ref, 12, 1, 4))
    stream = stream_of(slice(None))
    middle = stream + branch_attn
    middle_ref[0] = middle
    add_stat(0, stream)
    add_stat(1, branch_attn)
    factor = lax.rsqrt(jnp.mean(middle * middle, axis=-1, keepdims=True) + 1e-06)
    normed_ref[...] = (middle * factor * gain_two).astype(BF16)

    def ffn_step(c):
        pre_act = dot_nn(normed_ref[...], stack_quads(w_ref, 16 + c, 4, 4))
        hidden, slope = gelu_parts(pre_act)
        hidden = hidden.astype(BF16)
        hidden_ref[0, c] = hidden
        slope_ref[0, c] = slope.astype(BF16)
        part_sum = dot_nn(hidden, stack_quads(w_ref, 32 + 4 * c, 1, 4))
        out_ref[...] = part_sum if c == 0 else out_ref[...] + part_sum

    for c in range(4):
        ffn_step(c)
        if c < 3:
            serve(f"ffn{c}")
    branch_ffn = out_ref[...]
    add_stat(2, branch_ffn)
    output = middle_ref[0] + branch_ffn
    out_ref[...] = output

    @pl.when(layer + 1 < layers)
    def _():
        sent_ref[layer + 1] = out_ref[...].astype(BF16)

    serve("ffn3")

    @pl.when(layer == layers - 1)
    def _():
        bins = width // 8
        lane = lax.broadcasted_iota(jnp.int32, (1, width), 1)
        is_real = lax.rem(lane, 2 * bins) < bins
        stem = lane // (2 * bins)
        present = jnp.zeros((1, width), F32)
        for k in range(4):
            present = jnp.where(stem == k, present_flags[k].astype(F32), present)
        inverse = 1.0 / jnp.full((1, 1), frame_total, jnp.int32).astype(F32)

        def loss_step(i, _):
            at = pl.ds(pl.multiple_of(i * rows, rows), rows)
            output = out_ref[at]
            square = output * output
            other = jnp.where(
                is_real, pltpu.roll(square, width - bins, 1), pltpu.roll(square, bins, 1)
            )
            magnitude = jnp.sqrt(square + other + 0.01)
            goal = target_ref[:, at].T
            goal = jnp.concatenate(
                [goal[:, (k // 2) * bins : (k // 2 + 1) * bins] for k in range(8)], axis=1
            )
            differ = magnitude - goal
            smooth = jnp.sqrt(differ * differ + 0.01)
            valid = (lax.broadcasted_iota(jnp.int32, (rows, 1), 0) + i * rows < length).astype(F32)
            weight = valid * present
            loss_grad_ref[at] = weight * differ * output * inverse / (smooth * magnitude)
            stats_ref[0, 3:4] += jnp.sum(
                jnp.where(is_real, weight * smooth, 0.0), axis=0, keepdims=True
            )
            return 0

        lax.fori_loop(0, chunks, loss_step, 0)
        gather.end(layers)
        for k in range(layers):
            keep_copy(k).wait()


class Scatter(Slabs):
    PARTS = ((3, 4), (1, 3), (0, 1))

    def __init__(self, refs, sems):
        self.grads, self.core_in, self.x_in, self.y_in, self.stage, self.z_in, self.last_in = refs
        super().__init__(self.grads.shape[3])
        self.core_sems, self.x_sems, self.y_sems, self.z_sems, self.last_sems = sems
        self.mine = self.slab_of(self.x, self.core)
        self.z = self.z_peers[0]

    def core_copy(self, layer, number):
        slot = lax.rem(layer, 2)
        first, last = self.PARTS[number]
        zs = pl.ds(first, last - first)
        return remote(
            self.grads.at[slot, zs, :, self.half_of(1 - self.core)], self.core_in.at[slot, zs],
            self.core_sems.at[0, slot, number], self.core_sems.at[1, slot, number], *self.core_peer(),
        )

    def x_copy(self, layer, z):
        slot = lax.rem(layer, 2)
        return remote(
            self.grads.at[slot, z, :, self.edge_of(1 - self.x, self.core)], self.x_in.at[layer, z],
            self.x_sems.at[0, layer, z], self.x_sems.at[1, layer, z], *self.x_peer(),
        )

    def y_copy(self, layer, z):
        slot = lax.rem(layer, 2)
        return remote(
            self.grads.at[slot, z, 1 - self.y, self.mine], self.y_in.at[layer, z],
            self.y_sems.at[0, layer, z], self.y_sems.at[1, layer, z], *self.y_peer(),
        )

    def z_copy(self, layer, z):
        place = jnp.maximum(self.z_peers[z] - 1, 0)
        return remote(
            self.stage.at[layer, z], self.z_in.at[layer, place],
            self.z_sems.at[0, layer, z], self.z_sems.at[1, layer, place], self.section, z * 2 + self.y,
        )

    def z_landed(self, layer, place):
        ref = self.z_in.at[layer, place]
        return remote(ref, ref, self.z_sems.at[0, layer, 0], self.z_sems.at[1, layer, place], *self.z_peer(place + 1))

    def last_copy(self, layer):
        place = jnp.maximum(lax.rem(self.section - layer + 4, 4) - 1, 0)
        return remote(
            self.stage.at[layer, self.z], self.last_in.at[place],
            self.last_sems.at[0, layer], self.last_sems.at[1, place], layer, self.group,
        )

    def last_landed(self, place):
        return remote(
            self.last_in.at[place], self.last_in.at[place],
            self.last_sems.at[0, 0], self.last_sems.at[1, place], self.section, self.group,
        )

    def add_core(self, layer, number):
        slot = lax.rem(layer, 2)
        self.core_copy(layer, number).wait_recv()
        rows = self.half_of(self.core)
        first, last = self.PARTS[number]

        def add(i, _):
            z, y = i // 2, lax.rem(i, 2)
            self.grads[slot, z, y, rows] = self.grads[slot, z, y, rows] + self.core_in[slot, z, y]
            return 0

        lax.fori_loop(2 * first, 2 * last, add, 0)
        for z in range(first, last):
            self.x_copy(layer, z).start()

    def add_x(self, layer, z):
        slot = lax.rem(layer, 2)
        self.x_copy(layer, z).wait_recv()
        rows = self.edge_of(self.x, self.core)
        inner = pl.ds(pl.multiple_of((self.slab - self.edge) * self.x, 16), self.edge)
        self.grads[slot, z, 1 - self.y, rows] = (
            self.grads[slot, z, 1 - self.y, rows] + self.x_in[layer, z, 1 - self.y]
        )
        self.y_copy(layer, z).start()
        self.stage[layer, z] = self.grads[slot, z, self.y, self.mine]
        self.stage[layer, z, inner] = self.stage[layer, z, inner] + self.x_in[layer, z, self.y]

    def add_y(self, layer, z):
        self.y_copy(layer, z).wait_recv()
        self.stage[layer, z] = self.stage[layer, z] + self.y_in[layer, z]

        @pl.when(self.z != z)
        def _():
            self.z_copy(layer, z).start()

    def add_z(self, layer, result_ref):
        for place in range(3):
            self.z_landed(layer, place).wait_recv()
        total = self.stage[layer, self.z].astype(F32)
        for k in range(3):
            total = total + self.z_in[layer, k].astype(F32)

        @pl.when(layer == self.section)
        def _():
            result_ref[...] = jnp.zeros_like(result_ref)
            result_ref[self.mine] = total

        @pl.when(layer != self.section)
        def _():
            self.stage[layer, self.z] = total.astype(BF16)
            self.last_copy(layer).start()

    def wait_sends(self, layer, last):
        for number in (2,) if last else (0, 1):
            self.core_copy(layer, number).wait_send()
        for z in (0, 1) if last else (2, 3):
            self.x_copy(layer, z).wait_send()
            self.y_copy(layer, z).wait_send()

    def end(self, layers):
        def per_layer(layer, _):
            for z in range(4):
                @pl.when(self.z != z)
                def _():
                    self.z_copy(layer, z).wait_send()

            @pl.when(layer != self.section)
            def _():
                self.last_copy(layer).wait_send()

            return 0

        lax.fori_loop(0, layers, per_layer, 0)

    def collect(self, result_ref):
        for place in (0, 2, 1):
            self.last_landed(place).wait_recv()
            peer = lax.rem(self.section + place + 1, 4)
            rows = self.slab_of(peer // 2, lax.rem(peer, 2))
            result_ref[rows] = result_ref[rows] + self.last_in[place].astype(F32)


class Totals:
    def __init__(self, refs, sems):
        self.stage_in, self.z_in, self.norm_section, self.norm_group = refs
        self.stage_sems, self.z_sems, self.section_sems, self.group_sems = sems
        self.section, self.group, self.core, self.y, self.z_peers = mesh_place()

    def stage_copy(self, k):
        peer = (
            (self.section + 1 - 2 * self.core, self.group),
            (self.section, self.group + 1 - 2 * self.y),
            (lax.rem(self.section + 2, 4), self.group),
        )[k]
        return remote(
            self.stage_in.at[2 * k], self.stage_in.at[2 * k + 1],
            self.stage_sems.at[0, k], self.stage_sems.at[1, k], *peer,
        )

    def z_copy(self, k):
        z = self.z_peers[0]
        return remote(
            self.z_in.at[z], self.z_in.at[z], self.z_sems.at[0, k - 1], self.z_sems.at[1, k - 1],
            self.section, self.z_peers[k] * 2 + self.y,
        )

    def z_landed(self, k):
        z = self.z_peers[k]
        return remote(
            self.z_in.at[z], self.z_in.at[z], self.z_sems.at[0, k - 1], self.z_sems.at[1, k - 1],
            self.section, self.z_peers[k] * 2 + self.y,
        )

    def begin(self, tile):
        self.stage_in[0] = tile
        self.stage_copy(0).start()

    def after_core(self):
        self.stage_copy(0).wait_recv()
        self.stage_in[2] = self.stage_in[0] + self.stage_in[1]
        self.stage_copy(1).start()

    def after_y(self):
        self.stage_copy(1).wait_recv()
        self.z_in[self.z_peers[0]] = self.stage_in[2] + self.stage_in[3]
        for k in range(1, 4):
            self.z_copy(k).start()

    def after_z(self):
        for k in range(1, 4):
            self.z_landed(k).wait_recv()
        self.stage_in[4] = self.z_in[0] + self.z_in[1] + self.z_in[2] + self.z_in[3]
        self.stage_copy(2).start()

    def after_x(self):
        self.stage_copy(2).wait_recv()
        return self.stage_in[4] + self.stage_in[5]

    def norm_copy(self, k):
        if k < 3:
            peer = (lax.rem(self.section + k + 1, 4), self.group)
            ref = self.norm_section.at[self.section]
            return remote(ref, ref, self.section_sems.at[0, k], self.section_sems.at[1, k], *peer)
        k = k - 3
        peer = (self.section, lax.rem(self.group + k + 1, 8))
        ref = self.norm_group.at[self.group]
        return remote(ref, ref, self.group_sems.at[0, k], self.group_sems.at[1, k], *peer)

    def norm_landed(self, k):
        if k < 3:
            ref = self.norm_section.at[lax.rem(self.section - k - 1 + 4, 4)]
            return remote(
                ref, ref, self.section_sems.at[0, k], self.section_sems.at[1, k], self.section, self.group
            )
        k = k - 3
        ref = self.norm_group.at[lax.rem(self.group - k - 1 + 8, 8)]
        return remote(ref, ref, self.group_sems.at[0, k], self.group_sems.at[1, k], self.section, self.group)

    def norm(self, value):
        self.norm_section[self.section] = value
        for k in range(3):
            self.norm_copy(k).start()
        for k in range(3):
            self.norm_landed(k).wait_recv()
        total = self.norm_section[0]
        for k in range(1, 4):
            total = total + self.norm_section[k]
        self.norm_group[self.group] = total
        for k in range(3, 10):
            self.norm_copy(k).start()
        for k in range(3, 10):
            self.norm_landed(k).wait_recv()
        total = self.norm_group[0]
        for k in range(1, 8):
            total = total + self.norm_group[k]
        return total

    def end(self):
        for k in range(3):
            self.stage_copy(k).wait_send()
        for k in range(1, 4):
            self.z_copy(k).wait_send()
        for k in range(10):
            self.norm_copy(k).wait_send()


def norm_reverse(value, gain, grad):
    factor = lax.rsqrt(jnp.mean(value * value, axis=-1, keepdims=True) + 1e-06)
    scaled = grad * gain
    mean = jnp.mean(value * scaled, axis=-1, keepdims=True)
    unit = value * factor
    back = factor * scaled - unit * (factor * factor * mean)
    return back, jnp.sum(grad * unit, axis=0, keepdims=True), (unit * gain).astype(BF16)


def backward_kernel(
    layers, half, loss_grad_ref, w_ref, gain_ref, sent_ref,
    probs_ref, qkv_ref, att_ref, middle_ref, hidden_ref, slope_ref, stats_ref,
    result_ref, totals_ref, square_ref,
    sends_ref, dffn_ref, dpre_ref, normed_ref, dmid_ref, datt_ref, dhold_ref, dqkv_ref,
    gain_grad_ref, *comm_refs,
):
    seg, width = loss_grad_ref.shape
    dim = width // HEADS
    part = width // 4
    layer = layers - 1 - pl.program_id(0)
    rows = 256
    chunks = seg // rows
    gain_one = gain_ref[0, 0:1]
    gain_two = gain_ref[0, 1:2]
    scatter = Scatter(comm_refs[:7], comm_refs[11:16])
    totals = Totals(comm_refs[7:11], comm_refs[16:])
    grads_ref = comm_refs[0]
    slot = lax.rem(layer, 2)

    @pl.when(layer == layers - 1)
    def _():
        scatter.greet_all()
        sends_ref[...] = jnp.zeros_like(sends_ref)
        gain_grad_ref[...] = jnp.zeros_like(gain_grad_ref)

    def put_grad(first, step, value):
        for r in range(4):
            quad = first + step * r
            owner = quad // 6
            at = pl.ds(pl.multiple_of(lax.rem(quad, 6) * part, part), part)
            grads_ref[slot, owner // 2, lax.rem(owner, 2), at] = value[r * part : (r + 1) * part].astype(BF16)

    def serve(back, here, *steps):
        @pl.when((layer + back < layers) & here)
        def _():
            for kind, *args in steps:
                getattr(scatter, kind)(layer + back, *args)

    serve(2, True, ("wait_sends", False))
    later = sends_ref[jnp.minimum(layer + 1, layers - 1)].astype(F32)
    skip = sends_ref[jnp.minimum(layer + half, layers - 1)].astype(F32)
    dmid_ref[...] = jnp.where(
        layer == layers - 1, loss_grad_ref[...], later + jnp.where(layer + half < layers, skip, 0.0)
    )
    dffn_ref[...] = dmid_ref[...].astype(BF16)
    for c in range(4):
        put_grad(32 + 4 * c, 1, dot_tn(hidden_ref[0, c], dffn_ref[...]))
    scatter.core_copy(layer, 0).start()

    def ffn_step(i, _):
        at = pl.ds(pl.multiple_of(i * rows, rows), rows)
        dffn = dffn_ref[at]
        dnormed = jnp.zeros((rows, width), F32)
        for c in range(4):
            dhidden = dot_nt(dffn, stack_quads(w_ref, 32 + 4 * c, 1, 4))
            dpre = (dhidden * slope_ref[0, c, at].astype(F32)).astype(BF16)
            dpre_ref[c, at] = dpre
            dnormed = dnormed + dot_nt(dpre, stack_quads(w_ref, 16 + c, 4, 4))
        back, gain_grad, normed = norm_reverse(middle_ref[0, at], gain_two, dnormed)
        gain_grad_ref[layer, 1:2] += gain_grad
        normed_ref[at] = normed
        dmid = dmid_ref[at] + back
        dmid_ref[at] = dmid
        datt = dmid.astype(BF16)
        datt_ref[at] = datt
        dattended = dot_nt(datt, stack_quads(w_ref, 12, 1, 4)).astype(BF16)
        dhold_ref[at] = dattended

        serve(1, i == 1, ("add_y", 3), ("add_x", 1), ("add_core", 2))
        serve(2, i == 1, ("add_y", 0))
        return 0

    lax.fori_loop(0, chunks, ffn_step, 0)

    serve(2, True, ("wait_sends", True))

    def ffn_grad_step(c, _):
        put_grad(16 + c, 4, dot_tn(normed_ref[...], dpre_ref[c]))
        return 0

    for c in range(4):
        ffn_grad_step(c, 0)
    put_grad(12, 1, dot_tn(att_ref[0], datt_ref[...]))
    scatter.core_copy(layer, 1).start()
    scatter.add_core(layer, 0)
    serve(1, True, ("add_x", 2))

    def head_step(h):
        queries, keys, values = (qkv_ref[0, t, :, h * dim : (h + 1) * dim] for t in range(3))
        probs = probs_ref[0, h]
        dhold = dhold_ref[:, h * dim : (h + 1) * dim]
        dprobs = dot_nt(dhold, values)
        wide = probs.astype(F32)
        dot_sum = jnp.sum(wide * dprobs, axis=-1, keepdims=True)
        dscores = (wide * (dprobs - dot_sum)).astype(BF16)
        return (
            (dot_nn(dscores, keys) * dim ** (-0.5)).astype(BF16),
            (dot_tn(dscores, queries) * dim ** (-0.5)).astype(BF16),
            dot_tn(probs, dhold).astype(BF16),
        )

    def put_heads(first, parts):
        for t in range(3):
            dqkv_ref[t, :, first * dim : (first + len(parts)) * dim] = jnp.concatenate([p[t] for p in parts], axis=1)

    put_heads(0, [head_step(h) for h in range(HEADS // 2)])
    scatter.add_core(layer, 1)
    serve(1, True, ("add_x", 0))

    put_heads(HEADS // 2, [head_step(h) for h in range(HEADS // 2, HEADS)])
    scatter.add_x(layer, 3)
    serve(1, True, ("add_y", 1))

    def qkv_step(i, _):
        at = pl.ds(pl.multiple_of(i * rows, rows), rows)
        dnormed = jnp.zeros((rows, width), F32)
        for t in range(3):
            dnormed = dnormed + dot_nt(dqkv_ref[t, at], stack_quads(w_ref, t, 3, 4))
        prev = sent_ref[layer, at].astype(F32)
        skip = sent_ref[jnp.maximum(layer + 1 - half, 0), at].astype(F32)
        stream = prev + jnp.where(layer >= half, skip, 0.0)
        back, gain_grad, normed = norm_reverse(stream, gain_one, dnormed)
        gain_grad_ref[layer, 0:1] += gain_grad
        normed_ref[at] = normed
        sends_ref[layer, at] = (dmid_ref[at] + back).astype(BF16)
        return 0

    lax.fori_loop(0, chunks, qkv_step, 0)

    def qkv_grad_step(t, _):
        put_grad(t, 3, dot_tn(normed_ref[...], dqkv_ref[t]))
        return 0

    for t in range(3):
        qkv_grad_step(t, 0)
    scatter.core_copy(layer, 2).start()
    serve(1, True, ("add_y", 2))
    serve(2, True, ("add_z", result_ref))

    @pl.when(layer == 0)
    def _():
        lane = lax.broadcasted_iota(jnp.int32, (1, width), 1)
        rows_out = [gain_grad_ref[k // 2, k % 2 : k % 2 + 1] for k in range(2 * layers)]
        for k in range(layers):
            row = jnp.zeros((1, width), F32)
            for i in range(4):
                value = jnp.sum(stats_ref[k, i : i + 1], axis=1, keepdims=True)
                row = jnp.where(lane == i, value, row)
            rows_out.append(row)
        rows_out.append(jnp.zeros((16 - 3 * layers, width), F32))
        totals.begin(jnp.concatenate(rows_out, axis=0))
        scatter.add_y(0, 3)
        scatter.add_x(0, 1)
        scatter.add_core(0, 2)
        scatter.add_y(1, 0)
        totals.after_core()
        scatter.add_x(0, 2)
        scatter.add_x(0, 0)
        totals.after_y()
        scatter.add_y(0, 1)
        scatter.add_y(0, 2)
        scatter.add_y(0, 0)
        scatter.add_z(1, result_ref)
        scatter.add_z(0, result_ref)
        totals.after_z()
        scatter.collect(result_ref)
        square = jnp.zeros((8, width), F32)
        for q in range(6):
            value = result_ref[q * part : (q + 1) * part]
            square = square + jnp.sum((value * value).reshape(part // 8, 8, width), axis=0)
        folded = square[:, :128] + square[:, 128:256] + square[:, 256:]
        square_ref[...] = totals.norm(folded)
        totals_ref[...] = totals.after_x()
        for back in (1, 0):
            for last in (False, True):
                scatter.wait_sends(back, last)
        scatter.end(layers)
        totals.end()


FF = 1536


def from_behind(value, axis, by):
    peers = lax.axis_size(axis)
    pairs = [(i, i + by) for i in range(peers) if 0 <= i + by < peers]
    return lax.ppermute(value, axis, pairs)


def unblock(blocks, row_count, col_count, block_size):
    return (
        blocks.reshape(row_count // block_size, col_count // block_size, block_size, block_size)
        .transpose(0, 2, 1, 3)
        .reshape(row_count, col_count)
    )


def to_blocks(matrix, block_size):
    row_count, col_count = matrix.shape
    return (
        matrix.reshape(row_count // block_size, block_size, col_count // block_size, block_size)
        .transpose(0, 2, 1, 3)
        .reshape(-1, block_size * block_size)
    )


def split_matrices(blocks, model_width):
    block_size = model_width // 4
    shapes = (
        (model_width, 3 * model_width),
        (model_width, model_width),
        (model_width, FF),
        (FF, model_width),
    )
    result = []
    offset = 0
    for row_count, col_count in shapes:
        number = row_count * col_count // (block_size * block_size)
        result.append(unblock(blocks[offset : offset + number], row_count, col_count, block_size))
        offset = offset + number
    return result


def rms_norm(stream, gain):
    factor = lax.rsqrt(jnp.mean(stream * stream, axis=-1, keepdims=True) + 1e-06)
    return (stream * factor * gain, factor)


def norm_back(stream, factor, gain, grad):
    scaled = grad * gain
    grad_in = factor * scaled - stream * factor**3 * jnp.mean(
        stream * scaled, axis=-1, keepdims=True
    )
    return (grad_in, jnp.sum(grad * stream * factor, axis=0))


def gelu_slope(pre_act):
    return (
        0.5 * (1.0 + lax.erf(pre_act * 0.7071067811865476))
        + pre_act * jnp.exp(-0.5 * pre_act * pre_act) * 0.3989422804014327
    )


def layer_forward(stream, matrices, gain_pair, length):
    w_qkv, w_out, w_up, w_down = matrices
    row_count, model_width = stream.shape
    head_dim = model_width // HEADS
    frames = jnp.arange(row_count)
    norm_one, scale_one = rms_norm(stream, gain_pair[0])
    normed = norm_one.astype(BF16)
    qkv_all = jnp.dot(normed, w_qkv, preferred_element_type=jnp.float32).astype(BF16)
    queries = qkv_all[:, :model_width].reshape(row_count, HEADS, head_dim)
    key_rows = qkv_all[:, model_width : 2 * model_width].reshape(row_count, HEADS, head_dim)
    value_rows = qkv_all[:, 2 * model_width :].reshape(row_count, HEADS, head_dim)
    masking = jnp.where(frames < length, 0.0, -1e30).astype(jnp.float32)
    scores = jnp.einsum(
        "qhe,khe->hqk", queries, key_rows, preferred_element_type=jnp.float32
    ) * head_dim ** (-0.5)
    attn_probs = jax.nn.softmax(scores + masking[None, None, :], axis=-1)
    probs_low = attn_probs.astype(BF16)
    attended = (
        jnp.einsum("hqk,khe->qhe", probs_low, value_rows, preferred_element_type=jnp.float32)
        .reshape(row_count, model_width)
        .astype(BF16)
    )
    branch_attn = jnp.dot(attended, w_out, preferred_element_type=jnp.float32)
    middle = stream + branch_attn
    norm_two, scale_two = rms_norm(middle, gain_pair[1])
    normed_two = norm_two.astype(BF16)
    pre_act = jnp.dot(normed_two, w_up, preferred_element_type=jnp.float32)
    hidden = jax.nn.gelu(pre_act, approximate=False).astype(BF16)
    branch_ffn = jnp.dot(hidden, w_down, preferred_element_type=jnp.float32)
    kept_vals = (
        scale_one,
        normed,
        queries,
        key_rows,
        value_rows,
        attn_probs,
        probs_low,
        attended,
        middle,
        scale_two,
        normed_two,
        pre_act,
        hidden,
    )
    return (middle + branch_ffn, branch_attn, branch_ffn, kept_vals)


def layer_backward(stream, matrices, gain_pair, length, upstream):
    w_qkv, w_out, w_up, w_down = matrices
    row_count, model_width = stream.shape
    head_dim = model_width // HEADS
    output, branch_attn, branch_ffn, kept_vals = layer_forward(stream, matrices, gain_pair, length)
    (
        scale_one,
        normed,
        queries,
        key_rows,
        value_rows,
        attn_probs,
        probs_low,
        attended,
        middle,
        scale_two,
        normed_two,
        pre_act,
        hidden,
    ) = kept_vals
    grad_ffn = upstream.astype(BF16)
    grad_down = jnp.dot(hidden.T, grad_ffn, preferred_element_type=jnp.float32)
    grad_hidden = jnp.dot(grad_ffn, w_down.T, preferred_element_type=jnp.float32)
    grad_pre = (grad_hidden * gelu_slope(pre_act)).astype(BF16)
    grad_up = jnp.dot(normed_two.T, grad_pre, preferred_element_type=jnp.float32)
    back_mid, gain_two = norm_back(
        middle,
        scale_two,
        gain_pair[1],
        jnp.dot(grad_pre, w_up.T, preferred_element_type=jnp.float32),
    )
    grad_mid = upstream + back_mid
    grad_branch = grad_mid.astype(BF16)
    grad_out = jnp.dot(attended.T, grad_branch, preferred_element_type=jnp.float32)
    grad_att = (
        jnp.dot(grad_branch, w_out.T, preferred_element_type=jnp.float32)
        .astype(BF16)
        .reshape(row_count, HEADS, head_dim)
    )
    grad_value = jnp.einsum("hqk,qhe->khe", probs_low, grad_att, preferred_element_type=jnp.float32)
    grad_probs = jnp.einsum(
        "qhe,khe->hqk", grad_att, value_rows, preferred_element_type=jnp.float32
    )
    grad_scores = (
        attn_probs * (grad_probs - jnp.sum(attn_probs * grad_probs, axis=-1, keepdims=True))
    ).astype(BF16)
    grad_query = jnp.einsum(
        "hqk,khe->qhe", grad_scores, key_rows, preferred_element_type=jnp.float32
    ) * head_dim ** (-0.5)
    grad_key = jnp.einsum(
        "hqk,qhe->khe", grad_scores, queries, preferred_element_type=jnp.float32
    ) * head_dim ** (-0.5)
    grad_qkv = jnp.concatenate(
        [
            grad_query.reshape(row_count, model_width),
            grad_key.reshape(row_count, model_width),
            grad_value.reshape(row_count, model_width),
        ],
        axis=1,
    ).astype(BF16)
    grad_wqkv = jnp.dot(normed.T, grad_qkv, preferred_element_type=jnp.float32)
    back_in, gain_one = norm_back(
        stream,
        scale_one,
        gain_pair[0],
        jnp.dot(grad_qkv, w_qkv.T, preferred_element_type=jnp.float32),
    )
    return (
        grad_mid + back_in,
        (grad_wqkv, grad_out, grad_up, grad_down),
        jnp.stack([gain_one, gain_two]),
    )


def spectral_terms(output, target, length, present_row, frame_count):
    row_count, model_width = output.shape
    bin_count = model_width // 8
    spectra = output.reshape(row_count, 4, 2, bin_count)
    real_part = spectra[:, :, 0]
    imag_part = spectra[:, :, 1]
    magnitude = jnp.sqrt(real_part * real_part + imag_part * imag_part + 0.01)
    differ = magnitude - target.reshape(row_count, 4, bin_count)
    smooth_err = jnp.sqrt(differ * differ + 0.01)
    weight = (jnp.arange(row_count) < length).astype(jnp.float32)[:, None, None] * present_row[
        None, :, None
    ]
    loss_slope = weight * differ / smooth_err / magnitude / frame_count
    grad_spec = jnp.stack([loss_slope * real_part, loss_slope * imag_part], axis=2).reshape(
        row_count, model_width
    )
    return (jnp.sum(smooth_err * weight), grad_spec)


def pipelined_body(
    x_in,
    targets,
    valid_len,
    present_stems,
    w_master,
    norm_gains,
    gain_m,
    gain_v,
    l_stats,
    r_stats,
    l_roots,
    r_roots,
    step_count,
):
    model_width = x_in.shape[1]
    block_size = model_width // 4
    sections = lax.axis_size("section")
    section_idx = lax.axis_index("section")
    half_way = sections // 2
    groups = lax.axis_size("dp")
    group_idx = lax.axis_index("dp")
    micro_count = valid_len.shape[0] // groups
    seg_len = x_in.shape[0] // micro_count
    own_blocks = w_master.shape[1]
    own_gain = norm_gains.shape[2]
    full_w, full_g = (
        lax.all_gather(w_master.astype(BF16), "dp", axis=1, tiled=True),
        lax.all_gather(norm_gains.astype(BF16), "dp", axis=2, tiled=True),
    )
    matrices = split_matrices(full_w[0], model_width)
    gain_pair = full_g[0].astype(jnp.float32)
    lengths = lax.dynamic_slice_in_dim(valid_len, group_idx * micro_count, micro_count)
    stem_flags = lax.dynamic_slice_in_dim(
        present_stems, group_idx * micro_count, micro_count
    ).astype(jnp.float32)
    frame_count = jnp.sum(valid_len).astype(jnp.float32)
    decoder = section_idx >= half_way
    encoder = section_idx < half_way
    is_last = section_idx == sections - 1
    act_shape = (micro_count, seg_len, model_width)

    def forward_step(step_idx, loop_state):
        in_rows, kept_prev, skip_store, loss_grads, loss_sum, sq_sums = loop_state
        micro_idx = step_idx - section_idx
        active = (micro_idx >= 0) & (micro_idx < micro_count)
        slot_idx = jnp.clip(micro_idx, 0, micro_count - 1)
        fresh_rows = lax.dynamic_slice_in_dim(x_in, slot_idx * seg_len, seg_len, 0)
        previous = jnp.where(section_idx == 0, fresh_rows, in_rows)
        stream = previous.astype(jnp.float32) + jnp.where(
            decoder, skip_store[slot_idx].astype(jnp.float32), 0.0
        )
        length = lengths[slot_idx]
        target = lax.dynamic_slice_in_dim(targets, slot_idx * seg_len, seg_len, 0)

        def forward_compute_fn(operand):
            output, branch_attn, branch_ffn, kept_vals = layer_forward(
                stream, matrices, gain_pair, length
            )
            valid = (jnp.arange(seg_len) < length).astype(jnp.float32)[:, None]
            squares = jnp.stack(
                [
                    jnp.sum(valid * stream * stream),
                    jnp.sum(valid * branch_attn * branch_attn),
                    jnp.sum(valid * branch_ffn * branch_ffn),
                ]
            )
            seg_loss, grad_spec = spectral_terms(
                output, target, length, stem_flags[slot_idx], frame_count
            )
            return (output, squares, seg_loss, grad_spec)

        def forward_spare_fn(operand):
            empty = jnp.zeros((seg_len, model_width), jnp.float32)
            return (empty, jnp.zeros((3,), jnp.float32), jnp.zeros((), jnp.float32), empty)

        output, squares, seg_loss, grad_spec = lax.cond(
            active, forward_compute_fn, forward_spare_fn, 0
        )
        kept_prev = kept_prev.at[slot_idx].set(jnp.where(active, previous, kept_prev[slot_idx]))
        loss_grads = loss_grads.at[slot_idx].set(
            jnp.where(active & is_last, grad_spec, loss_grads[slot_idx])
        )
        loss_sum = loss_sum + jnp.where(is_last, seg_loss, 0.0)
        sq_sums = sq_sums + squares
        sent_rows = output.astype(BF16)
        in_rows = from_behind(sent_rows, "section", 1)
        from_encoder = from_behind(sent_rows, "section", half_way)
        recv_idx = step_idx - section_idx + half_way
        usable = decoder & (recv_idx >= 0) & (recv_idx < micro_count)
        recv_slot = jnp.clip(recv_idx, 0, micro_count - 1)
        skip_store = skip_store.at[recv_slot].set(
            jnp.where(usable, from_encoder, skip_store[recv_slot])
        )
        return (in_rows, kept_prev, skip_store, loss_grads, loss_sum, sq_sums)

    start_state = (
        jnp.zeros((seg_len, model_width), BF16),
        jnp.zeros(act_shape, BF16),
        jnp.zeros(act_shape, BF16),
        jnp.zeros(act_shape, jnp.float32),
        jnp.zeros((), jnp.float32),
        jnp.zeros((3,), jnp.float32),
    )
    unused_rows, kept_prev, skip_store, loss_grads, loss_sum, sq_sums = lax.fori_loop(
        0, micro_count + sections - 1, forward_step, start_state
    )

    def backward_step(step_idx, loop_state):
        in_grads, skip_grad_store, grad_mats, grad_gains = loop_state
        micro_idx = step_idx - (sections - 1 - section_idx)
        active = (micro_idx >= 0) & (micro_idx < micro_count)
        slot_idx = jnp.clip(micro_idx, 0, micro_count - 1)
        upstream = jnp.where(
            is_last,
            loss_grads[slot_idx],
            in_grads.astype(jnp.float32)
            + jnp.where(encoder, skip_grad_store[slot_idx].astype(jnp.float32), 0.0),
        )
        stream = kept_prev[slot_idx].astype(jnp.float32) + jnp.where(
            decoder, skip_store[slot_idx].astype(jnp.float32), 0.0
        )
        length = lengths[slot_idx]

        def backward_compute_fn(operand):
            return layer_backward(stream, matrices, gain_pair, length, upstream)

        def backward_spare_fn(operand):
            return (
                jnp.zeros_like(stream),
                tuple((jnp.zeros(mat.shape, jnp.float32) for mat in matrices)),
                jnp.zeros((2, model_width), jnp.float32),
            )

        grad_stream, layer_mats, layer_gains = lax.cond(
            active, backward_compute_fn, backward_spare_fn, 0
        )
        grad_mats = tuple((total + piece for total, piece in zip(grad_mats, layer_mats)))
        grad_gains = grad_gains + layer_gains
        grad_rows = grad_stream.astype(BF16)
        in_grads = from_behind(grad_rows, "section", -1)
        from_decoder = from_behind(grad_rows, "section", -half_way)
        recv_idx = micro_idx + half_way
        usable = encoder & (recv_idx >= 0) & (recv_idx < micro_count)
        recv_slot = jnp.clip(recv_idx, 0, micro_count - 1)
        skip_grad_store = skip_grad_store.at[recv_slot].set(
            jnp.where(usable, from_decoder, skip_grad_store[recv_slot])
        )
        return (in_grads, skip_grad_store, grad_mats, grad_gains)

    back_state = (
        jnp.zeros((seg_len, model_width), BF16),
        jnp.zeros(act_shape, BF16),
        tuple((jnp.zeros(mat.shape, jnp.float32) for mat in matrices)),
        jnp.zeros((2, model_width), jnp.float32),
    )
    unused_grads, unused_store, grad_mats, grad_gains = lax.fori_loop(
        0, micro_count + sections - 1, backward_step, back_state
    )
    grad_all = jnp.concatenate([to_blocks(mat, block_size) for mat in grad_mats], axis=0)
    summed_w, summed_g = lax.psum((grad_all, grad_gains), "dp")
    own_grad = lax.dynamic_slice_in_dim(summed_w, group_idx * own_blocks, own_blocks, 0)
    own_gain_grad = lax.dynamic_slice_in_dim(summed_g, group_idx * own_gain, own_gain, 1)
    own_square = jnp.sum(own_grad * own_grad) + jnp.sum(own_gain_grad * own_gain_grad)
    rows_local = jnp.zeros((sections, 3), jnp.float32).at[section_idx].set(sq_sums)
    total_square, loss_value, rows_total = lax.psum(
        (own_square, loss_sum / frame_count, rows_local), ("section", "dp")
    )
    grad_norm = jnp.sqrt(total_square)
    clip_limit = 0.00015 * math.sqrt(
        sections * (own_blocks * groups * block_size * block_size + 2 * model_width)
    )
    factor = clip_limit / jnp.maximum(grad_norm, clip_limit)
    grad_blocks = own_grad * factor
    square = (own_blocks, block_size, block_size)
    shaped = grad_blocks.reshape(square)
    highest = lax.Precision.HIGHEST
    l_new = 0.95 * l_stats[0].reshape(square) + 0.05 * jnp.einsum(
        "bij,bkj->bik", shaped, shaped, precision=highest
    )
    r_new = 0.95 * r_stats[0].reshape(square) + 0.05 * jnp.einsum(
        "bji,bjk->bik", shaped, shaped, precision=highest
    )
    left_side = jnp.einsum("bij,bjk->bik", l_roots[0].reshape(square), shaped, precision=highest)
    precond = jnp.einsum("bij,bjk->bik", left_side, r_roots[0].reshape(square), precision=highest)
    master = w_master[0]
    w_new = master - 0.5 * (precond.reshape(master.shape) + 0.01 * master)
    gain_grad = own_gain_grad * factor
    m_new = 0.9 * gain_m[0] + 0.1 * gain_grad
    v_new = 0.999 * gain_v[0] + 0.001 * gain_grad * gain_grad
    step_num = step_count[0].astype(jnp.float32)
    m_hat = m_new / (1.0 - jnp.power(0.9, step_num))
    v_hat = v_new / (1.0 - jnp.power(0.999, step_num))
    gains_new = norm_gains[0] - 0.5 * m_hat / (jnp.sqrt(v_hat) + 1e-08)
    rms = jnp.sqrt(rows_total[section_idx] / (frame_count * model_width)).reshape(1, 3)
    return (
        w_new[None],
        grad_blocks[None],
        l_new.reshape(master.shape)[None],
        r_new.reshape(master.shape)[None],
        gains_new[None],
        m_new[None],
        v_new[None],
        loss_value,
        grad_norm,
        rms,
    )


def layer_block(shape):
    return pl.BlockSpec((1,) + shape, lambda i: (i,) + (0,) * len(shape))


def whole_block(shape):
    return pl.BlockSpec(shape, lambda i: (0,) * len(shape))


def held_block(shape):
    return pl.BlockSpec(shape, lambda i: (0,) * len(shape), pipeline_mode=pl.Buffered(1))


def forward(layers, micro, valid_len, present_stems, x_in, targets, flat_w, gain):
    width = x_in.shape[1]
    seg = x_in.shape[0] // micro
    dim = width // HEADS
    part = width // 4
    half = layers // 2
    shapes = (
        (HEADS, seg, seg), (3, seg, width), (seg, width), (seg, width), (4, seg, width), (4, seg, width)
    )
    kinds = (BF16, BF16, BF16, F32, BF16, BF16)

    def slot():
        return jnp.minimum(lax.axis_index("section"), micro - 1)

    return pl.pallas_call(
        functools.partial(forward_kernel, layers, half, micro),
        grid=(layers,),
        in_specs=[
            pl.BlockSpec(memory_space=pltpu.SMEM),
            pl.BlockSpec(memory_space=pltpu.SMEM),
            pl.BlockSpec((seg, width), lambda i: (slot(), 0)),
            pl.BlockSpec((width // 2, seg), lambda i: (0, slot())),
            pl.BlockSpec(memory_space=pltpu.VMEM),
            pl.BlockSpec(memory_space=pltpu.VMEM),
        ],
        out_specs=[layer_block(s) for s in shapes]
        + [whole_block((layers, seg, width)), whole_block((seg, width)), whole_block((layers, 8, width))]
        + [pl.BlockSpec(memory_space=pl.ANY), whole_block((layers, 8, width))],
        out_shape=[jax.ShapeDtypeStruct((layers,) + s, k) for s, k in zip(shapes, kinds)]
        + [
            jax.ShapeDtypeStruct((layers, seg, width), BF16),
            jax.ShapeDtypeStruct((seg, width), F32),
            jax.ShapeDtypeStruct((layers, 8, width), F32),
            jax.ShapeDtypeStruct((layers, 48 * part, width), BF16),
            jax.ShapeDtypeStruct((layers, 8, width), F32),
        ],
        scratch_shapes=[
            pltpu.VMEM((seg, width), F32),
            pltpu.VMEM((seg, width), BF16),
            pltpu.VMEM((layers, 48 * part, width), BF16),
            pltpu.VMEM((layers, 8, 8, 128), F32),
            pltpu.VMEM((6 * part, width), BF16),
            pltpu.VMEM((8, 128), F32),
            pltpu.VMEM((4, part, 128), F32),
            pltpu.SemaphoreType.DMA((2, 3)),
            pltpu.SemaphoreType.DMA((2, layers, 4)),
            pltpu.SemaphoreType.DMA((2, layers, 4)),
            pltpu.SemaphoreType.DMA((2, layers, 8)),
            pltpu.SemaphoreType.DMA((2, layers, 8)),
            pltpu.SemaphoreType.DMA((2, 10)),
            pltpu.SemaphoreType.DMA((layers,)),
        ],
        compiler_params=pltpu.CompilerParams(
            vmem_limit_bytes=VMEM_LIMIT, collective_id=0, has_side_effects=True
        ),
    )(valid_len, present_stems, x_in, targets.T, flat_w, gain)


def backward(layers, loss_grad, full_w, full_g, sent, saved, stats):
    seg, width = loss_grad.shape
    dim = width // HEADS
    part = width // 4
    half = layers // 2

    def from_end(array):
        shape = array.shape[1:]
        return pl.BlockSpec((1,) + shape, lambda i: (layers - 1 - i,) + (0,) * len(shape))

    return pl.pallas_call(
        functools.partial(backward_kernel, layers, half),
        grid=(layers,),
        in_specs=[
            held_block((seg, width)),
            from_end(full_w),
            from_end(full_g),
            held_block((layers, seg, width)),
        ]
        + [from_end(a) for a in saved]
        + [pl.BlockSpec(memory_space=pltpu.VMEM)],
        out_specs=[pl.BlockSpec(memory_space=pltpu.VMEM)] * 3,
        out_shape=[
            jax.ShapeDtypeStruct((6 * part, width), F32),
            jax.ShapeDtypeStruct((16, width), F32),
            jax.ShapeDtypeStruct((8, 128), F32),
        ],
        scratch_shapes=[
            pltpu.VMEM((layers, seg, width), BF16),
            pltpu.VMEM((seg, width), BF16),
            pltpu.VMEM((4, seg, width), BF16),
            pltpu.VMEM((seg, width), BF16),
            pltpu.VMEM((seg, width), F32),
            pltpu.VMEM((seg, width), BF16),
            pltpu.VMEM((seg, width), BF16),
            pltpu.VMEM((3, seg, width), BF16),
            pltpu.VMEM((layers, 8, width), F32),
            pltpu.VMEM((2, 4, 2, 576, width), BF16),
            pltpu.VMEM((2, 4, 2, 288, width), BF16),
            pltpu.VMEM((layers, 4, 2, 80, width), BF16),
            pltpu.VMEM((layers, 4, 208, width), BF16),
            pltpu.VMEM((layers, 4, 208, width), BF16),
            pltpu.VMEM((layers, 3, 208, width), BF16),
            pltpu.VMEM((3, 208, width), BF16),
            pltpu.VMEM((6, 16, width), F32),
            pltpu.VMEM((4, 16, width), F32),
            pltpu.VMEM((4, 8, 128), F32),
            pltpu.VMEM((8, 8, 128), F32),
            pltpu.SemaphoreType.DMA((2, 2, 3)),
            pltpu.SemaphoreType.DMA((2, layers, 4)),
            pltpu.SemaphoreType.DMA((2, layers, 4)),
            pltpu.SemaphoreType.DMA((2, layers, 4)),
            pltpu.SemaphoreType.DMA((2, layers)),
            pltpu.SemaphoreType.DMA((2, 3)),
            pltpu.SemaphoreType.DMA((2, 3)),
            pltpu.SemaphoreType.DMA((2, 3)),
            pltpu.SemaphoreType.DMA((2, 7)),
        ],
        compiler_params=pltpu.CompilerParams(
            vmem_limit_bytes=VMEM_LIMIT, collective_id=1, has_side_effects=True
        ),
    )(loss_grad, full_w, full_g, sent, *saved, stats)


def split(value):
    high = value.astype(BF16)
    return high, (value - high.astype(F32)).astype(BF16)


def dot_split(dot, left, right):
    return dot(left[0], right[0]) + (dot(left[0], right[1]) + dot(left[1], right[0]))


def update_kernel(
    layers, limit, length_ref, step_ref, square_ref, tile_ref, quads_ref, w_ref, l_ref, r_ref, lroot_ref, rroot_ref,
    gain_ref, gain_m_ref, gain_v_ref,
    w_out, grad_out, l_out, r_out, gain_out, m_out, v_out, loss_out, norm_out, rms_out,
    block_ref,
):
    part, width = quads_ref.shape[1:]
    gains = tile_ref[: 2 * layers]
    norm = jnp.sqrt(jnp.sum(square_ref[...], keepdims=True) + jnp.sum(gains * gains, keepdims=True))
    factor = limit / jnp.maximum(norm, limit)

    def quad_step(q, _):
        for c in range(4):
            base = 4 * q + c
            load_block(lroot_ref, base, block_ref.at[0])
            load_block(rroot_ref, base, block_ref.at[1])
            grad = quads_ref[q, :, part * c : part * (c + 1)] * factor
            pair = split(grad)
            left = dot_split(dot_nn, split(block_ref[0, :, :part]), pair)
            pre = dot_split(dot_nn, split(left), split(block_ref[1, :, :part]))
            for i, value in enumerate((
                grad, pre, dot_split(dot_nt, pair, pair), dot_split(dot_tn, pair, pair)
            )):
                block_ref[2 + i, :, :part] = value
            parts = [flat_parts(block_ref.at[2 + i]) for i in range(4)]
            for m in range(3):
                at = (pl.ds(base + 8 * m, 24, stride=24), slice(None))
                grad_out[at] = parts[0][m]
                master = w_ref[at]
                w_out[at] = master - 0.5 * (parts[1][m] + 0.01 * master)
                l_out[at] = 0.95 * l_ref[at] + 0.05 * parts[2][m]
                r_out[at] = 0.95 * r_ref[at] + 0.05 * parts[3][m]
        return 0

    lax.fori_loop(0, 2, quad_step, 0)

    @pl.when(pl.program_id(0) == 0)
    def _():
        section, group = lax.axis_index("section"), lax.axis_index("dp")
        share = gain_ref.shape[1]
        row = tile_ref[:2]
        for k in range(1, layers):
            row = jnp.where(section == k, tile_ref[2 * k : 2 * k + 2], row)
        own = row[:, :share]
        for g in range(1, width // share):
            own = jnp.where(group == g, row[:, g * share : (g + 1) * share], own)
        grad = own * factor
        m_new = 0.9 * gain_m_ref[...] + 0.1 * grad
        v_new = 0.999 * gain_v_ref[...] + 0.001 * grad * grad
        step = jnp.full((1, 1), step_ref[0], jnp.int32).astype(F32)
        m_hat = m_new / (1.0 - jnp.exp(step * math.log(0.9)))
        v_hat = v_new / (1.0 - jnp.exp(step * math.log(0.999)))
        gain_out[...] = gain_ref[...] - 0.5 * m_hat / (jnp.sqrt(v_hat) + 1e-08)
        m_out[...] = m_new
        v_out[...] = v_new
        norm_out[...] = norm
        frames = length_ref[0]
        for k in range(1, length_ref.shape[0]):
            frames = frames + length_ref[k]
        frames = jnp.full((1, 1), frames, jnp.int32).astype(F32)
        loss_out[...] = tile_ref[2 * layers : 2 * layers + 1, 3:4] / frames
        squares = tile_ref[2 * layers : 2 * layers + 1, :3]
        for k in range(1, layers):
            squares = jnp.where(section == k, tile_ref[2 * layers + k : 2 * layers + k + 1, :3], squares)
        rms_out[...] = jnp.sqrt(squares / (frames * width))


def update(layers, limit, valid_len, step_count, squares, tile, quads, flats, gains):
    blocks = 4 * quads.shape[0]
    part, width = quads.shape[1:]
    rows = flats[0].shape[0]
    whole = [pl.BlockSpec(memory_space=pltpu.VMEM)]
    flat = [pl.BlockSpec((rows // 3, 128), lambda i: (i, 0))]
    share = gains[0].shape
    return pl.pallas_call(
        functools.partial(update_kernel, layers, limit),
        grid=(3,),
        in_specs=[pl.BlockSpec(memory_space=pltpu.SMEM)] * 2 + whole * 2
        + [pl.BlockSpec((2, part, width), lambda i: (i, 0, 0))] + flat * 5 + whole * 3,
        out_specs=flat * 4 + whole * 6,
        out_shape=[jax.ShapeDtypeStruct((rows, 128), F32)] * 4
        + [jax.ShapeDtypeStruct(share, F32)] * 3
        + [jax.ShapeDtypeStruct((1, 1), F32)] * 2 + [jax.ShapeDtypeStruct((1, 3), F32)],
        scratch_shapes=[pltpu.VMEM((6, part, 128), F32)],
        compiler_params=pltpu.CompilerParams(vmem_limit_bytes=VMEM_LIMIT),
    )(valid_len, step_count, squares, tile, quads, *flats, *gains)


def body(
    x_in, targets, valid_len, present_stems, w_master, norm_gains, gain_m, gain_v,
    l_stats, r_stats, l_roots, r_roots, step_count,
):
    width = x_in.shape[1]
    part = width // 4
    layers = lax.axis_size("section")
    groups = lax.axis_size("dp")
    micro = valid_len.shape[0] // groups
    own_blocks = w_master.shape[1]
    flats = [flat_rows(a[0]) for a in (w_master, l_stats, r_stats, l_roots, r_roots)]
    *saved, sent, loss_grad, stats, full_w, full_g = forward(
        layers, micro, valid_len, present_stems, x_in, targets, flats[0], norm_gains[0]
    )
    own_quads, tile, squares = backward(layers, loss_grad, full_w, full_g, sent, saved, stats)
    clip_limit = 0.00015 * math.sqrt(layers * (own_blocks * groups * part * part + 2 * width))
    *news, gains_new, m_new, v_new, loss_value, grad_norm, rms = update(
        layers, clip_limit, valid_len, step_count, squares, tile, own_quads.reshape(-1, part, width), flats,
        (norm_gains[0], gain_m[0], gain_v[0]),
    )
    w_new, grad_blocks, l_new, r_new = (from_flat_rows(a, own_blocks)[None] for a in news)
    return (
        w_new,
        grad_blocks,
        l_new,
        r_new,
        gains_new[None],
        m_new[None],
        v_new[None],
        loss_value.reshape(()),
        grad_norm.reshape(()),
        rms,
    )


def solution(mesh):
    def step(*args):
        layers, groups = mesh.shape["section"], mesh.shape["dp"]
        micro, own_blocks = args[2].shape[0] // groups, args[4].shape[1]
        if micro <= layers == 4 and groups == 8 and own_blocks == 24:
            return body(*args)
        return pipelined_body(*args)

    block = P("section", "dp", None)
    gain = P("section", None, "dp")
    return jax.shard_map(
        step,
        mesh=mesh,
        in_specs=(
            P("dp", None), P("dp", None), P(), P(), block, gain, gain, gain, block, block, block, block, P(),
        ),
        out_specs=(block, block, block, block, gain, gain, gain, P(), P(), P("section", None)),
        check_vma=False,
    )
```

```python
import functools
import math

import jax
import jax.numpy as jnp
from jax import lax
from jax.experimental import pallas as pl
from jax.experimental.pallas import tpu as pltpu
from jax.sharding import PartitionSpec as P

HEADS = 8
F32 = jnp.float32
BF16 = jnp.bfloat16
VMEM_LIMIT = 61 * 1024 * 1024


def dot_nn(a, b):
    return lax.dot_general(a, b, (((1,), (0,)), ((), ())), preferred_element_type=F32)


def dot_nt(a, b):
    return lax.dot_general(a, b, (((1,), (1,)), ((), ())), preferred_element_type=F32)


def dot_tn(a, b):
    return lax.dot_general(a, b, (((0,), (0,)), ((), ())), preferred_element_type=F32)


def gelu_parts(x):
    ax = jnp.abs(x)
    bell = jnp.exp(-0.5 * x * x)
    t = 1.0 / (1.0 + (0.3275911 * 0.7071067811865476) * ax)
    poly = t * (
        0.5 * 0.254829592
        + t
        * (
            0.5 * -0.284496736
            + t * (0.5 * 1.421413741 + t * (0.5 * -1.453152027 + t * (0.5 * 1.061405429)))
        )
    )
    tail = poly * bell
    cdf = jnp.where(x >= 0.0, 1.0 - tail, tail)
    return x * cdf, cdf + x * bell * 0.3989422804014327


def stack_quads(w_ref, first, step, number):
    part = w_ref.shape[2] // 4
    if step == 1:
        return w_ref[0, first * part : (first + number) * part]
    return jnp.concatenate(
        [w_ref[0, (first + step * i) * part : (first + step * i + 1) * part] for i in range(number)], axis=0
    )


def flat_rows(array):
    blocks, area = array.shape
    return (
        array.reshape(blocks // 8, 8, area // 128, 128).transpose(0, 2, 1, 3).reshape(-1, 128)
    )


def from_flat_rows(rows, blocks):
    return (
        rows.reshape(blocks // 8, -1, 8, 128).transpose(0, 2, 1, 3).reshape(blocks, -1)
    )


def load_block(rows_ref, base, block_ref):
    lane = lax.broadcasted_iota(jnp.int32, (24, 128), 1)
    a, b, c = (rows_ref[pl.ds(base + 8 * m, 24, stride=24), :] for m in range(3))
    block_ref[pl.ds(0, 24, stride=4), :] = a
    block_ref[pl.ds(1, 24, stride=4), :] = jnp.where(lane < 32, pltpu.roll(a, 32, 1), pltpu.roll(b, 32, 1))
    block_ref[pl.ds(2, 24, stride=4), :] = jnp.where(lane < 64, pltpu.roll(b, 64, 1), pltpu.roll(c, 64, 1))
    block_ref[pl.ds(3, 24, stride=4), :] = pltpu.roll(c, 96, 1)


def flat_parts(block_ref):
    lane = lax.broadcasted_iota(jnp.int32, (24, 128), 1)
    a, b, c, d = (block_ref[pl.ds(r, 24, stride=4), :] for r in range(4))
    b, c, d = pltpu.roll(b, 96, 1), pltpu.roll(c, 64, 1), pltpu.roll(d, 32, 1)
    return jnp.where(lane < 96, a, b), jnp.where(lane < 64, b, c), jnp.where(lane < 32, c, d)


MESH = pl.DeviceIdType.MESH


def mesh_place():
    section = lax.axis_index("section")
    group = lax.axis_index("dp")
    core = lax.rem(section, 2)
    y = lax.rem(group, 2)
    z = group // 2
    z_peers = (z, z + 1 - 2 * lax.rem(z, 2), lax.rem(z + 2, 4), 3 - z)
    return section, group, core, y, z_peers


def remote(source, target, send_sem, recv_sem, section, group):
    return pltpu.make_async_remote_copy(
        src_ref=source, dst_ref=target, send_sem=send_sem, recv_sem=recv_sem,
        device_id=(section, group), device_id_type=MESH,
    )


def greet(places):
    barrier = pltpu.get_barrier_semaphore()
    for place in places:
        pl.semaphore_signal(barrier, inc=1, device_id=place, device_id_type=MESH)
    pl.semaphore_wait(barrier, len(places))


class Slabs:
    def __init__(self, rows):
        self.section, self.group, self.core, self.y, self.z_peers = mesh_place()
        self.x = self.section // 2
        self.rows, self.half = rows, rows // 2
        self.edge = self.half * 5 // 18
        self.slab = self.half - self.edge

    def slab_of(self, x, core):
        return pl.ds(pl.multiple_of(self.half * core + self.edge * x, 16), self.slab)

    def edge_of(self, x, core):
        return pl.ds(pl.multiple_of(self.half * core + self.slab * x, 16), self.edge)

    def half_of(self, core):
        return pl.ds(pl.multiple_of(self.half * core, 16), self.half)

    def x_peer(self):
        return lax.rem(self.section + 2, 4), self.group

    def y_peer(self):
        return self.section, self.group + 1 - 2 * self.y

    def z_peer(self, k):
        return self.section, self.z_peers[k] * 2 + self.y

    def core_peer(self):
        return self.section + 1 - 2 * self.core, self.group

    def greet_all(self):
        greet(
            [(lax.rem(self.section + k, 4), self.group) for k in range(1, 4)]
            + [(self.section, lax.rem(self.group + k, 8)) for k in range(1, 8)]
        )


class Gather(Slabs):
    def __init__(self, own_ref, gain_ref, w_ref, gains_ref, sems):
        super().__init__(own_ref.shape[0])
        self.own, self.gain, self.w, self.gains = own_ref, gain_ref, w_ref, gains_ref
        self.spread, self.z_sems, self.y_sems, self.x_sems, self.core_sems, self.gain_sems, self.local = sems
        self.others = [lax.rem(self.section + k, 4) for k in range(1, 4)]

    def chunk(self, k):
        y = self.y if k < 4 else 1 - self.y
        return self.z_peers[k % 4] * 2 + y

    def at(self, layer, group, rows):
        return self.w.at[layer, pl.ds(pl.multiple_of(group * self.rows + rows.start, 16), rows.size)]

    def spread_copy(self, k):
        peer = self.others[k]
        rows = self.slab_of(peer // 2, lax.rem(peer, 2))
        return remote(
            self.own.at[rows], self.at(self.section, self.group, rows),
            self.spread.at[0, k], self.spread.at[1, k], peer, self.group,
        )

    def spread_wait(self, layer):
        ref = self.at(layer, self.group, self.slab_of(self.x, self.core))
        for k in range(3):
            @pl.when(lax.rem(layer + k + 1, 4) == self.section)
            def _():
                remote(ref, ref, self.spread.at[0, k], self.spread.at[1, k], self.others[0], self.group).wait_recv()

    def z_copy(self, layer, k, landed=False):
        ref = self.at(layer, self.chunk(k) if landed else self.group, self.slab_of(self.x, self.core))
        return remote(ref, ref, self.z_sems.at[0, layer, k], self.z_sems.at[1, layer, k], *self.z_peer(k))

    def y_copy(self, layer, k, landed=False):
        ref = self.at(layer, self.chunk(k + 4 if landed else k), self.slab_of(self.x, self.core))
        return remote(ref, ref, self.y_sems.at[0, layer, k], self.y_sems.at[1, layer, k], *self.y_peer())

    def x_copy(self, layer, k, landed=False):
        ref = self.at(layer, self.chunk(k), self.edge_of(1 - self.x if landed else self.x, self.core))
        return remote(ref, ref, self.x_sems.at[0, layer, k], self.x_sems.at[1, layer, k], *self.x_peer())

    def core_copy(self, layer, k, landed=False):
        ref = self.at(layer, self.chunk(k), self.half_of(1 - self.core if landed else self.core))
        return remote(ref, ref, self.core_sems.at[0, layer, k], self.core_sems.at[1, layer, k], *self.core_peer())

    def gain_copy(self, k):
        if k < 7:
            peer = lax.rem(self.group + k + 1, 8)
            return remote(
                self.gain, self.gains.at[self.section, self.group],
                self.gain_sems.at[0, k], self.gain_sems.at[1, k], self.section, peer,
            )
        ref = self.gains.at[self.section]
        return remote(
            ref, ref, self.gain_sems.at[0, k], self.gain_sems.at[1, k], self.others[k - 7], self.group
        )

    def gain_landed(self, k):
        if k < 7:
            ref = self.gains.at[self.section, lax.rem(self.group - k - 1 + 8, 8)]
        else:
            ref = self.gains.at[lax.rem(self.section - (k - 6) + 4, 4)]
        return remote(ref, ref, self.gain_sems.at[0, k], self.gain_sems.at[1, k], self.section, self.group)

    def spread_own(self):
        for k in range(3):
            self.spread_copy(k).start()

    def begin(self):
        @pl.when(self.section == 0)
        def _():
            self.spread_own()

        for k in range(7):
            self.gain_copy(k).start()
        rows = self.slab_of(self.x, self.core)
        self.w[self.section, pl.ds(pl.multiple_of(self.group * self.rows + rows.start, 16), rows.size)] = self.own[rows]
        self.gains[self.section, self.group] = self.gain[...]

    def share_gains(self):
        for k in range(7):
            self.gain_landed(k).wait_recv()
        for k in range(7, 10):
            self.gain_copy(k).start()

    def wait_gains(self):
        for k in range(7, 10):
            self.gain_landed(k).wait_recv()

    def kick(self, layer):
        self.spread_wait(layer)
        for k in range(1, 4):
            self.z_copy(layer, k).start()
        self.y_copy(layer, 0).start()
        self.x_copy(layer, 0).start()

    def serve_z(self, layer, k):
        self.z_copy(layer, k, True).wait_recv()
        self.y_copy(layer, k).start()
        self.x_copy(layer, k).start()

    def serve_y(self, layer, k):
        self.y_copy(layer, k, True).wait_recv()
        self.x_copy(layer, k + 4).start()

    def serve_x(self, layer, k):
        self.x_copy(layer, k, True).wait_recv()
        self.core_copy(layer, k).start()

    def finish_first(self, layer):
        for k in range(8):
            @pl.when(self.z_peers[k % 4] == 0)
            def _():
                self.core_copy(layer, k, True).wait_recv()

    def finish_rest(self, layer):
        for k in range(8):
            @pl.when(self.z_peers[k % 4] != 0)
            def _():
                self.core_copy(layer, k, True).wait_recv()

    def end(self, layers):
        for k in range(3):
            self.spread_copy(k).wait_send()
        for k in range(10):
            self.gain_copy(k).wait_send()

        def per_layer(layer, _):
            for k in range(1, 4):
                self.z_copy(layer, k).wait_send()
            for k in range(4):
                self.y_copy(layer, k).wait_send()
            for k in range(8):
                self.x_copy(layer, k).wait_send()
                self.core_copy(layer, k).wait_send()
            return 0

        lax.fori_loop(0, layers, per_layer, 0)


def segment_info(micro, length_ref, stems_ref):
    section, group = lax.axis_index("section"), lax.axis_index("dp")
    at = group * micro + jnp.minimum(section, micro - 1)
    used = (section < micro).astype(jnp.int32)
    frames = length_ref[0]
    for k in range(1, length_ref.shape[0]):
        frames = frames + length_ref[k]
    return length_ref[at] * used, [stems_ref[at, k] * used for k in range(4)], frames


FIRST_POINTS = {"qkv": "z2 y1 x0 x1", "heads": "z3 x2 x4 x5", "attended": "y2", "ffn1": "x3", "ffn2": "y3 x6", "ffn3": "x7"}
POINTS = {"qkv": "x0 x1", "heads": "z3 x2 x4 x5", "attended": "y2", "ffn0": "x3", "ffn1": "y3", "ffn2": "x6", "ffn3": "x7"}
AHEAD_POINTS = {"attended": "z1 y0", "ffn2": "z2", "ffn3": "y1"}


def forward_kernel(
    layers, half, micro, length_ref, stems_ref, x_ref, target_ref, flat_ref, raw_gain_ref,
    probs_ref, qkv_ref, att_ref, middle_ref, hidden_ref, slope_ref, sent_ref, loss_grad_ref, stats_ref,
    full_ref, gains_out_ref,
    out_ref, normed_ref, w_all_ref, gains_ref, own_ref, own_gain_ref, block_ref, *sems,
):
    seg, width = x_ref.shape
    dim = width // HEADS
    part = width // 4
    layer = pl.program_id(0)
    rows = 256
    chunks = seg // rows
    length, present_flags, frame_total = segment_info(micro, length_ref, stems_ref)
    gather = Gather(own_ref, own_gain_ref, w_all_ref, gains_ref, sems)
    w_ref = w_all_ref.at[pl.ds(layer, 1)]

    def own_step(q, _):
        for c in range(4):
            block = 4 * q + c
            load_block(flat_ref, (block // 8) * 576 + lax.rem(block, 8), block_ref.at[c])
        quad = jnp.concatenate([block_ref[c, :, :part] for c in range(4)], axis=1)
        own_ref[pl.ds(pl.multiple_of(q * part, part), part)] = quad.astype(BF16)
        return 0

    def keep_copy(index):
        return pltpu.make_async_copy(w_all_ref.at[index], full_ref.at[index], gather.local.at[index])

    @pl.when(layer == 0)
    def _():
        gather.greet_all()
        lax.fori_loop(0, flat_ref.shape[0] // 288, own_step, 0)
        own_gain_ref[...] = jnp.zeros_like(own_gain_ref)
        own_gain_ref[:2, : raw_gain_ref.shape[1]] = raw_gain_ref[...]
        gather.begin()
        sent_ref[0] = x_ref[...]
        stats_ref[...] = jnp.zeros_like(stats_ref)
        gather.kick(0)

        @pl.when(gather.section != 0)
        def _():
            gather.spread_own()

        gather.share_gains()
        gather.serve_z(0, 1)
        gather.serve_z(0, 2)
        gather.kick(1)
        gather.serve_x(0, 0)
        gather.serve_x(0, 1)
        gather.serve_z(0, 3)
        gather.wait_gains()
        gather.serve_y(0, 0)
        gather.serve_x(0, 2)
        gather.serve_y(0, 1)
        gather.serve_y(0, 2)
        gather.serve_x(0, 3)
        gather.serve_y(0, 3)
        for k in range(4, 8):
            gather.serve_x(0, k)
        gather.serve_z(1, 1)
        gather.serve_y(1, 0)

    @pl.when(layer + 2 < layers)
    def _():
        gather.kick(layer + 2)

    gather.finish_first(layer)
    more = layer + 1 < layers

    def serve(point):
        for here, steps, later in (
            (layer == 0, FIRST_POINTS.get(point, ""), ""),
            (layer > 0, POINTS.get(point, ""), ""),
            (layer >= 0, "", AHEAD_POINTS.get(point, "")),
        ):
            for names, back in ((steps, 1), (later, 2)):
                if names:
                    @pl.when((layer + back < layers) & here)
                    def _():
                        for name in names.split():
                            getattr(gather, "serve_" + name[0])(layer + back, int(name[1]))

    def stream_of(at):
        prev = sent_ref[layer, at].astype(F32)
        skip = sent_ref[jnp.maximum(layer + 1 - half, 0), at].astype(F32)
        return prev + jnp.where(layer >= half, skip, 0.0)

    def gain_row(which):
        return jnp.concatenate(
            [gains_ref[layer, g, which : which + 1, : width // 8] for g in range(8)], axis=1
        ).astype(BF16).astype(F32)

    gain_one = gain_row(0)
    gain_two = gain_row(1)
    gains_out_ref[layer, 0:1] = gain_one
    gains_out_ref[layer, 1:2] = gain_two

    first_stream = stream_of(slice(None))
    first_factor = lax.rsqrt(jnp.mean(first_stream * first_stream, axis=-1, keepdims=True) + 1e-06)
    first_normed = (first_stream * first_factor * gain_one).astype(BF16)
    for t in range(3):
        qkv_ref[0, t] = dot_nn(first_normed, stack_quads(w_ref, t, 3, 4)).astype(BF16)
    serve("qkv")
    frames = lax.broadcasted_iota(jnp.int32, (1, seg), 1)
    masking = jnp.where(frames < length, 0.0, -1e30).astype(F32)

    def head_step(h):
        queries, keys, values = (qkv_ref[0, t, :, h * dim : (h + 1) * dim] for t in range(3))
        scores = dot_nt(queries, keys) * dim ** (-0.5) + masking
        top = jnp.max(scores, axis=-1, keepdims=True)
        expd = jnp.exp(scores - top)
        probs = (expd * (1.0 / jnp.sum(expd, axis=-1, keepdims=True))).astype(BF16)
        probs_ref[0, h] = probs
        return dot_nn(probs, values).astype(BF16)

    def put_heads(first):
        heads = [head_step(h) for h in range(first, first + HEADS // 2)]
        att_ref[0, :, first * dim : (first + HEADS // 2) * dim] = jnp.concatenate(heads, axis=1)

    put_heads(0)
    serve("heads")
    put_heads(HEADS // 2)
    serve("attended")
    gather.finish_rest(layer)
    keep_copy(layer).start()

    valid = (lax.broadcasted_iota(jnp.int32, (seg, 1), 0) < length).astype(F32)

    def add_stat(k, value):
        stats_ref[layer, k : k + 1] = jnp.sum(valid * value * value, axis=0, keepdims=True)

    branch_attn = dot_nn(att_ref[0], stack_quads(w_ref, 12, 1, 4))
    stream = stream_of(slice(None))
    middle = stream + branch_attn
    middle_ref[0] = middle
    add_stat(0, stream)
    add_stat(1, branch_attn)
    factor = lax.rsqrt(jnp.mean(middle * middle, axis=-1, keepdims=True) + 1e-06)
    normed_ref[...] = (middle * factor * gain_two).astype(BF16)

    def ffn_step(c):
        pre_act = dot_nn(normed_ref[...], stack_quads(w_ref, 16 + c, 4, 4))
        hidden, slope = gelu_parts(pre_act)
        hidden = hidden.astype(BF16)
        hidden_ref[0, c] = hidden
        slope_ref[0, c] = slope.astype(BF16)
        part_sum = dot_nn(hidden, stack_quads(w_ref, 32 + 4 * c, 1, 4))
        out_ref[...] = part_sum if c == 0 else out_ref[...] + part_sum

    for c in range(4):
        ffn_step(c)
        if c < 3:
            serve(f"ffn{c}")
    branch_ffn = out_ref[...]
    add_stat(2, branch_ffn)
    output = middle_ref[0] + branch_ffn
    out_ref[...] = output

    @pl.when(layer + 1 < layers)
    def _():
        sent_ref[layer + 1] = out_ref[...].astype(BF16)

    serve("ffn3")

    @pl.when(layer == layers - 1)
    def _():
        bins = width // 8
        lane = lax.broadcasted_iota(jnp.int32, (1, width), 1)
        is_real = lax.rem(lane, 2 * bins) < bins
        stem = lane // (2 * bins)
        present = jnp.zeros((1, width), F32)
        for k in range(4):
            present = jnp.where(stem == k, present_flags[k].astype(F32), present)
        inverse = 1.0 / jnp.full((1, 1), frame_total, jnp.int32).astype(F32)

        def loss_step(i, _):
            at = pl.ds(pl.multiple_of(i * rows, rows), rows)
            output = out_ref[at]
            square = output * output
            other = jnp.where(
                is_real, pltpu.roll(square, width - bins, 1), pltpu.roll(square, bins, 1)
            )
            magnitude = jnp.sqrt(square + other + 0.01)
            goal = target_ref[:, at].T
            goal = jnp.concatenate(
                [goal[:, (k // 2) * bins : (k // 2 + 1) * bins] for k in range(8)], axis=1
            )
            differ = magnitude - goal
            smooth = jnp.sqrt(differ * differ + 0.01)
            valid = (lax.broadcasted_iota(jnp.int32, (rows, 1), 0) + i * rows < length).astype(F32)
            weight = valid * present
            loss_grad_ref[at] = weight * differ * output * inverse / (smooth * magnitude)
            stats_ref[0, 3:4] += jnp.sum(
                jnp.where(is_real, weight * smooth, 0.0), axis=0, keepdims=True
            )
            return 0

        lax.fori_loop(0, chunks, loss_step, 0)
        gather.end(layers)
        for k in range(layers):
            keep_copy(k).wait()


class Scatter(Slabs):
    PARTS = ((3, 4), (1, 3), (0, 1))

    def __init__(self, refs, sems):
        self.grads, self.core_in, self.x_in, self.y_in, self.stage, self.z_in, self.last_in = refs
        super().__init__(self.grads.shape[3])
        self.core_sems, self.x_sems, self.y_sems, self.z_sems, self.last_sems = sems
        self.mine = self.slab_of(self.x, self.core)
        self.z = self.z_peers[0]

    def core_copy(self, layer, number):
        slot = lax.rem(layer, 2)
        first, last = self.PARTS[number]
        zs = pl.ds(first, last - first)
        return remote(
            self.grads.at[slot, zs, :, self.half_of(1 - self.core)], self.core_in.at[slot, zs],
            self.core_sems.at[0, slot, number], self.core_sems.at[1, slot, number], *self.core_peer(),
        )

    def x_copy(self, layer, z):
        slot = lax.rem(layer, 2)
        return remote(
            self.grads.at[slot, z, :, self.edge_of(1 - self.x, self.core)], self.x_in.at[layer, z],
            self.x_sems.at[0, layer, z], self.x_sems.at[1, layer, z], *self.x_peer(),
        )

    def y_copy(self, layer, z):
        slot = lax.rem(layer, 2)
        return remote(
            self.grads.at[slot, z, 1 - self.y, self.mine], self.y_in.at[layer, z],
            self.y_sems.at[0, layer, z], self.y_sems.at[1, layer, z], *self.y_peer(),
        )

    def z_copy(self, layer, z):
        place = jnp.maximum(self.z_peers[z] - 1, 0)
        return remote(
            self.stage.at[layer, z], self.z_in.at[layer, place],
            self.z_sems.at[0, layer, z], self.z_sems.at[1, layer, place], self.section, z * 2 + self.y,
        )

    def z_landed(self, layer, place):
        ref = self.z_in.at[layer, place]
        return remote(ref, ref, self.z_sems.at[0, layer, 0], self.z_sems.at[1, layer, place], *self.z_peer(place + 1))

    def last_copy(self, layer):
        place = jnp.maximum(lax.rem(self.section - layer + 4, 4) - 1, 0)
        return remote(
            self.stage.at[layer, self.z], self.last_in.at[place],
            self.last_sems.at[0, layer], self.last_sems.at[1, place], layer, self.group,
        )

    def last_landed(self, place):
        return remote(
            self.last_in.at[place], self.last_in.at[place],
            self.last_sems.at[0, 0], self.last_sems.at[1, place], self.section, self.group,
        )

    def add_core(self, layer, number):
        slot = lax.rem(layer, 2)
        self.core_copy(layer, number).wait_recv()
        rows = self.half_of(self.core)
        first, last = self.PARTS[number]

        def add(i, _):
            z, y = i // 2, lax.rem(i, 2)
            self.grads[slot, z, y, rows] = self.grads[slot, z, y, rows] + self.core_in[slot, z, y]
            return 0

        lax.fori_loop(2 * first, 2 * last, add, 0)
        for z in range(first, last):
            self.x_copy(layer, z).start()

    def add_x(self, layer, z):
        slot = lax.rem(layer, 2)
        self.x_copy(layer, z).wait_recv()
        rows = self.edge_of(self.x, self.core)
        inner = pl.ds(pl.multiple_of((self.slab - self.edge) * self.x, 16), self.edge)
        self.grads[slot, z, 1 - self.y, rows] = (
            self.grads[slot, z, 1 - self.y, rows] + self.x_in[layer, z, 1 - self.y]
        )
        self.y_copy(layer, z).start()
        self.stage[layer, z] = self.grads[slot, z, self.y, self.mine]
        self.stage[layer, z, inner] = self.stage[layer, z, inner] + self.x_in[layer, z, self.y]

    def add_y(self, layer, z):
        self.y_copy(layer, z).wait_recv()
        self.stage[layer, z] = self.stage[layer, z] + self.y_in[layer, z]

        @pl.when(self.z != z)
        def _():
            self.z_copy(layer, z).start()

    def add_z(self, layer, result_ref):
        for place in range(3):
            self.z_landed(layer, place).wait_recv()
        total = self.stage[layer, self.z].astype(F32)
        for k in range(3):
            total = total + self.z_in[layer, k].astype(F32)

        @pl.when(layer == self.section)
        def _():
            result_ref[...] = jnp.zeros_like(result_ref)
            result_ref[self.mine] = total

        @pl.when(layer != self.section)
        def _():
            self.stage[layer, self.z] = total.astype(BF16)
            self.last_copy(layer).start()

    def wait_sends(self, layer, last):
        for number in (2,) if last else (0, 1):
            self.core_copy(layer, number).wait_send()
        for z in (0, 1) if last else (2, 3):
            self.x_copy(layer, z).wait_send()
            self.y_copy(layer, z).wait_send()

    def end(self, layers):
        def per_layer(layer, _):
            for z in range(4):
                @pl.when(self.z != z)
                def _():
                    self.z_copy(layer, z).wait_send()

            @pl.when(layer != self.section)
            def _():
                self.last_copy(layer).wait_send()

            return 0

        lax.fori_loop(0, layers, per_layer, 0)

    def collect(self, result_ref):
        for place in (0, 2, 1):
            self.last_landed(place).wait_recv()
            peer = lax.rem(self.section + place + 1, 4)
            rows = self.slab_of(peer // 2, lax.rem(peer, 2))
            result_ref[rows] = result_ref[rows] + self.last_in[place].astype(F32)


class Totals:
    def __init__(self, refs, sems):
        self.stage_in, self.z_in, self.norm_section, self.norm_group = refs
        self.stage_sems, self.z_sems, self.section_sems, self.group_sems = sems
        self.section, self.group, self.core, self.y, self.z_peers = mesh_place()

    def stage_copy(self, k):
        peer = (
            (self.section + 1 - 2 * self.core, self.group),
            (self.section, self.group + 1 - 2 * self.y),
            (lax.rem(self.section + 2, 4), self.group),
        )[k]
        return remote(
            self.stage_in.at[2 * k], self.stage_in.at[2 * k + 1],
            self.stage_sems.at[0, k], self.stage_sems.at[1, k], *peer,
        )

    def z_copy(self, k):
        z = self.z_peers[0]
        return remote(
            self.z_in.at[z], self.z_in.at[z], self.z_sems.at[0, k - 1], self.z_sems.at[1, k - 1],
            self.section, self.z_peers[k] * 2 + self.y,
        )

    def z_landed(self, k):
        z = self.z_peers[k]
        return remote(
            self.z_in.at[z], self.z_in.at[z], self.z_sems.at[0, k - 1], self.z_sems.at[1, k - 1],
            self.section, self.z_peers[k] * 2 + self.y,
        )

    def begin(self, tile):
        self.stage_in[0] = tile
        self.stage_copy(0).start()

    def after_core(self):
        self.stage_copy(0).wait_recv()
        self.stage_in[2] = self.stage_in[0] + self.stage_in[1]
        self.stage_copy(1).start()

    def after_y(self):
        self.stage_copy(1).wait_recv()
        self.z_in[self.z_peers[0]] = self.stage_in[2] + self.stage_in[3]
        for k in range(1, 4):
            self.z_copy(k).start()

    def after_z(self):
        for k in range(1, 4):
            self.z_landed(k).wait_recv()
        self.stage_in[4] = self.z_in[0] + self.z_in[1] + self.z_in[2] + self.z_in[3]
        self.stage_copy(2).start()

    def after_x(self):
        self.stage_copy(2).wait_recv()
        return self.stage_in[4] + self.stage_in[5]

    def norm_copy(self, k):
        if k < 3:
            peer = (lax.rem(self.section + k + 1, 4), self.group)
            ref = self.norm_section.at[self.section]
            return remote(ref, ref, self.section_sems.at[0, k], self.section_sems.at[1, k], *peer)
        k = k - 3
        peer = (self.section, lax.rem(self.group + k + 1, 8))
        ref = self.norm_group.at[self.group]
        return remote(ref, ref, self.group_sems.at[0, k], self.group_sems.at[1, k], *peer)

    def norm_landed(self, k):
        if k < 3:
            ref = self.norm_section.at[lax.rem(self.section - k - 1 + 4, 4)]
            return remote(
                ref, ref, self.section_sems.at[0, k], self.section_sems.at[1, k], self.section, self.group
            )
        k = k - 3
        ref = self.norm_group.at[lax.rem(self.group - k - 1 + 8, 8)]
        return remote(ref, ref, self.group_sems.at[0, k], self.group_sems.at[1, k], self.section, self.group)

    def norm(self, value):
        self.norm_section[self.section] = value
        for k in range(3):
            self.norm_copy(k).start()
        for k in range(3):
            self.norm_landed(k).wait_recv()
        total = self.norm_section[0]
        for k in range(1, 4):
            total = total + self.norm_section[k]
        self.norm_group[self.group] = total
        for k in range(3, 10):
            self.norm_copy(k).start()
        for k in range(3, 10):
            self.norm_landed(k).wait_recv()
        total = self.norm_group[0]
        for k in range(1, 8):
            total = total + self.norm_group[k]
        return total

    def end(self):
        for k in range(3):
            self.stage_copy(k).wait_send()
        for k in range(1, 4):
            self.z_copy(k).wait_send()
        for k in range(10):
            self.norm_copy(k).wait_send()


def norm_reverse(value, gain, grad):
    factor = lax.rsqrt(jnp.mean(value * value, axis=-1, keepdims=True) + 1e-06)
    scaled = grad * gain
    mean = jnp.mean(value * scaled, axis=-1, keepdims=True)
    unit = value * factor
    back = factor * scaled - unit * (factor * factor * mean)
    return back, jnp.sum(grad * unit, axis=0, keepdims=True), (unit * gain).astype(BF16)


def backward_kernel(
    layers, half, loss_grad_ref, w_ref, gain_ref, sent_ref,
    probs_ref, qkv_ref, att_ref, middle_ref, hidden_ref, slope_ref, stats_ref,
    result_ref, totals_ref, square_ref,
    sends_ref, dffn_ref, dpre_ref, normed_ref, dmid_ref, datt_ref, dhold_ref, dqkv_ref,
    gain_grad_ref, *comm_refs,
):
    seg, width = loss_grad_ref.shape
    dim = width // HEADS
    part = width // 4
    layer = layers - 1 - pl.program_id(0)
    rows = 512
    chunks = seg // rows
    gain_one = gain_ref[0, 0:1]
    gain_two = gain_ref[0, 1:2]
    scatter = Scatter(comm_refs[:7], comm_refs[11:16])
    totals = Totals(comm_refs[7:11], comm_refs[16:])
    grads_ref = comm_refs[0]
    slot = lax.rem(layer, 2)

    @pl.when(layer == layers - 1)
    def _():
        scatter.greet_all()
        sends_ref[...] = jnp.zeros_like(sends_ref)
        gain_grad_ref[...] = jnp.zeros_like(gain_grad_ref)

    def put_grad(first, step, value):
        for r in range(4):
            quad = first + step * r
            owner = quad // 6
            at = pl.ds(pl.multiple_of(lax.rem(quad, 6) * part, part), part)
            grads_ref[slot, owner // 2, lax.rem(owner, 2), at] = value[r * part : (r + 1) * part].astype(BF16)

    def serve(back, here, *steps):
        @pl.when((layer + back < layers) & here)
        def _():
            for kind, *args in steps:
                getattr(scatter, kind)(layer + back, *args)

    serve(2, True, ("wait_sends", False))
    later = sends_ref[jnp.minimum(layer + 1, layers - 1)].astype(F32)
    skip = sends_ref[jnp.minimum(layer + half, layers - 1)].astype(F32)
    dmid_ref[...] = jnp.where(
        layer == layers - 1, loss_grad_ref[...], later + jnp.where(layer + half < layers, skip, 0.0)
    )
    dffn_ref[...] = dmid_ref[...].astype(BF16)
    for c in range(4):
        put_grad(32 + 4 * c, 1, dot_tn(hidden_ref[0, c], dffn_ref[...]))
    scatter.core_copy(layer, 0).start()

    def ffn_step(i, _):
        at = pl.ds(pl.multiple_of(i * rows, rows), rows)
        dffn = dffn_ref[at]
        dnormed = jnp.zeros((rows, width), F32)
        for c in range(4):
            dhidden = dot_nt(dffn, stack_quads(w_ref, 32 + 4 * c, 1, 4))
            dpre = (dhidden * slope_ref[0, c, at].astype(F32)).astype(BF16)
            dpre_ref[c, at] = dpre
            dnormed = dnormed + dot_nt(dpre, stack_quads(w_ref, 16 + c, 4, 4))
        back, gain_grad, normed = norm_reverse(middle_ref[0, at], gain_two, dnormed)
        gain_grad_ref[layer, 1:2] += gain_grad
        normed_ref[at] = normed
        dmid = dmid_ref[at] + back
        dmid_ref[at] = dmid
        datt = dmid.astype(BF16)
        datt_ref[at] = datt
        dattended = dot_nt(datt, stack_quads(w_ref, 12, 1, 4)).astype(BF16)
        dhold_ref[at] = dattended

        serve(1, i == 0, ("add_y", 3), ("add_x", 1), ("add_core", 2))
        serve(2, i == 0, ("add_y", 0))
        return 0

    lax.fori_loop(0, chunks, ffn_step, 0)

    serve(2, True, ("wait_sends", True))

    def ffn_grad_step(c, _):
        put_grad(16 + c, 4, dot_tn(normed_ref[...], dpre_ref[c]))
        return 0

    for c in range(4):
        ffn_grad_step(c, 0)
    put_grad(12, 1, dot_tn(att_ref[0], datt_ref[...]))
    scatter.core_copy(layer, 1).start()
    scatter.add_core(layer, 0)
    serve(1, True, ("add_x", 2))

    def head_step(h):
        queries, keys, values = (qkv_ref[0, t, :, h * dim : (h + 1) * dim] for t in range(3))
        probs = probs_ref[0, h]
        dhold = dhold_ref[:, h * dim : (h + 1) * dim]
        dprobs = dot_nt(dhold, values)
        wide = probs.astype(F32)
        dot_sum = jnp.sum(wide * dprobs, axis=-1, keepdims=True)
        dscores = (wide * (dprobs - dot_sum)).astype(BF16)
        return (
            (dot_nn(dscores, keys) * dim ** (-0.5)).astype(BF16),
            (dot_tn(dscores, queries) * dim ** (-0.5)).astype(BF16),
            dot_tn(probs, dhold).astype(BF16),
        )

    def put_heads(first, parts):
        for t in range(3):
            dqkv_ref[t, :, first * dim : (first + len(parts)) * dim] = jnp.concatenate([p[t] for p in parts], axis=1)

    put_heads(0, [head_step(h) for h in range(HEADS // 2)])
    scatter.add_core(layer, 1)
    serve(1, True, ("add_x", 0))

    put_heads(HEADS // 2, [head_step(h) for h in range(HEADS // 2, HEADS)])
    scatter.add_x(layer, 3)
    serve(1, True, ("add_y", 1))

    def qkv_step(i, _):
        at = pl.ds(pl.multiple_of(i * rows, rows), rows)
        dnormed = jnp.zeros((rows, width), F32)
        for t in range(3):
            dnormed = dnormed + dot_nt(dqkv_ref[t, at], stack_quads(w_ref, t, 3, 4))
        prev = sent_ref[layer, at].astype(F32)
        skip = sent_ref[jnp.maximum(layer + 1 - half, 0), at].astype(F32)
        stream = prev + jnp.where(layer >= half, skip, 0.0)
        back, gain_grad, normed = norm_reverse(stream, gain_one, dnormed)
        gain_grad_ref[layer, 0:1] += gain_grad
        normed_ref[at] = normed
        sends_ref[layer, at] = (dmid_ref[at] + back).astype(BF16)
        return 0

    lax.fori_loop(0, chunks, qkv_step, 0)

    def qkv_grad_step(t, _):
        put_grad(t, 3, dot_tn(normed_ref[...], dqkv_ref[t]))
        return 0

    for t in range(3):
        qkv_grad_step(t, 0)
    scatter.core_copy(layer, 2).start()
    serve(1, True, ("add_y", 2))
    serve(2, True, ("add_z", result_ref))

    @pl.when(layer == 0)
    def _():
        lane = lax.broadcasted_iota(jnp.int32, (1, width), 1)
        rows_out = [gain_grad_ref[k // 2, k % 2 : k % 2 + 1] for k in range(2 * layers)]
        for k in range(layers):
            row = jnp.zeros((1, width), F32)
            for i in range(4):
                value = jnp.sum(stats_ref[k, i : i + 1], axis=1, keepdims=True)
                row = jnp.where(lane == i, value, row)
            rows_out.append(row)
        rows_out.append(jnp.zeros((16 - 3 * layers, width), F32))
        totals.begin(jnp.concatenate(rows_out, axis=0))
        scatter.add_y(0, 3)
        scatter.add_x(0, 1)
        scatter.add_core(0, 2)
        scatter.add_y(1, 0)
        totals.after_core()
        scatter.add_x(0, 2)
        scatter.add_x(0, 0)
        totals.after_y()
        scatter.add_y(0, 1)
        scatter.add_y(0, 2)
        scatter.add_y(0, 0)
        scatter.add_z(1, result_ref)
        scatter.add_z(0, result_ref)
        totals.after_z()
        scatter.collect(result_ref)
        square = jnp.zeros((8, width), F32)
        for q in range(6):
            value = result_ref[q * part : (q + 1) * part]
            square = square + jnp.sum((value * value).reshape(part // 8, 8, width), axis=0)
        folded = square[:, :128] + square[:, 128:256] + square[:, 256:]
        square_ref[...] = totals.norm(folded)
        totals_ref[...] = totals.after_x()
        for back in (1, 0):
            for last in (False, True):
                scatter.wait_sends(back, last)
        scatter.end(layers)
        totals.end()


FF = 1536


def from_behind(value, axis, by):
    peers = lax.axis_size(axis)
    pairs = [(i, i + by) for i in range(peers) if 0 <= i + by < peers]
    return lax.ppermute(value, axis, pairs)


def unblock(blocks, row_count, col_count, block_size):
    return (
        blocks.reshape(row_count // block_size, col_count // block_size, block_size, block_size)
        .transpose(0, 2, 1, 3)
        .reshape(row_count, col_count)
    )


def to_blocks(matrix, block_size):
    row_count, col_count = matrix.shape
    return (
        matrix.reshape(row_count // block_size, block_size, col_count // block_size, block_size)
        .transpose(0, 2, 1, 3)
        .reshape(-1, block_size * block_size)
    )


def split_matrices(blocks, model_width):
    block_size = model_width // 4
    shapes = (
        (model_width, 3 * model_width),
        (model_width, model_width),
        (model_width, FF),
        (FF, model_width),
    )
    result = []
    offset = 0
    for row_count, col_count in shapes:
        number = row_count * col_count // (block_size * block_size)
        result.append(unblock(blocks[offset : offset + number], row_count, col_count, block_size))
        offset = offset + number
    return result


def rms_norm(stream, gain):
    factor = lax.rsqrt(jnp.mean(stream * stream, axis=-1, keepdims=True) + 1e-06)
    return (stream * factor * gain, factor)


def norm_back(stream, factor, gain, grad):
    scaled = grad * gain
    grad_in = factor * scaled - stream * factor**3 * jnp.mean(
        stream * scaled, axis=-1, keepdims=True
    )
    return (grad_in, jnp.sum(grad * stream * factor, axis=0))


def gelu_slope(pre_act):
    return (
        0.5 * (1.0 + lax.erf(pre_act * 0.7071067811865476))
        + pre_act * jnp.exp(-0.5 * pre_act * pre_act) * 0.3989422804014327
    )


def layer_forward(stream, matrices, gain_pair, length):
    w_qkv, w_out, w_up, w_down = matrices
    row_count, model_width = stream.shape
    head_dim = model_width // HEADS
    frames = jnp.arange(row_count)
    norm_one, scale_one = rms_norm(stream, gain_pair[0])
    normed = norm_one.astype(BF16)
    qkv_all = jnp.dot(normed, w_qkv, preferred_element_type=jnp.float32).astype(BF16)
    queries = qkv_all[:, :model_width].reshape(row_count, HEADS, head_dim)
    key_rows = qkv_all[:, model_width : 2 * model_width].reshape(row_count, HEADS, head_dim)
    value_rows = qkv_all[:, 2 * model_width :].reshape(row_count, HEADS, head_dim)
    masking = jnp.where(frames < length, 0.0, -1e30).astype(jnp.float32)
    scores = jnp.einsum(
        "qhe,khe->hqk", queries, key_rows, preferred_element_type=jnp.float32
    ) * head_dim ** (-0.5)
    attn_probs = jax.nn.softmax(scores + masking[None, None, :], axis=-1)
    probs_low = attn_probs.astype(BF16)
    attended = (
        jnp.einsum("hqk,khe->qhe", probs_low, value_rows, preferred_element_type=jnp.float32)
        .reshape(row_count, model_width)
        .astype(BF16)
    )
    branch_attn = jnp.dot(attended, w_out, preferred_element_type=jnp.float32)
    middle = stream + branch_attn
    norm_two, scale_two = rms_norm(middle, gain_pair[1])
    normed_two = norm_two.astype(BF16)
    pre_act = jnp.dot(normed_two, w_up, preferred_element_type=jnp.float32)
    hidden = jax.nn.gelu(pre_act, approximate=False).astype(BF16)
    branch_ffn = jnp.dot(hidden, w_down, preferred_element_type=jnp.float32)
    kept_vals = (
        scale_one,
        normed,
        queries,
        key_rows,
        value_rows,
        attn_probs,
        probs_low,
        attended,
        middle,
        scale_two,
        normed_two,
        pre_act,
        hidden,
    )
    return (middle + branch_ffn, branch_attn, branch_ffn, kept_vals)


def layer_backward(stream, matrices, gain_pair, length, upstream):
    w_qkv, w_out, w_up, w_down = matrices
    row_count, model_width = stream.shape
    head_dim = model_width // HEADS
    output, branch_attn, branch_ffn, kept_vals = layer_forward(stream, matrices, gain_pair, length)
    (
        scale_one,
        normed,
        queries,
        key_rows,
        value_rows,
        attn_probs,
        probs_low,
        attended,
        middle,
        scale_two,
        normed_two,
        pre_act,
        hidden,
    ) = kept_vals
    grad_ffn = upstream.astype(BF16)
    grad_down = jnp.dot(hidden.T, grad_ffn, preferred_element_type=jnp.float32)
    grad_hidden = jnp.dot(grad_ffn, w_down.T, preferred_element_type=jnp.float32)
    grad_pre = (grad_hidden * gelu_slope(pre_act)).astype(BF16)
    grad_up = jnp.dot(normed_two.T, grad_pre, preferred_element_type=jnp.float32)
    back_mid, gain_two = norm_back(
        middle,
        scale_two,
        gain_pair[1],
        jnp.dot(grad_pre, w_up.T, preferred_element_type=jnp.float32),
    )
    grad_mid = upstream + back_mid
    grad_branch = grad_mid.astype(BF16)
    grad_out = jnp.dot(attended.T, grad_branch, preferred_element_type=jnp.float32)
    grad_att = (
        jnp.dot(grad_branch, w_out.T, preferred_element_type=jnp.float32)
        .astype(BF16)
        .reshape(row_count, HEADS, head_dim)
    )
    grad_value = jnp.einsum("hqk,qhe->khe", probs_low, grad_att, preferred_element_type=jnp.float32)
    grad_probs = jnp.einsum(
        "qhe,khe->hqk", grad_att, value_rows, preferred_element_type=jnp.float32
    )
    grad_scores = (
        attn_probs * (grad_probs - jnp.sum(attn_probs * grad_probs, axis=-1, keepdims=True))
    ).astype(BF16)
    grad_query = jnp.einsum(
        "hqk,khe->qhe", grad_scores, key_rows, preferred_element_type=jnp.float32
    ) * head_dim ** (-0.5)
    grad_key = jnp.einsum(
        "hqk,qhe->khe", grad_scores, queries, preferred_element_type=jnp.float32
    ) * head_dim ** (-0.5)
    grad_qkv = jnp.concatenate(
        [
            grad_query.reshape(row_count, model_width),
            grad_key.reshape(row_count, model_width),
            grad_value.reshape(row_count, model_width),
        ],
        axis=1,
    ).astype(BF16)
    grad_wqkv = jnp.dot(normed.T, grad_qkv, preferred_element_type=jnp.float32)
    back_in, gain_one = norm_back(
        stream,
        scale_one,
        gain_pair[0],
        jnp.dot(grad_qkv, w_qkv.T, preferred_element_type=jnp.float32),
    )
    return (
        grad_mid + back_in,
        (grad_wqkv, grad_out, grad_up, grad_down),
        jnp.stack([gain_one, gain_two]),
    )


def spectral_terms(output, target, length, present_row, frame_count):
    row_count, model_width = output.shape
    bin_count = model_width // 8
    spectra = output.reshape(row_count, 4, 2, bin_count)
    real_part = spectra[:, :, 0]
    imag_part = spectra[:, :, 1]
    magnitude = jnp.sqrt(real_part * real_part + imag_part * imag_part + 0.01)
    differ = magnitude - target.reshape(row_count, 4, bin_count)
    smooth_err = jnp.sqrt(differ * differ + 0.01)
    weight = (jnp.arange(row_count) < length).astype(jnp.float32)[:, None, None] * present_row[
        None, :, None
    ]
    loss_slope = weight * differ / smooth_err / magnitude / frame_count
    grad_spec = jnp.stack([loss_slope * real_part, loss_slope * imag_part], axis=2).reshape(
        row_count, model_width
    )
    return (jnp.sum(smooth_err * weight), grad_spec)


def pipelined_body(
    x_in,
    targets,
    valid_len,
    present_stems,
    w_master,
    norm_gains,
    gain_m,
    gain_v,
    l_stats,
    r_stats,
    l_roots,
    r_roots,
    step_count,
):
    model_width = x_in.shape[1]
    block_size = model_width // 4
    sections = lax.axis_size("section")
    section_idx = lax.axis_index("section")
    half_way = sections // 2
    groups = lax.axis_size("dp")
    group_idx = lax.axis_index("dp")
    micro_count = valid_len.shape[0] // groups
    seg_len = x_in.shape[0] // micro_count
    own_blocks = w_master.shape[1]
    own_gain = norm_gains.shape[2]
    full_w, full_g = (
        lax.all_gather(w_master.astype(BF16), "dp", axis=1, tiled=True),
        lax.all_gather(norm_gains.astype(BF16), "dp", axis=2, tiled=True),
    )
    matrices = split_matrices(full_w[0], model_width)
    gain_pair = full_g[0].astype(jnp.float32)
    lengths = lax.dynamic_slice_in_dim(valid_len, group_idx * micro_count, micro_count)
    stem_flags = lax.dynamic_slice_in_dim(
        present_stems, group_idx * micro_count, micro_count
    ).astype(jnp.float32)
    frame_count = jnp.sum(valid_len).astype(jnp.float32)
    decoder = section_idx >= half_way
    encoder = section_idx < half_way
    is_last = section_idx == sections - 1
    act_shape = (micro_count, seg_len, model_width)

    def forward_step(step_idx, loop_state):
        in_rows, kept_prev, skip_store, loss_grads, loss_sum, sq_sums = loop_state
        micro_idx = step_idx - section_idx
        active = (micro_idx >= 0) & (micro_idx < micro_count)
        slot_idx = jnp.clip(micro_idx, 0, micro_count - 1)
        fresh_rows = lax.dynamic_slice_in_dim(x_in, slot_idx * seg_len, seg_len, 0)
        previous = jnp.where(section_idx == 0, fresh_rows, in_rows)
        stream = previous.astype(jnp.float32) + jnp.where(
            decoder, skip_store[slot_idx].astype(jnp.float32), 0.0
        )
        length = lengths[slot_idx]
        target = lax.dynamic_slice_in_dim(targets, slot_idx * seg_len, seg_len, 0)

        def forward_compute_fn(operand):
            output, branch_attn, branch_ffn, kept_vals = layer_forward(
                stream, matrices, gain_pair, length
            )
            valid = (jnp.arange(seg_len) < length).astype(jnp.float32)[:, None]
            squares = jnp.stack(
                [
                    jnp.sum(valid * stream * stream),
                    jnp.sum(valid * branch_attn * branch_attn),
                    jnp.sum(valid * branch_ffn * branch_ffn),
                ]
            )
            seg_loss, grad_spec = spectral_terms(
                output, target, length, stem_flags[slot_idx], frame_count
            )
            return (output, squares, seg_loss, grad_spec)

        def forward_spare_fn(operand):
            empty = jnp.zeros((seg_len, model_width), jnp.float32)
            return (empty, jnp.zeros((3,), jnp.float32), jnp.zeros((), jnp.float32), empty)

        output, squares, seg_loss, grad_spec = lax.cond(
            active, forward_compute_fn, forward_spare_fn, 0
        )
        kept_prev = kept_prev.at[slot_idx].set(jnp.where(active, previous, kept_prev[slot_idx]))
        loss_grads = loss_grads.at[slot_idx].set(
            jnp.where(active & is_last, grad_spec, loss_grads[slot_idx])
        )
        loss_sum = loss_sum + jnp.where(is_last, seg_loss, 0.0)
        sq_sums = sq_sums + squares
        sent_rows = output.astype(BF16)
        in_rows = from_behind(sent_rows, "section", 1)
        from_encoder = from_behind(sent_rows, "section", half_way)
        recv_idx = step_idx - section_idx + half_way
        usable = decoder & (recv_idx >= 0) & (recv_idx < micro_count)
        recv_slot = jnp.clip(recv_idx, 0, micro_count - 1)
        skip_store = skip_store.at[recv_slot].set(
            jnp.where(usable, from_encoder, skip_store[recv_slot])
        )
        return (in_rows, kept_prev, skip_store, loss_grads, loss_sum, sq_sums)

    start_state = (
        jnp.zeros((seg_len, model_width), BF16),
        jnp.zeros(act_shape, BF16),
        jnp.zeros(act_shape, BF16),
        jnp.zeros(act_shape, jnp.float32),
        jnp.zeros((), jnp.float32),
        jnp.zeros((3,), jnp.float32),
    )
    unused_rows, kept_prev, skip_store, loss_grads, loss_sum, sq_sums = lax.fori_loop(
        0, micro_count + sections - 1, forward_step, start_state
    )

    def backward_step(step_idx, loop_state):
        in_grads, skip_grad_store, grad_mats, grad_gains = loop_state
        micro_idx = step_idx - (sections - 1 - section_idx)
        active = (micro_idx >= 0) & (micro_idx < micro_count)
        slot_idx = jnp.clip(micro_idx, 0, micro_count - 1)
        upstream = jnp.where(
            is_last,
            loss_grads[slot_idx],
            in_grads.astype(jnp.float32)
            + jnp.where(encoder, skip_grad_store[slot_idx].astype(jnp.float32), 0.0),
        )
        stream = kept_prev[slot_idx].astype(jnp.float32) + jnp.where(
            decoder, skip_store[slot_idx].astype(jnp.float32), 0.0
        )
        length = lengths[slot_idx]

        def backward_compute_fn(operand):
            return layer_backward(stream, matrices, gain_pair, length, upstream)

        def backward_spare_fn(operand):
            return (
                jnp.zeros_like(stream),
                tuple((jnp.zeros(mat.shape, jnp.float32) for mat in matrices)),
                jnp.zeros((2, model_width), jnp.float32),
            )

        grad_stream, layer_mats, layer_gains = lax.cond(
            active, backward_compute_fn, backward_spare_fn, 0
        )
        grad_mats = tuple((total + piece for total, piece in zip(grad_mats, layer_mats)))
        grad_gains = grad_gains + layer_gains
        grad_rows = grad_stream.astype(BF16)
        in_grads = from_behind(grad_rows, "section", -1)
        from_decoder = from_behind(grad_rows, "section", -half_way)
        recv_idx = micro_idx + half_way
        usable = encoder & (recv_idx >= 0) & (recv_idx < micro_count)
        recv_slot = jnp.clip(recv_idx, 0, micro_count - 1)
        skip_grad_store = skip_grad_store.at[recv_slot].set(
            jnp.where(usable, from_decoder, skip_grad_store[recv_slot])
        )
        return (in_grads, skip_grad_store, grad_mats, grad_gains)

    back_state = (
        jnp.zeros((seg_len, model_width), BF16),
        jnp.zeros(act_shape, BF16),
        tuple((jnp.zeros(mat.shape, jnp.float32) for mat in matrices)),
        jnp.zeros((2, model_width), jnp.float32),
    )
    unused_grads, unused_store, grad_mats, grad_gains = lax.fori_loop(
        0, micro_count + sections - 1, backward_step, back_state
    )
    grad_all = jnp.concatenate([to_blocks(mat, block_size) for mat in grad_mats], axis=0)
    summed_w, summed_g = lax.psum((grad_all, grad_gains), "dp")
    own_grad = lax.dynamic_slice_in_dim(summed_w, group_idx * own_blocks, own_blocks, 0)
    own_gain_grad = lax.dynamic_slice_in_dim(summed_g, group_idx * own_gain, own_gain, 1)
    own_square = jnp.sum(own_grad * own_grad) + jnp.sum(own_gain_grad * own_gain_grad)
    rows_local = jnp.zeros((sections, 3), jnp.float32).at[section_idx].set(sq_sums)
    total_square, loss_value, rows_total = lax.psum(
        (own_square, loss_sum / frame_count, rows_local), ("section", "dp")
    )
    grad_norm = jnp.sqrt(total_square)
    clip_limit = 0.00015 * math.sqrt(
        sections * (own_blocks * groups * block_size * block_size + 2 * model_width)
    )
    factor = clip_limit / jnp.maximum(grad_norm, clip_limit)
    grad_blocks = own_grad * factor
    square = (own_blocks, block_size, block_size)
    shaped = grad_blocks.reshape(square)
    highest = lax.Precision.HIGHEST
    l_new = 0.95 * l_stats[0].reshape(square) + 0.05 * jnp.einsum(
        "bij,bkj->bik", shaped, shaped, precision=highest
    )
    r_new = 0.95 * r_stats[0].reshape(square) + 0.05 * jnp.einsum(
        "bji,bjk->bik", shaped, shaped, precision=highest
    )
    left_side = jnp.einsum("bij,bjk->bik", l_roots[0].reshape(square), shaped, precision=highest)
    precond = jnp.einsum("bij,bjk->bik", left_side, r_roots[0].reshape(square), precision=highest)
    master = w_master[0]
    w_new = master - 0.5 * (precond.reshape(master.shape) + 0.01 * master)
    gain_grad = own_gain_grad * factor
    m_new = 0.9 * gain_m[0] + 0.1 * gain_grad
    v_new = 0.999 * gain_v[0] + 0.001 * gain_grad * gain_grad
    step_num = step_count[0].astype(jnp.float32)
    m_hat = m_new / (1.0 - jnp.power(0.9, step_num))
    v_hat = v_new / (1.0 - jnp.power(0.999, step_num))
    gains_new = norm_gains[0] - 0.5 * m_hat / (jnp.sqrt(v_hat) + 1e-08)
    rms = jnp.sqrt(rows_total[section_idx] / (frame_count * model_width)).reshape(1, 3)
    return (
        w_new[None],
        grad_blocks[None],
        l_new.reshape(master.shape)[None],
        r_new.reshape(master.shape)[None],
        gains_new[None],
        m_new[None],
        v_new[None],
        loss_value,
        grad_norm,
        rms,
    )


def layer_block(shape):
    return pl.BlockSpec((1,) + shape, lambda i: (i,) + (0,) * len(shape))


def whole_block(shape):
    return pl.BlockSpec(shape, lambda i: (0,) * len(shape))


def held_block(shape):
    return pl.BlockSpec(shape, lambda i: (0,) * len(shape), pipeline_mode=pl.Buffered(1))


def forward(layers, micro, valid_len, present_stems, x_in, targets, flat_w, gain):
    width = x_in.shape[1]
    seg = x_in.shape[0] // micro
    dim = width // HEADS
    part = width // 4
    half = layers // 2
    shapes = (
        (HEADS, seg, seg), (3, seg, width), (seg, width), (seg, width), (4, seg, width), (4, seg, width)
    )
    kinds = (BF16, BF16, BF16, F32, BF16, BF16)

    def slot():
        return jnp.minimum(lax.axis_index("section"), micro - 1)

    return pl.pallas_call(
        functools.partial(forward_kernel, layers, half, micro),
        grid=(layers,),
        in_specs=[
            pl.BlockSpec(memory_space=pltpu.SMEM),
            pl.BlockSpec(memory_space=pltpu.SMEM),
            pl.BlockSpec((seg, width), lambda i: (slot(), 0)),
            pl.BlockSpec((width // 2, seg), lambda i: (0, slot())),
            pl.BlockSpec(memory_space=pltpu.VMEM),
            pl.BlockSpec(memory_space=pltpu.VMEM),
        ],
        out_specs=[layer_block(s) for s in shapes]
        + [whole_block((layers, seg, width)), whole_block((seg, width)), whole_block((layers, 8, width))]
        + [pl.BlockSpec(memory_space=pl.ANY), whole_block((layers, 8, width))],
        out_shape=[jax.ShapeDtypeStruct((layers,) + s, k) for s, k in zip(shapes, kinds)]
        + [
            jax.ShapeDtypeStruct((layers, seg, width), BF16),
            jax.ShapeDtypeStruct((seg, width), F32),
            jax.ShapeDtypeStruct((layers, 8, width), F32),
            jax.ShapeDtypeStruct((layers, 48 * part, width), BF16),
            jax.ShapeDtypeStruct((layers, 8, width), F32),
        ],
        scratch_shapes=[
            pltpu.VMEM((seg, width), F32),
            pltpu.VMEM((seg, width), BF16),
            pltpu.VMEM((layers, 48 * part, width), BF16),
            pltpu.VMEM((layers, 8, 8, 128), F32),
            pltpu.VMEM((6 * part, width), BF16),
            pltpu.VMEM((8, 128), F32),
            pltpu.VMEM((4, part, 128), F32),
            pltpu.SemaphoreType.DMA((2, 3)),
            pltpu.SemaphoreType.DMA((2, layers, 4)),
            pltpu.SemaphoreType.DMA((2, layers, 4)),
            pltpu.SemaphoreType.DMA((2, layers, 8)),
            pltpu.SemaphoreType.DMA((2, layers, 8)),
            pltpu.SemaphoreType.DMA((2, 10)),
            pltpu.SemaphoreType.DMA((layers,)),
        ],
        compiler_params=pltpu.CompilerParams(
            vmem_limit_bytes=VMEM_LIMIT, collective_id=0, has_side_effects=True
        ),
    )(valid_len, present_stems, x_in, targets.T, flat_w, gain)


def backward(layers, loss_grad, full_w, full_g, sent, saved, stats):
    seg, width = loss_grad.shape
    dim = width // HEADS
    part = width // 4
    half = layers // 2

    def from_end(array):
        shape = array.shape[1:]
        return pl.BlockSpec((1,) + shape, lambda i: (layers - 1 - i,) + (0,) * len(shape))

    return pl.pallas_call(
        functools.partial(backward_kernel, layers, half),
        grid=(layers,),
        in_specs=[
            held_block((seg, width)),
            from_end(full_w),
            from_end(full_g),
            held_block((layers, seg, width)),
        ]
        + [from_end(a) for a in saved]
        + [pl.BlockSpec(memory_space=pltpu.VMEM)],
        out_specs=[pl.BlockSpec(memory_space=pltpu.VMEM)] * 3,
        out_shape=[
            jax.ShapeDtypeStruct((6 * part, width), F32),
            jax.ShapeDtypeStruct((16, width), F32),
            jax.ShapeDtypeStruct((8, 128), F32),
        ],
        scratch_shapes=[
            pltpu.VMEM((layers, seg, width), BF16),
            pltpu.VMEM((seg, width), BF16),
            pltpu.VMEM((4, seg, width), BF16),
            pltpu.VMEM((seg, width), BF16),
            pltpu.VMEM((seg, width), F32),
            pltpu.VMEM((seg, width), BF16),
            pltpu.VMEM((seg, width), BF16),
            pltpu.VMEM((3, seg, width), BF16),
            pltpu.VMEM((layers, 8, width), F32),
            pltpu.VMEM((2, 4, 2, 576, width), BF16),
            pltpu.VMEM((2, 4, 2, 288, width), BF16),
            pltpu.VMEM((layers, 4, 2, 80, width), BF16),
            pltpu.VMEM((layers, 4, 208, width), BF16),
            pltpu.VMEM((layers, 4, 208, width), BF16),
            pltpu.VMEM((layers, 3, 208, width), BF16),
            pltpu.VMEM((3, 208, width), BF16),
            pltpu.VMEM((6, 16, width), F32),
            pltpu.VMEM((4, 16, width), F32),
            pltpu.VMEM((4, 8, 128), F32),
            pltpu.VMEM((8, 8, 128), F32),
            pltpu.SemaphoreType.DMA((2, 2, 3)),
            pltpu.SemaphoreType.DMA((2, layers, 4)),
            pltpu.SemaphoreType.DMA((2, layers, 4)),
            pltpu.SemaphoreType.DMA((2, layers, 4)),
            pltpu.SemaphoreType.DMA((2, layers)),
            pltpu.SemaphoreType.DMA((2, 3)),
            pltpu.SemaphoreType.DMA((2, 3)),
            pltpu.SemaphoreType.DMA((2, 3)),
            pltpu.SemaphoreType.DMA((2, 7)),
        ],
        compiler_params=pltpu.CompilerParams(
            vmem_limit_bytes=VMEM_LIMIT, collective_id=1, has_side_effects=True
        ),
    )(loss_grad, full_w, full_g, sent, *saved, stats)


def split(value):
    high = value.astype(BF16)
    return high, (value - high.astype(F32)).astype(BF16)


def dot_split(dot, left, right):
    return dot(left[0], right[0]) + (dot(left[0], right[1]) + dot(left[1], right[0]))


def update_kernel(
    layers, limit, length_ref, step_ref, square_ref, tile_ref, quads_ref, w_ref, l_ref, r_ref, lroot_ref, rroot_ref,
    gain_ref, gain_m_ref, gain_v_ref,
    w_out, grad_out, l_out, r_out, gain_out, m_out, v_out, loss_out, norm_out, rms_out,
    block_ref,
):
    part, width = quads_ref.shape[1:]
    gains = tile_ref[: 2 * layers]
    norm = jnp.sqrt(jnp.sum(square_ref[...], keepdims=True) + jnp.sum(gains * gains, keepdims=True))
    factor = limit / jnp.maximum(norm, limit)

    def quad_step(q, _):
        for c in range(4):
            base = 4 * q + c
            load_block(lroot_ref, base, block_ref.at[0])
            load_block(rroot_ref, base, block_ref.at[1])
            grad = quads_ref[q, :, part * c : part * (c + 1)] * factor
            pair = split(grad)
            left = dot_split(dot_nn, split(block_ref[0, :, :part]), pair)
            pre = dot_split(dot_nn, split(left), split(block_ref[1, :, :part]))
            for i, value in enumerate((
                grad, pre, dot_split(dot_nt, pair, pair), dot_split(dot_tn, pair, pair)
            )):
                block_ref[2 + i, :, :part] = value
            parts = [flat_parts(block_ref.at[2 + i]) for i in range(4)]
            for m in range(3):
                at = (pl.ds(base + 8 * m, 24, stride=24), slice(None))
                grad_out[at] = parts[0][m]
                master = w_ref[at]
                w_out[at] = master - 0.5 * (parts[1][m] + 0.01 * master)
                l_out[at] = 0.95 * l_ref[at] + 0.05 * parts[2][m]
                r_out[at] = 0.95 * r_ref[at] + 0.05 * parts[3][m]
        return 0

    for q in range(2):
        quad_step(q, 0)

    @pl.when(pl.program_id(0) == 0)
    def _():
        section, group = lax.axis_index("section"), lax.axis_index("dp")
        share = gain_ref.shape[1]
        row = tile_ref[:2]
        for k in range(1, layers):
            row = jnp.where(section == k, tile_ref[2 * k : 2 * k + 2], row)
        own = row[:, :share]
        for g in range(1, width // share):
            own = jnp.where(group == g, row[:, g * share : (g + 1) * share], own)
        grad = own * factor
        m_new = 0.9 * gain_m_ref[...] + 0.1 * grad
        v_new = 0.999 * gain_v_ref[...] + 0.001 * grad * grad
        step = jnp.full((1, 1), step_ref[0], jnp.int32).astype(F32)
        m_hat = m_new / (1.0 - jnp.exp(step * math.log(0.9)))
        v_hat = v_new / (1.0 - jnp.exp(step * math.log(0.999)))
        gain_out[...] = gain_ref[...] - 0.5 * m_hat / (jnp.sqrt(v_hat) + 1e-08)
        m_out[...] = m_new
        v_out[...] = v_new
        norm_out[...] = norm
        frames = length_ref[0]
        for k in range(1, length_ref.shape[0]):
            frames = frames + length_ref[k]
        frames = jnp.full((1, 1), frames, jnp.int32).astype(F32)
        loss_out[...] = tile_ref[2 * layers : 2 * layers + 1, 3:4] / frames
        squares = tile_ref[2 * layers : 2 * layers + 1, :3]
        for k in range(1, layers):
            squares = jnp.where(section == k, tile_ref[2 * layers + k : 2 * layers + k + 1, :3], squares)
        rms_out[...] = jnp.sqrt(squares / (frames * width))


def update(layers, limit, valid_len, step_count, squares, tile, quads, flats, gains):
    blocks = 4 * quads.shape[0]
    part, width = quads.shape[1:]
    rows = flats[0].shape[0]
    whole = [pl.BlockSpec(memory_space=pltpu.VMEM)]
    flat = [pl.BlockSpec((rows // 3, 128), lambda i: (i, 0))]
    share = gains[0].shape
    return pl.pallas_call(
        functools.partial(update_kernel, layers, limit),
        grid=(3,),
        in_specs=[pl.BlockSpec(memory_space=pltpu.SMEM)] * 2 + whole * 2
        + [pl.BlockSpec((2, part, width), lambda i: (i, 0, 0))] + flat * 5 + whole * 3,
        out_specs=flat * 4 + whole * 6,
        out_shape=[jax.ShapeDtypeStruct((rows, 128), F32)] * 4
        + [jax.ShapeDtypeStruct(share, F32)] * 3
        + [jax.ShapeDtypeStruct((1, 1), F32)] * 2 + [jax.ShapeDtypeStruct((1, 3), F32)],
        scratch_shapes=[pltpu.VMEM((6, part, 128), F32)],
        compiler_params=pltpu.CompilerParams(vmem_limit_bytes=VMEM_LIMIT),
    )(valid_len, step_count, squares, tile, quads, *flats, *gains)


def body(
    x_in, targets, valid_len, present_stems, w_master, norm_gains, gain_m, gain_v,
    l_stats, r_stats, l_roots, r_roots, step_count,
):
    width = x_in.shape[1]
    part = width // 4
    layers = lax.axis_size("section")
    groups = lax.axis_size("dp")
    micro = valid_len.shape[0] // groups
    own_blocks = w_master.shape[1]
    flats = [flat_rows(a[0]) for a in (w_master, l_stats, r_stats, l_roots, r_roots)]
    *saved, sent, loss_grad, stats, full_w, full_g = forward(
        layers, micro, valid_len, present_stems, x_in, targets, flats[0], norm_gains[0]
    )
    own_quads, tile, squares = backward(layers, loss_grad, full_w, full_g, sent, saved, stats)
    clip_limit = 0.00015 * math.sqrt(layers * (own_blocks * groups * part * part + 2 * width))
    *news, gains_new, m_new, v_new, loss_value, grad_norm, rms = update(
        layers, clip_limit, valid_len, step_count, squares, tile, own_quads.reshape(-1, part, width), flats,
        (norm_gains[0], gain_m[0], gain_v[0]),
    )
    w_new, grad_blocks, l_new, r_new = (from_flat_rows(a, own_blocks)[None] for a in news)
    return (
        w_new,
        grad_blocks,
        l_new,
        r_new,
        gains_new[None],
        m_new[None],
        v_new[None],
        loss_value.reshape(()),
        grad_norm.reshape(()),
        rms,
    )


def solution(mesh):
    def step(*args):
        layers, groups = mesh.shape["section"], mesh.shape["dp"]
        micro, own_blocks = args[2].shape[0] // groups, args[4].shape[1]
        if micro <= layers == 4 and groups == 8 and own_blocks == 24:
            return body(*args)
        return pipelined_body(*args)

    block = P("section", "dp", None)
    gain = P("section", None, "dp")
    return jax.shard_map(
        step,
        mesh=mesh,
        in_specs=(
            P("dp", None), P("dp", None), P(), P(), block, gain, gain, gain, block, block, block, block, P(),
        ),
        out_specs=(block, block, block, block, gain, gain, gain, P(), P(), P("section", None)),
        check_vma=False,
    )
```

```python
import functools
import math

import jax
import jax.numpy as jnp
from jax import lax
from jax.experimental import pallas as pl
from jax.experimental.pallas import tpu as pltpu
from jax.sharding import PartitionSpec as P

HEADS = 8
F32 = jnp.float32
BF16 = jnp.bfloat16
VMEM_LIMIT = 61 * 1024 * 1024


def dot_nn(a, b):
    return lax.dot_general(a, b, (((1,), (0,)), ((), ())), preferred_element_type=F32)


def dot_nt(a, b):
    return lax.dot_general(a, b, (((1,), (1,)), ((), ())), preferred_element_type=F32)


def dot_tn(a, b):
    return lax.dot_general(a, b, (((0,), (0,)), ((), ())), preferred_element_type=F32)


def gelu_parts(x):
    ax = jnp.abs(x)
    bell = jnp.exp(-0.5 * x * x)
    t = 1.0 / (1.0 + (0.3275911 * 0.7071067811865476) * ax)
    poly = t * (
        0.5 * 0.254829592
        + t
        * (
            0.5 * -0.284496736
            + t * (0.5 * 1.421413741 + t * (0.5 * -1.453152027 + t * (0.5 * 1.061405429)))
        )
    )
    tail = poly * bell
    cdf = jnp.where(x >= 0.0, 1.0 - tail, tail)
    return x * cdf, cdf + x * bell * 0.3989422804014327


def stack_quads(w_ref, first, step, number):
    part = w_ref.shape[2] // 4
    if step == 1:
        return w_ref[0, first * part : (first + number) * part]
    return jnp.concatenate(
        [w_ref[0, (first + step * i) * part : (first + step * i + 1) * part] for i in range(number)], axis=0
    )


def flat_rows(array):
    blocks, area = array.shape
    return (
        array.reshape(blocks // 8, 8, area // 128, 128).transpose(0, 2, 1, 3).reshape(-1, 128)
    )


def from_flat_rows(rows, blocks):
    return (
        rows.reshape(blocks // 8, -1, 8, 128).transpose(0, 2, 1, 3).reshape(blocks, -1)
    )


def load_block(rows_ref, base, block_ref):
    lane = lax.broadcasted_iota(jnp.int32, (24, 128), 1)
    a, b, c = (rows_ref[pl.ds(base + 8 * m, 24, stride=24), :] for m in range(3))
    block_ref[pl.ds(0, 24, stride=4), :] = a
    block_ref[pl.ds(1, 24, stride=4), :] = jnp.where(lane < 32, pltpu.roll(a, 32, 1), pltpu.roll(b, 32, 1))
    block_ref[pl.ds(2, 24, stride=4), :] = jnp.where(lane < 64, pltpu.roll(b, 64, 1), pltpu.roll(c, 64, 1))
    block_ref[pl.ds(3, 24, stride=4), :] = pltpu.roll(c, 96, 1)


def flat_parts(block_ref):
    lane = lax.broadcasted_iota(jnp.int32, (24, 128), 1)
    a, b, c, d = (block_ref[pl.ds(r, 24, stride=4), :] for r in range(4))
    b, c, d = pltpu.roll(b, 96, 1), pltpu.roll(c, 64, 1), pltpu.roll(d, 32, 1)
    return jnp.where(lane < 96, a, b), jnp.where(lane < 64, b, c), jnp.where(lane < 32, c, d)


MESH = pl.DeviceIdType.MESH


def mesh_place():
    section = lax.axis_index("section")
    group = lax.axis_index("dp")
    core = lax.rem(section, 2)
    y = lax.rem(group, 2)
    z = group // 2
    z_peers = (z, z + 1 - 2 * lax.rem(z, 2), lax.rem(z + 2, 4), 3 - z)
    return section, group, core, y, z_peers


def remote(source, target, send_sem, recv_sem, section, group):
    return pltpu.make_async_remote_copy(
        src_ref=source, dst_ref=target, send_sem=send_sem, recv_sem=recv_sem,
        device_id=(section, group), device_id_type=MESH,
    )


class Slabs:
    def __init__(self, rows):
        self.section, self.group, self.core, self.y, self.z_peers = mesh_place()
        self.x = self.section // 2
        self.rows, self.half = rows, rows // 2
        self.edge = self.half * 5 // 18
        self.slab = self.half - self.edge

    def slab_of(self, x, core):
        return pl.ds(pl.multiple_of(self.half * core + self.edge * x, 16), self.slab)

    def edge_of(self, x, core):
        return pl.ds(pl.multiple_of(self.half * core + self.slab * x, 16), self.edge)

    def half_of(self, core):
        return pl.ds(pl.multiple_of(self.half * core, 16), self.half)

    def x_peer(self):
        return lax.rem(self.section + 2, 4), self.group

    def y_peer(self):
        return self.section, self.group + 1 - 2 * self.y

    def z_peer(self, k):
        return self.section, self.z_peers[k] * 2 + self.y

    def core_peer(self):
        return self.section + 1 - 2 * self.core, self.group

    def signal_all(self):
        barrier = pltpu.get_barrier_semaphore()
        for k in range(1, 4):
            place = (lax.rem(self.section + k, 4), self.group)
            pl.semaphore_signal(barrier, inc=1, device_id=place, device_id_type=MESH)
        for k in range(1, 8):
            place = (self.section, lax.rem(self.group + k, 8))
            pl.semaphore_signal(barrier, inc=1, device_id=place, device_id_type=MESH)

    def wait_all(self):
        pl.semaphore_wait(pltpu.get_barrier_semaphore(), 10)


class Gather(Slabs):
    def __init__(self, own_ref, gain_ref, w_ref, gains_ref, sems):
        super().__init__(own_ref.shape[0])
        self.own, self.gain, self.w, self.gains = own_ref, gain_ref, w_ref, gains_ref
        self.spread, self.z_sems, self.y_sems, self.x_sems, self.core_sems, self.gain_sems, self.local = sems
        self.others = [lax.rem(self.section + k, 4) for k in range(1, 4)]

    def chunk(self, k):
        y = self.y if k < 4 else 1 - self.y
        return self.z_peers[k % 4] * 2 + y

    def at(self, layer, group, rows):
        return self.w.at[layer, pl.ds(pl.multiple_of(group * self.rows + rows.start, 16), rows.size)]

    def spread_copy(self, k):
        peer = self.others[k]
        rows = self.slab_of(peer // 2, lax.rem(peer, 2))
        return remote(
            self.own.at[rows], self.at(self.section, self.group, rows),
            self.spread.at[0, k], self.spread.at[1, k], peer, self.group,
        )

    def spread_wait(self, layer):
        ref = self.at(layer, self.group, self.slab_of(self.x, self.core))
        for k in range(3):
            @pl.when(lax.rem(layer + k + 1, 4) == self.section)
            def _():
                remote(ref, ref, self.spread.at[0, k], self.spread.at[1, k], self.others[0], self.group).wait_recv()

    def z_copy(self, layer, k, landed=False):
        ref = self.at(layer, self.chunk(k) if landed else self.group, self.slab_of(self.x, self.core))
        return remote(ref, ref, self.z_sems.at[0, layer, k], self.z_sems.at[1, layer, k], *self.z_peer(k))

    def y_copy(self, layer, k, landed=False):
        ref = self.at(layer, self.chunk(k + 4 if landed else k), self.slab_of(self.x, self.core))
        return remote(ref, ref, self.y_sems.at[0, layer, k], self.y_sems.at[1, layer, k], *self.y_peer())

    def x_copy(self, layer, k, landed=False):
        ref = self.at(layer, self.chunk(k), self.edge_of(1 - self.x if landed else self.x, self.core))
        return remote(ref, ref, self.x_sems.at[0, layer, k], self.x_sems.at[1, layer, k], *self.x_peer())

    def core_copy(self, layer, k, landed=False):
        ref = self.at(layer, self.chunk(k), self.half_of(1 - self.core if landed else self.core))
        return remote(ref, ref, self.core_sems.at[0, layer, k], self.core_sems.at[1, layer, k], *self.core_peer())

    def gain_copy(self, k):
        if k < 7:
            peer = lax.rem(self.group + k + 1, 8)
            return remote(
                self.gain, self.gains.at[self.section, self.group],
                self.gain_sems.at[0, k], self.gain_sems.at[1, k], self.section, peer,
            )
        ref = self.gains.at[self.section]
        return remote(
            ref, ref, self.gain_sems.at[0, k], self.gain_sems.at[1, k], self.others[k - 7], self.group
        )

    def gain_landed(self, k):
        if k < 7:
            ref = self.gains.at[self.section, lax.rem(self.group - k - 1 + 8, 8)]
        else:
            ref = self.gains.at[lax.rem(self.section - (k - 6) + 4, 4)]
        return remote(ref, ref, self.gain_sems.at[0, k], self.gain_sems.at[1, k], self.section, self.group)

    def spread_own(self):
        for k in range(3):
            self.spread_copy(k).start()

    def begin(self):
        @pl.when(self.section == 0)
        def _():
            self.spread_own()

        for k in range(7):
            self.gain_copy(k).start()
        rows = self.slab_of(self.x, self.core)
        self.w[self.section, pl.ds(pl.multiple_of(self.group * self.rows + rows.start, 16), rows.size)] = self.own[rows]
        self.gains[self.section, self.group] = self.gain[...]

    def share_gains(self):
        for k in range(7):
            self.gain_landed(k).wait_recv()
        for k in range(7, 10):
            self.gain_copy(k).start()

    def wait_gains(self):
        for k in range(7, 10):
            self.gain_landed(k).wait_recv()

    def kick(self, layer):
        self.spread_wait(layer)
        for k in range(1, 4):
            self.z_copy(layer, k).start()
        self.y_copy(layer, 0).start()
        self.x_copy(layer, 0).start()

    def serve_z(self, layer, k):
        self.z_copy(layer, k, True).wait_recv()
        self.y_copy(layer, k).start()
        self.x_copy(layer, k).start()

    def serve_y(self, layer, k):
        self.y_copy(layer, k, True).wait_recv()
        self.x_copy(layer, k + 4).start()

    def serve_x(self, layer, k):
        self.x_copy(layer, k, True).wait_recv()
        self.core_copy(layer, k).start()

    def finish_first(self, layer):
        for k in range(8):
            @pl.when(self.z_peers[k % 4] == 0)
            def _():
                self.core_copy(layer, k, True).wait_recv()

    def finish_rest(self, layer):
        for k in range(8):
            @pl.when(self.z_peers[k % 4] != 0)
            def _():
                self.core_copy(layer, k, True).wait_recv()

    def end(self, layers):
        for k in range(3):
            self.spread_copy(k).wait_send()
        for k in range(10):
            self.gain_copy(k).wait_send()

        def per_layer(layer, _):
            for k in range(1, 4):
                self.z_copy(layer, k).wait_send()
            for k in range(4):
                self.y_copy(layer, k).wait_send()
            for k in range(8):
                self.x_copy(layer, k).wait_send()
                self.core_copy(layer, k).wait_send()
            return 0

        lax.fori_loop(0, layers, per_layer, 0)


def segment_info(micro, length_ref, stems_ref):
    section, group = lax.axis_index("section"), lax.axis_index("dp")
    at = group * micro + jnp.minimum(section, micro - 1)
    used = (section < micro).astype(jnp.int32)
    frames = length_ref[0]
    for k in range(1, length_ref.shape[0]):
        frames = frames + length_ref[k]
    return length_ref[at] * used, [stems_ref[at, k] * used for k in range(4)], frames


FIRST_POINTS = {"qkv": "z2 y1 x0 x1", "heads": "z3 x2 x4 x5", "attended": "y2", "ffn1": "x3", "ffn2": "y3 x6", "ffn3": "x7"}
POINTS = {"qkv": "x0 x1", "heads": "z3 x2 x4 x5", "attended": "y2", "ffn0": "x3", "ffn1": "y3", "ffn2": "x6", "ffn3": "x7"}
AHEAD_POINTS = {"attended": "z1 y0", "ffn2": "z2", "ffn3": "y1"}


def forward_kernel(
    layers, half, micro, length_ref, stems_ref, x_ref, target_ref, flat_ref, raw_gain_ref,
    probs_ref, qkv_ref, att_ref, middle_ref, hidden_ref, slope_ref, sent_ref, loss_grad_ref, stats_ref,
    full_ref, gains_out_ref,
    out_ref, normed_ref, w_all_ref, gains_ref, own_ref, own_gain_ref, block_ref, *sems,
):
    seg, width = x_ref.shape
    dim = width // HEADS
    part = width // 4
    layer = pl.program_id(0)
    rows = 256
    chunks = seg // rows
    length, present_flags, frame_total = segment_info(micro, length_ref, stems_ref)
    gather = Gather(own_ref, own_gain_ref, w_all_ref, gains_ref, sems)
    w_ref = w_all_ref.at[pl.ds(layer, 1)]

    def own_step(q, _):
        for c in range(4):
            block = 4 * q + c
            load_block(flat_ref, (block // 8) * 576 + lax.rem(block, 8), block_ref.at[c])
        quad = jnp.concatenate([block_ref[c, :, :part] for c in range(4)], axis=1)
        own_ref[pl.ds(pl.multiple_of(q * part, part), part)] = quad.astype(BF16)
        return 0

    def keep_copy(index):
        return pltpu.make_async_copy(w_all_ref.at[index], full_ref.at[index], gather.local.at[index])

    @pl.when(layer == 0)
    def _():
        gather.signal_all()
        for q in range(flat_ref.shape[0] // 288):
            own_step(q, 0)
        own_gain_ref[...] = jnp.zeros_like(own_gain_ref)
        own_gain_ref[:2, : raw_gain_ref.shape[1]] = raw_gain_ref[...]
        gather.wait_all()
        gather.begin()
        sent_ref[0] = x_ref[...]
        stats_ref[...] = jnp.zeros_like(stats_ref)
        gather.kick(0)

        @pl.when(gather.section != 0)
        def _():
            gather.spread_own()

        gather.share_gains()
        gather.serve_z(0, 1)
        gather.serve_z(0, 2)
        gather.kick(1)
        gather.serve_x(0, 0)
        gather.serve_x(0, 1)
        gather.serve_z(0, 3)
        gather.wait_gains()
        gather.serve_y(0, 0)
        gather.serve_x(0, 2)
        gather.serve_y(0, 1)
        gather.serve_y(0, 2)
        gather.serve_x(0, 3)
        gather.serve_y(0, 3)
        for k in range(4, 8):
            gather.serve_x(0, k)
        gather.serve_z(1, 1)
        gather.serve_y(1, 0)

    @pl.when(layer + 2 < layers)
    def _():
        gather.kick(layer + 2)

    gather.finish_first(layer)
    more = layer + 1 < layers

    def serve(point):
        for here, steps, later in (
            (layer == 0, FIRST_POINTS.get(point, ""), ""),
            (layer > 0, POINTS.get(point, ""), ""),
            (layer >= 0, "", AHEAD_POINTS.get(point, "")),
        ):
            for names, back in ((steps, 1), (later, 2)):
                if names:
                    @pl.when((layer + back < layers) & here)
                    def _():
                        for name in names.split():
                            getattr(gather, "serve_" + name[0])(layer + back, int(name[1]))

    def stream_of(at):
        prev = sent_ref[layer, at].astype(F32)
        skip = sent_ref[jnp.maximum(layer + 1 - half, 0), at].astype(F32)
        return prev + jnp.where(layer >= half, skip, 0.0)

    def gain_row(which):
        return jnp.concatenate(
            [gains_ref[layer, g, which : which + 1, : width // 8] for g in range(8)], axis=1
        ).astype(BF16).astype(F32)

    gain_one = gain_row(0)
    gain_two = gain_row(1)
    gains_out_ref[layer, 0:1] = gain_one
    gains_out_ref[layer, 1:2] = gain_two

    first_stream = stream_of(slice(None))
    first_factor = lax.rsqrt(jnp.mean(first_stream * first_stream, axis=-1, keepdims=True) + 1e-06)
    first_normed = (first_stream * first_factor * gain_one).astype(BF16)
    for t in range(3):
        qkv_ref[0, t] = dot_nn(first_normed, stack_quads(w_ref, t, 3, 4)).astype(BF16)
    serve("qkv")
    frames = lax.broadcasted_iota(jnp.int32, (1, seg), 1)
    masking = jnp.where(frames < length, 0.0, -1e30).astype(F32)

    def head_step(h):
        queries, keys, values = (qkv_ref[0, t, :, h * dim : (h + 1) * dim] for t in range(3))
        scores = dot_nt(queries, keys) * dim ** (-0.5) + masking
        top = jnp.max(scores, axis=-1, keepdims=True)
        expd = jnp.exp(scores - top)
        probs = (expd * (1.0 / jnp.sum(expd, axis=-1, keepdims=True))).astype(BF16)
        probs_ref[0, h] = probs
        return dot_nn(probs, values).astype(BF16)

    def put_heads(first):
        heads = [head_step(h) for h in range(first, first + HEADS // 2)]
        att_ref[0, :, first * dim : (first + HEADS // 2) * dim] = jnp.concatenate(heads, axis=1)

    put_heads(0)
    serve("heads")
    put_heads(HEADS // 2)
    serve("attended")
    gather.finish_rest(layer)
    keep_copy(layer).start()

    valid = (lax.broadcasted_iota(jnp.int32, (seg, 1), 0) < length).astype(F32)

    def add_stat(k, value):
        stats_ref[layer, k : k + 1] = jnp.sum(valid * value * value, axis=0, keepdims=True)

    branch_attn = dot_nn(att_ref[0], stack_quads(w_ref, 12, 1, 4))
    stream = stream_of(slice(None))
    middle = stream + branch_attn
    middle_ref[0] = middle
    add_stat(0, stream)
    add_stat(1, branch_attn)
    factor = lax.rsqrt(jnp.mean(middle * middle, axis=-1, keepdims=True) + 1e-06)
    normed_ref[...] = (middle * factor * gain_two).astype(BF16)

    def ffn_step(c):
        pre_act = dot_nn(normed_ref[...], stack_quads(w_ref, 16 + c, 4, 4))
        hidden, slope = gelu_parts(pre_act)
        hidden = hidden.astype(BF16)
        hidden_ref[0, c] = hidden
        slope_ref[0, c] = slope.astype(BF16)
        part_sum = dot_nn(hidden, stack_quads(w_ref, 32 + 4 * c, 1, 4))
        out_ref[...] = part_sum if c == 0 else out_ref[...] + part_sum

    for c in range(4):
        ffn_step(c)
        if c < 3:
            serve(f"ffn{c}")
    branch_ffn = out_ref[...]
    add_stat(2, branch_ffn)
    output = middle_ref[0] + branch_ffn
    out_ref[...] = output

    @pl.when(layer + 1 < layers)
    def _():
        sent_ref[layer + 1] = out_ref[...].astype(BF16)

    serve("ffn3")

    @pl.when(layer == layers - 1)
    def _():
        bins = width // 8
        lane = lax.broadcasted_iota(jnp.int32, (1, width), 1)
        is_real = lax.rem(lane, 2 * bins) < bins
        stem = lane // (2 * bins)
        present = jnp.zeros((1, width), F32)
        for k in range(4):
            present = jnp.where(stem == k, present_flags[k].astype(F32), present)
        inverse = 1.0 / jnp.full((1, 1), frame_total, jnp.int32).astype(F32)

        def loss_step(i, _):
            at = pl.ds(pl.multiple_of(i * rows, rows), rows)
            output = out_ref[at]
            square = output * output
            other = jnp.where(
                is_real, pltpu.roll(square, width - bins, 1), pltpu.roll(square, bins, 1)
            )
            magnitude = jnp.sqrt(square + other + 0.01)
            goal = target_ref[:, at].T
            goal = jnp.concatenate(
                [goal[:, (k // 2) * bins : (k // 2 + 1) * bins] for k in range(8)], axis=1
            )
            differ = magnitude - goal
            smooth = jnp.sqrt(differ * differ + 0.01)
            valid = (lax.broadcasted_iota(jnp.int32, (rows, 1), 0) + i * rows < length).astype(F32)
            weight = valid * present
            loss_grad_ref[at] = weight * differ * output * inverse / (smooth * magnitude)
            stats_ref[0, 3:4] += jnp.sum(
                jnp.where(is_real, weight * smooth, 0.0), axis=0, keepdims=True
            )
            return 0

        lax.fori_loop(0, chunks, loss_step, 0)
        gather.end(layers)
        for k in range(layers):
            keep_copy(k).wait()


class Scatter(Slabs):
    PARTS = ((3, 4), (1, 3), (0, 1))

    def __init__(self, refs, sems):
        self.grads, self.core_in, self.x_in, self.y_in, self.stage, self.z_in, self.last_in = refs
        super().__init__(self.grads.shape[3])
        self.core_sems, self.x_sems, self.y_sems, self.z_sems, self.last_sems = sems
        self.mine = self.slab_of(self.x, self.core)
        self.z = self.z_peers[0]

    def core_copy(self, layer, number):
        slot = lax.rem(layer, 2)
        first, last = self.PARTS[number]
        zs = pl.ds(first, last - first)
        return remote(
            self.grads.at[slot, zs, :, self.half_of(1 - self.core)], self.core_in.at[slot, zs],
            self.core_sems.at[0, slot, number], self.core_sems.at[1, slot, number], *self.core_peer(),
        )

    def x_copy(self, layer, z):
        slot = lax.rem(layer, 2)
        return remote(
            self.grads.at[slot, z, :, self.edge_of(1 - self.x, self.core)], self.x_in.at[layer, z],
            self.x_sems.at[0, layer, z], self.x_sems.at[1, layer, z], *self.x_peer(),
        )

    def y_copy(self, layer, z):
        slot = lax.rem(layer, 2)
        return remote(
            self.grads.at[slot, z, 1 - self.y, self.mine], self.y_in.at[layer, z],
            self.y_sems.at[0, layer, z], self.y_sems.at[1, layer, z], *self.y_peer(),
        )

    def z_copy(self, layer, z):
        place = jnp.maximum(self.z_peers[z] - 1, 0)
        return remote(
            self.stage.at[layer, z], self.z_in.at[layer, place],
            self.z_sems.at[0, layer, z], self.z_sems.at[1, layer, place], self.section, z * 2 + self.y,
        )

    def z_landed(self, layer, place):
        ref = self.z_in.at[layer, place]
        return remote(ref, ref, self.z_sems.at[0, layer, 0], self.z_sems.at[1, layer, place], *self.z_peer(place + 1))

    def last_copy(self, layer):
        place = jnp.maximum(lax.rem(self.section - layer + 4, 4) - 1, 0)
        return remote(
            self.stage.at[layer, self.z], self.last_in.at[place],
            self.last_sems.at[0, layer], self.last_sems.at[1, place], layer, self.group,
        )

    def last_landed(self, place):
        return remote(
            self.last_in.at[place], self.last_in.at[place],
            self.last_sems.at[0, 0], self.last_sems.at[1, place], self.section, self.group,
        )

    def add_core(self, layer, number):
        slot = lax.rem(layer, 2)
        self.core_copy(layer, number).wait_recv()
        rows = self.half_of(self.core)
        first, last = self.PARTS[number]

        def add(i, _):
            z, y = i // 2, lax.rem(i, 2)
            self.grads[slot, z, y, rows] = self.grads[slot, z, y, rows] + self.core_in[slot, z, y]
            return 0

        lax.fori_loop(2 * first, 2 * last, add, 0)
        for z in range(first, last):
            self.x_copy(layer, z).start()

    def add_x(self, layer, z):
        slot = lax.rem(layer, 2)
        self.x_copy(layer, z).wait_recv()
        rows = self.edge_of(self.x, self.core)
        inner = pl.ds(pl.multiple_of((self.slab - self.edge) * self.x, 16), self.edge)
        self.grads[slot, z, 1 - self.y, rows] = (
            self.grads[slot, z, 1 - self.y, rows] + self.x_in[layer, z, 1 - self.y]
        )
        self.y_copy(layer, z).start()
        self.stage[layer, z] = self.grads[slot, z, self.y, self.mine]
        self.stage[layer, z, inner] = self.stage[layer, z, inner] + self.x_in[layer, z, self.y]

    def add_y(self, layer, z):
        self.y_copy(layer, z).wait_recv()
        self.stage[layer, z] = self.stage[layer, z] + self.y_in[layer, z]

        @pl.when(self.z != z)
        def _():
            self.z_copy(layer, z).start()

    def add_z(self, layer, result_ref):
        for place in range(3):
            self.z_landed(layer, place).wait_recv()
        total = self.stage[layer, self.z].astype(F32)
        for k in range(3):
            total = total + self.z_in[layer, k].astype(F32)

        @pl.when(layer == self.section)
        def _():
            result_ref[...] = jnp.zeros_like(result_ref)
            result_ref[self.mine] = total

        @pl.when(layer != self.section)
        def _():
            self.stage[layer, self.z] = total.astype(BF16)
            self.last_copy(layer).start()

    def wait_sends(self, layer, last):
        for number in (2,) if last else (0, 1):
            self.core_copy(layer, number).wait_send()
        for z in (0, 1) if last else (2, 3):
            self.x_copy(layer, z).wait_send()
            self.y_copy(layer, z).wait_send()

    def end(self, layers):
        def per_layer(layer, _):
            for z in range(4):
                @pl.when(self.z != z)
                def _():
                    self.z_copy(layer, z).wait_send()

            @pl.when(layer != self.section)
            def _():
                self.last_copy(layer).wait_send()

            return 0

        lax.fori_loop(0, layers, per_layer, 0)

    def collect(self, result_ref):
        for place in (0, 2, 1):
            self.last_landed(place).wait_recv()
            peer = lax.rem(self.section + place + 1, 4)
            rows = self.slab_of(peer // 2, lax.rem(peer, 2))
            result_ref[rows] = result_ref[rows] + self.last_in[place].astype(F32)


class Totals:
    def __init__(self, refs, sems):
        self.stage_in, self.z_in, self.norm_section, self.norm_group = refs
        self.stage_sems, self.z_sems, self.section_sems, self.group_sems = sems
        self.section, self.group, self.core, self.y, self.z_peers = mesh_place()

    def stage_copy(self, k):
        peer = (
            (self.section + 1 - 2 * self.core, self.group),
            (self.section, self.group + 1 - 2 * self.y),
            (lax.rem(self.section + 2, 4), self.group),
        )[k]
        return remote(
            self.stage_in.at[2 * k], self.stage_in.at[2 * k + 1],
            self.stage_sems.at[0, k], self.stage_sems.at[1, k], *peer,
        )

    def z_copy(self, k):
        z = self.z_peers[0]
        return remote(
            self.z_in.at[z], self.z_in.at[z], self.z_sems.at[0, k - 1], self.z_sems.at[1, k - 1],
            self.section, self.z_peers[k] * 2 + self.y,
        )

    def z_landed(self, k):
        z = self.z_peers[k]
        return remote(
            self.z_in.at[z], self.z_in.at[z], self.z_sems.at[0, k - 1], self.z_sems.at[1, k - 1],
            self.section, self.z_peers[k] * 2 + self.y,
        )

    def begin(self, tile):
        self.stage_in[0] = tile
        self.stage_copy(0).start()

    def after_core(self):
        self.stage_copy(0).wait_recv()
        self.stage_in[2] = self.stage_in[0] + self.stage_in[1]
        self.stage_copy(1).start()

    def after_y(self):
        self.stage_copy(1).wait_recv()
        self.z_in[self.z_peers[0]] = self.stage_in[2] + self.stage_in[3]
        for k in range(1, 4):
            self.z_copy(k).start()

    def after_z(self):
        for k in range(1, 4):
            self.z_landed(k).wait_recv()
        self.stage_in[4] = self.z_in[0] + self.z_in[1] + self.z_in[2] + self.z_in[3]
        self.stage_copy(2).start()

    def after_x(self):
        self.stage_copy(2).wait_recv()
        return self.stage_in[4] + self.stage_in[5]

    def norm_copy(self, k):
        if k < 3:
            peer = (lax.rem(self.section + k + 1, 4), self.group)
            ref = self.norm_section.at[self.section]
            return remote(ref, ref, self.section_sems.at[0, k], self.section_sems.at[1, k], *peer)
        k = k - 3
        peer = (self.section, lax.rem(self.group + k + 1, 8))
        ref = self.norm_group.at[self.group]
        return remote(ref, ref, self.group_sems.at[0, k], self.group_sems.at[1, k], *peer)

    def norm_landed(self, k):
        if k < 3:
            ref = self.norm_section.at[lax.rem(self.section - k - 1 + 4, 4)]
            return remote(
                ref, ref, self.section_sems.at[0, k], self.section_sems.at[1, k], self.section, self.group
            )
        k = k - 3
        ref = self.norm_group.at[lax.rem(self.group - k - 1 + 8, 8)]
        return remote(ref, ref, self.group_sems.at[0, k], self.group_sems.at[1, k], self.section, self.group)

    def norm(self, value):
        self.norm_section[self.section] = value
        for k in range(3):
            self.norm_copy(k).start()
        for k in range(3):
            self.norm_landed(k).wait_recv()
        total = self.norm_section[0]
        for k in range(1, 4):
            total = total + self.norm_section[k]
        self.norm_group[self.group] = total
        for k in range(3, 10):
            self.norm_copy(k).start()
        for k in range(3, 10):
            self.norm_landed(k).wait_recv()
        total = self.norm_group[0]
        for k in range(1, 8):
            total = total + self.norm_group[k]
        return total

    def end(self):
        for k in range(3):
            self.stage_copy(k).wait_send()
        for k in range(1, 4):
            self.z_copy(k).wait_send()
        for k in range(10):
            self.norm_copy(k).wait_send()


def norm_reverse(value, gain, grad):
    factor = lax.rsqrt(jnp.mean(value * value, axis=-1, keepdims=True) + 1e-06)
    scaled = grad * gain
    mean = jnp.mean(value * scaled, axis=-1, keepdims=True)
    unit = value * factor
    back = factor * scaled - unit * (factor * factor * mean)
    return back, jnp.sum(grad * unit, axis=0, keepdims=True), (unit * gain).astype(BF16)


def backward_kernel(
    layers, half, loss_grad_ref, w_ref, gain_ref, sent_ref,
    probs_ref, qkv_ref, att_ref, middle_ref, hidden_ref, slope_ref, stats_ref,
    result_ref, totals_ref, square_ref,
    sends_ref, dffn_ref, dpre_ref, normed_ref, dmid_ref, datt_ref, dhold_ref, dqkv_ref,
    gain_grad_ref, *comm_refs,
):
    seg, width = loss_grad_ref.shape
    dim = width // HEADS
    part = width // 4
    layer = layers - 1 - pl.program_id(0)
    rows = 512
    chunks = seg // rows
    gain_one = gain_ref[0, 0:1]
    gain_two = gain_ref[0, 1:2]
    scatter = Scatter(comm_refs[:7], comm_refs[11:16])
    totals = Totals(comm_refs[7:11], comm_refs[16:])
    grads_ref = comm_refs[0]
    slot = lax.rem(layer, 2)

    @pl.when(layer == layers - 1)
    def _():
        scatter.signal_all()
        sends_ref[...] = jnp.zeros_like(sends_ref)
        gain_grad_ref[...] = jnp.zeros_like(gain_grad_ref)

    def put_grad(first, step, value):
        for r in range(4):
            quad = first + step * r
            owner = quad // 6
            at = pl.ds(pl.multiple_of(lax.rem(quad, 6) * part, part), part)
            grads_ref[slot, owner // 2, lax.rem(owner, 2), at] = value[r * part : (r + 1) * part].astype(BF16)

    def serve(back, here, *steps):
        @pl.when((layer + back < layers) & here)
        def _():
            for kind, *args in steps:
                getattr(scatter, kind)(layer + back, *args)

    serve(2, True, ("wait_sends", False))
    later = sends_ref[jnp.minimum(layer + 1, layers - 1)].astype(F32)
    skip = sends_ref[jnp.minimum(layer + half, layers - 1)].astype(F32)
    dmid_ref[...] = jnp.where(
        layer == layers - 1, loss_grad_ref[...], later + jnp.where(layer + half < layers, skip, 0.0)
    )
    dffn_ref[...] = dmid_ref[...].astype(BF16)
    for c in range(4):
        put_grad(32 + 4 * c, 1, dot_tn(hidden_ref[0, c], dffn_ref[...]))

    @pl.when(layer == layers - 1)
    def _():
        scatter.wait_all()

    scatter.core_copy(layer, 0).start()

    def ffn_step(i, _):
        at = pl.ds(pl.multiple_of(i * rows, rows), rows)
        dffn = dffn_ref[at]
        dnormed = jnp.zeros((rows, width), F32)
        for c in range(4):
            dhidden = dot_nt(dffn, stack_quads(w_ref, 32 + 4 * c, 1, 4))
            dpre = (dhidden * slope_ref[0, c, at].astype(F32)).astype(BF16)
            dpre_ref[c, at] = dpre
            dnormed = dnormed + dot_nt(dpre, stack_quads(w_ref, 16 + c, 4, 4))
        back, gain_grad, normed = norm_reverse(middle_ref[0, at], gain_two, dnormed)
        gain_grad_ref[layer, 1:2] += gain_grad
        normed_ref[at] = normed
        dmid = dmid_ref[at] + back
        dmid_ref[at] = dmid
        datt = dmid.astype(BF16)
        datt_ref[at] = datt
        dattended = dot_nt(datt, stack_quads(w_ref, 12, 1, 4)).astype(BF16)
        dhold_ref[at] = dattended

        serve(1, i == 0, ("add_y", 3), ("add_x", 1), ("add_core", 2))
        serve(2, i == 0, ("add_y", 0))
        return 0

    lax.fori_loop(0, chunks, ffn_step, 0)

    serve(2, True, ("wait_sends", True))

    def ffn_grad_step(c, _):
        put_grad(16 + c, 4, dot_tn(normed_ref[...], dpre_ref[c]))
        return 0

    for c in range(4):
        ffn_grad_step(c, 0)
    put_grad(12, 1, dot_tn(att_ref[0], datt_ref[...]))
    scatter.core_copy(layer, 1).start()
    scatter.add_core(layer, 0)
    serve(1, True, ("add_x", 2))

    def head_step(h):
        queries, keys, values = (qkv_ref[0, t, :, h * dim : (h + 1) * dim] for t in range(3))
        probs = probs_ref[0, h]
        dhold = dhold_ref[:, h * dim : (h + 1) * dim]
        dprobs = dot_nt(dhold, values)
        wide = probs.astype(F32)
        dot_sum = jnp.sum(wide * dprobs, axis=-1, keepdims=True)
        dscores = (wide * (dprobs - dot_sum)).astype(BF16)
        return (
            (dot_nn(dscores, keys) * dim ** (-0.5)).astype(BF16),
            (dot_tn(dscores, queries) * dim ** (-0.5)).astype(BF16),
            dot_tn(probs, dhold).astype(BF16),
        )

    def put_heads(first, parts):
        for t in range(3):
            dqkv_ref[t, :, first * dim : (first + len(parts)) * dim] = jnp.concatenate([p[t] for p in parts], axis=1)

    put_heads(0, [head_step(h) for h in range(HEADS // 2)])
    scatter.add_core(layer, 1)
    serve(1, True, ("add_x", 0))

    put_heads(HEADS // 2, [head_step(h) for h in range(HEADS // 2, HEADS)])
    scatter.add_x(layer, 3)
    serve(1, True, ("add_y", 1))

    def qkv_step(i, _):
        at = pl.ds(pl.multiple_of(i * rows, rows), rows)
        dnormed = jnp.zeros((rows, width), F32)
        for t in range(3):
            dnormed = dnormed + dot_nt(dqkv_ref[t, at], stack_quads(w_ref, t, 3, 4))
        prev = sent_ref[layer, at].astype(F32)
        skip = sent_ref[jnp.maximum(layer + 1 - half, 0), at].astype(F32)
        stream = prev + jnp.where(layer >= half, skip, 0.0)
        back, gain_grad, normed = norm_reverse(stream, gain_one, dnormed)
        gain_grad_ref[layer, 0:1] += gain_grad
        normed_ref[at] = normed
        sends_ref[layer, at] = (dmid_ref[at] + back).astype(BF16)
        return 0

    lax.fori_loop(0, chunks, qkv_step, 0)

    def qkv_grad_step(t, _):
        put_grad(t, 3, dot_tn(normed_ref[...], dqkv_ref[t]))
        return 0

    for t in range(3):
        qkv_grad_step(t, 0)
    scatter.core_copy(layer, 2).start()
    serve(1, True, ("add_y", 2))
    serve(2, True, ("add_z", result_ref))

    @pl.when(layer == 0)
    def _():
        lane = lax.broadcasted_iota(jnp.int32, (1, width), 1)
        rows_out = [gain_grad_ref[k // 2, k % 2 : k % 2 + 1] for k in range(2 * layers)]
        for k in range(layers):
            row = jnp.zeros((1, width), F32)
            for i in range(4):
                value = jnp.sum(stats_ref[k, i : i + 1], axis=1, keepdims=True)
                row = jnp.where(lane == i, value, row)
            rows_out.append(row)
        rows_out.append(jnp.zeros((16 - 3 * layers, width), F32))
        totals.begin(jnp.concatenate(rows_out, axis=0))
        scatter.add_y(0, 3)
        scatter.add_x(0, 1)
        scatter.add_core(0, 2)
        scatter.add_y(1, 0)
        totals.after_core()
        scatter.add_x(0, 2)
        scatter.add_x(0, 0)
        totals.after_y()
        scatter.add_y(0, 1)
        scatter.add_y(0, 2)
        scatter.add_y(0, 0)
        scatter.add_z(1, result_ref)
        scatter.add_z(0, result_ref)
        totals.after_z()
        scatter.collect(result_ref)
        square = jnp.zeros((8, width), F32)
        for q in range(6):
            value = result_ref[q * part : (q + 1) * part]
            square = square + jnp.sum((value * value).reshape(part // 8, 8, width), axis=0)
        folded = square[:, :128] + square[:, 128:256] + square[:, 256:]
        square_ref[...] = totals.norm(folded)
        totals_ref[...] = totals.after_x()
        for back in (1, 0):
            for last in (False, True):
                scatter.wait_sends(back, last)
        scatter.end(layers)
        totals.end()


FF = 1536


def from_behind(value, axis, by):
    peers = lax.axis_size(axis)
    pairs = [(i, i + by) for i in range(peers) if 0 <= i + by < peers]
    return lax.ppermute(value, axis, pairs)


def unblock(blocks, row_count, col_count, block_size):
    return (
        blocks.reshape(row_count // block_size, col_count // block_size, block_size, block_size)
        .transpose(0, 2, 1, 3)
        .reshape(row_count, col_count)
    )


def to_blocks(matrix, block_size):
    row_count, col_count = matrix.shape
    return (
        matrix.reshape(row_count // block_size, block_size, col_count // block_size, block_size)
        .transpose(0, 2, 1, 3)
        .reshape(-1, block_size * block_size)
    )


def split_matrices(blocks, model_width):
    block_size = model_width // 4
    shapes = (
        (model_width, 3 * model_width),
        (model_width, model_width),
        (model_width, FF),
        (FF, model_width),
    )
    result = []
    offset = 0
    for row_count, col_count in shapes:
        number = row_count * col_count // (block_size * block_size)
        result.append(unblock(blocks[offset : offset + number], row_count, col_count, block_size))
        offset = offset + number
    return result


def rms_norm(stream, gain):
    factor = lax.rsqrt(jnp.mean(stream * stream, axis=-1, keepdims=True) + 1e-06)
    return (stream * factor * gain, factor)


def norm_back(stream, factor, gain, grad):
    scaled = grad * gain
    grad_in = factor * scaled - stream * factor**3 * jnp.mean(
        stream * scaled, axis=-1, keepdims=True
    )
    return (grad_in, jnp.sum(grad * stream * factor, axis=0))


def gelu_slope(pre_act):
    return (
        0.5 * (1.0 + lax.erf(pre_act * 0.7071067811865476))
        + pre_act * jnp.exp(-0.5 * pre_act * pre_act) * 0.3989422804014327
    )


def layer_forward(stream, matrices, gain_pair, length):
    w_qkv, w_out, w_up, w_down = matrices
    row_count, model_width = stream.shape
    head_dim = model_width // HEADS
    frames = jnp.arange(row_count)
    norm_one, scale_one = rms_norm(stream, gain_pair[0])
    normed = norm_one.astype(BF16)
    qkv_all = jnp.dot(normed, w_qkv, preferred_element_type=jnp.float32).astype(BF16)
    queries = qkv_all[:, :model_width].reshape(row_count, HEADS, head_dim)
    key_rows = qkv_all[:, model_width : 2 * model_width].reshape(row_count, HEADS, head_dim)
    value_rows = qkv_all[:, 2 * model_width :].reshape(row_count, HEADS, head_dim)
    masking = jnp.where(frames < length, 0.0, -1e30).astype(jnp.float32)
    scores = jnp.einsum(
        "qhe,khe->hqk", queries, key_rows, preferred_element_type=jnp.float32
    ) * head_dim ** (-0.5)
    attn_probs = jax.nn.softmax(scores + masking[None, None, :], axis=-1)
    probs_low = attn_probs.astype(BF16)
    attended = (
        jnp.einsum("hqk,khe->qhe", probs_low, value_rows, preferred_element_type=jnp.float32)
        .reshape(row_count, model_width)
        .astype(BF16)
    )
    branch_attn = jnp.dot(attended, w_out, preferred_element_type=jnp.float32)
    middle = stream + branch_attn
    norm_two, scale_two = rms_norm(middle, gain_pair[1])
    normed_two = norm_two.astype(BF16)
    pre_act = jnp.dot(normed_two, w_up, preferred_element_type=jnp.float32)
    hidden = jax.nn.gelu(pre_act, approximate=False).astype(BF16)
    branch_ffn = jnp.dot(hidden, w_down, preferred_element_type=jnp.float32)
    kept_vals = (
        scale_one,
        normed,
        queries,
        key_rows,
        value_rows,
        attn_probs,
        probs_low,
        attended,
        middle,
        scale_two,
        normed_two,
        pre_act,
        hidden,
    )
    return (middle + branch_ffn, branch_attn, branch_ffn, kept_vals)


def layer_backward(stream, matrices, gain_pair, length, upstream):
    w_qkv, w_out, w_up, w_down = matrices
    row_count, model_width = stream.shape
    head_dim = model_width // HEADS
    output, branch_attn, branch_ffn, kept_vals = layer_forward(stream, matrices, gain_pair, length)
    (
        scale_one,
        normed,
        queries,
        key_rows,
        value_rows,
        attn_probs,
        probs_low,
        attended,
        middle,
        scale_two,
        normed_two,
        pre_act,
        hidden,
    ) = kept_vals
    grad_ffn = upstream.astype(BF16)
    grad_down = jnp.dot(hidden.T, grad_ffn, preferred_element_type=jnp.float32)
    grad_hidden = jnp.dot(grad_ffn, w_down.T, preferred_element_type=jnp.float32)
    grad_pre = (grad_hidden * gelu_slope(pre_act)).astype(BF16)
    grad_up = jnp.dot(normed_two.T, grad_pre, preferred_element_type=jnp.float32)
    back_mid, gain_two = norm_back(
        middle,
        scale_two,
        gain_pair[1],
        jnp.dot(grad_pre, w_up.T, preferred_element_type=jnp.float32),
    )
    grad_mid = upstream + back_mid
    grad_branch = grad_mid.astype(BF16)
    grad_out = jnp.dot(attended.T, grad_branch, preferred_element_type=jnp.float32)
    grad_att = (
        jnp.dot(grad_branch, w_out.T, preferred_element_type=jnp.float32)
        .astype(BF16)
        .reshape(row_count, HEADS, head_dim)
    )
    grad_value = jnp.einsum("hqk,qhe->khe", probs_low, grad_att, preferred_element_type=jnp.float32)
    grad_probs = jnp.einsum(
        "qhe,khe->hqk", grad_att, value_rows, preferred_element_type=jnp.float32
    )
    grad_scores = (
        attn_probs * (grad_probs - jnp.sum(attn_probs * grad_probs, axis=-1, keepdims=True))
    ).astype(BF16)
    grad_query = jnp.einsum(
        "hqk,khe->qhe", grad_scores, key_rows, preferred_element_type=jnp.float32
    ) * head_dim ** (-0.5)
    grad_key = jnp.einsum(
        "hqk,qhe->khe", grad_scores, queries, preferred_element_type=jnp.float32
    ) * head_dim ** (-0.5)
    grad_qkv = jnp.concatenate(
        [
            grad_query.reshape(row_count, model_width),
            grad_key.reshape(row_count, model_width),
            grad_value.reshape(row_count, model_width),
        ],
        axis=1,
    ).astype(BF16)
    grad_wqkv = jnp.dot(normed.T, grad_qkv, preferred_element_type=jnp.float32)
    back_in, gain_one = norm_back(
        stream,
        scale_one,
        gain_pair[0],
        jnp.dot(grad_qkv, w_qkv.T, preferred_element_type=jnp.float32),
    )
    return (
        grad_mid + back_in,
        (grad_wqkv, grad_out, grad_up, grad_down),
        jnp.stack([gain_one, gain_two]),
    )


def spectral_terms(output, target, length, present_row, frame_count):
    row_count, model_width = output.shape
    bin_count = model_width // 8
    spectra = output.reshape(row_count, 4, 2, bin_count)
    real_part = spectra[:, :, 0]
    imag_part = spectra[:, :, 1]
    magnitude = jnp.sqrt(real_part * real_part + imag_part * imag_part + 0.01)
    differ = magnitude - target.reshape(row_count, 4, bin_count)
    smooth_err = jnp.sqrt(differ * differ + 0.01)
    weight = (jnp.arange(row_count) < length).astype(jnp.float32)[:, None, None] * present_row[
        None, :, None
    ]
    loss_slope = weight * differ / smooth_err / magnitude / frame_count
    grad_spec = jnp.stack([loss_slope * real_part, loss_slope * imag_part], axis=2).reshape(
        row_count, model_width
    )
    return (jnp.sum(smooth_err * weight), grad_spec)


def pipelined_body(
    x_in,
    targets,
    valid_len,
    present_stems,
    w_master,
    norm_gains,
    gain_m,
    gain_v,
    l_stats,
    r_stats,
    l_roots,
    r_roots,
    step_count,
):
    model_width = x_in.shape[1]
    block_size = model_width // 4
    sections = lax.axis_size("section")
    section_idx = lax.axis_index("section")
    half_way = sections // 2
    groups = lax.axis_size("dp")
    group_idx = lax.axis_index("dp")
    micro_count = valid_len.shape[0] // groups
    seg_len = x_in.shape[0] // micro_count
    own_blocks = w_master.shape[1]
    own_gain = norm_gains.shape[2]
    full_w, full_g = (
        lax.all_gather(w_master.astype(BF16), "dp", axis=1, tiled=True),
        lax.all_gather(norm_gains.astype(BF16), "dp", axis=2, tiled=True),
    )
    matrices = split_matrices(full_w[0], model_width)
    gain_pair = full_g[0].astype(jnp.float32)
    lengths = lax.dynamic_slice_in_dim(valid_len, group_idx * micro_count, micro_count)
    stem_flags = lax.dynamic_slice_in_dim(
        present_stems, group_idx * micro_count, micro_count
    ).astype(jnp.float32)
    frame_count = jnp.sum(valid_len).astype(jnp.float32)
    decoder = section_idx >= half_way
    encoder = section_idx < half_way
    is_last = section_idx == sections - 1
    act_shape = (micro_count, seg_len, model_width)

    def forward_step(step_idx, loop_state):
        in_rows, kept_prev, skip_store, loss_grads, loss_sum, sq_sums = loop_state
        micro_idx = step_idx - section_idx
        active = (micro_idx >= 0) & (micro_idx < micro_count)
        slot_idx = jnp.clip(micro_idx, 0, micro_count - 1)
        fresh_rows = lax.dynamic_slice_in_dim(x_in, slot_idx * seg_len, seg_len, 0)
        previous = jnp.where(section_idx == 0, fresh_rows, in_rows)
        stream = previous.astype(jnp.float32) + jnp.where(
            decoder, skip_store[slot_idx].astype(jnp.float32), 0.0
        )
        length = lengths[slot_idx]
        target = lax.dynamic_slice_in_dim(targets, slot_idx * seg_len, seg_len, 0)

        def forward_compute_fn(operand):
            output, branch_attn, branch_ffn, kept_vals = layer_forward(
                stream, matrices, gain_pair, length
            )
            valid = (jnp.arange(seg_len) < length).astype(jnp.float32)[:, None]
            squares = jnp.stack(
                [
                    jnp.sum(valid * stream * stream),
                    jnp.sum(valid * branch_attn * branch_attn),
                    jnp.sum(valid * branch_ffn * branch_ffn),
                ]
            )
            seg_loss, grad_spec = spectral_terms(
                output, target, length, stem_flags[slot_idx], frame_count
            )
            return (output, squares, seg_loss, grad_spec)

        def forward_spare_fn(operand):
            empty = jnp.zeros((seg_len, model_width), jnp.float32)
            return (empty, jnp.zeros((3,), jnp.float32), jnp.zeros((), jnp.float32), empty)

        output, squares, seg_loss, grad_spec = lax.cond(
            active, forward_compute_fn, forward_spare_fn, 0
        )
        kept_prev = kept_prev.at[slot_idx].set(jnp.where(active, previous, kept_prev[slot_idx]))
        loss_grads = loss_grads.at[slot_idx].set(
            jnp.where(active & is_last, grad_spec, loss_grads[slot_idx])
        )
        loss_sum = loss_sum + jnp.where(is_last, seg_loss, 0.0)
        sq_sums = sq_sums + squares
        sent_rows = output.astype(BF16)
        in_rows = from_behind(sent_rows, "section", 1)
        from_encoder = from_behind(sent_rows, "section", half_way)
        recv_idx = step_idx - section_idx + half_way
        usable = decoder & (recv_idx >= 0) & (recv_idx < micro_count)
        recv_slot = jnp.clip(recv_idx, 0, micro_count - 1)
        skip_store = skip_store.at[recv_slot].set(
            jnp.where(usable, from_encoder, skip_store[recv_slot])
        )
        return (in_rows, kept_prev, skip_store, loss_grads, loss_sum, sq_sums)

    start_state = (
        jnp.zeros((seg_len, model_width), BF16),
        jnp.zeros(act_shape, BF16),
        jnp.zeros(act_shape, BF16),
        jnp.zeros(act_shape, jnp.float32),
        jnp.zeros((), jnp.float32),
        jnp.zeros((3,), jnp.float32),
    )
    unused_rows, kept_prev, skip_store, loss_grads, loss_sum, sq_sums = lax.fori_loop(
        0, micro_count + sections - 1, forward_step, start_state
    )

    def backward_step(step_idx, loop_state):
        in_grads, skip_grad_store, grad_mats, grad_gains = loop_state
        micro_idx = step_idx - (sections - 1 - section_idx)
        active = (micro_idx >= 0) & (micro_idx < micro_count)
        slot_idx = jnp.clip(micro_idx, 0, micro_count - 1)
        upstream = jnp.where(
            is_last,
            loss_grads[slot_idx],
            in_grads.astype(jnp.float32)
            + jnp.where(encoder, skip_grad_store[slot_idx].astype(jnp.float32), 0.0),
        )
        stream = kept_prev[slot_idx].astype(jnp.float32) + jnp.where(
            decoder, skip_store[slot_idx].astype(jnp.float32), 0.0
        )
        length = lengths[slot_idx]

        def backward_compute_fn(operand):
            return layer_backward(stream, matrices, gain_pair, length, upstream)

        def backward_spare_fn(operand):
            return (
                jnp.zeros_like(stream),
                tuple((jnp.zeros(mat.shape, jnp.float32) for mat in matrices)),
                jnp.zeros((2, model_width), jnp.float32),
            )

        grad_stream, layer_mats, layer_gains = lax.cond(
            active, backward_compute_fn, backward_spare_fn, 0
        )
        grad_mats = tuple((total + piece for total, piece in zip(grad_mats, layer_mats)))
        grad_gains = grad_gains + layer_gains
        grad_rows = grad_stream.astype(BF16)
        in_grads = from_behind(grad_rows, "section", -1)
        from_decoder = from_behind(grad_rows, "section", -half_way)
        recv_idx = micro_idx + half_way
        usable = encoder & (recv_idx >= 0) & (recv_idx < micro_count)
        recv_slot = jnp.clip(recv_idx, 0, micro_count - 1)
        skip_grad_store = skip_grad_store.at[recv_slot].set(
            jnp.where(usable, from_decoder, skip_grad_store[recv_slot])
        )
        return (in_grads, skip_grad_store, grad_mats, grad_gains)

    back_state = (
        jnp.zeros((seg_len, model_width), BF16),
        jnp.zeros(act_shape, BF16),
        tuple((jnp.zeros(mat.shape, jnp.float32) for mat in matrices)),
        jnp.zeros((2, model_width), jnp.float32),
    )
    unused_grads, unused_store, grad_mats, grad_gains = lax.fori_loop(
        0, micro_count + sections - 1, backward_step, back_state
    )
    grad_all = jnp.concatenate([to_blocks(mat, block_size) for mat in grad_mats], axis=0)
    summed_w, summed_g = lax.psum((grad_all, grad_gains), "dp")
    own_grad = lax.dynamic_slice_in_dim(summed_w, group_idx * own_blocks, own_blocks, 0)
    own_gain_grad = lax.dynamic_slice_in_dim(summed_g, group_idx * own_gain, own_gain, 1)
    own_square = jnp.sum(own_grad * own_grad) + jnp.sum(own_gain_grad * own_gain_grad)
    rows_local = jnp.zeros((sections, 3), jnp.float32).at[section_idx].set(sq_sums)
    total_square, loss_value, rows_total = lax.psum(
        (own_square, loss_sum / frame_count, rows_local), ("section", "dp")
    )
    grad_norm = jnp.sqrt(total_square)
    clip_limit = 0.00015 * math.sqrt(
        sections * (own_blocks * groups * block_size * block_size + 2 * model_width)
    )
    factor = clip_limit / jnp.maximum(grad_norm, clip_limit)
    grad_blocks = own_grad * factor
    square = (own_blocks, block_size, block_size)
    shaped = grad_blocks.reshape(square)
    highest = lax.Precision.HIGHEST
    l_new = 0.95 * l_stats[0].reshape(square) + 0.05 * jnp.einsum(
        "bij,bkj->bik", shaped, shaped, precision=highest
    )
    r_new = 0.95 * r_stats[0].reshape(square) + 0.05 * jnp.einsum(
        "bji,bjk->bik", shaped, shaped, precision=highest
    )
    left_side = jnp.einsum("bij,bjk->bik", l_roots[0].reshape(square), shaped, precision=highest)
    precond = jnp.einsum("bij,bjk->bik", left_side, r_roots[0].reshape(square), precision=highest)
    master = w_master[0]
    w_new = master - 0.5 * (precond.reshape(master.shape) + 0.01 * master)
    gain_grad = own_gain_grad * factor
    m_new = 0.9 * gain_m[0] + 0.1 * gain_grad
    v_new = 0.999 * gain_v[0] + 0.001 * gain_grad * gain_grad
    step_num = step_count[0].astype(jnp.float32)
    m_hat = m_new / (1.0 - jnp.power(0.9, step_num))
    v_hat = v_new / (1.0 - jnp.power(0.999, step_num))
    gains_new = norm_gains[0] - 0.5 * m_hat / (jnp.sqrt(v_hat) + 1e-08)
    rms = jnp.sqrt(rows_total[section_idx] / (frame_count * model_width)).reshape(1, 3)
    return (
        w_new[None],
        grad_blocks[None],
        l_new.reshape(master.shape)[None],
        r_new.reshape(master.shape)[None],
        gains_new[None],
        m_new[None],
        v_new[None],
        loss_value,
        grad_norm,
        rms,
    )


def layer_block(shape):
    return pl.BlockSpec((1,) + shape, lambda i: (i,) + (0,) * len(shape))


def whole_block(shape):
    return pl.BlockSpec(shape, lambda i: (0,) * len(shape))


def held_block(shape):
    return pl.BlockSpec(shape, lambda i: (0,) * len(shape), pipeline_mode=pl.Buffered(1))


def forward(layers, micro, valid_len, present_stems, x_in, targets, flat_w, gain):
    width = x_in.shape[1]
    seg = x_in.shape[0] // micro
    dim = width // HEADS
    part = width // 4
    half = layers // 2
    shapes = (
        (HEADS, seg, seg), (3, seg, width), (seg, width), (seg, width), (4, seg, width), (4, seg, width)
    )
    kinds = (BF16, BF16, BF16, F32, BF16, BF16)

    def slot():
        return jnp.minimum(lax.axis_index("section"), micro - 1)

    return pl.pallas_call(
        functools.partial(forward_kernel, layers, half, micro),
        grid=(layers,),
        in_specs=[
            pl.BlockSpec(memory_space=pltpu.SMEM),
            pl.BlockSpec(memory_space=pltpu.SMEM),
            pl.BlockSpec((seg, width), lambda i: (slot(), 0)),
            pl.BlockSpec((width // 2, seg), lambda i: (0, slot())),
            pl.BlockSpec(memory_space=pltpu.VMEM),
            pl.BlockSpec(memory_space=pltpu.VMEM),
        ],
        out_specs=[layer_block(s) for s in shapes]
        + [whole_block((layers, seg, width)), whole_block((seg, width)), whole_block((layers, 8, width))]
        + [pl.BlockSpec(memory_space=pl.ANY), whole_block((layers, 8, width))],
        out_shape=[jax.ShapeDtypeStruct((layers,) + s, k) for s, k in zip(shapes, kinds)]
        + [
            jax.ShapeDtypeStruct((layers, seg, width), BF16),
            jax.ShapeDtypeStruct((seg, width), F32),
            jax.ShapeDtypeStruct((layers, 8, width), F32),
            jax.ShapeDtypeStruct((layers, 48 * part, width), BF16),
            jax.ShapeDtypeStruct((layers, 8, width), F32),
        ],
        scratch_shapes=[
            pltpu.VMEM((seg, width), F32),
            pltpu.VMEM((seg, width), BF16),
            pltpu.VMEM((layers, 48 * part, width), BF16),
            pltpu.VMEM((layers, 8, 8, 128), F32),
            pltpu.VMEM((6 * part, width), BF16),
            pltpu.VMEM((8, 128), F32),
            pltpu.VMEM((4, part, 128), F32),
            pltpu.SemaphoreType.DMA((2, 3)),
            pltpu.SemaphoreType.DMA((2, layers, 4)),
            pltpu.SemaphoreType.DMA((2, layers, 4)),
            pltpu.SemaphoreType.DMA((2, layers, 8)),
            pltpu.SemaphoreType.DMA((2, layers, 8)),
            pltpu.SemaphoreType.DMA((2, 10)),
            pltpu.SemaphoreType.DMA((layers,)),
        ],
        compiler_params=pltpu.CompilerParams(
            vmem_limit_bytes=VMEM_LIMIT, collective_id=0, has_side_effects=True
        ),
    )(valid_len, present_stems, x_in, targets.T, flat_w, gain)


def backward(layers, loss_grad, full_w, full_g, sent, saved, stats):
    seg, width = loss_grad.shape
    dim = width // HEADS
    part = width // 4
    half = layers // 2

    def from_end(array):
        shape = array.shape[1:]
        return pl.BlockSpec((1,) + shape, lambda i: (layers - 1 - i,) + (0,) * len(shape))

    return pl.pallas_call(
        functools.partial(backward_kernel, layers, half),
        grid=(layers,),
        in_specs=[
            held_block((seg, width)),
            from_end(full_w),
            from_end(full_g),
            held_block((layers, seg, width)),
        ]
        + [from_end(a) for a in saved]
        + [pl.BlockSpec(memory_space=pltpu.VMEM)],
        out_specs=[pl.BlockSpec(memory_space=pltpu.VMEM)] * 3,
        out_shape=[
            jax.ShapeDtypeStruct((6 * part, width), F32),
            jax.ShapeDtypeStruct((16, width), F32),
            jax.ShapeDtypeStruct((8, 128), F32),
        ],
        scratch_shapes=[
            pltpu.VMEM((layers, seg, width), BF16),
            pltpu.VMEM((seg, width), BF16),
            pltpu.VMEM((4, seg, width), BF16),
            pltpu.VMEM((seg, width), BF16),
            pltpu.VMEM((seg, width), F32),
            pltpu.VMEM((seg, width), BF16),
            pltpu.VMEM((seg, width), BF16),
            pltpu.VMEM((3, seg, width), BF16),
            pltpu.VMEM((layers, 8, width), F32),
            pltpu.VMEM((2, 4, 2, 576, width), BF16),
            pltpu.VMEM((2, 4, 2, 288, width), BF16),
            pltpu.VMEM((layers, 4, 2, 80, width), BF16),
            pltpu.VMEM((layers, 4, 208, width), BF16),
            pltpu.VMEM((layers, 4, 208, width), BF16),
            pltpu.VMEM((layers, 3, 208, width), BF16),
            pltpu.VMEM((3, 208, width), BF16),
            pltpu.VMEM((6, 16, width), F32),
            pltpu.VMEM((4, 16, width), F32),
            pltpu.VMEM((4, 8, 128), F32),
            pltpu.VMEM((8, 8, 128), F32),
            pltpu.SemaphoreType.DMA((2, 2, 3)),
            pltpu.SemaphoreType.DMA((2, layers, 4)),
            pltpu.SemaphoreType.DMA((2, layers, 4)),
            pltpu.SemaphoreType.DMA((2, layers, 4)),
            pltpu.SemaphoreType.DMA((2, layers)),
            pltpu.SemaphoreType.DMA((2, 3)),
            pltpu.SemaphoreType.DMA((2, 3)),
            pltpu.SemaphoreType.DMA((2, 3)),
            pltpu.SemaphoreType.DMA((2, 7)),
        ],
        compiler_params=pltpu.CompilerParams(
            vmem_limit_bytes=VMEM_LIMIT, collective_id=1, has_side_effects=True
        ),
    )(loss_grad, full_w, full_g, sent, *saved, stats)


def split(value):
    high = value.astype(BF16)
    return high, (value - high.astype(F32)).astype(BF16)


def dot_split(dot, left, right):
    return dot(left[0], right[0]) + (dot(left[0], right[1]) + dot(left[1], right[0]))


def update_kernel(
    layers, limit, length_ref, step_ref, square_ref, tile_ref, quads_ref, w_ref, l_ref, r_ref, lroot_ref, rroot_ref,
    gain_ref, gain_m_ref, gain_v_ref,
    w_out, grad_out, l_out, r_out, gain_out, m_out, v_out, loss_out, norm_out, rms_out,
    block_ref,
):
    part, width = quads_ref.shape[1:]
    gains = tile_ref[: 2 * layers]
    norm = jnp.sqrt(jnp.sum(square_ref[...], keepdims=True) + jnp.sum(gains * gains, keepdims=True))
    factor = limit / jnp.maximum(norm, limit)

    def quad_step(q, _):
        for c in range(4):
            base = 4 * q + c
            load_block(lroot_ref, base, block_ref.at[0])
            load_block(rroot_ref, base, block_ref.at[1])
            grad = quads_ref[q, :, part * c : part * (c + 1)] * factor
            pair = split(grad)
            left = dot_split(dot_nn, split(block_ref[0, :, :part]), pair)
            pre = dot_split(dot_nn, split(left), split(block_ref[1, :, :part]))
            for i, value in enumerate((
                grad, pre, dot_split(dot_nt, pair, pair), dot_split(dot_tn, pair, pair)
            )):
                block_ref[2 + i, :, :part] = value
            parts = [flat_parts(block_ref.at[2 + i]) for i in range(4)]
            for m in range(3):
                at = (pl.ds(base + 8 * m, 24, stride=24), slice(None))
                grad_out[at] = parts[0][m]
                master = w_ref[at]
                w_out[at] = master - 0.5 * (parts[1][m] + 0.01 * master)
                l_out[at] = 0.95 * l_ref[at] + 0.05 * parts[2][m]
                r_out[at] = 0.95 * r_ref[at] + 0.05 * parts[3][m]
        return 0

    for q in range(2):
        quad_step(q, 0)

    @pl.when(pl.program_id(0) == 0)
    def _():
        section, group = lax.axis_index("section"), lax.axis_index("dp")
        share = gain_ref.shape[1]
        row = tile_ref[:2]
        for k in range(1, layers):
            row = jnp.where(section == k, tile_ref[2 * k : 2 * k + 2], row)
        own = row[:, :share]
        for g in range(1, width // share):
            own = jnp.where(group == g, row[:, g * share : (g + 1) * share], own)
        grad = own * factor
        m_new = 0.9 * gain_m_ref[...] + 0.1 * grad
        v_new = 0.999 * gain_v_ref[...] + 0.001 * grad * grad
        step = jnp.full((1, 1), step_ref[0], jnp.int32).astype(F32)
        m_hat = m_new / (1.0 - jnp.exp(step * math.log(0.9)))
        v_hat = v_new / (1.0 - jnp.exp(step * math.log(0.999)))
        gain_out[...] = gain_ref[...] - 0.5 * m_hat / (jnp.sqrt(v_hat) + 1e-08)
        m_out[...] = m_new
        v_out[...] = v_new
        norm_out[...] = norm
        frames = length_ref[0]
        for k in range(1, length_ref.shape[0]):
            frames = frames + length_ref[k]
        frames = jnp.full((1, 1), frames, jnp.int32).astype(F32)
        loss_out[...] = tile_ref[2 * layers : 2 * layers + 1, 3:4] / frames
        squares = tile_ref[2 * layers : 2 * layers + 1, :3]
        for k in range(1, layers):
            squares = jnp.where(section == k, tile_ref[2 * layers + k : 2 * layers + k + 1, :3], squares)
        rms_out[...] = jnp.sqrt(squares / (frames * width))


def update(layers, limit, valid_len, step_count, squares, tile, quads, flats, gains):
    blocks = 4 * quads.shape[0]
    part, width = quads.shape[1:]
    rows = flats[0].shape[0]
    whole = [pl.BlockSpec(memory_space=pltpu.VMEM)]
    flat = [pl.BlockSpec((rows // 3, 128), lambda i: (i, 0))]
    share = gains[0].shape
    return pl.pallas_call(
        functools.partial(update_kernel, layers, limit),
        grid=(3,),
        in_specs=[pl.BlockSpec(memory_space=pltpu.SMEM)] * 2 + whole * 2
        + [pl.BlockSpec((2, part, width), lambda i: (i, 0, 0))] + flat * 5 + whole * 3,
        out_specs=flat * 4 + whole * 6,
        out_shape=[jax.ShapeDtypeStruct((rows, 128), F32)] * 4
        + [jax.ShapeDtypeStruct(share, F32)] * 3
        + [jax.ShapeDtypeStruct((1, 1), F32)] * 2 + [jax.ShapeDtypeStruct((1, 3), F32)],
        scratch_shapes=[pltpu.VMEM((6, part, 128), F32)],
        compiler_params=pltpu.CompilerParams(vmem_limit_bytes=VMEM_LIMIT),
    )(valid_len, step_count, squares, tile, quads, *flats, *gains)


def body(
    x_in, targets, valid_len, present_stems, w_master, norm_gains, gain_m, gain_v,
    l_stats, r_stats, l_roots, r_roots, step_count,
):
    width = x_in.shape[1]
    part = width // 4
    layers = lax.axis_size("section")
    groups = lax.axis_size("dp")
    micro = valid_len.shape[0] // groups
    own_blocks = w_master.shape[1]
    flats = [flat_rows(a[0]) for a in (w_master, l_stats, r_stats, l_roots, r_roots)]
    *saved, sent, loss_grad, stats, full_w, full_g = forward(
        layers, micro, valid_len, present_stems, x_in, targets, flats[0], norm_gains[0]
    )
    own_quads, tile, squares = backward(layers, loss_grad, full_w, full_g, sent, saved, stats)
    clip_limit = 0.00015 * math.sqrt(layers * (own_blocks * groups * part * part + 2 * width))
    *news, gains_new, m_new, v_new, loss_value, grad_norm, rms = update(
        layers, clip_limit, valid_len, step_count, squares, tile, own_quads.reshape(-1, part, width), flats,
        (norm_gains[0], gain_m[0], gain_v[0]),
    )
    w_new, grad_blocks, l_new, r_new = (from_flat_rows(a, own_blocks)[None] for a in news)
    return (
        w_new,
        grad_blocks,
        l_new,
        r_new,
        gains_new[None],
        m_new[None],
        v_new[None],
        loss_value.reshape(()),
        grad_norm.reshape(()),
        rms,
    )


def solution(mesh):
    def step(*args):
        layers, groups = mesh.shape["section"], mesh.shape["dp"]
        micro, own_blocks = args[2].shape[0] // groups, args[4].shape[1]
        if micro <= layers == 4 and groups == 8 and own_blocks == 24:
            return body(*args)
        return pipelined_body(*args)

    block = P("section", "dp", None)
    gain = P("section", None, "dp")
    return jax.shard_map(
        step,
        mesh=mesh,
        in_specs=(
            P("dp", None), P("dp", None), P(), P(), block, gain, gain, gain, block, block, block, block, P(),
        ),
        out_specs=(block, block, block, block, gain, gain, gain, P(), P(), P("section", None)),
        check_vma=False,
    )
```

```python
import functools
import math

import jax
import jax.numpy as jnp
from jax import lax
from jax.experimental import pallas as pl
from jax.experimental.pallas import tpu as pltpu
from jax.sharding import PartitionSpec as P

HEADS = 8
F32 = jnp.float32
BF16 = jnp.bfloat16
VMEM_LIMIT = 61 * 1024 * 1024


def dot_nn(a, b):
    return lax.dot_general(a, b, (((1,), (0,)), ((), ())), preferred_element_type=F32)


def dot_nt(a, b):
    return lax.dot_general(a, b, (((1,), (1,)), ((), ())), preferred_element_type=F32)


def dot_tn(a, b):
    return lax.dot_general(a, b, (((0,), (0,)), ((), ())), preferred_element_type=F32)


def gelu_parts(x):
    ax = jnp.abs(x)
    bell = jnp.exp(-0.5 * x * x)
    t = 1.0 / (1.0 + (0.3275911 * 0.7071067811865476) * ax)
    poly = t * (
        0.5 * 0.254829592
        + t
        * (
            0.5 * -0.284496736
            + t * (0.5 * 1.421413741 + t * (0.5 * -1.453152027 + t * (0.5 * 1.061405429)))
        )
    )
    tail = poly * bell
    cdf = jnp.where(x >= 0.0, 1.0 - tail, tail)
    return x * cdf, cdf + x * bell * 0.3989422804014327


def stack_quads(w_ref, first, step, number):
    part = w_ref.shape[2] // 4
    if step == 1:
        return w_ref[0, first * part : (first + number) * part]
    return jnp.concatenate(
        [w_ref[0, (first + step * i) * part : (first + step * i + 1) * part] for i in range(number)], axis=0
    )


def flat_rows(array):
    blocks, area = array.shape
    return (
        array.reshape(blocks // 8, 8, area // 128, 128).transpose(0, 2, 1, 3).reshape(-1, 128)
    )


def from_flat_rows(rows, blocks):
    return (
        rows.reshape(blocks // 8, -1, 8, 128).transpose(0, 2, 1, 3).reshape(blocks, -1)
    )


def load_block(rows_ref, base, block_ref):
    lane = lax.broadcasted_iota(jnp.int32, (24, 128), 1)
    a, b, c = (rows_ref[pl.ds(base + 8 * m, 24, stride=24), :] for m in range(3))
    block_ref[pl.ds(0, 24, stride=4), :] = a
    block_ref[pl.ds(1, 24, stride=4), :] = jnp.where(lane < 32, pltpu.roll(a, 32, 1), pltpu.roll(b, 32, 1))
    block_ref[pl.ds(2, 24, stride=4), :] = jnp.where(lane < 64, pltpu.roll(b, 64, 1), pltpu.roll(c, 64, 1))
    block_ref[pl.ds(3, 24, stride=4), :] = pltpu.roll(c, 96, 1)


def flat_parts(block_ref):
    lane = lax.broadcasted_iota(jnp.int32, (24, 128), 1)
    a, b, c, d = (block_ref[pl.ds(r, 24, stride=4), :] for r in range(4))
    b, c, d = pltpu.roll(b, 96, 1), pltpu.roll(c, 64, 1), pltpu.roll(d, 32, 1)
    return jnp.where(lane < 96, a, b), jnp.where(lane < 64, b, c), jnp.where(lane < 32, c, d)


MESH = pl.DeviceIdType.MESH


def mesh_place():
    section = lax.axis_index("section")
    group = lax.axis_index("dp")
    core = lax.rem(section, 2)
    y = lax.rem(group, 2)
    z = group // 2
    z_peers = (z, z + 1 - 2 * lax.rem(z, 2), lax.rem(z + 2, 4), 3 - z)
    return section, group, core, y, z_peers


def remote(source, target, send_sem, recv_sem, section, group):
    return pltpu.make_async_remote_copy(
        src_ref=source, dst_ref=target, send_sem=send_sem, recv_sem=recv_sem,
        device_id=(section, group), device_id_type=MESH,
    )


class Slabs:
    def __init__(self, rows):
        self.section, self.group, self.core, self.y, self.z_peers = mesh_place()
        self.x = self.section // 2
        self.rows, self.half = rows, rows // 2
        self.edge = self.half * 5 // 18
        self.slab = self.half - self.edge

    def slab_of(self, x, core):
        return pl.ds(pl.multiple_of(self.half * core + self.edge * x, 16), self.slab)

    def edge_of(self, x, core):
        return pl.ds(pl.multiple_of(self.half * core + self.slab * x, 16), self.edge)

    def half_of(self, core):
        return pl.ds(pl.multiple_of(self.half * core, 16), self.half)

    def x_peer(self):
        return lax.rem(self.section + 2, 4), self.group

    def y_peer(self):
        return self.section, self.group + 1 - 2 * self.y

    def z_peer(self, k):
        return self.section, self.z_peers[k] * 2 + self.y

    def core_peer(self):
        return self.section + 1 - 2 * self.core, self.group

    def signal_all(self):
        barrier = pltpu.get_barrier_semaphore()
        for k in range(1, 4):
            place = (lax.rem(self.section + k, 4), self.group)
            pl.semaphore_signal(barrier, inc=1, device_id=place, device_id_type=MESH)
        for k in range(1, 8):
            place = (self.section, lax.rem(self.group + k, 8))
            pl.semaphore_signal(barrier, inc=1, device_id=place, device_id_type=MESH)

    def wait_all(self):
        pl.semaphore_wait(pltpu.get_barrier_semaphore(), 10)


class Gather(Slabs):
    def __init__(self, own_ref, gain_ref, w_ref, gains_ref, sems):
        super().__init__(own_ref.shape[0])
        self.own, self.gain, self.w, self.gains = own_ref, gain_ref, w_ref, gains_ref
        self.spread, self.z_sems, self.y_sems, self.x_sems, self.core_sems, self.gain_sems, self.local = sems
        self.others = [lax.rem(self.section + k, 4) for k in range(1, 4)]

    def chunk(self, k):
        y = self.y if k < 4 else 1 - self.y
        return self.z_peers[k % 4] * 2 + y

    def at(self, layer, group, rows):
        return self.w.at[layer, pl.ds(pl.multiple_of(group * self.rows + rows.start, 16), rows.size)]

    def spread_copy(self, k):
        peer = self.others[k]
        rows = self.slab_of(peer // 2, lax.rem(peer, 2))
        return remote(
            self.own.at[rows], self.at(self.section, self.group, rows),
            self.spread.at[0, k], self.spread.at[1, k], peer, self.group,
        )

    def spread_wait(self, layer):
        ref = self.at(layer, self.group, self.slab_of(self.x, self.core))
        for k in range(3):
            @pl.when(lax.rem(layer + k + 1, 4) == self.section)
            def _():
                remote(ref, ref, self.spread.at[0, k], self.spread.at[1, k], self.others[0], self.group).wait_recv()

    def z_copy(self, layer, k, landed=False):
        ref = self.at(layer, self.chunk(k) if landed else self.group, self.slab_of(self.x, self.core))
        return remote(ref, ref, self.z_sems.at[0, layer, k], self.z_sems.at[1, layer, k], *self.z_peer(k))

    def y_copy(self, layer, k, landed=False):
        ref = self.at(layer, self.chunk(k + 4 if landed else k), self.slab_of(self.x, self.core))
        return remote(ref, ref, self.y_sems.at[0, layer, k], self.y_sems.at[1, layer, k], *self.y_peer())

    def x_copy(self, layer, k, landed=False):
        ref = self.at(layer, self.chunk(k), self.edge_of(1 - self.x if landed else self.x, self.core))
        return remote(ref, ref, self.x_sems.at[0, layer, k], self.x_sems.at[1, layer, k], *self.x_peer())

    def core_copy(self, layer, k, landed=False):
        ref = self.at(layer, self.chunk(k), self.half_of(1 - self.core if landed else self.core))
        return remote(ref, ref, self.core_sems.at[0, layer, k], self.core_sems.at[1, layer, k], *self.core_peer())

    def gain_copy(self, k):
        if k < 7:
            peer = lax.rem(self.group + k + 1, 8)
            return remote(
                self.gain, self.gains.at[self.section, self.group],
                self.gain_sems.at[0, k], self.gain_sems.at[1, k], self.section, peer,
            )
        ref = self.gains.at[self.section]
        return remote(
            ref, ref, self.gain_sems.at[0, k], self.gain_sems.at[1, k], self.others[k - 7], self.group
        )

    def gain_landed(self, k):
        if k < 7:
            ref = self.gains.at[self.section, lax.rem(self.group - k - 1 + 8, 8)]
        else:
            ref = self.gains.at[lax.rem(self.section - (k - 6) + 4, 4)]
        return remote(ref, ref, self.gain_sems.at[0, k], self.gain_sems.at[1, k], self.section, self.group)

    def spread_own(self):
        for k in range(3):
            self.spread_copy(k).start()

    def begin(self):
        @pl.when(self.section == 0)
        def _():
            self.spread_own()

        for k in range(7):
            self.gain_copy(k).start()
        rows = self.slab_of(self.x, self.core)
        self.w[self.section, pl.ds(pl.multiple_of(self.group * self.rows + rows.start, 16), rows.size)] = self.own[rows]
        self.gains[self.section, self.group] = self.gain[...]

    def share_gains(self):
        for k in range(7):
            self.gain_landed(k).wait_recv()
        for k in range(7, 10):
            self.gain_copy(k).start()

    def wait_gains(self):
        for k in range(7, 10):
            self.gain_landed(k).wait_recv()

    def kick(self, layer):
        self.spread_wait(layer)
        for k in range(1, 4):
            self.z_copy(layer, k).start()
        self.y_copy(layer, 0).start()
        self.x_copy(layer, 0).start()

    def serve_z(self, layer, k):
        self.z_copy(layer, k, True).wait_recv()
        self.y_copy(layer, k).start()
        self.x_copy(layer, k).start()

    def serve_y(self, layer, k):
        self.y_copy(layer, k, True).wait_recv()
        self.x_copy(layer, k + 4).start()

    def serve_x(self, layer, k):
        self.x_copy(layer, k, True).wait_recv()
        self.core_copy(layer, k).start()

    def finish_first(self, layer):
        for k in range(8):
            @pl.when(self.z_peers[k % 4] == 0)
            def _():
                self.core_copy(layer, k, True).wait_recv()

    def finish_rest(self, layer):
        for k in range(8):
            @pl.when(self.z_peers[k % 4] != 0)
            def _():
                self.core_copy(layer, k, True).wait_recv()

    def end(self, layers):
        for k in range(3):
            self.spread_copy(k).wait_send()
        for k in range(10):
            self.gain_copy(k).wait_send()

        def per_layer(layer, _):
            for k in range(1, 4):
                self.z_copy(layer, k).wait_send()
            for k in range(4):
                self.y_copy(layer, k).wait_send()
            for k in range(8):
                self.x_copy(layer, k).wait_send()
                self.core_copy(layer, k).wait_send()
            return 0

        lax.fori_loop(0, layers, per_layer, 0)


def segment_info(micro, length_ref, stems_ref):
    section, group = lax.axis_index("section"), lax.axis_index("dp")
    at = group * micro + jnp.minimum(section, micro - 1)
    used = (section < micro).astype(jnp.int32)
    frames = length_ref[0]
    for k in range(1, length_ref.shape[0]):
        frames = frames + length_ref[k]
    return length_ref[at] * used, [stems_ref[at, k] * used for k in range(4)], frames


FIRST_POINTS = {"qkv": "z2 y1 x0 x1", "heads": "z3 x2 x4 x5", "attended": "y2", "ffn1": "x3", "ffn2": "y3 x6", "ffn3": "x7"}
POINTS = {"qkv": "x0 x1 z3", "heads": "x2 x4 x5", "attended": "y2 x3", "ffn1": "y3", "ffn2": "x6", "ffn3": "x7"}
AHEAD_POINTS = {"attended": "z1 y0", "ffn2": "z2", "ffn3": "y1"}


def forward_kernel(
    layers, half, micro, length_ref, stems_ref, x_ref, target_ref, flat_ref, raw_gain_ref,
    probs_ref, qkv_ref, att_ref, middle_ref, hidden_ref, slope_ref, sent_ref, loss_grad_ref, stats_ref,
    full_ref, gains_out_ref,
    out_ref, normed_ref, w_all_ref, gains_ref, own_ref, own_gain_ref, block_ref, *sems,
):
    seg, width = x_ref.shape
    dim = width // HEADS
    part = width // 4
    layer = pl.program_id(0)
    rows = 256
    chunks = seg // rows
    length, present_flags, frame_total = segment_info(micro, length_ref, stems_ref)
    gather = Gather(own_ref, own_gain_ref, w_all_ref, gains_ref, sems)
    w_ref = w_all_ref.at[pl.ds(layer, 1)]

    def own_step(q, _):
        for c in range(4):
            block = 4 * q + c
            load_block(flat_ref, (block // 8) * 576 + lax.rem(block, 8), block_ref.at[c])
        quad = jnp.concatenate([block_ref[c, :, :part] for c in range(4)], axis=1)
        own_ref[pl.ds(pl.multiple_of(q * part, part), part)] = quad.astype(BF16)
        return 0

    def keep_copy(index):
        return pltpu.make_async_copy(w_all_ref.at[index], full_ref.at[index], gather.local.at[index])

    @pl.when(layer == 0)
    def _():
        gather.signal_all()
        for q in range(flat_ref.shape[0] // 288):
            own_step(q, 0)
        own_gain_ref[...] = jnp.zeros_like(own_gain_ref)
        own_gain_ref[:2, : raw_gain_ref.shape[1]] = raw_gain_ref[...]
        gather.wait_all()
        gather.begin()
        sent_ref[0] = x_ref[...]
        stats_ref[...] = jnp.zeros_like(stats_ref)
        gather.kick(0)

        @pl.when(gather.section != 0)
        def _():
            gather.spread_own()

        gather.share_gains()
        gather.serve_z(0, 1)
        gather.serve_z(0, 2)
        gather.kick(1)
        gather.serve_x(0, 0)
        gather.serve_x(0, 1)
        gather.serve_z(0, 3)
        gather.wait_gains()
        gather.serve_y(0, 0)
        gather.serve_x(0, 2)
        gather.serve_y(0, 1)
        gather.serve_y(0, 2)
        gather.serve_x(0, 3)
        gather.serve_y(0, 3)
        for k in range(4, 8):
            gather.serve_x(0, k)
        gather.serve_z(1, 1)
        gather.serve_y(1, 0)

    @pl.when(layer + 2 < layers)
    def _():
        gather.kick(layer + 2)

    gather.finish_first(layer)
    more = layer + 1 < layers

    def serve(point):
        for here, steps, later in (
            (layer == 0, FIRST_POINTS.get(point, ""), ""),
            (layer > 0, POINTS.get(point, ""), ""),
            (layer >= 0, "", AHEAD_POINTS.get(point, "")),
        ):
            for names, back in ((steps, 1), (later, 2)):
                if names:
                    @pl.when((layer + back < layers) & here)
                    def _():
                        for name in names.split():
                            getattr(gather, "serve_" + name[0])(layer + back, int(name[1]))

    def stream_of(at):
        prev = sent_ref[layer, at].astype(F32)
        skip = sent_ref[jnp.maximum(layer + 1 - half, 0), at].astype(F32)
        return prev + jnp.where(layer >= half, skip, 0.0)

    def gain_row(which):
        return jnp.concatenate(
            [gains_ref[layer, g, which : which + 1, : width // 8] for g in range(8)], axis=1
        ).astype(BF16).astype(F32)

    gain_one = gain_row(0)
    gain_two = gain_row(1)
    gains_out_ref[layer, 0:1] = gain_one
    gains_out_ref[layer, 1:2] = gain_two

    first_stream = stream_of(slice(None))
    first_factor = lax.rsqrt(jnp.mean(first_stream * first_stream, axis=-1, keepdims=True) + 1e-06)
    first_normed = (first_stream * first_factor * gain_one).astype(BF16)
    for t in range(3):
        qkv_ref[0, t] = dot_nn(first_normed, stack_quads(w_ref, t, 3, 4)).astype(BF16)
    serve("qkv")
    frames = lax.broadcasted_iota(jnp.int32, (1, seg), 1)
    masking = jnp.where(frames < length, 0.0, -1e30).astype(F32)

    def head_step(h):
        queries, keys, values = (qkv_ref[0, t, :, h * dim : (h + 1) * dim] for t in range(3))
        scores = dot_nt(queries, keys) * dim ** (-0.5) + masking
        top = jnp.max(scores, axis=-1, keepdims=True)
        expd = jnp.exp(scores - top)
        probs = (expd * (1.0 / jnp.sum(expd, axis=-1, keepdims=True))).astype(BF16)
        probs_ref[0, h] = probs
        return dot_nn(probs, values).astype(BF16)

    def put_heads(first):
        heads = [head_step(h) for h in range(first, first + HEADS // 2)]
        att_ref[0, :, first * dim : (first + HEADS // 2) * dim] = jnp.concatenate(heads, axis=1)

    put_heads(0)
    serve("heads")
    put_heads(HEADS // 2)
    serve("attended")
    gather.finish_rest(layer)
    keep_copy(layer).start()

    valid = (lax.broadcasted_iota(jnp.int32, (seg, 1), 0) < length).astype(F32)

    def add_stat(k, value):
        stats_ref[layer, k : k + 1] = jnp.sum(valid * value * value, axis=0, keepdims=True)

    branch_attn = dot_nn(att_ref[0], stack_quads(w_ref, 12, 1, 4))
    stream = stream_of(slice(None))
    middle = stream + branch_attn
    middle_ref[0] = middle
    add_stat(0, stream)
    add_stat(1, branch_attn)
    factor = lax.rsqrt(jnp.mean(middle * middle, axis=-1, keepdims=True) + 1e-06)
    normed_ref[...] = (middle * factor * gain_two).astype(BF16)

    def ffn_step(c):
        pre_act = dot_nn(normed_ref[...], stack_quads(w_ref, 16 + c, 4, 4))
        hidden, slope = gelu_parts(pre_act)
        hidden = hidden.astype(BF16)
        hidden_ref[0, c] = hidden
        slope_ref[0, c] = slope.astype(BF16)
        part_sum = dot_nn(hidden, stack_quads(w_ref, 32 + 4 * c, 1, 4))
        out_ref[...] = part_sum if c == 0 else out_ref[...] + part_sum

    for c in range(4):
        ffn_step(c)
        if c < 3:
            serve(f"ffn{c}")
    branch_ffn = out_ref[...]
    add_stat(2, branch_ffn)
    output = middle_ref[0] + branch_ffn
    out_ref[...] = output

    @pl.when(layer + 1 < layers)
    def _():
        sent_ref[layer + 1] = out_ref[...].astype(BF16)

    serve("ffn3")

    @pl.when(layer == layers - 1)
    def _():
        bins = width // 8
        lane = lax.broadcasted_iota(jnp.int32, (1, width), 1)
        is_real = lax.rem(lane, 2 * bins) < bins
        stem = lane // (2 * bins)
        present = jnp.zeros((1, width), F32)
        for k in range(4):
            present = jnp.where(stem == k, present_flags[k].astype(F32), present)
        inverse = 1.0 / jnp.full((1, 1), frame_total, jnp.int32).astype(F32)

        def loss_step(i, _):
            at = pl.ds(pl.multiple_of(i * rows, rows), rows)
            output = out_ref[at]
            square = output * output
            other = jnp.where(
                is_real, pltpu.roll(square, width - bins, 1), pltpu.roll(square, bins, 1)
            )
            magnitude = jnp.sqrt(square + other + 0.01)
            goal = target_ref[:, at].T
            goal = jnp.concatenate(
                [goal[:, (k // 2) * bins : (k // 2 + 1) * bins] for k in range(8)], axis=1
            )
            differ = magnitude - goal
            smooth = jnp.sqrt(differ * differ + 0.01)
            valid = (lax.broadcasted_iota(jnp.int32, (rows, 1), 0) + i * rows < length).astype(F32)
            weight = valid * present
            loss_grad_ref[at] = weight * differ * output * inverse / (smooth * magnitude)
            stats_ref[0, 3:4] += jnp.sum(
                jnp.where(is_real, weight * smooth, 0.0), axis=0, keepdims=True
            )
            return 0

        lax.fori_loop(0, chunks, loss_step, 0)
        gather.end(layers)
        for k in range(layers):
            keep_copy(k).wait()


class Scatter(Slabs):
    PARTS = ((3, 4), (1, 3), (0, 1))

    def __init__(self, refs, sems):
        self.grads, self.core_in, self.x_in, self.y_in, self.stage, self.z_in, self.last_in = refs
        super().__init__(self.grads.shape[3])
        self.core_sems, self.x_sems, self.y_sems, self.z_sems, self.last_sems = sems
        self.mine = self.slab_of(self.x, self.core)
        self.z = self.z_peers[0]

    def core_copy(self, layer, number):
        slot = lax.rem(layer, 2)
        first, last = self.PARTS[number]
        zs = pl.ds(first, last - first)
        return remote(
            self.grads.at[slot, zs, :, self.half_of(1 - self.core)], self.core_in.at[slot, zs],
            self.core_sems.at[0, slot, number], self.core_sems.at[1, slot, number], *self.core_peer(),
        )

    def x_copy(self, layer, z):
        slot = lax.rem(layer, 2)
        return remote(
            self.grads.at[slot, z, :, self.edge_of(1 - self.x, self.core)], self.x_in.at[layer, z],
            self.x_sems.at[0, layer, z], self.x_sems.at[1, layer, z], *self.x_peer(),
        )

    def y_copy(self, layer, z):
        slot = lax.rem(layer, 2)
        return remote(
            self.grads.at[slot, z, 1 - self.y, self.mine], self.y_in.at[layer, z],
            self.y_sems.at[0, layer, z], self.y_sems.at[1, layer, z], *self.y_peer(),
        )

    def z_copy(self, layer, z):
        place = jnp.maximum(self.z_peers[z] - 1, 0)
        return remote(
            self.stage.at[layer, z], self.z_in.at[layer, place],
            self.z_sems.at[0, layer, z], self.z_sems.at[1, layer, place], self.section, z * 2 + self.y,
        )

    def z_landed(self, layer, place):
        ref = self.z_in.at[layer, place]
        return remote(ref, ref, self.z_sems.at[0, layer, 0], self.z_sems.at[1, layer, place], *self.z_peer(place + 1))

    def last_copy(self, layer):
        place = jnp.maximum(lax.rem(self.section - layer + 4, 4) - 1, 0)
        return remote(
            self.stage.at[layer, self.z], self.last_in.at[place],
            self.last_sems.at[0, layer], self.last_sems.at[1, place], layer, self.group,
        )

    def last_landed(self, place):
        return remote(
            self.last_in.at[place], self.last_in.at[place],
            self.last_sems.at[0, 0], self.last_sems.at[1, place], self.section, self.group,
        )

    def add_core(self, layer, number):
        slot = lax.rem(layer, 2)
        self.core_copy(layer, number).wait_recv()
        rows = self.half_of(self.core)
        first, last = self.PARTS[number]

        def add(i, _):
            z, y = i // 2, lax.rem(i, 2)
            self.grads[slot, z, y, rows] = self.grads[slot, z, y, rows] + self.core_in[slot, z, y]
            return 0

        lax.fori_loop(2 * first, 2 * last, add, 0)
        for z in range(first, last):
            self.x_copy(layer, z).start()

    def add_x(self, layer, z):
        slot = lax.rem(layer, 2)
        self.x_copy(layer, z).wait_recv()
        rows = self.edge_of(self.x, self.core)
        inner = pl.ds(pl.multiple_of((self.slab - self.edge) * self.x, 16), self.edge)
        self.grads[slot, z, 1 - self.y, rows] = (
            self.grads[slot, z, 1 - self.y, rows] + self.x_in[layer, z, 1 - self.y]
        )
        self.y_copy(layer, z).start()
        self.stage[layer, z] = self.grads[slot, z, self.y, self.mine]
        self.stage[layer, z, inner] = self.stage[layer, z, inner] + self.x_in[layer, z, self.y]

    def add_y(self, layer, z):
        self.y_copy(layer, z).wait_recv()
        self.stage[layer, z] = self.stage[layer, z] + self.y_in[layer, z]

        @pl.when(self.z != z)
        def _():
            self.z_copy(layer, z).start()

    def add_z(self, layer, result_ref):
        for place in range(3):
            self.z_landed(layer, place).wait_recv()
        total = self.stage[layer, self.z].astype(F32)
        for k in range(3):
            total = total + self.z_in[layer, k].astype(F32)

        @pl.when(layer == self.section)
        def _():
            result_ref[...] = jnp.zeros_like(result_ref)
            result_ref[self.mine] = total

        @pl.when(layer != self.section)
        def _():
            self.stage[layer, self.z] = total.astype(BF16)
            self.last_copy(layer).start()

    def wait_sends(self, layer, last):
        for number in (2,) if last else (0, 1):
            self.core_copy(layer, number).wait_send()
        for z in (0, 1) if last else (2, 3):
            self.x_copy(layer, z).wait_send()
            self.y_copy(layer, z).wait_send()

    def end(self, layers):
        def per_layer(layer, _):
            for z in range(4):
                @pl.when(self.z != z)
                def _():
                    self.z_copy(layer, z).wait_send()

            @pl.when(layer != self.section)
            def _():
                self.last_copy(layer).wait_send()

            return 0

        lax.fori_loop(0, layers, per_layer, 0)

    def collect(self, result_ref):
        for place in (0, 2, 1):
            self.last_landed(place).wait_recv()
            peer = lax.rem(self.section + place + 1, 4)
            rows = self.slab_of(peer // 2, lax.rem(peer, 2))
            result_ref[rows] = result_ref[rows] + self.last_in[place].astype(F32)


class Totals:
    def __init__(self, refs, sems):
        self.stage_in, self.z_in, self.norm_section, self.norm_group = refs
        self.stage_sems, self.z_sems, self.section_sems, self.group_sems = sems
        self.section, self.group, self.core, self.y, self.z_peers = mesh_place()

    def stage_copy(self, k):
        peer = (
            (self.section + 1 - 2 * self.core, self.group),
            (self.section, self.group + 1 - 2 * self.y),
            (lax.rem(self.section + 2, 4), self.group),
        )[k]
        return remote(
            self.stage_in.at[2 * k], self.stage_in.at[2 * k + 1],
            self.stage_sems.at[0, k], self.stage_sems.at[1, k], *peer,
        )

    def z_copy(self, k):
        z = self.z_peers[0]
        return remote(
            self.z_in.at[z], self.z_in.at[z], self.z_sems.at[0, k - 1], self.z_sems.at[1, k - 1],
            self.section, self.z_peers[k] * 2 + self.y,
        )

    def z_landed(self, k):
        z = self.z_peers[k]
        return remote(
            self.z_in.at[z], self.z_in.at[z], self.z_sems.at[0, k - 1], self.z_sems.at[1, k - 1],
            self.section, self.z_peers[k] * 2 + self.y,
        )

    def begin(self, tile):
        self.stage_in[0] = tile
        self.stage_copy(0).start()

    def after_core(self):
        self.stage_copy(0).wait_recv()
        self.stage_in[2] = self.stage_in[0] + self.stage_in[1]
        self.stage_copy(1).start()

    def after_y(self):
        self.stage_copy(1).wait_recv()
        self.z_in[self.z_peers[0]] = self.stage_in[2] + self.stage_in[3]
        for k in range(1, 4):
            self.z_copy(k).start()

    def after_z(self):
        for k in range(1, 4):
            self.z_landed(k).wait_recv()
        self.stage_in[4] = self.z_in[0] + self.z_in[1] + self.z_in[2] + self.z_in[3]
        self.stage_copy(2).start()

    def after_x(self):
        self.stage_copy(2).wait_recv()
        return self.stage_in[4] + self.stage_in[5]

    def norm_copy(self, k):
        if k < 3:
            peer = (lax.rem(self.section + k + 1, 4), self.group)
            ref = self.norm_section.at[self.section]
            return remote(ref, ref, self.section_sems.at[0, k], self.section_sems.at[1, k], *peer)
        k = k - 3
        peer = (self.section, lax.rem(self.group + k + 1, 8))
        ref = self.norm_group.at[self.group]
        return remote(ref, ref, self.group_sems.at[0, k], self.group_sems.at[1, k], *peer)

    def norm_landed(self, k):
        if k < 3:
            ref = self.norm_section.at[lax.rem(self.section - k - 1 + 4, 4)]
            return remote(
                ref, ref, self.section_sems.at[0, k], self.section_sems.at[1, k], self.section, self.group
            )
        k = k - 3
        ref = self.norm_group.at[lax.rem(self.group - k - 1 + 8, 8)]
        return remote(ref, ref, self.group_sems.at[0, k], self.group_sems.at[1, k], self.section, self.group)

    def norm(self, value):
        self.norm_section[self.section] = value
        for k in range(3):
            self.norm_copy(k).start()
        for k in range(3):
            self.norm_landed(k).wait_recv()
        total = self.norm_section[0]
        for k in range(1, 4):
            total = total + self.norm_section[k]
        self.norm_group[self.group] = total
        for k in range(3, 10):
            self.norm_copy(k).start()
        for k in range(3, 10):
            self.norm_landed(k).wait_recv()
        total = self.norm_group[0]
        for k in range(1, 8):
            total = total + self.norm_group[k]
        return total

    def end(self):
        for k in range(3):
            self.stage_copy(k).wait_send()
        for k in range(1, 4):
            self.z_copy(k).wait_send()
        for k in range(10):
            self.norm_copy(k).wait_send()


def norm_reverse(value, gain, grad):
    factor = lax.rsqrt(jnp.mean(value * value, axis=-1, keepdims=True) + 1e-06)
    scaled = grad * gain
    mean = jnp.mean(value * scaled, axis=-1, keepdims=True)
    unit = value * factor
    back = factor * scaled - unit * (factor * factor * mean)
    return back, jnp.sum(grad * unit, axis=0, keepdims=True), (unit * gain).astype(BF16)


def backward_kernel(
    layers, half, loss_grad_ref, w_ref, gain_ref, sent_ref,
    probs_ref, qkv_ref, att_ref, middle_ref, hidden_ref, slope_ref, stats_ref,
    result_ref, totals_ref, square_ref,
    sends_ref, dffn_ref, dpre_ref, normed_ref, dmid_ref, datt_ref, dhold_ref, dqkv_ref,
    gain_grad_ref, *comm_refs,
):
    seg, width = loss_grad_ref.shape
    dim = width // HEADS
    part = width // 4
    layer = layers - 1 - pl.program_id(0)
    rows = 512
    chunks = seg // rows
    gain_one = gain_ref[0, 0:1]
    gain_two = gain_ref[0, 1:2]
    scatter = Scatter(comm_refs[:7], comm_refs[11:16])
    totals = Totals(comm_refs[7:11], comm_refs[16:])
    grads_ref = comm_refs[0]
    slot = lax.rem(layer, 2)

    @pl.when(layer == layers - 1)
    def _():
        scatter.signal_all()
        sends_ref[...] = jnp.zeros_like(sends_ref)
        gain_grad_ref[...] = jnp.zeros_like(gain_grad_ref)

    def put_grad(first, step, value):
        for r in range(4):
            quad = first + step * r
            owner = quad // 6
            at = pl.ds(pl.multiple_of(lax.rem(quad, 6) * part, part), part)
            grads_ref[slot, owner // 2, lax.rem(owner, 2), at] = value[r * part : (r + 1) * part].astype(BF16)

    def serve(back, here, *steps):
        @pl.when((layer + back < layers) & here)
        def _():
            for kind, *args in steps:
                getattr(scatter, kind)(layer + back, *args)

    serve(2, True, ("wait_sends", False))
    later = sends_ref[jnp.minimum(layer + 1, layers - 1)].astype(F32)
    skip = sends_ref[jnp.minimum(layer + half, layers - 1)].astype(F32)
    dmid_ref[...] = jnp.where(
        layer == layers - 1, loss_grad_ref[...], later + jnp.where(layer + half < layers, skip, 0.0)
    )
    dffn_ref[...] = dmid_ref[...].astype(BF16)
    for c in range(4):
        put_grad(32 + 4 * c, 1, dot_tn(hidden_ref[0, c], dffn_ref[...]))

    @pl.when(layer == layers - 1)
    def _():
        scatter.wait_all()

    scatter.core_copy(layer, 0).start()

    def ffn_step(i, _):
        at = pl.ds(pl.multiple_of(i * rows, rows), rows)
        dffn = dffn_ref[at]
        dnormed = jnp.zeros((rows, width), F32)
        for c in range(4):
            dhidden = dot_nt(dffn, stack_quads(w_ref, 32 + 4 * c, 1, 4))
            dpre = (dhidden * slope_ref[0, c, at].astype(F32)).astype(BF16)
            dpre_ref[c, at] = dpre
            dnormed = dnormed + dot_nt(dpre, stack_quads(w_ref, 16 + c, 4, 4))
        back, gain_grad, normed = norm_reverse(middle_ref[0, at], gain_two, dnormed)
        gain_grad_ref[layer, 1:2] += gain_grad
        normed_ref[at] = normed
        dmid = dmid_ref[at] + back
        dmid_ref[at] = dmid
        datt = dmid.astype(BF16)
        datt_ref[at] = datt
        dattended = dot_nt(datt, stack_quads(w_ref, 12, 1, 4)).astype(BF16)
        dhold_ref[at] = dattended

        serve(1, i == 0, ("add_y", 3), ("add_x", 1), ("add_core", 2))
        serve(2, i == 0, ("add_y", 0))
        return 0

    lax.fori_loop(0, chunks, ffn_step, 0)

    serve(2, True, ("wait_sends", True))

    def ffn_grad_step(c, _):
        put_grad(16 + c, 4, dot_tn(normed_ref[...], dpre_ref[c]))
        return 0

    for c in range(4):
        ffn_grad_step(c, 0)
    put_grad(12, 1, dot_tn(att_ref[0], datt_ref[...]))
    scatter.core_copy(layer, 1).start()
    scatter.add_core(layer, 0)
    serve(1, True, ("add_x", 2))

    def head_step(h):
        queries, keys, values = (qkv_ref[0, t, :, h * dim : (h + 1) * dim] for t in range(3))
        probs = probs_ref[0, h]
        dhold = dhold_ref[:, h * dim : (h + 1) * dim]
        dprobs = dot_nt(dhold, values)
        wide = probs.astype(F32)
        dot_sum = jnp.sum(wide * dprobs, axis=-1, keepdims=True)
        dscores = (wide * (dprobs - dot_sum)).astype(BF16)
        return (
            (dot_nn(dscores, keys) * dim ** (-0.5)).astype(BF16),
            (dot_tn(dscores, queries) * dim ** (-0.5)).astype(BF16),
            dot_tn(probs, dhold).astype(BF16),
        )

    def put_heads(first, parts):
        for t in range(3):
            dqkv_ref[t, :, first * dim : (first + len(parts)) * dim] = jnp.concatenate([p[t] for p in parts], axis=1)

    put_heads(0, [head_step(h) for h in range(HEADS // 2)])
    scatter.add_core(layer, 1)
    serve(1, True, ("add_x", 0))

    put_heads(HEADS // 2, [head_step(h) for h in range(HEADS // 2, HEADS)])
    scatter.add_x(layer, 3)
    serve(1, True, ("add_y", 1))

    def qkv_step(i, _):
        at = pl.ds(pl.multiple_of(i * rows, rows), rows)
        dnormed = jnp.zeros((rows, width), F32)
        for t in range(3):
            dnormed = dnormed + dot_nt(dqkv_ref[t, at], stack_quads(w_ref, t, 3, 4))
        prev = sent_ref[layer, at].astype(F32)
        skip = sent_ref[jnp.maximum(layer + 1 - half, 0), at].astype(F32)
        stream = prev + jnp.where(layer >= half, skip, 0.0)
        back, gain_grad, normed = norm_reverse(stream, gain_one, dnormed)
        gain_grad_ref[layer, 0:1] += gain_grad
        normed_ref[at] = normed
        sends_ref[layer, at] = (dmid_ref[at] + back).astype(BF16)
        return 0

    lax.fori_loop(0, chunks, qkv_step, 0)

    def qkv_grad_step(t, _):
        put_grad(t, 3, dot_tn(normed_ref[...], dqkv_ref[t]))
        return 0

    for t in range(3):
        qkv_grad_step(t, 0)
    scatter.core_copy(layer, 2).start()
    serve(1, True, ("add_y", 2))
    serve(2, True, ("add_z", result_ref))

    @pl.when(layer == 0)
    def _():
        lane = lax.broadcasted_iota(jnp.int32, (1, width), 1)
        rows_out = [gain_grad_ref[k // 2, k % 2 : k % 2 + 1] for k in range(2 * layers)]
        for k in range(layers):
            row = jnp.zeros((1, width), F32)
            for i in range(4):
                value = jnp.sum(stats_ref[k, i : i + 1], axis=1, keepdims=True)
                row = jnp.where(lane == i, value, row)
            rows_out.append(row)
        rows_out.append(jnp.zeros((16 - 3 * layers, width), F32))
        totals.begin(jnp.concatenate(rows_out, axis=0))
        scatter.add_core(0, 2)
        scatter.add_y(0, 3)
        scatter.add_x(0, 1)
        scatter.add_y(1, 0)
        totals.after_core()
        scatter.add_x(0, 2)
        scatter.add_x(0, 0)
        totals.after_y()
        scatter.add_y(0, 1)
        scatter.add_y(0, 2)
        scatter.add_y(0, 0)
        scatter.add_z(1, result_ref)
        scatter.add_z(0, result_ref)
        totals.after_z()
        scatter.collect(result_ref)
        square = jnp.zeros((8, width), F32)
        for q in range(6):
            value = result_ref[q * part : (q + 1) * part]
            square = square + jnp.sum((value * value).reshape(part // 8, 8, width), axis=0)
        folded = square[:, :128] + square[:, 128:256] + square[:, 256:]
        square_ref[...] = totals.norm(folded)
        totals_ref[...] = totals.after_x()
        for back in (1, 0):
            for last in (False, True):
                scatter.wait_sends(back, last)
        scatter.end(layers)
        totals.end()


FF = 1536


def from_behind(value, axis, by):
    peers = lax.axis_size(axis)
    pairs = [(i, i + by) for i in range(peers) if 0 <= i + by < peers]
    return lax.ppermute(value, axis, pairs)


def unblock(blocks, row_count, col_count, block_size):
    return (
        blocks.reshape(row_count // block_size, col_count // block_size, block_size, block_size)
        .transpose(0, 2, 1, 3)
        .reshape(row_count, col_count)
    )


def to_blocks(matrix, block_size):
    row_count, col_count = matrix.shape
    return (
        matrix.reshape(row_count // block_size, block_size, col_count // block_size, block_size)
        .transpose(0, 2, 1, 3)
        .reshape(-1, block_size * block_size)
    )


def split_matrices(blocks, model_width):
    block_size = model_width // 4
    shapes = (
        (model_width, 3 * model_width),
        (model_width, model_width),
        (model_width, FF),
        (FF, model_width),
    )
    result = []
    offset = 0
    for row_count, col_count in shapes:
        number = row_count * col_count // (block_size * block_size)
        result.append(unblock(blocks[offset : offset + number], row_count, col_count, block_size))
        offset = offset + number
    return result


def rms_norm(stream, gain):
    factor = lax.rsqrt(jnp.mean(stream * stream, axis=-1, keepdims=True) + 1e-06)
    return (stream * factor * gain, factor)


def norm_back(stream, factor, gain, grad):
    scaled = grad * gain
    grad_in = factor * scaled - stream * factor**3 * jnp.mean(
        stream * scaled, axis=-1, keepdims=True
    )
    return (grad_in, jnp.sum(grad * stream * factor, axis=0))


def gelu_slope(pre_act):
    return (
        0.5 * (1.0 + lax.erf(pre_act * 0.7071067811865476))
        + pre_act * jnp.exp(-0.5 * pre_act * pre_act) * 0.3989422804014327
    )


def layer_forward(stream, matrices, gain_pair, length):
    w_qkv, w_out, w_up, w_down = matrices
    row_count, model_width = stream.shape
    head_dim = model_width // HEADS
    frames = jnp.arange(row_count)
    norm_one, scale_one = rms_norm(stream, gain_pair[0])
    normed = norm_one.astype(BF16)
    qkv_all = jnp.dot(normed, w_qkv, preferred_element_type=jnp.float32).astype(BF16)
    queries = qkv_all[:, :model_width].reshape(row_count, HEADS, head_dim)
    key_rows = qkv_all[:, model_width : 2 * model_width].reshape(row_count, HEADS, head_dim)
    value_rows = qkv_all[:, 2 * model_width :].reshape(row_count, HEADS, head_dim)
    masking = jnp.where(frames < length, 0.0, -1e30).astype(jnp.float32)
    scores = jnp.einsum(
        "qhe,khe->hqk", queries, key_rows, preferred_element_type=jnp.float32
    ) * head_dim ** (-0.5)
    attn_probs = jax.nn.softmax(scores + masking[None, None, :], axis=-1)
    probs_low = attn_probs.astype(BF16)
    attended = (
        jnp.einsum("hqk,khe->qhe", probs_low, value_rows, preferred_element_type=jnp.float32)
        .reshape(row_count, model_width)
        .astype(BF16)
    )
    branch_attn = jnp.dot(attended, w_out, preferred_element_type=jnp.float32)
    middle = stream + branch_attn
    norm_two, scale_two = rms_norm(middle, gain_pair[1])
    normed_two = norm_two.astype(BF16)
    pre_act = jnp.dot(normed_two, w_up, preferred_element_type=jnp.float32)
    hidden = jax.nn.gelu(pre_act, approximate=False).astype(BF16)
    branch_ffn = jnp.dot(hidden, w_down, preferred_element_type=jnp.float32)
    kept_vals = (
        scale_one,
        normed,
        queries,
        key_rows,
        value_rows,
        attn_probs,
        probs_low,
        attended,
        middle,
        scale_two,
        normed_two,
        pre_act,
        hidden,
    )
    return (middle + branch_ffn, branch_attn, branch_ffn, kept_vals)


def layer_backward(stream, matrices, gain_pair, length, upstream):
    w_qkv, w_out, w_up, w_down = matrices
    row_count, model_width = stream.shape
    head_dim = model_width // HEADS
    output, branch_attn, branch_ffn, kept_vals = layer_forward(stream, matrices, gain_pair, length)
    (
        scale_one,
        normed,
        queries,
        key_rows,
        value_rows,
        attn_probs,
        probs_low,
        attended,
        middle,
        scale_two,
        normed_two,
        pre_act,
        hidden,
    ) = kept_vals
    grad_ffn = upstream.astype(BF16)
    grad_down = jnp.dot(hidden.T, grad_ffn, preferred_element_type=jnp.float32)
    grad_hidden = jnp.dot(grad_ffn, w_down.T, preferred_element_type=jnp.float32)
    grad_pre = (grad_hidden * gelu_slope(pre_act)).astype(BF16)
    grad_up = jnp.dot(normed_two.T, grad_pre, preferred_element_type=jnp.float32)
    back_mid, gain_two = norm_back(
        middle,
        scale_two,
        gain_pair[1],
        jnp.dot(grad_pre, w_up.T, preferred_element_type=jnp.float32),
    )
    grad_mid = upstream + back_mid
    grad_branch = grad_mid.astype(BF16)
    grad_out = jnp.dot(attended.T, grad_branch, preferred_element_type=jnp.float32)
    grad_att = (
        jnp.dot(grad_branch, w_out.T, preferred_element_type=jnp.float32)
        .astype(BF16)
        .reshape(row_count, HEADS, head_dim)
    )
    grad_value = jnp.einsum("hqk,qhe->khe", probs_low, grad_att, preferred_element_type=jnp.float32)
    grad_probs = jnp.einsum(
        "qhe,khe->hqk", grad_att, value_rows, preferred_element_type=jnp.float32
    )
    grad_scores = (
        attn_probs * (grad_probs - jnp.sum(attn_probs * grad_probs, axis=-1, keepdims=True))
    ).astype(BF16)
    grad_query = jnp.einsum(
        "hqk,khe->qhe", grad_scores, key_rows, preferred_element_type=jnp.float32
    ) * head_dim ** (-0.5)
    grad_key = jnp.einsum(
        "hqk,qhe->khe", grad_scores, queries, preferred_element_type=jnp.float32
    ) * head_dim ** (-0.5)
    grad_qkv = jnp.concatenate(
        [
            grad_query.reshape(row_count, model_width),
            grad_key.reshape(row_count, model_width),
            grad_value.reshape(row_count, model_width),
        ],
        axis=1,
    ).astype(BF16)
    grad_wqkv = jnp.dot(normed.T, grad_qkv, preferred_element_type=jnp.float32)
    back_in, gain_one = norm_back(
        stream,
        scale_one,
        gain_pair[0],
        jnp.dot(grad_qkv, w_qkv.T, preferred_element_type=jnp.float32),
    )
    return (
        grad_mid + back_in,
        (grad_wqkv, grad_out, grad_up, grad_down),
        jnp.stack([gain_one, gain_two]),
    )


def spectral_terms(output, target, length, present_row, frame_count):
    row_count, model_width = output.shape
    bin_count = model_width // 8
    spectra = output.reshape(row_count, 4, 2, bin_count)
    real_part = spectra[:, :, 0]
    imag_part = spectra[:, :, 1]
    magnitude = jnp.sqrt(real_part * real_part + imag_part * imag_part + 0.01)
    differ = magnitude - target.reshape(row_count, 4, bin_count)
    smooth_err = jnp.sqrt(differ * differ + 0.01)
    weight = (jnp.arange(row_count) < length).astype(jnp.float32)[:, None, None] * present_row[
        None, :, None
    ]
    loss_slope = weight * differ / smooth_err / magnitude / frame_count
    grad_spec = jnp.stack([loss_slope * real_part, loss_slope * imag_part], axis=2).reshape(
        row_count, model_width
    )
    return (jnp.sum(smooth_err * weight), grad_spec)


def pipelined_body(
    x_in,
    targets,
    valid_len,
    present_stems,
    w_master,
    norm_gains,
    gain_m,
    gain_v,
    l_stats,
    r_stats,
    l_roots,
    r_roots,
    step_count,
):
    model_width = x_in.shape[1]
    block_size = model_width // 4
    sections = lax.axis_size("section")
    section_idx = lax.axis_index("section")
    half_way = sections // 2
    groups = lax.axis_size("dp")
    group_idx = lax.axis_index("dp")
    micro_count = valid_len.shape[0] // groups
    seg_len = x_in.shape[0] // micro_count
    own_blocks = w_master.shape[1]
    own_gain = norm_gains.shape[2]
    full_w, full_g = (
        lax.all_gather(w_master.astype(BF16), "dp", axis=1, tiled=True),
        lax.all_gather(norm_gains.astype(BF16), "dp", axis=2, tiled=True),
    )
    matrices = split_matrices(full_w[0], model_width)
    gain_pair = full_g[0].astype(jnp.float32)
    lengths = lax.dynamic_slice_in_dim(valid_len, group_idx * micro_count, micro_count)
    stem_flags = lax.dynamic_slice_in_dim(
        present_stems, group_idx * micro_count, micro_count
    ).astype(jnp.float32)
    frame_count = jnp.sum(valid_len).astype(jnp.float32)
    decoder = section_idx >= half_way
    encoder = section_idx < half_way
    is_last = section_idx == sections - 1
    act_shape = (micro_count, seg_len, model_width)

    def forward_step(step_idx, loop_state):
        in_rows, kept_prev, skip_store, loss_grads, loss_sum, sq_sums = loop_state
        micro_idx = step_idx - section_idx
        active = (micro_idx >= 0) & (micro_idx < micro_count)
        slot_idx = jnp.clip(micro_idx, 0, micro_count - 1)
        fresh_rows = lax.dynamic_slice_in_dim(x_in, slot_idx * seg_len, seg_len, 0)
        previous = jnp.where(section_idx == 0, fresh_rows, in_rows)
        stream = previous.astype(jnp.float32) + jnp.where(
            decoder, skip_store[slot_idx].astype(jnp.float32), 0.0
        )
        length = lengths[slot_idx]
        target = lax.dynamic_slice_in_dim(targets, slot_idx * seg_len, seg_len, 0)

        def forward_compute_fn(operand):
            output, branch_attn, branch_ffn, kept_vals = layer_forward(
                stream, matrices, gain_pair, length
            )
            valid = (jnp.arange(seg_len) < length).astype(jnp.float32)[:, None]
            squares = jnp.stack(
                [
                    jnp.sum(valid * stream * stream),
                    jnp.sum(valid * branch_attn * branch_attn),
                    jnp.sum(valid * branch_ffn * branch_ffn),
                ]
            )
            seg_loss, grad_spec = spectral_terms(
                output, target, length, stem_flags[slot_idx], frame_count
            )
            return (output, squares, seg_loss, grad_spec)

        def forward_spare_fn(operand):
            empty = jnp.zeros((seg_len, model_width), jnp.float32)
            return (empty, jnp.zeros((3,), jnp.float32), jnp.zeros((), jnp.float32), empty)

        output, squares, seg_loss, grad_spec = lax.cond(
            active, forward_compute_fn, forward_spare_fn, 0
        )
        kept_prev = kept_prev.at[slot_idx].set(jnp.where(active, previous, kept_prev[slot_idx]))
        loss_grads = loss_grads.at[slot_idx].set(
            jnp.where(active & is_last, grad_spec, loss_grads[slot_idx])
        )
        loss_sum = loss_sum + jnp.where(is_last, seg_loss, 0.0)
        sq_sums = sq_sums + squares
        sent_rows = output.astype(BF16)
        in_rows = from_behind(sent_rows, "section", 1)
        from_encoder = from_behind(sent_rows, "section", half_way)
        recv_idx = step_idx - section_idx + half_way
        usable = decoder & (recv_idx >= 0) & (recv_idx < micro_count)
        recv_slot = jnp.clip(recv_idx, 0, micro_count - 1)
        skip_store = skip_store.at[recv_slot].set(
            jnp.where(usable, from_encoder, skip_store[recv_slot])
        )
        return (in_rows, kept_prev, skip_store, loss_grads, loss_sum, sq_sums)

    start_state = (
        jnp.zeros((seg_len, model_width), BF16),
        jnp.zeros(act_shape, BF16),
        jnp.zeros(act_shape, BF16),
        jnp.zeros(act_shape, jnp.float32),
        jnp.zeros((), jnp.float32),
        jnp.zeros((3,), jnp.float32),
    )
    unused_rows, kept_prev, skip_store, loss_grads, loss_sum, sq_sums = lax.fori_loop(
        0, micro_count + sections - 1, forward_step, start_state
    )

    def backward_step(step_idx, loop_state):
        in_grads, skip_grad_store, grad_mats, grad_gains = loop_state
        micro_idx = step_idx - (sections - 1 - section_idx)
        active = (micro_idx >= 0) & (micro_idx < micro_count)
        slot_idx = jnp.clip(micro_idx, 0, micro_count - 1)
        upstream = jnp.where(
            is_last,
            loss_grads[slot_idx],
            in_grads.astype(jnp.float32)
            + jnp.where(encoder, skip_grad_store[slot_idx].astype(jnp.float32), 0.0),
        )
        stream = kept_prev[slot_idx].astype(jnp.float32) + jnp.where(
            decoder, skip_store[slot_idx].astype(jnp.float32), 0.0
        )
        length = lengths[slot_idx]

        def backward_compute_fn(operand):
            return layer_backward(stream, matrices, gain_pair, length, upstream)

        def backward_spare_fn(operand):
            return (
                jnp.zeros_like(stream),
                tuple((jnp.zeros(mat.shape, jnp.float32) for mat in matrices)),
                jnp.zeros((2, model_width), jnp.float32),
            )

        grad_stream, layer_mats, layer_gains = lax.cond(
            active, backward_compute_fn, backward_spare_fn, 0
        )
        grad_mats = tuple((total + piece for total, piece in zip(grad_mats, layer_mats)))
        grad_gains = grad_gains + layer_gains
        grad_rows = grad_stream.astype(BF16)
        in_grads = from_behind(grad_rows, "section", -1)
        from_decoder = from_behind(grad_rows, "section", -half_way)
        recv_idx = micro_idx + half_way
        usable = encoder & (recv_idx >= 0) & (recv_idx < micro_count)
        recv_slot = jnp.clip(recv_idx, 0, micro_count - 1)
        skip_grad_store = skip_grad_store.at[recv_slot].set(
            jnp.where(usable, from_decoder, skip_grad_store[recv_slot])
        )
        return (in_grads, skip_grad_store, grad_mats, grad_gains)

    back_state = (
        jnp.zeros((seg_len, model_width), BF16),
        jnp.zeros(act_shape, BF16),
        tuple((jnp.zeros(mat.shape, jnp.float32) for mat in matrices)),
        jnp.zeros((2, model_width), jnp.float32),
    )
    unused_grads, unused_store, grad_mats, grad_gains = lax.fori_loop(
        0, micro_count + sections - 1, backward_step, back_state
    )
    grad_all = jnp.concatenate([to_blocks(mat, block_size) for mat in grad_mats], axis=0)
    summed_w, summed_g = lax.psum((grad_all, grad_gains), "dp")
    own_grad = lax.dynamic_slice_in_dim(summed_w, group_idx * own_blocks, own_blocks, 0)
    own_gain_grad = lax.dynamic_slice_in_dim(summed_g, group_idx * own_gain, own_gain, 1)
    own_square = jnp.sum(own_grad * own_grad) + jnp.sum(own_gain_grad * own_gain_grad)
    rows_local = jnp.zeros((sections, 3), jnp.float32).at[section_idx].set(sq_sums)
    total_square, loss_value, rows_total = lax.psum(
        (own_square, loss_sum / frame_count, rows_local), ("section", "dp")
    )
    grad_norm = jnp.sqrt(total_square)
    clip_limit = 0.00015 * math.sqrt(
        sections * (own_blocks * groups * block_size * block_size + 2 * model_width)
    )
    factor = clip_limit / jnp.maximum(grad_norm, clip_limit)
    grad_blocks = own_grad * factor
    square = (own_blocks, block_size, block_size)
    shaped = grad_blocks.reshape(square)
    highest = lax.Precision.HIGHEST
    l_new = 0.95 * l_stats[0].reshape(square) + 0.05 * jnp.einsum(
        "bij,bkj->bik", shaped, shaped, precision=highest
    )
    r_new = 0.95 * r_stats[0].reshape(square) + 0.05 * jnp.einsum(
        "bji,bjk->bik", shaped, shaped, precision=highest
    )
    left_side = jnp.einsum("bij,bjk->bik", l_roots[0].reshape(square), shaped, precision=highest)
    precond = jnp.einsum("bij,bjk->bik", left_side, r_roots[0].reshape(square), precision=highest)
    master = w_master[0]
    w_new = master - 0.5 * (precond.reshape(master.shape) + 0.01 * master)
    gain_grad = own_gain_grad * factor
    m_new = 0.9 * gain_m[0] + 0.1 * gain_grad
    v_new = 0.999 * gain_v[0] + 0.001 * gain_grad * gain_grad
    step_num = step_count[0].astype(jnp.float32)
    m_hat = m_new / (1.0 - jnp.power(0.9, step_num))
    v_hat = v_new / (1.0 - jnp.power(0.999, step_num))
    gains_new = norm_gains[0] - 0.5 * m_hat / (jnp.sqrt(v_hat) + 1e-08)
    rms = jnp.sqrt(rows_total[section_idx] / (frame_count * model_width)).reshape(1, 3)
    return (
        w_new[None],
        grad_blocks[None],
        l_new.reshape(master.shape)[None],
        r_new.reshape(master.shape)[None],
        gains_new[None],
        m_new[None],
        v_new[None],
        loss_value,
        grad_norm,
        rms,
    )


def layer_block(shape):
    return pl.BlockSpec((1,) + shape, lambda i: (i,) + (0,) * len(shape))


def whole_block(shape):
    return pl.BlockSpec(shape, lambda i: (0,) * len(shape))


def held_block(shape):
    return pl.BlockSpec(shape, lambda i: (0,) * len(shape), pipeline_mode=pl.Buffered(1))


def forward(layers, micro, valid_len, present_stems, x_in, targets, flat_w, gain):
    width = x_in.shape[1]
    seg = x_in.shape[0] // micro
    dim = width // HEADS
    part = width // 4
    half = layers // 2
    shapes = (
        (HEADS, seg, seg), (3, seg, width), (seg, width), (seg, width), (4, seg, width), (4, seg, width)
    )
    kinds = (BF16, BF16, BF16, F32, BF16, BF16)

    def slot():
        return jnp.minimum(lax.axis_index("section"), micro - 1)

    return pl.pallas_call(
        functools.partial(forward_kernel, layers, half, micro),
        grid=(layers,),
        in_specs=[
            pl.BlockSpec(memory_space=pltpu.SMEM),
            pl.BlockSpec(memory_space=pltpu.SMEM),
            pl.BlockSpec((seg, width), lambda i: (slot(), 0)),
            pl.BlockSpec((width // 2, seg), lambda i: (0, slot())),
            pl.BlockSpec(memory_space=pltpu.VMEM),
            pl.BlockSpec(memory_space=pltpu.VMEM),
        ],
        out_specs=[layer_block(s) for s in shapes]
        + [whole_block((layers, seg, width)), whole_block((seg, width)), whole_block((layers, 8, width))]
        + [pl.BlockSpec(memory_space=pl.ANY), whole_block((layers, 8, width))],
        out_shape=[jax.ShapeDtypeStruct((layers,) + s, k) for s, k in zip(shapes, kinds)]
        + [
            jax.ShapeDtypeStruct((layers, seg, width), BF16),
            jax.ShapeDtypeStruct((seg, width), F32),
            jax.ShapeDtypeStruct((layers, 8, width), F32),
            jax.ShapeDtypeStruct((layers, 48 * part, width), BF16),
            jax.ShapeDtypeStruct((layers, 8, width), F32),
        ],
        scratch_shapes=[
            pltpu.VMEM((seg, width), F32),
            pltpu.VMEM((seg, width), BF16),
            pltpu.VMEM((layers, 48 * part, width), BF16),
            pltpu.VMEM((layers, 8, 8, 128), F32),
            pltpu.VMEM((6 * part, width), BF16),
            pltpu.VMEM((8, 128), F32),
            pltpu.VMEM((4, part, 128), F32),
            pltpu.SemaphoreType.DMA((2, 3)),
            pltpu.SemaphoreType.DMA((2, layers, 4)),
            pltpu.SemaphoreType.DMA((2, layers, 4)),
            pltpu.SemaphoreType.DMA((2, layers, 8)),
            pltpu.SemaphoreType.DMA((2, layers, 8)),
            pltpu.SemaphoreType.DMA((2, 10)),
            pltpu.SemaphoreType.DMA((layers,)),
        ],
        compiler_params=pltpu.CompilerParams(
            vmem_limit_bytes=VMEM_LIMIT, collective_id=0, has_side_effects=True
        ),
    )(valid_len, present_stems, x_in, targets.T, flat_w, gain)


def backward(layers, loss_grad, full_w, full_g, sent, saved, stats):
    seg, width = loss_grad.shape
    dim = width // HEADS
    part = width // 4
    half = layers // 2

    def from_end(array):
        shape = array.shape[1:]
        return pl.BlockSpec((1,) + shape, lambda i: (layers - 1 - i,) + (0,) * len(shape))

    return pl.pallas_call(
        functools.partial(backward_kernel, layers, half),
        grid=(layers,),
        in_specs=[
            held_block((seg, width)),
            from_end(full_w),
            from_end(full_g),
            held_block((layers, seg, width)),
        ]
        + [from_end(a) for a in saved]
        + [pl.BlockSpec(memory_space=pltpu.VMEM)],
        out_specs=[pl.BlockSpec(memory_space=pltpu.VMEM)] * 3,
        out_shape=[
            jax.ShapeDtypeStruct((6 * part, width), F32),
            jax.ShapeDtypeStruct((16, width), F32),
            jax.ShapeDtypeStruct((8, 128), F32),
        ],
        scratch_shapes=[
            pltpu.VMEM((layers, seg, width), BF16),
            pltpu.VMEM((seg, width), BF16),
            pltpu.VMEM((4, seg, width), BF16),
            pltpu.VMEM((seg, width), BF16),
            pltpu.VMEM((seg, width), F32),
            pltpu.VMEM((seg, width), BF16),
            pltpu.VMEM((seg, width), BF16),
            pltpu.VMEM((3, seg, width), BF16),
            pltpu.VMEM((layers, 8, width), F32),
            pltpu.VMEM((2, 4, 2, 576, width), BF16),
            pltpu.VMEM((2, 4, 2, 288, width), BF16),
            pltpu.VMEM((layers, 4, 2, 80, width), BF16),
            pltpu.VMEM((layers, 4, 208, width), BF16),
            pltpu.VMEM((layers, 4, 208, width), BF16),
            pltpu.VMEM((layers, 3, 208, width), BF16),
            pltpu.VMEM((3, 208, width), BF16),
            pltpu.VMEM((6, 16, width), F32),
            pltpu.VMEM((4, 16, width), F32),
            pltpu.VMEM((4, 8, 128), F32),
            pltpu.VMEM((8, 8, 128), F32),
            pltpu.SemaphoreType.DMA((2, 2, 3)),
            pltpu.SemaphoreType.DMA((2, layers, 4)),
            pltpu.SemaphoreType.DMA((2, layers, 4)),
            pltpu.SemaphoreType.DMA((2, layers, 4)),
            pltpu.SemaphoreType.DMA((2, layers)),
            pltpu.SemaphoreType.DMA((2, 3)),
            pltpu.SemaphoreType.DMA((2, 3)),
            pltpu.SemaphoreType.DMA((2, 3)),
            pltpu.SemaphoreType.DMA((2, 7)),
        ],
        compiler_params=pltpu.CompilerParams(
            vmem_limit_bytes=VMEM_LIMIT, collective_id=1, has_side_effects=True
        ),
    )(loss_grad, full_w, full_g, sent, *saved, stats)


def split(value):
    high = value.astype(BF16)
    return high, (value - high.astype(F32)).astype(BF16)


def dot_split(dot, left, right):
    return dot(left[0], right[0]) + (dot(left[0], right[1]) + dot(left[1], right[0]))


def update_kernel(
    layers, limit, length_ref, step_ref, square_ref, tile_ref, quads_ref, w_ref, l_ref, r_ref, lroot_ref, rroot_ref,
    gain_ref, gain_m_ref, gain_v_ref,
    w_out, grad_out, l_out, r_out, gain_out, m_out, v_out, loss_out, norm_out, rms_out,
    block_ref,
):
    part, width = quads_ref.shape[1:]
    gains = tile_ref[: 2 * layers]
    norm = jnp.sqrt(jnp.sum(square_ref[...], keepdims=True) + jnp.sum(gains * gains, keepdims=True))
    factor = limit / jnp.maximum(norm, limit)

    def quad_step(q, _):
        for c in range(4):
            base = 4 * q + c
            load_block(lroot_ref, base, block_ref.at[0])
            load_block(rroot_ref, base, block_ref.at[1])
            grad = quads_ref[q, :, part * c : part * (c + 1)] * factor
            pair = split(grad)
            left = dot_split(dot_nn, split(block_ref[0, :, :part]), pair)
            pre = dot_split(dot_nn, split(left), split(block_ref[1, :, :part]))
            for i, value in enumerate((
                grad, pre, dot_split(dot_nt, pair, pair), dot_split(dot_tn, pair, pair)
            )):
                block_ref[2 + i, :, :part] = value
            parts = [flat_parts(block_ref.at[2 + i]) for i in range(4)]
            for m in range(3):
                at = (pl.ds(base + 8 * m, 24, stride=24), slice(None))
                grad_out[at] = parts[0][m]
                master = w_ref[at]
                w_out[at] = master - 0.5 * (parts[1][m] + 0.01 * master)
                l_out[at] = 0.95 * l_ref[at] + 0.05 * parts[2][m]
                r_out[at] = 0.95 * r_ref[at] + 0.05 * parts[3][m]
        return 0

    for q in range(2):
        quad_step(q, 0)

    @pl.when(pl.program_id(0) == 0)
    def _():
        section, group = lax.axis_index("section"), lax.axis_index("dp")
        share = gain_ref.shape[1]
        row = tile_ref[:2]
        for k in range(1, layers):
            row = jnp.where(section == k, tile_ref[2 * k : 2 * k + 2], row)
        own = row[:, :share]
        for g in range(1, width // share):
            own = jnp.where(group == g, row[:, g * share : (g + 1) * share], own)
        grad = own * factor
        m_new = 0.9 * gain_m_ref[...] + 0.1 * grad
        v_new = 0.999 * gain_v_ref[...] + 0.001 * grad * grad
        step = jnp.full((1, 1), step_ref[0], jnp.int32).astype(F32)
        m_hat = m_new / (1.0 - jnp.exp(step * math.log(0.9)))
        v_hat = v_new / (1.0 - jnp.exp(step * math.log(0.999)))
        gain_out[...] = gain_ref[...] - 0.5 * m_hat / (jnp.sqrt(v_hat) + 1e-08)
        m_out[...] = m_new
        v_out[...] = v_new
        norm_out[...] = norm
        frames = length_ref[0]
        for k in range(1, length_ref.shape[0]):
            frames = frames + length_ref[k]
        frames = jnp.full((1, 1), frames, jnp.int32).astype(F32)
        loss_out[...] = tile_ref[2 * layers : 2 * layers + 1, 3:4] / frames
        squares = tile_ref[2 * layers : 2 * layers + 1, :3]
        for k in range(1, layers):
            squares = jnp.where(section == k, tile_ref[2 * layers + k : 2 * layers + k + 1, :3], squares)
        rms_out[...] = jnp.sqrt(squares / (frames * width))


def update(layers, limit, valid_len, step_count, squares, tile, quads, flats, gains):
    blocks = 4 * quads.shape[0]
    part, width = quads.shape[1:]
    rows = flats[0].shape[0]
    whole = [pl.BlockSpec(memory_space=pltpu.VMEM)]
    flat = [pl.BlockSpec((rows // 3, 128), lambda i: (i, 0))]
    share = gains[0].shape
    return pl.pallas_call(
        functools.partial(update_kernel, layers, limit),
        grid=(3,),
        in_specs=[pl.BlockSpec(memory_space=pltpu.SMEM)] * 2 + whole * 2
        + [pl.BlockSpec((2, part, width), lambda i: (i, 0, 0))] + flat * 5 + whole * 3,
        out_specs=flat * 4 + whole * 6,
        out_shape=[jax.ShapeDtypeStruct((rows, 128), F32)] * 4
        + [jax.ShapeDtypeStruct(share, F32)] * 3
        + [jax.ShapeDtypeStruct((1, 1), F32)] * 2 + [jax.ShapeDtypeStruct((1, 3), F32)],
        scratch_shapes=[pltpu.VMEM((6, part, 128), F32)],
        compiler_params=pltpu.CompilerParams(vmem_limit_bytes=VMEM_LIMIT),
    )(valid_len, step_count, squares, tile, quads, *flats, *gains)


def body(
    x_in, targets, valid_len, present_stems, w_master, norm_gains, gain_m, gain_v,
    l_stats, r_stats, l_roots, r_roots, step_count,
):
    width = x_in.shape[1]
    part = width // 4
    layers = lax.axis_size("section")
    groups = lax.axis_size("dp")
    micro = valid_len.shape[0] // groups
    own_blocks = w_master.shape[1]
    flats = [flat_rows(a[0]) for a in (w_master, l_stats, r_stats, l_roots, r_roots)]
    *saved, sent, loss_grad, stats, full_w, full_g = forward(
        layers, micro, valid_len, present_stems, x_in, targets, flats[0], norm_gains[0]
    )
    own_quads, tile, squares = backward(layers, loss_grad, full_w, full_g, sent, saved, stats)
    clip_limit = 0.00015 * math.sqrt(layers * (own_blocks * groups * part * part + 2 * width))
    *news, gains_new, m_new, v_new, loss_value, grad_norm, rms = update(
        layers, clip_limit, valid_len, step_count, squares, tile, own_quads.reshape(-1, part, width), flats,
        (norm_gains[0], gain_m[0], gain_v[0]),
    )
    w_new, grad_blocks, l_new, r_new = (from_flat_rows(a, own_blocks)[None] for a in news)
    return (
        w_new,
        grad_blocks,
        l_new,
        r_new,
        gains_new[None],
        m_new[None],
        v_new[None],
        loss_value.reshape(()),
        grad_norm.reshape(()),
        rms,
    )


def solution(mesh):
    def step(*args):
        layers, groups = mesh.shape["section"], mesh.shape["dp"]
        micro, own_blocks = args[2].shape[0] // groups, args[4].shape[1]
        if micro <= layers == 4 and groups == 8 and own_blocks == 24:
            return body(*args)
        return pipelined_body(*args)

    block = P("section", "dp", None)
    gain = P("section", None, "dp")
    return jax.shard_map(
        step,
        mesh=mesh,
        in_specs=(
            P("dp", None), P("dp", None), P(), P(), block, gain, gain, gain, block, block, block, block, P(),
        ),
        out_specs=(block, block, block, block, gain, gain, gain, P(), P(), P("section", None)),
        check_vma=False,
    )
```
